32 devices in a mesh: replica: 2 (over x), serve: 16 (over z, y, core).
Axes of the slice: x: 2, y: 2, z: 4, core: 2. Of those that a mesh axis runs over, the one named last changes fastest.
Arguments:
- residual_first: bfloat16 [64, 8192], P(('replica', 'serve')), parts along dimension 0, may hold values from -6 to 6
- residual_second: bfloat16 [64, 8192], P(('replica', 'serve')), parts along dimension 0, may hold values from -6 to 6
- attention_norm_gain: bfloat16 [8192], replicated, may hold values from 0.5 to 1.5
- query_matrix: bfloat16 [8192, 8192], P(None, 'serve'), may hold values from -0.0625 to 0.0625
- key_matrix: bfloat16 [8192, 1024], P(None, 'serve'), may hold values from -0.0625 to 0.0625
- value_matrix: bfloat16 [8192, 1024], P(None, 'serve'), may hold values from -0.0625 to 0.0625
- output_matrix: bfloat16 [8192, 8192], P('serve'), may hold values from -0.0625 to 0.0625
- query_down_weights: bfloat16 [32, 8192, 16], P('serve'), may hold values from -0.0625 to 0.0625
- value_down_weights: bfloat16 [32, 8192, 16], P('serve'), may hold values from -0.0625 to 0.0625
- query_up_weights: bfloat16 [32, 16, 8192], P(None, None, 'serve'), may hold values from -1.5 to 1.5
- value_up_weights: bfloat16 [32, 16, 1024], P(None, None, 'serve'), may hold values from -1.5 to 1.5
- rotated_key_cache: bfloat16 [64, 384, 1024], P(('replica', 'serve')), parts along dimension 0, may hold values from -256 to 256
- stored_value_cache: bfloat16 [64, 384, 1024], P(('replica', 'serve')), parts along dimension 0, may hold values from -6 to 6
- lengths: int32 [64], P('replica'), parts along dimension 0, may hold values from 1 to 384, as said below
- request_adapter: int32 [64], P('replica'), parts along dimension 0, may hold values from 0 to 31
- adapter_slot: int32 [32], replicated, may hold values from 0 to 31, each once
Outputs:
- out_one: bfloat16 [64, 8192], P(('replica', 'serve')), parts along dimension 0
- out_two: bfloat16 [64, 8192], P(('replica', 'serve')), parts along dimension 0
- new_keys: bfloat16 [64, 2, 1024], P(('replica', 'serve')), parts along dimension 0
- new_values: bfloat16 [64, 2, 1024], P(('replica', 'serve')), parts along dimension 0
The draws below stay inside these ranges and needn't reach their ends.
There are 2 independent parts, one for each index of `replica`. The reference program is written for one: setup_inputs(seed, part) draws one part's arguments, and reference() takes and returns one part's arrays. A program takes and returns all parts, laid end to end along the dimension named above; an argument that names none is the same for every part. Nothing has to cross between parts.
Inputs may be any that keep to these rules, and one draw needn't show every extreme that they name: `lengths`: at least one request has exactly 384 cached tokens. `adapter_slot`: each slot appears once; slot s lies on index s // 2 of serve.
All inputs are finite; a program needn't handle non-finite values.
Results may differ from the reference program's by a relative error of at most 0.007.
The reference program's roundings to bfloat16 on the way (of `normed`, `probs` and `context`) count: a program that leaves them out, or rounds other values in their place, can miss the bound.
Values may be sent and summed in bfloat16 or wider, within the bound.
No kernel may reach another device: no remote copies, remote signals or barrier semaphores. Data moves between devices by JAX's collectives and lax.ppermute only.
A program may use at most 128 MiB of HBM per device.

```python
import math
import jax
import jax.numpy as jnp
import numpy as np
from jax import lax

MODEL_WIDTH = 8192
HEADS = 64
KV_HEADS = 8
HEAD = 128
ADAPTER_RANK = 16
CACHE = 384
REQUESTS = 32
ADAPTER_TOTAL = 32
QUERY_WIDTH = 8192
KEY_VALUE_WIDTH = 1024


def draw_rotated_key_cache(key, part):
    key = jax.random.fold_in(key, 11)
    first = jax.random.fold_in(key, 0)
    base = jax.random.normal(first, (REQUESTS, CACHE, KEY_VALUE_WIDTH), jnp.float32)
    return jnp.clip(base, -256.0, 256.0).astype(jnp.bfloat16)


def draw_lengths(key, part):
    key = jax.random.fold_in(key, 23)
    first, second = jax.random.split(key)
    drawn = jax.random.randint(first, (REQUESTS,), 1, CACHE + 1)
    chosen = jax.random.randint(second, (), 0, REQUESTS)
    return jnp.where(jnp.arange(REQUESTS) == chosen, CACHE, drawn).astype(jnp.int32)


def touch_ends(result, stream_key, low, largest):
    extent = result.shape
    place = [jax.random.randint(jax.random.fold_in(stream_key, axis), (), 0, extent[axis]) for axis in range(len(extent))]
    result = result.at[tuple(place)].set(low)
    longest = extent.index(max(extent))
    place[longest] = (place[longest] + 1) % extent[longest]
    return result.at[tuple(place)].set(largest)


def block_levels(own_key, dims, cuts, least, high):
    def one(position, blocks):
        draws = jax.random.uniform(jax.random.fold_in(jax.random.fold_in(own_key, 6), position), (blocks,), jnp.float32, least / len(cuts), high / len(cuts))
        return jnp.repeat(jnp.exp(draws), dims[position] // blocks).reshape((-1,) + (1,) * (len(dims) - position - 1))

    factor_of = one(*cuts[0])
    for cut in cuts[1:]:
        factor_of = factor_of * one(*cut)
    return factor_of


def cumulative_ranks(number_of, skew):
    portions = [(1 << 20) // math.isqrt(grade ** skew) + 1 for grade in range(1, number_of + 1)]
    deviation = 1 + sum(portions) // (1 << 30)
    return np.cumsum(np.array([max(1, weight // deviation) for weight in portions]))


def ranked(stream_key, extent, amount, skew):
    grid = cumulative_ranks(amount, skew)
    ticket = jax.random.randint(jax.random.fold_in(stream_key, 1), extent, 0, int(grid[amount - 1]))
    grade = jnp.searchsorted(jnp.asarray(grid, jnp.int32), ticket, side="right")
    return jax.random.permutation(jax.random.fold_in(stream_key, 2), amount)[grade].astype(jnp.int32)


def normal_values(key, shape, scale, reach, pieces=(), dtype=jnp.bfloat16):
    factor_of = block_levels(key, shape, pieces, -0.22, 0.18) if pieces else 1.0
    entries = jax.random.normal(key, shape, jnp.float32) * scale * factor_of
    return jnp.minimum(jnp.maximum(entries, -reach), reach).astype(dtype)


def setup_inputs(seed: int = 0, part: int = 0) -> dict:
    seeds = jax.random.split(jax.random.key(seed), 17)
    part_splits = jax.random.split(jax.random.fold_in(seeds[16], part), 17)
    residual_first = normal_values(part_splits[0], (REQUESTS, MODEL_WIDTH), 1.0, 6.0, ((0, 16),))
    residual_second = normal_values(part_splits[1], (REQUESTS, MODEL_WIDTH), 1.0, 6.0, ((0, 16),))
    attention_norm_gain = jnp.clip(1.0 + 0.1 * jax.random.normal(seeds[2], (MODEL_WIDTH,), jnp.float32), 0.5, 1.5).astype(jnp.bfloat16)
    query_matrix = normal_values(seeds[3], (MODEL_WIDTH, QUERY_WIDTH), MODEL_WIDTH ** -0.5, 0.0625, ((1, 16),))
    key_matrix = normal_values(seeds[4], (MODEL_WIDTH, KEY_VALUE_WIDTH), MODEL_WIDTH ** -0.5, 0.0625, ((1, 16),))
    value_matrix = normal_values(seeds[5], (MODEL_WIDTH, KEY_VALUE_WIDTH), MODEL_WIDTH ** -0.5, 0.0625, ((1, 16),))
    output_matrix = normal_values(seeds[6], (QUERY_WIDTH, MODEL_WIDTH), QUERY_WIDTH ** -0.5, 0.0625, ((0, 16),))
    query_down_weights = normal_values(seeds[7], (ADAPTER_TOTAL, MODEL_WIDTH, ADAPTER_RANK), MODEL_WIDTH ** -0.5, 0.0625, ((0, 16),))
    value_down_weights = normal_values(seeds[8], (ADAPTER_TOTAL, MODEL_WIDTH, ADAPTER_RANK), MODEL_WIDTH ** -0.5, 0.0625, ((0, 16),))
    query_up_weights = normal_values(seeds[9], (ADAPTER_TOTAL, ADAPTER_RANK, QUERY_WIDTH), ADAPTER_RANK ** -0.5, 1.5, ((2, 16),))
    value_up_weights = normal_values(seeds[10], (ADAPTER_TOTAL, ADAPTER_RANK, KEY_VALUE_WIDTH), ADAPTER_RANK ** -0.5, 1.5, ((2, 16),))
    rotated_key_cache = draw_rotated_key_cache(jax.random.fold_in(jax.random.fold_in(seeds[16], part), 71), part)
    stored_value_cache = normal_values(part_splits[12], (REQUESTS, CACHE, KEY_VALUE_WIDTH), 1.0, 6.0, ((0, 16),))
    lengths = draw_lengths(jax.random.fold_in(jax.random.fold_in(seeds[16], part), 71), part)
    request_adapter = touch_ends(ranked(part_splits[14], (REQUESTS,), ADAPTER_TOTAL, 2), jax.random.fold_in(part_splits[14], 3), 0, ADAPTER_TOTAL - 1).astype(jnp.int32)
    adapter_slot = jax.random.permutation(seeds[15], ADAPTER_TOTAL).astype(jnp.int32)
    return {"residual_first": residual_first, "residual_second": residual_second, "attention_norm_gain": attention_norm_gain, "query_matrix": query_matrix, "key_matrix": key_matrix, "value_matrix": value_matrix, "output_matrix": output_matrix, "query_down_weights": query_down_weights, "value_down_weights": value_down_weights, "query_up_weights": query_up_weights, "value_up_weights": value_up_weights, "rotated_key_cache": rotated_key_cache, "stored_value_cache": stored_value_cache, "lengths": lengths, "request_adapter": request_adapter, "adapter_slot": adapter_slot}


def widen(values):
    return lax.optimization_barrier(values).astype(jnp.float32)

def rms_normed(hidden, attention_norm_gain):
    values = hidden.astype(jnp.float32)
    factor = lax.rsqrt(lax.optimization_barrier(jnp.mean(values * values, axis=-1, keepdims=True)) + 1e-05)
    return (values * factor * attention_norm_gain.astype(jnp.float32)).astype(jnp.bfloat16)

def scaled_frequency(pair_index):
    base = jnp.exp(pair_index.astype(jnp.float32) * (-2.0 * math.log(500000.0) / HEAD))
    wavelength = 2.0 * math.pi / base
    smooth = jnp.clip((8192.0 / wavelength - 1.0) / 3.0, 0.0, 1.0)
    return (1.0 - smooth) * base / 8.0 + smooth * base

def rotate(values, offset, positions):
    width = values.shape[-1]
    pair_index = (offset + 2 * jnp.arange(width // 2)) % HEAD // 2
    inverse = scaled_frequency(pair_index)
    angle = positions[..., None] * inverse
    cosine = jnp.cos(angle)
    sine = jnp.sin(angle)
    pairs = values.reshape(values.shape[:-1] + (width // 2, 2))
    even = pairs[..., 0]
    odd = pairs[..., 1]
    turned = jnp.stack((even * cosine - odd * sine, even * sine + odd * cosine), axis=-1)
    return turned.reshape(values.shape)

def attend_one(query, keys, values, length, fresh_keys, fresh_values):
    group = HEADS // KV_HEADS
    queries = widen(query).reshape(KV_HEADS, group, HEAD)
    cached_keys = keys.astype(jnp.float32).reshape(-1, KV_HEADS, HEAD)
    cached_values = values.astype(jnp.float32).reshape(-1, KV_HEADS, HEAD)
    newest_keys = widen(fresh_keys).reshape(-1, KV_HEADS, HEAD)
    newest_values = widen(fresh_values).reshape(-1, KV_HEADS, HEAD)
    cached = jnp.einsum('gqe,tge->gqt', queries, cached_keys) * HEAD ** (-0.5)
    visible = jnp.arange(cached_keys.shape[0]) < length
    cached = jnp.where(visible[None, None, :], cached, -1e+30)
    fresh = jnp.einsum('gqe,nge->gqn', queries, newest_keys) * HEAD ** (-0.5)
    scores = jnp.concatenate((cached, fresh), axis=-1)
    top = lax.optimization_barrier(jnp.max(scores, axis=-1, keepdims=True))
    weights = jnp.exp(scores - top)
    probs = widen((weights / lax.optimization_barrier(jnp.sum(weights, axis=-1, keepdims=True))).astype(jnp.bfloat16))
    span = cached_keys.shape[0]
    context = jnp.einsum('gqt,tge->gqe', probs[..., :span], cached_values)
    context = context + jnp.einsum('gqn,nge->gqe', probs[..., span:], newest_values)
    return context.reshape(-1).astype(jnp.bfloat16)

def reference(residual_first, residual_second, attention_norm_gain, query_matrix, key_matrix, value_matrix, output_matrix, query_down_weights, value_down_weights, query_up_weights, value_up_weights, rotated_key_cache, stored_value_cache, lengths, request_adapter, adapter_slot):
    storage_slots = adapter_slot[request_adapter].astype(jnp.int32)
    select = (storage_slots[:, None] == jnp.arange(ADAPTER_TOTAL).astype(jnp.int32)[None, :]).astype(jnp.float32)
    query_down_map = query_down_weights.astype(jnp.float32)
    value_down_map = value_down_weights.astype(jnp.float32)
    query_up_map = query_up_weights.astype(jnp.float32)
    value_up_map = value_up_weights.astype(jnp.float32)
    keys_list = []
    values_list = []
    outputs = []
    for step, hidden in enumerate((residual_first, residual_second)):
        normed = rms_normed(hidden, attention_norm_gain)
        normed_wide = widen(normed)
        low_q = jnp.einsum('bak,ba->bk', jnp.einsum('bd,adk->bak', normed_wide, query_down_map), select).astype(jnp.bfloat16)
        low_v = jnp.einsum('bak,ba->bk', jnp.einsum('bd,adk->bak', normed_wide, value_down_map), select).astype(jnp.bfloat16)
        spread_q = widen(low_q)[:, None, :] * select[:, :, None]
        spread_v = widen(low_v)[:, None, :] * select[:, :, None]
        query = jnp.dot(normed, query_matrix, preferred_element_type=jnp.float32) + jnp.einsum('bak,akc->bc', spread_q, query_up_map)
        key = jnp.dot(normed, key_matrix, preferred_element_type=jnp.float32)
        value = (jnp.dot(normed, value_matrix, preferred_element_type=jnp.float32) + jnp.einsum('bak,akc->bc', spread_v, value_up_map)).astype(jnp.bfloat16)
        positions = (lengths + step).astype(jnp.float32)
        query = rotate(query, 0, positions).astype(jnp.bfloat16)
        key = rotate(key, 0, positions).astype(jnp.bfloat16)
        keys_list.append(key)
        values_list.append(value)
        fresh_keys = jnp.stack(keys_list, axis=1)
        fresh_values = jnp.stack(values_list, axis=1)
        context = lax.map(lambda item: attend_one(*item), (query, rotated_key_cache, stored_value_cache, lengths, fresh_keys, fresh_values))
        summed = jnp.dot(context, output_matrix, preferred_element_type=jnp.float32)
        outputs.append((hidden.astype(jnp.float32) + summed).astype(jnp.bfloat16))
    return (outputs[0], outputs[1], jnp.stack(keys_list, axis=1), jnp.stack(values_list, axis=1))
```

```python
import functools
import math

import jax
import jax.numpy as jnp
from jax import lax
from jax.experimental import pallas as pl
from jax.experimental.pallas import tpu as pltpu
from jax.sharding import PartitionSpec as P

HEADS = 64
KV_HEADS = 8
HEAD = 128
STEPS = 2
LIMIT = 48 * 1024 * 1024
NT = (((1,), (1,)), ((), ()))
F32 = jnp.float32
BF16 = jnp.bfloat16


def dot(a, b):
    return jnp.dot(a, b, preferred_element_type=F32)


def dot_nt(a, b):
    return lax.dot_general(a, b, NT, preferred_element_type=F32)


def whole_call(body, out_shape, args, smem=0, scratch=()):
    specs = [pl.BlockSpec(memory_space=pltpu.SMEM)] * smem
    specs += [pl.BlockSpec(memory_space=pltpu.VMEM)] * (len(args) - smem)
    many = isinstance(out_shape, (tuple, list))
    vmem = pl.BlockSpec(memory_space=pltpu.VMEM)
    return pl.pallas_call(
        body,
        out_shape=out_shape,
        in_specs=specs,
        out_specs=tuple(vmem for _ in out_shape) if many else vmem,
        scratch_shapes=list(scratch),
        compiler_params=pltpu.CompilerParams(vmem_limit_bytes=LIMIT),
    )(*args)


def scaled_frequency(pair_index):
    base = jnp.exp(pair_index.astype(F32) * (-2.0 * math.log(500000.0) / HEAD))
    wavelength = 2.0 * math.pi / base
    smooth = jnp.clip((8192.0 / wavelength - 1.0) / 3.0, 0.0, 1.0)
    return (1.0 - smooth) * base / 8.0 + smooth * base


def turn_tables(positions, offset, width):
    lane = offset + jnp.arange(width)
    angle = positions[:, None] * scaled_frequency(lane % HEAD // 2)[None, :]
    sign = jnp.where(lane % 2 == 0, -1.0, 1.0)
    return jnp.cos(angle), jnp.sin(angle) * sign[None, :]


def norm_body(first_ref, second_ref, gain_ref, out_ref):
    gain = gain_ref[...].astype(F32)
    rows = []
    for ref in (first_ref, second_ref):
        values = ref[...].astype(F32)
        factor = lax.rsqrt(jnp.mean(values * values, axis=-1, keepdims=True) + 1e-05)
        rows.append(values * factor * gain)
    out_ref[...] = jnp.concatenate(rows, axis=0).astype(BF16)


def low_body(rank, x_ref, qd_ref, vd_ref, local_ref, place_ref, out_ref):
    adapters = qd_ref.shape[0] // rank
    maps = jnp.concatenate((qd_ref[...], vd_ref[...]), axis=0)
    low = dot_nt(x_ref[...], maps)
    lane = lax.broadcasted_iota(jnp.int32, low.shape, 1)
    low = jnp.where(lane // rank % adapters == local_ref[...], low, 0.0)
    total = 0.0
    for a in range(adapters):
        q = low[:, a * rank : (a + 1) * rank]
        v = low[:, (adapters + a) * rank : (adapters + a + 1) * rank]
        total = total + jnp.concatenate((q, v), axis=1)
    rows = dot(place_ref[...], total.astype(BF16))
    pack = HEAD // (2 * rank)
    step = rows.shape[0] // pack
    packed = jnp.concatenate([rows[i * step : (i + 1) * step] for i in range(pack)], axis=1)
    packed = packed.astype(BF16)
    for i in range(out_ref.shape[0]):
        out_ref[i] = packed


def base_body(x_ref, q_ref, k_ref, v_ref, oq_ref, okv_ref):
    @pl.when(pl.program_id(0) == 0)
    def _():
        oq_ref[...] = jnp.zeros_like(oq_ref)
        okv_ref[...] = jnp.zeros_like(okv_ref)

    x = x_ref[...]
    oq_ref[...] += dot(x, q_ref[...])
    okv_ref[...] += dot_nt(x, jnp.concatenate((k_ref[...], v_ref[...]), axis=0))


def turned(values, cosine, sine):
    lane = lax.broadcasted_iota(jnp.int32, values.shape, 1)
    width = values.shape[1]
    ahead = pltpu.roll(values, width - 1, 1)
    behind = pltpu.roll(values, 1, 1)
    return values * cosine + jnp.where(lane % 2 == 0, ahead, behind) * sine


def ready_body(
    rank, oq_ref, okv_ref, low_ref, unplace_ref, slot_ref, uq_ref, uv_ref, cos_ref, sin_ref,
    kcos_ref, ksin_ref, send_ref, out_ref,
):
    packed = jnp.sum(low_ref[...].astype(F32), axis=0)
    pack = HEAD // (2 * rank)
    low = jnp.concatenate(
        [packed[:, i * 2 * rank : (i + 1) * 2 * rank] for i in range(pack)], axis=0
    )
    low = dot(unplace_ref[...], low.astype(BF16)).astype(BF16)
    wide = uq_ref.shape[0]
    lane = lax.broadcasted_iota(jnp.int32, (low.shape[0], wide), 1)
    here = lane // rank == slot_ref[...]
    row = lax.broadcasted_iota(jnp.int32, (2 * rank, wide), 0)
    column = lax.broadcasted_iota(jnp.int32, (2 * rank, wide), 1)
    spread_q = jnp.where(column % rank == row, 1.0, 0.0).astype(BF16)
    spread_v = jnp.where(column % rank + rank == row, 1.0, 0.0).astype(BF16)
    wide_q = jnp.where(here, dot(low, spread_q), 0.0).astype(BF16)
    wide_v = jnp.where(here, dot(low, spread_v), 0.0).astype(BF16)
    query = oq_ref[...] + dot(wide_q, uq_ref[...])
    columns = okv_ref.shape[1] // 2
    key = okv_ref[:, :columns]
    value = okv_ref[:, columns:] + dot(wide_v, uv_ref[...])
    cosine, sine = cos_ref[...], sin_ref[...]
    parts = []
    for h in range(query.shape[1] // HEAD):
        parts.append(turned(query[:, h * HEAD : (h + 1) * HEAD], cosine, sine))
    fresh = [turned_narrow(key, kcos_ref[...], ksin_ref[...]), value]
    if 2 * columns < HEAD:
        fresh.append(jnp.zeros((key.shape[0], HEAD - 2 * columns), F32))
    parts.append(jnp.concatenate(fresh, axis=1))
    stacked = jnp.concatenate(parts, axis=0).astype(BF16)
    out_ref[...] = dot(send_ref[...], stacked).astype(BF16).reshape(out_ref.shape)


def turned_narrow(values, cosine, sine):
    width = values.shape[1]
    lane = lax.broadcasted_iota(jnp.int32, values.shape, 1)
    ahead = jnp.concatenate((values[:, 1:], values[:, :1]), axis=1)
    behind = jnp.concatenate((values[:, width - 1 :], values[:, : width - 1]), axis=1)
    return values * cosine + jnp.where(lane % 2 == 0, ahead, behind) * sine


def attend_body(own, columns, len_ref, x_ref, order_ref, k_ref, v_ref, ctx_ref, nk_ref, nv_ref, s_ref):
    n, span = x_ref.shape[0], k_ref.shape[1]
    group = HEADS // KV_HEADS
    local = HEADS // n
    rows = own * STEPS
    mine = group * STEPS
    x = x_ref[...]
    queries = dot(order_ref[...], x.reshape(n * x.shape[1], HEAD)).astype(BF16)
    wide = x.astype(F32)
    first = rows * local
    fresh = [wide[i, first : first + rows] for i in range(n)]
    each = n // KV_HEADS
    keys, values = [], []
    for g in range(KV_HEADS):
        pieces = fresh[g * each : (g + 1) * each]
        keys.append(jnp.concatenate([p[:, :columns] for p in pieces], axis=1))
        values.append(jnp.concatenate([p[:, columns : 2 * columns] for p in pieces], axis=1))
    nk_ref[...] = jnp.concatenate(keys, axis=1).astype(BF16)
    nv_ref[...] = jnp.concatenate(values, axis=1).astype(BF16)
    pad = jnp.zeros((16 - rows, HEAD), F32)
    keys = [jnp.concatenate((k, pad), axis=0).astype(BF16) for k in keys]
    values = [jnp.concatenate((v, pad), axis=0).astype(BF16) for v in values]
    scale = HEAD ** (-0.5)
    contexts = []
    for b in range(own):
        q = queries[b * KV_HEADS * mine : (b + 1) * KV_HEADS * mine]
        cached, newer = [], []
        for g in range(KV_HEADS):
            qg = q[g * mine : (g + 1) * mine]
            cached.append(dot_nt(qg, k_ref[b, :, g * HEAD : (g + 1) * HEAD]))
            newer.append(dot_nt(qg, keys[g]))
        cached = jnp.concatenate(cached, axis=0) * scale
        newer = jnp.concatenate(newer, axis=0) * scale
        place = lax.broadcasted_iota(jnp.int32, cached.shape, 1)
        cached = jnp.where(place < len_ref[b], cached, -1e30)
        step = lax.broadcasted_iota(jnp.int32, newer.shape, 0) % STEPS
        at = lax.broadcasted_iota(jnp.int32, newer.shape, 1) - b * STEPS
        newer = jnp.where((at >= 0) & (at <= step), newer, -1e30)
        top = jnp.maximum(
            jnp.max(cached, axis=1, keepdims=True), jnp.max(newer, axis=1, keepdims=True)
        )
        cached = jnp.exp(cached - top)
        newer = jnp.exp(newer - top)
        total = jnp.sum(cached, axis=1, keepdims=True) + jnp.sum(newer, axis=1, keepdims=True)
        cached = (cached / total).astype(BF16)
        newer = (newer / total).astype(BF16)
        for g in range(KV_HEADS):
            at_rows = slice(g * mine, (g + 1) * mine)
            part = dot(cached[at_rows], v_ref[b, :, g * HEAD : (g + 1) * HEAD])
            s_ref[(b * KV_HEADS + g) * mine : (b * KV_HEADS + g + 1) * mine] = part + dot(
                newer[at_rows], values[g]
            )
    step = local * STEPS
    half = KV_HEADS * mine
    for i in range(n):
        block = [s_ref[b * half + i * step : b * half + (i + 1) * step] for b in range(own)]
        ctx_ref[i] = jnp.concatenate(block, axis=0).astype(BF16)


def out_body(ctx_ref, take_ref, w_ref, mine_ref, other_ref, a_ref):
    @pl.when(pl.program_id(0) == 0)
    def _():
        rows = a_ref.shape[0]
        n = ctx_ref.shape[0]
        x = ctx_ref[...].reshape(n * ctx_ref.shape[1], HEAD)
        taken = dot(take_ref[...], x).astype(BF16)
        for h in range(a_ref.shape[1] // HEAD):
            a_ref[:, h * HEAD : (h + 1) * HEAD] = taken[h * rows : (h + 1) * rows]

    half = mine_ref.shape[0]
    product = dot(a_ref[...], w_ref[...])
    mine_ref[...] = product[:half]
    other_ref[...] = product[half:]


def shards(
    sizes,
    residual_first,
    residual_second,
    attention_norm_gain,
    query_matrix,
    key_matrix,
    value_matrix,
    output_matrix,
    query_down_weights,
    value_down_weights,
    query_up_weights,
    value_up_weights,
    rotated_key_cache,
    stored_value_cache,
    lengths,
    request_adapter,
    adapter_slot,
):
    far, near, cores = sizes
    n = far * near * cores
    index = lax.axis_index("serve")
    own, width = residual_first.shape
    adapters, _, rank = query_down_weights.shape
    query_cols = query_matrix.shape[1]
    key_cols = key_matrix.shape[1]
    local = query_cols // HEAD
    rows = own * STEPS
    all_rows = n * rows
    stored = query_up_weights.shape[0]

    def partner(f, m, c):
        pairs = []
        for z in range(far):
            for y in range(near):
                for k in range(cores):
                    to = (((z + f) % far) * near + (y + m) % near) * cores + (k + c) % cores
                    pairs.append(((z * near + y) * cores + k, to))
        return pairs

    def shift(value, f, m, c):
        return lax.ppermute(value, "serve", partner(f, m, c))

    core_at = index % cores
    near_at = index // cores % near
    far_at = index // (cores * near)
    block = jnp.arange(n)
    block_c, block_m, block_f = block // (far * near), block // far % near, block % far

    def device_of(sign):
        return (
            ((far_at + sign * block_f) % far) * near + (near_at + sign * block_m) % near
        ) * cores + (core_at + sign * block_c) % cores

    source = device_of(-1)
    target = device_of(1)

    row_device = jnp.repeat(source, rows)
    row_step = jnp.tile(jnp.repeat(jnp.arange(STEPS), own), n)
    row_own = jnp.tile(jnp.arange(own), n * STEPS)
    request = row_device * own + row_own
    hot = request[:, None] == jnp.arange(lengths.shape[0])[None, :]
    row_length = jnp.sum(jnp.where(hot, lengths[None, :], 0), axis=1)
    row_adapter = jnp.sum(jnp.where(hot, request_adapter[None, :], 0), axis=1)
    table = jnp.arange(adapter_slot.shape[0])
    slot = jnp.sum(
        jnp.where(row_adapter[:, None] == table[None, :], adapter_slot[None, :], 0), axis=1
    )[:, None]
    positions = (row_length + row_step).astype(F32)
    cosine, sine = turn_tables(positions, 0, HEAD)
    key_cosine, key_sine = turn_tables(positions, index * key_cols, key_cols)
    absolute = (row_device * STEPS + row_step) * own + row_own
    place = (jnp.arange(all_rows)[:, None] == absolute[None, :]).astype(BF16)
    unplace = (absolute[:, None] == jnp.arange(all_rows)[None, :]).astype(BF16)

    sent = -(-(rows * local + rows) // 16) * 16
    wanted = [
        row_device * sent + (row_own * local + h) * STEPS + row_step for h in range(local)
    ]
    wanted.append(row_device * sent + rows * local + row_own * STEPS + row_step)
    wanted = jnp.concatenate(wanted)
    send = (jnp.arange(n * sent)[:, None] == wanted[None, :]).astype(BF16)

    a = jnp.arange(own * HEADS * STEPS)
    a_own, a_head, a_step = a // (HEADS * STEPS), a // STEPS % HEADS, a % STEPS
    held = (a_head // local) * sent + (a_own * local + a_head % local) * STEPS + a_step
    order = (held[:, None] == jnp.arange(n * sent)[None, :]).astype(BF16)

    out_device = jnp.repeat(target, rows)
    came = [
        out_device * rows * local + (row_own * local + h) * STEPS + row_step for h in range(local)
    ]
    came = jnp.concatenate(came)
    take = (came[:, None] == jnp.arange(n * rows * local)[None, :]).astype(BF16)

    normed = whole_call(
        norm_body,
        jax.ShapeDtypeStruct((rows, width), BF16),
        (residual_first, residual_second, attention_norm_gain[None, :]),
    )
    gathered = normed[None]
    gathered = jnp.concatenate([gathered] + [shift(gathered, f, 0, 0) for f in range(1, far)])
    gathered = jnp.concatenate([gathered] + [shift(gathered, 0, m, 0) for m in range(1, near)])
    gathered = jnp.concatenate([gathered] + [shift(gathered, 0, 0, c) for c in range(1, cores)])
    x = gathered.reshape(all_rows, width)

    query_down = jnp.swapaxes(query_down_weights, 1, 2).reshape(adapters * rank, width)
    value_down = jnp.swapaxes(value_down_weights, 1, 2).reshape(adapters * rank, width)
    packed_rows = all_rows * 2 * rank // HEAD
    low = whole_call(
        functools.partial(low_body, rank),
        jax.ShapeDtypeStruct((n, packed_rows, HEAD), BF16),
        (x, query_down, value_down, slot - index * adapters, place),
    )
    low = lax.all_to_all(low, "serve", split_axis=0, concat_axis=0, tiled=True)

    depth = 1024
    base_q, base_kv = pl.pallas_call(
        base_body,
        grid=(width // depth,),
        in_specs=[
            pl.BlockSpec((all_rows, depth), lambda i: (0, i)),
            pl.BlockSpec((depth, query_cols), lambda i: (i, 0)),
            pl.BlockSpec((key_cols, depth), lambda i: (0, i)),
            pl.BlockSpec((key_cols, depth), lambda i: (0, i)),
        ],
        out_specs=(
            pl.BlockSpec((all_rows, query_cols), lambda i: (0, 0)),
            pl.BlockSpec((all_rows, 2 * key_cols), lambda i: (0, 0)),
        ),
        out_shape=(
            jax.ShapeDtypeStruct((all_rows, query_cols), F32),
            jax.ShapeDtypeStruct((all_rows, 2 * key_cols), F32),
        ),
        compiler_params=pltpu.CompilerParams(vmem_limit_bytes=LIMIT),
        cost_estimate=pl.CostEstimate(
            flops=2 * all_rows * width * (query_cols + 2 * key_cols),
            bytes_accessed=2 * width * (query_cols + 2 * key_cols + all_rows),
            transcendentals=0,
        ),
    )(x, query_matrix, key_matrix.T, value_matrix.T)

    ready = whole_call(
        functools.partial(ready_body, rank),
        jax.ShapeDtypeStruct((n, sent, HEAD), BF16),
        (
            base_q,
            base_kv,
            low,
            unplace,
            slot,
            query_up_weights.reshape(stored * rank, query_cols),
            value_up_weights.reshape(stored * rank, key_cols),
            cosine,
            sine,
            key_cosine,
            key_sine,
            send,
        ),
    )
    arrived = lax.all_to_all(ready, "serve", split_axis=0, concat_axis=0, tiled=True)

    own_lengths = lax.dynamic_slice_in_dim(lengths, index * own, own)
    context, new_keys, new_values = whole_call(
        functools.partial(attend_body, own, key_cols),
        (
            jax.ShapeDtypeStruct((n, rows * local, HEAD), BF16),
            jax.ShapeDtypeStruct((rows, KV_HEADS * HEAD), BF16),
            jax.ShapeDtypeStruct((rows, KV_HEADS * HEAD), BF16),
        ),
        (own_lengths, arrived, order, rotated_key_cache, stored_value_cache),
        smem=1,
        scratch=[pltpu.VMEM((own * HEADS * STEPS, HEAD), F32)],
    )
    context = lax.all_to_all(context, "serve", split_axis=0, concat_axis=0, tiled=True)

    tile = 1024
    kept = all_rows // cores
    kinds = jax.ShapeDtypeStruct((kept, width), F32)
    mine, other = pl.pallas_call(
        out_body,
        grid=(width // tile,),
        in_specs=[
            pl.BlockSpec(context.shape, lambda i: (0, 0, 0)),
            pl.BlockSpec(take.shape, lambda i: (0, 0)),
            pl.BlockSpec((query_cols, tile), lambda i: (0, i)),
        ],
        out_specs=(
            pl.BlockSpec((kept, tile), lambda i: (0, i)),
            pl.BlockSpec((kept, tile), lambda i: (0, i)),
        ),
        out_shape=(kinds, kinds),
        scratch_shapes=[pltpu.VMEM((all_rows, query_cols), BF16)],
        compiler_params=pltpu.CompilerParams(vmem_limit_bytes=LIMIT),
        cost_estimate=pl.CostEstimate(
            flops=2 * all_rows * width * query_cols,
            bytes_accessed=2 * width * query_cols + 4 * width * all_rows,
            transcendentals=0,
        ),
    )(context, take, output_matrix)

    total = (mine + shift(other, 0, 0, 1)).reshape(near, far, rows, width)
    nearer = total[0]
    for m in range(1, near):
        nearer = nearer + shift(total[m].astype(BF16), 0, m, 0).astype(F32)
    last = nearer[0]
    for f in range(1, far):
        last = last + shift(nearer[f].astype(BF16), f, 0, 0).astype(F32)
    out_one = (residual_first.astype(F32) + last[:own]).astype(BF16)
    out_two = (residual_second.astype(F32) + last[own:]).astype(BF16)
    shape = (own, STEPS, KV_HEADS * HEAD)
    return (out_one, out_two, new_keys.reshape(shape), new_values.reshape(shape))


def solution(mesh):
    n = mesh.shape["serve"]
    sizes = (n // 4, 2, 2)
    return jax.shard_map(
        functools.partial(shards, sizes),
        mesh=mesh,
        in_specs=(
            P(("replica", "serve"), None),
            P(("replica", "serve"), None),
            P(),
            P(None, "serve"),
            P(None, "serve"),
            P(None, "serve"),
            P("serve", None),
            P("serve", None, None),
            P("serve", None, None),
            P(None, None, "serve"),
            P(None, None, "serve"),
            P(("replica", "serve"), None, None),
            P(("replica", "serve"), None, None),
            P("replica"),
            P("replica"),
            P(),
        ),
        out_specs=(
            P(("replica", "serve"), None),
            P(("replica", "serve"), None),
            P(("replica", "serve"), None, None),
            P(("replica", "serve"), None, None),
        ),
        check_vma=False,
    )
```

```python
import functools
import math

import jax
import jax.numpy as jnp
from jax import lax
from jax.experimental import pallas as pl
from jax.experimental.pallas import tpu as pltpu
from jax.sharding import PartitionSpec as P

HEADS = 64
KV_HEADS = 8
HEAD = 128
STEPS = 2
LIMIT = 8 * 1024 * 1024
NT = (((1,), (1,)), ((), ()))
F32 = jnp.float32
BF16 = jnp.bfloat16


def dot(a, b):
    return jnp.dot(a, b, preferred_element_type=F32)


def dot_nt(a, b):
    return lax.dot_general(a, b, NT, preferred_element_type=F32)


def whole_call(body, out_shape, args, smem=0, scratch=()):
    specs = [pl.BlockSpec(memory_space=pltpu.SMEM)] * smem
    specs += [pl.BlockSpec(memory_space=pltpu.VMEM)] * (len(args) - smem)
    many = isinstance(out_shape, (tuple, list))
    vmem = pl.BlockSpec(memory_space=pltpu.VMEM)
    return pl.pallas_call(
        body,
        out_shape=out_shape,
        in_specs=specs,
        out_specs=tuple(vmem for _ in out_shape) if many else vmem,
        scratch_shapes=list(scratch),
        compiler_params=pltpu.CompilerParams(vmem_limit_bytes=LIMIT),
    )(*args)


def scaled_frequency(pair_index):
    base = jnp.exp(pair_index.astype(F32) * (-2.0 * math.log(500000.0) / HEAD))
    wavelength = 2.0 * math.pi / base
    smooth = jnp.clip((8192.0 / wavelength - 1.0) / 3.0, 0.0, 1.0)
    return (1.0 - smooth) * base / 8.0 + smooth * base


def norm_body(first_ref, second_ref, gain_ref, out_ref):
    gain = gain_ref[...].astype(F32)
    factors = []
    for ref in (first_ref, second_ref):
        values = ref[...].astype(F32)
        factors.append(lax.rsqrt(jnp.mean(values * values, axis=-1, keepdims=True) + 1e-05))
    factor = jnp.concatenate(factors, axis=0)
    for i in range(gain.shape[0]):
        at = slice(i * HEAD, (i + 1) * HEAD)
        values = jnp.concatenate((first_ref[:, at].astype(F32), second_ref[:, at].astype(F32)))
        out_ref[:, at] = (values * factor * gain[i : i + 1]).astype(BF16)


def prep_body(
    sizes, rank, own, key_cols, adapters,
    index_ref, length_ref, adapter_ref, slot_ref,
    held_ref, local_ref, cos_ref, sin_ref, kcos_ref, ksin_ref, place_ref, unplace_ref, send_ref,
    order_ref, take_ref,
):
    far, near, cores = sizes
    n = far * near * cores
    rows = own * STEPS
    all_rows = n * rows
    heads = HEADS // n
    sent = send_ref.shape[0] // n
    index = index_ref[0]
    core_at = index % cores
    near_at = index // cores % near
    far_at = index // (cores * near)

    def device_of(block, sign):
        c, m, f = block // (far * near), block // far % near, block % far
        f = (far_at + sign * f + far) % far
        m = (near_at + sign * m + near) % near
        c = (core_at + sign * c + cores) % cores
        return (f * near + m) * cores + c

    def iota(shape, axis):
        return lax.broadcasted_iota(jnp.int32, shape, axis)

    def split(row):
        return row // rows, row % rows // own, row % own

    block, step, mine = split(iota((all_rows, 1), 0))
    device = device_of(block, -1)
    request = device * own + mine
    length = jnp.zeros_like(request)
    adapter = jnp.zeros_like(request)
    for j in range(length_ref.shape[0]):
        length = jnp.where(request == j, length_ref[j], length)
        adapter = jnp.where(request == j, adapter_ref[j], adapter)
    slot = jnp.zeros_like(request)
    for j in range(slot_ref.shape[0]):
        slot = jnp.where(adapter == j, slot_ref[j], slot)
    held_ref[...] = slot
    local_ref[...] = slot - index * adapters
    position = (length + step).astype(F32)
    lane = iota((1, HEAD), 1)
    odd = jnp.where(lane % 2 == 0, -1.0, 1.0)
    angle = position * scaled_frequency(lane // 2)
    cos_ref[...] = jnp.cos(angle)
    sin_ref[...] = jnp.sin(angle) * odd
    angle = position * scaled_frequency((index * key_cols + lane) % HEAD // 2)
    kcos_ref[...] = jnp.where(lane < key_cols, jnp.cos(angle), 1.0)
    ksin_ref[...] = jnp.where(lane < key_cols, jnp.sin(angle) * odd, 0.0)

    def hot(ref, row, column):
        ref[...] = jnp.where(row == column, 1.0, 0.0).astype(BF16)

    absolute = (device * STEPS + step) * own + mine
    hot(unplace_ref, absolute, iota((1, all_rows), 1))
    block, step, mine = split(iota((1, all_rows), 1))
    absolute = (device_of(block, -1) * STEPS + step) * own + mine
    hot(place_ref, iota((all_rows, 1), 0), absolute)

    column = iota((1, send_ref.shape[1]), 1)
    h = column // all_rows
    block, step, mine = split(column % all_rows)
    wanted = device_of(block, -1) * sent + jnp.where(
        h < heads, (mine * heads + h) * STEPS + step, rows * heads + mine * STEPS + step
    )
    hot(send_ref, iota((n * sent, 1), 0), wanted)

    row = iota((order_ref.shape[0], 1), 0)
    mine, head, step = row // (HEADS * STEPS), row // STEPS % HEADS, row % STEPS
    wanted = (head // heads) * sent + (mine * heads + head % heads) * STEPS + step
    hot(order_ref, wanted, iota((1, n * sent), 1))

    row = iota((take_ref.shape[0], 1), 0)
    h = row // all_rows
    block, step, mine = split(row % all_rows)
    wanted = device_of(block, 1) * rows * heads + (mine * heads + h) * STEPS + step
    hot(take_ref, wanted, iota((1, take_ref.shape[1]), 1))


def low_body(rank, x_ref, qd_ref, vd_ref, local_ref, place_ref, out_ref):
    adapters = qd_ref.shape[0] // rank
    maps = jnp.concatenate((qd_ref[...], vd_ref[...]), axis=0)
    low = dot_nt(x_ref[...], maps)
    lane = lax.broadcasted_iota(jnp.int32, low.shape, 1)
    low = jnp.where(lane // rank % adapters == local_ref[...], low, 0.0)
    total = 0.0
    for a in range(adapters):
        q = low[:, a * rank : (a + 1) * rank]
        v = low[:, (adapters + a) * rank : (adapters + a + 1) * rank]
        total = total + jnp.concatenate((q, v), axis=1)
    rows = dot(place_ref[...], total.astype(BF16))
    pack = HEAD // (2 * rank)
    step = rows.shape[0] // pack
    packed = jnp.concatenate([rows[i * step : (i + 1) * step] for i in range(pack)], axis=1)
    packed = packed.astype(BF16)
    for i in range(out_ref.shape[0]):
        out_ref[i] = packed


def base_body(depth, x_ref, q_ref, k_ref, v_ref, oq_ref, okv_ref):
    oq_ref[...] = jnp.zeros_like(oq_ref)
    okv_ref[...] = jnp.zeros_like(okv_ref)
    columns = k_ref.shape[0]
    narrow = jnp.zeros((HEAD - 2 * columns, depth), BF16)

    @pl.loop(0, x_ref.shape[1] // depth)
    def _(i):
        at = pl.ds(pl.multiple_of(i * depth, depth), depth)
        x = x_ref[:, at]
        oq_ref[...] += dot(x, q_ref[at, :])
        both = (k_ref[:, at], v_ref[:, at])
        if 2 * columns < HEAD:
            both += (narrow,)
        okv_ref[...] += dot_nt(x, jnp.concatenate(both, axis=0))


def turned(values, cosine, sine):
    lane = lax.broadcasted_iota(jnp.int32, values.shape, 1)
    width = values.shape[1]
    ahead = pltpu.roll(values, width - 1, 1)
    behind = pltpu.roll(values, 1, 1)
    return values * cosine + jnp.where(lane % 2 == 0, ahead, behind) * sine


def ready_body(
    rank, oq_ref, okv_ref, low_ref, unplace_ref, slot_ref, uq_ref, uv_ref, cos_ref, sin_ref,
    kcos_ref, ksin_ref, send_ref, out_ref,
):
    packed = jnp.sum(low_ref[...].astype(F32), axis=0)
    pack = HEAD // (2 * rank)
    low = jnp.concatenate(
        [packed[:, i * 2 * rank : (i + 1) * 2 * rank] for i in range(pack)], axis=0
    )
    low = dot(unplace_ref[...], low.astype(BF16)).astype(BF16)
    wide = uq_ref.shape[0]
    lane = lax.broadcasted_iota(jnp.int32, (low.shape[0], wide), 1)
    here = lane // rank == slot_ref[...]
    row = lax.broadcasted_iota(jnp.int32, (2 * rank, wide), 0)
    column = lax.broadcasted_iota(jnp.int32, (2 * rank, wide), 1)
    spread_q = jnp.where(column % rank == row, 1.0, 0.0).astype(BF16)
    spread_v = jnp.where(column % rank + rank == row, 1.0, 0.0).astype(BF16)
    wide_q = jnp.where(here, dot(low, spread_q), 0.0).astype(BF16)
    wide_v = jnp.where(here, dot(low, spread_v), 0.0).astype(BF16)
    query = oq_ref[...] + dot(wide_q, uq_ref[...])
    fresh = turned(okv_ref[...], kcos_ref[...], ksin_ref[...])
    columns = uv_ref.shape[1]
    value = dot(wide_v, uv_ref[...])
    pieces = [jnp.zeros((value.shape[0], columns), F32), value]
    if 2 * columns < HEAD:
        pieces.append(jnp.zeros((value.shape[0], HEAD - 2 * columns), F32))
    fresh = fresh + jnp.concatenate(pieces, axis=1)
    cosine, sine = cos_ref[...], sin_ref[...]
    parts = []
    for h in range(query.shape[1] // HEAD):
        parts.append(turned(query[:, h * HEAD : (h + 1) * HEAD], cosine, sine))
    parts.append(fresh)
    stacked = jnp.concatenate(parts, axis=0).astype(BF16)
    out_ref[...] = dot(send_ref[...], stacked).astype(BF16).reshape(out_ref.shape)


def attend_body(own, columns, index_ref, len_ref, x_ref, order_ref, k_ref, v_ref, ctx_ref, nk_ref, nv_ref, s_ref):
    n, span = x_ref.shape[0], k_ref.shape[1]
    group = HEADS // KV_HEADS
    local = HEADS // n
    rows = own * STEPS
    mine = group * STEPS
    x = x_ref[...]
    queries = dot(order_ref[...], x.reshape(n * x.shape[1], HEAD)).astype(BF16)
    wide = x.astype(F32)
    first = rows * local
    fresh = [wide[i, first : first + rows] for i in range(n)]
    each = n // KV_HEADS
    keys, values = [], []
    for g in range(KV_HEADS):
        pieces = fresh[g * each : (g + 1) * each]
        keys.append(jnp.concatenate([p[:, :columns] for p in pieces], axis=1))
        values.append(jnp.concatenate([p[:, columns : 2 * columns] for p in pieces], axis=1))
    nk_ref[...] = jnp.concatenate(keys, axis=1).astype(BF16)
    nv_ref[...] = jnp.concatenate(values, axis=1).astype(BF16)
    pad = jnp.zeros((16 - rows, HEAD), F32)
    keys = [jnp.concatenate((k, pad), axis=0).astype(BF16) for k in keys]
    values = [jnp.concatenate((v, pad), axis=0).astype(BF16) for v in values]
    scale = HEAD ** (-0.5)
    contexts = []
    for b in range(own):
        q = queries[b * KV_HEADS * mine : (b + 1) * KV_HEADS * mine]
        cached, newer = [], []
        for g in range(KV_HEADS):
            qg = q[g * mine : (g + 1) * mine]
            cached.append(dot_nt(qg, k_ref[b, :, g * HEAD : (g + 1) * HEAD]))
            newer.append(dot_nt(qg, keys[g]))
        cached = jnp.concatenate(cached, axis=0) * scale
        newer = jnp.concatenate(newer, axis=0) * scale
        place = lax.broadcasted_iota(jnp.int32, cached.shape, 1)
        cached = jnp.where(place < len_ref[index_ref[0] * own + b], cached, -1e30)
        step = lax.broadcasted_iota(jnp.int32, newer.shape, 0) % STEPS
        at = lax.broadcasted_iota(jnp.int32, newer.shape, 1) - b * STEPS
        newer = jnp.where((at >= 0) & (at <= step), newer, -1e30)
        top = jnp.maximum(
            jnp.max(cached, axis=1, keepdims=True), jnp.max(newer, axis=1, keepdims=True)
        )
        cached = jnp.exp(cached - top)
        newer = jnp.exp(newer - top)
        total = jnp.sum(cached, axis=1, keepdims=True) + jnp.sum(newer, axis=1, keepdims=True)
        cached = (cached / total).astype(BF16)
        newer = (newer / total).astype(BF16)
        for g in range(KV_HEADS):
            at_rows = slice(g * mine, (g + 1) * mine)
            part = dot(cached[at_rows], v_ref[b, :, g * HEAD : (g + 1) * HEAD])
            s_ref[(b * KV_HEADS + g) * mine : (b * KV_HEADS + g + 1) * mine] = part + dot(
                newer[at_rows], values[g]
            )
    step = local * STEPS
    half = KV_HEADS * mine
    for i in range(n):
        block = [s_ref[b * half + i * step : b * half + (i + 1) * step] for b in range(own)]
        ctx_ref[i] = jnp.concatenate(block, axis=0).astype(BF16)


def out_body(tile, ctx_ref, take_ref, w_ref, mine_ref, other_ref, a_ref):
    rows = a_ref.shape[0]
    n = ctx_ref.shape[0]
    x = ctx_ref[...].reshape(n * ctx_ref.shape[1], HEAD)
    taken = dot(take_ref[...], x).astype(BF16)
    for h in range(a_ref.shape[1] // HEAD):
        a_ref[:, h * HEAD : (h + 1) * HEAD] = taken[h * rows : (h + 1) * rows]
    half = mine_ref.shape[0]

    @pl.loop(0, w_ref.shape[1] // tile)
    def _(i):
        at = pl.ds(pl.multiple_of(i * tile, tile), tile)
        product = dot(a_ref[...], w_ref[:, at])
        mine_ref[:, at] = product[:half]
        other_ref[:, at] = product[half:]


def shards(
    sizes,
    residual_first,
    residual_second,
    attention_norm_gain,
    query_matrix,
    key_matrix,
    value_matrix,
    output_matrix,
    query_down_weights,
    value_down_weights,
    query_up_weights,
    value_up_weights,
    rotated_key_cache,
    stored_value_cache,
    lengths,
    request_adapter,
    adapter_slot,
):
    far, near, cores = sizes
    n = far * near * cores
    index = lax.axis_index("serve")
    own, width = residual_first.shape
    adapters, _, rank = query_down_weights.shape
    query_cols = query_matrix.shape[1]
    key_cols = key_matrix.shape[1]
    local = query_cols // HEAD
    rows = own * STEPS
    all_rows = n * rows
    stored = query_up_weights.shape[0]

    def partner(f, m, c):
        pairs = []
        for z in range(far):
            for y in range(near):
                for k in range(cores):
                    to = (((z + f) % far) * near + (y + m) % near) * cores + (k + c) % cores
                    pairs.append(((z * near + y) * cores + k, to))
        return pairs

    def shift(value, f, m, c):
        return lax.ppermute(value, "serve", partner(f, m, c))

    normed = pl.pallas_call(
        norm_body,
        out_shape=jax.ShapeDtypeStruct((rows, width), BF16),
        compiler_params=pltpu.CompilerParams(vmem_limit_bytes=LIMIT),
    )(residual_first, residual_second, attention_norm_gain.reshape(width // HEAD, HEAD))
    sent = -(-(rows * local + rows) // 8) * 8
    narrow = jax.ShapeDtypeStruct((all_rows, 1), jnp.int32)
    table = jax.ShapeDtypeStruct((all_rows, HEAD), F32)
    square = jax.ShapeDtypeStruct((all_rows, all_rows), BF16)
    slot, near_slot, cosine, sine, key_cosine, key_sine, place, unplace, send, order, take = whole_call(
        functools.partial(prep_body, sizes, rank, own, key_cols, adapters),
        (
            narrow,
            narrow,
            table,
            table,
            table,
            table,
            square,
            square,
            jax.ShapeDtypeStruct((n * sent, all_rows * (local + 1)), BF16),
            jax.ShapeDtypeStruct((own * HEADS * STEPS, n * sent), BF16),
            jax.ShapeDtypeStruct((all_rows * local, n * rows * local), BF16),
        ),
        (index[None], lengths, request_adapter, adapter_slot),
        smem=4,
    )
    gathered = normed[None]
    gathered = jnp.concatenate([gathered] + [shift(gathered, f, 0, 0) for f in range(1, far)])
    gathered = jnp.concatenate([gathered] + [shift(gathered, 0, m, 0) for m in range(1, near)])
    gathered = jnp.concatenate([gathered] + [shift(gathered, 0, 0, c) for c in range(1, cores)])
    x = gathered.reshape(all_rows, width)

    query_down = jnp.swapaxes(query_down_weights, 1, 2).reshape(adapters * rank, width)
    value_down = jnp.swapaxes(value_down_weights, 1, 2).reshape(adapters * rank, width)
    packed_rows = all_rows * 2 * rank // HEAD
    low = whole_call(
        functools.partial(low_body, rank),
        jax.ShapeDtypeStruct((n, packed_rows, HEAD), BF16),
        (x, query_down, value_down, near_slot, place),
    )
    low = lax.all_to_all(low, "serve", split_axis=0, concat_axis=0, tiled=True)

    base_q, base_kv = whole_call(
        functools.partial(base_body, 2048),
        (
            jax.ShapeDtypeStruct((all_rows, query_cols), F32),
            jax.ShapeDtypeStruct((all_rows, HEAD), F32),
        ),
        (x, query_matrix, key_matrix.T, value_matrix.T),
    )

    ready = whole_call(
        functools.partial(ready_body, rank),
        jax.ShapeDtypeStruct((n, sent, HEAD), BF16),
        (
            base_q,
            base_kv,
            low,
            unplace,
            slot,
            query_up_weights.reshape(stored * rank, query_cols),
            value_up_weights.reshape(stored * rank, key_cols),
            cosine,
            sine,
            key_cosine,
            key_sine,
            send,
        ),
    )
    arrived = lax.all_to_all(ready, "serve", split_axis=0, concat_axis=0, tiled=True)

    context, new_keys, new_values = whole_call(
        functools.partial(attend_body, own, key_cols),
        (
            jax.ShapeDtypeStruct((n, rows * local, HEAD), BF16),
            jax.ShapeDtypeStruct((rows, KV_HEADS * HEAD), BF16),
            jax.ShapeDtypeStruct((rows, KV_HEADS * HEAD), BF16),
        ),
        (index[None], lengths, arrived, order, rotated_key_cache, stored_value_cache),
        smem=2,
        scratch=[pltpu.VMEM((own * HEADS * STEPS, HEAD), F32)],
    )
    context = lax.all_to_all(context, "serve", split_axis=0, concat_axis=0, tiled=True)

    kinds = jax.ShapeDtypeStruct((all_rows // cores, width), F32)
    mine, other = whole_call(
        functools.partial(out_body, 1024),
        (kinds, kinds),
        (context, take, output_matrix),
        scratch=[pltpu.VMEM((all_rows, query_cols), BF16)],
    )

    total = (mine + shift(other, 0, 0, 1)).reshape(near, far, rows, width)
    nearer = total[0]
    for m in range(1, near):
        nearer = nearer + shift(total[m].astype(BF16), 0, m, 0).astype(F32)
    last = nearer[0]
    for f in range(1, far):
        last = last + shift(nearer[f].astype(BF16), f, 0, 0).astype(F32)
    out_one = (residual_first.astype(F32) + last[:own]).astype(BF16)
    out_two = (residual_second.astype(F32) + last[own:]).astype(BF16)
    shape = (own, STEPS, KV_HEADS * HEAD)
    return (out_one, out_two, new_keys.reshape(shape), new_values.reshape(shape))


def solution(mesh):
    n = mesh.shape["serve"]
    sizes = (n // 4, 2, 2)
    return jax.shard_map(
        functools.partial(shards, sizes),
        mesh=mesh,
        in_specs=(
            P(("replica", "serve"), None),
            P(("replica", "serve"), None),
            P(),
            P(None, "serve"),
            P(None, "serve"),
            P(None, "serve"),
            P("serve", None),
            P("serve", None, None),
            P("serve", None, None),
            P(None, None, "serve"),
            P(None, None, "serve"),
            P(("replica", "serve"), None, None),
            P(("replica", "serve"), None, None),
            P("replica"),
            P("replica"),
            P(),
        ),
        out_specs=(
            P(("replica", "serve"), None),
            P(("replica", "serve"), None),
            P(("replica", "serve"), None, None),
            P(("replica", "serve"), None, None),
        ),
        check_vma=False,
    )
```

```python
import functools
import math

import jax
import jax.numpy as jnp
from jax import lax
from jax.experimental import pallas as pl
from jax.experimental.pallas import tpu as pltpu
from jax.sharding import PartitionSpec as P

HEADS = 64
KV_HEADS = 8
HEAD = 128
STEPS = 2
LIMIT = 8 * 1024 * 1024
NT = (((1,), (1,)), ((), ()))
F32 = jnp.float32
BF16 = jnp.bfloat16


def dot(a, b):
    return jnp.dot(a, b, preferred_element_type=F32)


def dot_nt(a, b):
    return lax.dot_general(a, b, NT, preferred_element_type=F32)


def whole_call(body, out_shape, args, smem=0, hbm=0, scratch=()):
    specs = [pl.BlockSpec(memory_space=pltpu.SMEM)] * smem
    specs += [pl.BlockSpec(memory_space=pltpu.HBM)] * hbm
    specs += [pl.BlockSpec(memory_space=pltpu.VMEM)] * (len(args) - smem - hbm)
    many = isinstance(out_shape, (tuple, list))
    vmem = pl.BlockSpec(memory_space=pltpu.VMEM)
    return pl.pallas_call(
        body,
        out_shape=out_shape,
        in_specs=specs,
        out_specs=tuple(vmem for _ in out_shape) if many else vmem,
        scratch_shapes=list(scratch),
        compiler_params=pltpu.CompilerParams(vmem_limit_bytes=LIMIT),
    )(*args)


def scaled_frequency(pair_index):
    base = jnp.exp(pair_index.astype(F32) * (-2.0 * math.log(500000.0) / HEAD))
    wavelength = 2.0 * math.pi / base
    smooth = jnp.clip((8192.0 / wavelength - 1.0) / 3.0, 0.0, 1.0)
    return (1.0 - smooth) * base / 8.0 + smooth * base


def fetch(pairs, sems):
    copies = [
        pltpu.make_async_copy(source, target, sems.at[i])
        for i, (source, target) in enumerate(pairs)
    ]
    for copy in copies:
        copy.start()
    for copy in copies:
        copy.wait()


def norm_body(first_hbm, second_hbm, gain_hbm, out_ref, first_ref, second_ref, gain_ref, sems):
    fetch(((first_hbm, first_ref), (second_hbm, second_ref), (gain_hbm, gain_ref)), sems)
    gain = gain_ref[...].astype(F32)
    factors = []
    for ref in (first_ref, second_ref):
        values = ref[...].astype(F32)
        factors.append(lax.rsqrt(jnp.mean(values * values, axis=-1, keepdims=True) + 1e-05))
    factor = jnp.concatenate(factors, axis=0)
    for i in range(gain.shape[0]):
        at = slice(i * HEAD, (i + 1) * HEAD)
        values = jnp.concatenate((first_ref[:, at].astype(F32), second_ref[:, at].astype(F32)))
        out_ref[:, at] = (values * factor * gain[i : i + 1]).astype(BF16)


def prep_body(
    sizes, rank, own, key_cols, adapters,
    index_ref, length_hbm, adapter_hbm, slot_hbm,
    held_ref, local_ref, cos_ref, sin_ref, kcos_ref, ksin_ref, place_ref, unplace_ref, send_ref,
    order_ref, take_ref, length_ref, adapter_ref, slot_ref, sems,
):
    fetch(((length_hbm, length_ref), (adapter_hbm, adapter_ref), (slot_hbm, slot_ref)), sems)
    far, near, cores = sizes
    n = far * near * cores
    rows = own * STEPS
    all_rows = n * rows
    heads = HEADS // n
    sent = send_ref.shape[0] // n
    index = index_ref[0]
    core_at = index % cores
    near_at = index // cores % near
    far_at = index // (cores * near)

    def device_of(block, sign):
        c, m, f = block // (far * near), block // far % near, block % far
        f = (far_at + sign * f + far) % far
        m = (near_at + sign * m + near) % near
        c = (core_at + sign * c + cores) % cores
        return (f * near + m) * cores + c

    def iota(shape, axis):
        return lax.broadcasted_iota(jnp.int32, shape, axis)

    def split(row):
        return row // rows, row % rows // own, row % own

    block, step, mine = split(iota((all_rows, 1), 0))
    device = device_of(block, -1)
    request = device * own + mine
    length = jnp.zeros_like(request)
    adapter = jnp.zeros_like(request)
    for j in range(length_ref.shape[0]):
        length = jnp.where(request == j, length_ref[j], length)
        adapter = jnp.where(request == j, adapter_ref[j], adapter)
    slot = jnp.zeros_like(request)
    for j in range(slot_ref.shape[0]):
        slot = jnp.where(adapter == j, slot_ref[j], slot)
    held_ref[...] = slot
    local_ref[...] = slot - index * adapters
    position = (length + step).astype(F32)
    lane = iota((1, HEAD), 1)
    odd = jnp.where(lane % 2 == 0, -1.0, 1.0)
    angle = position * scaled_frequency(lane // 2)
    cos_ref[...] = jnp.cos(angle)
    sin_ref[...] = jnp.sin(angle) * odd
    angle = position * scaled_frequency((index * key_cols + lane) % HEAD // 2)
    kcos_ref[...] = jnp.where(lane < key_cols, jnp.cos(angle), 1.0)
    ksin_ref[...] = jnp.where(lane < key_cols, jnp.sin(angle) * odd, 0.0)

    def hot(ref, row, column):
        ref[...] = jnp.where(row == column, 1.0, 0.0).astype(BF16)

    absolute = (device * STEPS + step) * own + mine
    hot(unplace_ref, absolute, iota((1, all_rows), 1))
    block, step, mine = split(iota((1, all_rows), 1))
    absolute = (device_of(block, -1) * STEPS + step) * own + mine
    hot(place_ref, iota((all_rows, 1), 0), absolute)

    column = iota((1, send_ref.shape[1]), 1)
    h = column // all_rows
    block, step, mine = split(column % all_rows)
    wanted = device_of(block, -1) * sent + jnp.where(
        h < heads, (mine * heads + h) * STEPS + step, rows * heads + mine * STEPS + step
    )
    hot(send_ref, iota((n * sent, 1), 0), wanted)

    row = iota((order_ref.shape[0], 1), 0)
    mine, head, step = row // (HEADS * STEPS), row // STEPS % HEADS, row % STEPS
    wanted = (head // heads) * sent + (mine * heads + head % heads) * STEPS + step
    hot(order_ref, wanted, iota((1, n * sent), 1))

    row = iota((take_ref.shape[0], 1), 0)
    h = row // all_rows
    block, step, mine = split(row % all_rows)
    wanted = device_of(block, 1) * rows * heads + (mine * heads + h) * STEPS + step
    hot(take_ref, wanted, iota((1, take_ref.shape[1]), 1))


def low_body(rank, groups, *refs):
    parts, (qd_ref, vd_ref, local_ref, place_ref, x_ref, out_ref) = refs[:groups], refs[groups:]
    rows = parts[0].shape[1]
    sets = max(1, 16 // rows)
    for p, part in enumerate(parts):
        for i in range(0, part.shape[0], sets):
            at = (p * part.shape[0] + i) * rows
            for lane in range(0, x_ref.shape[1], 1024):
                lanes = slice(lane, lane + 1024)
                block = [part[i + j, :, lanes].astype(F32) for j in range(sets)]
                x_ref[at : at + sets * rows, lanes] = jnp.concatenate(block, axis=0).astype(BF16)
    adapters = qd_ref.shape[0] // rank
    maps = jnp.concatenate((qd_ref[...], vd_ref[...]), axis=0)
    low = dot_nt(x_ref[...], maps)
    lane = lax.broadcasted_iota(jnp.int32, low.shape, 1)
    low = jnp.where(lane // rank % adapters == local_ref[...], low, 0.0)
    total = 0.0
    for a in range(adapters):
        q = low[:, a * rank : (a + 1) * rank]
        v = low[:, (adapters + a) * rank : (adapters + a + 1) * rank]
        total = total + jnp.concatenate((q, v), axis=1)
    rows = dot(place_ref[...], total.astype(BF16))
    pack = HEAD // (2 * rank)
    step = rows.shape[0] // pack
    packed = jnp.concatenate([rows[i * step : (i + 1) * step] for i in range(pack)], axis=1)
    out_ref[...] = packed.astype(BF16)


def join_body(*refs):
    total = refs[0][...].astype(F32)
    for ref in refs[1:-1]:
        total = total + ref[...].astype(F32)
    refs[-1][...] = total.astype(BF16)


def base_body(depth, x_ref, q_ref, k_ref, v_ref, oq_ref, okv_ref):
    oq_ref[...] = jnp.zeros_like(oq_ref)
    okv_ref[...] = jnp.zeros_like(okv_ref)
    columns = k_ref.shape[0]
    narrow = jnp.zeros((HEAD - 2 * columns, depth), BF16)

    @pl.loop(0, x_ref.shape[1] // depth)
    def _(i):
        at = pl.ds(pl.multiple_of(i * depth, depth), depth)
        x = x_ref[:, at]
        oq_ref[...] += dot(x, q_ref[at, :])
        both = (k_ref[:, at], v_ref[:, at])
        if 2 * columns < HEAD:
            both += (narrow,)
        okv_ref[...] += dot_nt(x, jnp.concatenate(both, axis=0))


def turned(values, cosine, sine):
    lane = lax.broadcasted_iota(jnp.int32, values.shape, 1)
    width = values.shape[1]
    ahead = pltpu.roll(values, width - 1, 1)
    behind = pltpu.roll(values, 1, 1)
    return values * cosine + jnp.where(lane % 2 == 0, ahead, behind) * sine


def ready_body(
    rank, lows, oq_ref, okv_ref, *refs
):
    low_refs = refs[:lows]
    (
        unplace_ref, slot_ref, uq_ref, uv_ref, cos_ref, sin_ref, kcos_ref, ksin_ref, send_ref, out_ref,
    ) = refs[lows:]
    packed = low_refs[0][...].astype(F32)
    for ref in low_refs[1:]:
        packed = packed + ref[...].astype(F32)
    pack = HEAD // (2 * rank)
    low = jnp.concatenate(
        [packed[:, i * 2 * rank : (i + 1) * 2 * rank] for i in range(pack)], axis=0
    )
    low = dot(unplace_ref[...], low.astype(BF16)).astype(BF16)
    wide = uq_ref.shape[0]
    lane = lax.broadcasted_iota(jnp.int32, (low.shape[0], wide), 1)
    here = lane // rank == slot_ref[...]
    row = lax.broadcasted_iota(jnp.int32, (2 * rank, wide), 0)
    column = lax.broadcasted_iota(jnp.int32, (2 * rank, wide), 1)
    spread_q = jnp.where(column % rank == row, 1.0, 0.0).astype(BF16)
    spread_v = jnp.where(column % rank + rank == row, 1.0, 0.0).astype(BF16)
    wide_q = jnp.where(here, dot(low, spread_q), 0.0).astype(BF16)
    wide_v = jnp.where(here, dot(low, spread_v), 0.0).astype(BF16)
    query = oq_ref[...] + dot(wide_q, uq_ref[...])
    fresh = turned(okv_ref[...], kcos_ref[...], ksin_ref[...])
    columns = uv_ref.shape[1]
    value = dot(wide_v, uv_ref[...])
    pieces = [jnp.zeros((value.shape[0], columns), F32), value]
    if 2 * columns < HEAD:
        pieces.append(jnp.zeros((value.shape[0], HEAD - 2 * columns), F32))
    fresh = fresh + jnp.concatenate(pieces, axis=1)
    cosine, sine = cos_ref[...], sin_ref[...]
    parts = []
    for h in range(query.shape[1] // HEAD):
        parts.append(turned(query[:, h * HEAD : (h + 1) * HEAD], cosine, sine))
    parts.append(fresh)
    stacked = jnp.concatenate(parts, axis=0).astype(BF16)
    out_ref[...] = dot(send_ref[...], stacked).astype(BF16).reshape(out_ref.shape)


def attend_body(own, columns, index_ref, len_ref, x_ref, order_ref, k_ref, v_ref, ctx_ref, nk_ref, nv_ref, s_ref):
    n, span = x_ref.shape[0], k_ref.shape[1]
    group = HEADS // KV_HEADS
    local = HEADS // n
    rows = own * STEPS
    mine = group * STEPS
    x = x_ref[...]
    queries = dot(order_ref[...], x.reshape(n * x.shape[1], HEAD)).astype(BF16)
    wide = x.astype(F32)
    first = rows * local
    fresh = [wide[i, first : first + rows] for i in range(n)]
    each = n // KV_HEADS
    keys, values = [], []
    for g in range(KV_HEADS):
        pieces = fresh[g * each : (g + 1) * each]
        keys.append(jnp.concatenate([p[:, :columns] for p in pieces], axis=1))
        values.append(jnp.concatenate([p[:, columns : 2 * columns] for p in pieces], axis=1))
    new_keys = jnp.concatenate(keys, axis=1)
    new_values = jnp.concatenate(values, axis=1)
    for b in range(own):
        at = slice(b * STEPS, (b + 1) * STEPS)
        nk_ref[b] = new_keys[at].astype(BF16)
        nv_ref[b] = new_values[at].astype(BF16)
    pad = jnp.zeros((16 - rows, HEAD), F32)
    keys = [jnp.concatenate((k, pad), axis=0).astype(BF16) for k in keys]
    values = [jnp.concatenate((v, pad), axis=0).astype(BF16) for v in values]
    scale = HEAD ** (-0.5)
    contexts = []
    for b in range(own):
        q = queries[b * KV_HEADS * mine : (b + 1) * KV_HEADS * mine]
        cached, newer = [], []
        for g in range(KV_HEADS):
            qg = q[g * mine : (g + 1) * mine]
            cached.append(dot_nt(qg, k_ref[b, :, g * HEAD : (g + 1) * HEAD]))
            newer.append(dot_nt(qg, keys[g]))
        cached = jnp.concatenate(cached, axis=0) * scale
        newer = jnp.concatenate(newer, axis=0) * scale
        place = lax.broadcasted_iota(jnp.int32, cached.shape, 1)
        cached = jnp.where(place < len_ref[index_ref[0] * own + b], cached, -1e30)
        step = lax.broadcasted_iota(jnp.int32, newer.shape, 0) % STEPS
        at = lax.broadcasted_iota(jnp.int32, newer.shape, 1) - b * STEPS
        newer = jnp.where((at >= 0) & (at <= step), newer, -1e30)
        top = jnp.maximum(
            jnp.max(cached, axis=1, keepdims=True), jnp.max(newer, axis=1, keepdims=True)
        )
        cached = jnp.exp(cached - top)
        newer = jnp.exp(newer - top)
        total = jnp.sum(cached, axis=1, keepdims=True) + jnp.sum(newer, axis=1, keepdims=True)
        cached = (cached / total).astype(BF16)
        newer = (newer / total).astype(BF16)
        for g in range(KV_HEADS):
            at_rows = slice(g * mine, (g + 1) * mine)
            part = dot(cached[at_rows], v_ref[b, :, g * HEAD : (g + 1) * HEAD])
            s_ref[(b * KV_HEADS + g) * mine : (b * KV_HEADS + g + 1) * mine] = part + dot(
                newer[at_rows], values[g]
            )
    step = local * STEPS
    half = KV_HEADS * mine
    for i in range(n):
        block = [s_ref[b * half + i * step : b * half + (i + 1) * step] for b in range(own)]
        ctx_ref[i] = jnp.concatenate(block, axis=0).astype(BF16)


def out_body(tile, ctx_ref, take_ref, w_ref, mine_ref, other_ref, a_ref):
    rows = a_ref.shape[0]
    n = ctx_ref.shape[0]
    x = ctx_ref[...].reshape(n * ctx_ref.shape[1], HEAD)
    taken = dot(take_ref[...], x).astype(BF16)
    for h in range(a_ref.shape[1] // HEAD):
        a_ref[:, h * HEAD : (h + 1) * HEAD] = taken[h * rows : (h + 1) * rows]
    half = mine_ref.shape[0]

    @pl.loop(0, w_ref.shape[1] // tile)
    def _(i):
        at = pl.ds(pl.multiple_of(i * tile, tile), tile)
        product = dot(a_ref[...], w_ref[:, at])
        mine_ref[:, at] = product[:half]
        other_ref[:, at] = product[half:]


def near_body(mine_ref, came_ref, *refs):
    rows = refs[0].shape[0]
    total = mine_ref[...] + came_ref[...]
    refs[0][...] = total[:rows]
    for m, ref in enumerate(refs[1:], 1):
        ref[...] = total[m * rows : (m + 1) * rows].astype(BF16)


def far_body(came, *refs):
    total = refs[0][...]
    for ref in refs[1 : 1 + came]:
        total = total + ref[...].astype(F32)
    refs = refs[1 + came :]
    rows = refs[0].shape[0]
    refs[0][...] = total[:rows]
    for f, ref in enumerate(refs[1:], 1):
        ref[...] = total[f * rows : (f + 1) * rows].astype(BF16)


def last_body(came, first_hbm, second_hbm, keep_ref, *refs):
    one_ref, two_ref, first_ref, second_ref, sems = refs[came:]
    fetch(((first_hbm, first_ref), (second_hbm, second_ref)), sems)
    total = keep_ref[...]
    for ref in refs[:came]:
        total = total + ref[...].astype(F32)
    own = one_ref.shape[0]
    one_ref[...] = (first_ref[...].astype(F32) + total[:own]).astype(BF16)
    two_ref[...] = (second_ref[...].astype(F32) + total[own:]).astype(BF16)


def shards(
    sizes,
    residual_first,
    residual_second,
    attention_norm_gain,
    query_matrix,
    key_matrix,
    value_matrix,
    output_matrix,
    query_down_weights,
    value_down_weights,
    query_up_weights,
    value_up_weights,
    rotated_key_cache,
    stored_value_cache,
    lengths,
    request_adapter,
    adapter_slot,
):
    far, near, cores = sizes
    n = far * near * cores
    index = lax.axis_index("serve")
    own, width = residual_first.shape
    adapters, _, rank = query_down_weights.shape
    query_cols = query_matrix.shape[1]
    key_cols = key_matrix.shape[1]
    local = query_cols // HEAD
    rows = own * STEPS
    all_rows = n * rows
    stored = query_up_weights.shape[0]

    def partner(f, m, c):
        pairs = []
        for z in range(far):
            for y in range(near):
                for k in range(cores):
                    to = (((z + f) % far) * near + (y + m) % near) * cores + (k + c) % cores
                    pairs.append(((z * near + y) * cores + k, to))
        return pairs

    def shift(value, f, m, c):
        return lax.ppermute(value, "serve", partner(f, m, c))

    gain = attention_norm_gain.reshape(width // HEAD, HEAD)
    normed = whole_call(
        norm_body,
        jax.ShapeDtypeStruct((rows, width), BF16),
        (residual_first, residual_second, gain),
        hbm=3,
        scratch=[
            pltpu.VMEM((own, width), BF16),
            pltpu.VMEM((own, width), BF16),
            pltpu.VMEM(gain.shape, BF16),
            pltpu.SemaphoreType.DMA((3,)),
        ],
    )
    sent = -(-(rows * local + rows) // 8) * 8
    narrow = jax.ShapeDtypeStruct((all_rows, 1), jnp.int32)
    table = jax.ShapeDtypeStruct((all_rows, HEAD), F32)
    square = jax.ShapeDtypeStruct((all_rows, all_rows), BF16)
    slot, near_slot, cosine, sine, key_cosine, key_sine, place, unplace, send, order, take = whole_call(
        functools.partial(prep_body, sizes, rank, own, key_cols, adapters),
        (
            narrow,
            narrow,
            table,
            table,
            table,
            table,
            square,
            square,
            jax.ShapeDtypeStruct((n * sent, all_rows * (local + 1)), BF16),
            jax.ShapeDtypeStruct((own * HEADS * STEPS, n * sent), BF16),
            jax.ShapeDtypeStruct((all_rows * local, n * rows * local), BF16),
        ),
        (index[None], lengths, request_adapter, adapter_slot),
        smem=1,
        hbm=3,
        scratch=[
            pltpu.SMEM(lengths.shape, jnp.int32),
            pltpu.SMEM(request_adapter.shape, jnp.int32),
            pltpu.SMEM(adapter_slot.shape, jnp.int32),
            pltpu.SemaphoreType.DMA((3,)),
        ],
    )
    normed = normed[None]
    groups = [jnp.concatenate([normed] + [shift(normed, f, 0, 0) for f in range(1, far)])]
    groups += [shift(groups[0], 0, m, 0) for m in range(1, near)]
    groups += [shift(group, 0, 0, c) for c in range(1, cores) for group in groups[:near]]

    query_down = jnp.swapaxes(query_down_weights, 1, 2).reshape(adapters * rank, width)
    value_down = jnp.swapaxes(value_down_weights, 1, 2).reshape(adapters * rank, width)
    packed_rows = all_rows * 2 * rank // HEAD
    x, low = whole_call(
        functools.partial(low_body, rank, len(groups)),
        (
            jax.ShapeDtypeStruct((all_rows, width), BF16),
            jax.ShapeDtypeStruct((packed_rows, HEAD), BF16),
        ),
        (*groups, query_down, value_down, near_slot, place),
    )
    lows = [shift(low, 0, m, c) for m in range(near) for c in range(cores) if m + c]
    low = whole_call(join_body, jax.ShapeDtypeStruct(low.shape, BF16), (low, *lows))
    lows = [low] + [shift(low, f, 0, 0) for f in range(1, far)]

    base_q, base_kv = whole_call(
        functools.partial(base_body, 2048),
        (
            jax.ShapeDtypeStruct((all_rows, query_cols), F32),
            jax.ShapeDtypeStruct((all_rows, HEAD), F32),
        ),
        (x, query_matrix, key_matrix.T, value_matrix.T),
    )

    ready = whole_call(
        functools.partial(ready_body, rank, len(lows)),
        jax.ShapeDtypeStruct((n, sent, HEAD), BF16),
        (
            base_q,
            base_kv,
            *lows,
            unplace,
            slot,
            query_up_weights.reshape(stored * rank, query_cols),
            value_up_weights.reshape(stored * rank, key_cols),
            cosine,
            sine,
            key_cosine,
            key_sine,
            send,
        ),
    )
    arrived = lax.all_to_all(ready, "serve", split_axis=0, concat_axis=0, tiled=True)

    context, new_keys, new_values = whole_call(
        functools.partial(attend_body, own, key_cols),
        (
            jax.ShapeDtypeStruct((n, rows * local, HEAD), BF16),
            jax.ShapeDtypeStruct((own, STEPS, KV_HEADS * HEAD), BF16),
            jax.ShapeDtypeStruct((own, STEPS, KV_HEADS * HEAD), BF16),
        ),
        (index[None], lengths, arrived, order, rotated_key_cache, stored_value_cache),
        smem=2,
        scratch=[pltpu.VMEM((own * HEADS * STEPS, HEAD), F32)],
    )
    context = lax.all_to_all(context, "serve", split_axis=0, concat_axis=0, tiled=True)

    kinds = jax.ShapeDtypeStruct((all_rows // cores, width), F32)
    mine, other = whole_call(
        functools.partial(out_body, 1024),
        (kinds, kinds),
        (context, take, output_matrix),
        scratch=[pltpu.VMEM((all_rows, query_cols), BF16)],
    )

    def kind(count, dtype):
        return jax.ShapeDtypeStruct((count * rows, width), dtype)

    keep, *others = whole_call(
        near_body,
        (kind(far, F32),) + (kind(far, BF16),) * (near - 1),
        (mine, shift(other, 0, 0, 1)),
    )
    others = [shift(other, 0, m, 0) for m, other in enumerate(others, 1)]
    keep, *others = whole_call(
        functools.partial(far_body, len(others)),
        (kind(1, F32),) + (kind(1, BF16),) * (far - 1),
        (keep, *others),
    )
    others = [shift(other, f, 0, 0) for f, other in enumerate(others, 1)]
    result = jax.ShapeDtypeStruct((own, width), BF16)
    out_one, out_two = whole_call(
        functools.partial(last_body, len(others)),
        (result, result),
        (residual_first, residual_second, keep, *others),
        hbm=2,
        scratch=[
            pltpu.VMEM((own, width), BF16),
            pltpu.VMEM((own, width), BF16),
            pltpu.SemaphoreType.DMA((2,)),
        ],
    )
    return (out_one, out_two, new_keys, new_values)


def solution(mesh):
    n = mesh.shape["serve"]
    sizes = (n // 4, 2, 2)
    return jax.shard_map(
        functools.partial(shards, sizes),
        mesh=mesh,
        in_specs=(
            P(("replica", "serve"), None),
            P(("replica", "serve"), None),
            P(),
            P(None, "serve"),
            P(None, "serve"),
            P(None, "serve"),
            P("serve", None),
            P("serve", None, None),
            P("serve", None, None),
            P(None, None, "serve"),
            P(None, None, "serve"),
            P(("replica", "serve"), None, None),
            P(("replica", "serve"), None, None),
            P("replica"),
            P("replica"),
            P(),
        ),
        out_specs=(
            P(("replica", "serve"), None),
            P(("replica", "serve"), None),
            P(("replica", "serve"), None, None),
            P(("replica", "serve"), None, None),
        ),
        check_vma=False,
    )
```

```python
import functools
import math

import jax
import jax.numpy as jnp
from jax import lax
from jax.experimental import pallas as pl
from jax.experimental.pallas import tpu as pltpu
from jax.sharding import PartitionSpec as P

HEADS = 64
KV_HEADS = 8
HEAD = 128
STEPS = 2
LIMIT = 8 * 1024 * 1024
PEAK = 1.15e9
NT = (((1,), (1,)), ((), ()))
F32 = jnp.float32
BF16 = jnp.bfloat16


def dot(a, b):
    return jnp.dot(a, b, preferred_element_type=F32)


def dot_nt(a, b):
    return lax.dot_general(a, b, NT, preferred_element_type=F32)


def whole_call(body, out_shape, args, cost, smem=0, hbm=0, scratch=()):
    specs = [pl.BlockSpec(memory_space=pltpu.SMEM)] * smem
    specs += [pl.BlockSpec(memory_space=pltpu.HBM)] * hbm
    specs += [pl.BlockSpec(memory_space=pltpu.VMEM)] * (len(args) - smem - hbm)
    many = isinstance(out_shape, (tuple, list))
    vmem = pl.BlockSpec(memory_space=pltpu.VMEM)
    return pl.pallas_call(
        body,
        out_shape=out_shape,
        in_specs=specs,
        out_specs=tuple(vmem for _ in out_shape) if many else vmem,
        scratch_shapes=list(scratch),
        compiler_params=pltpu.CompilerParams(vmem_limit_bytes=LIMIT),
        cost_estimate=pl.CostEstimate(
            flops=int(cost * PEAK), bytes_accessed=0, transcendentals=0
        ),
    )(*args)


def scaled_frequency(pair_index):
    base = jnp.exp(pair_index.astype(F32) * (-2.0 * math.log(500000.0) / HEAD))
    wavelength = 2.0 * math.pi / base
    smooth = jnp.clip((8192.0 / wavelength - 1.0) / 3.0, 0.0, 1.0)
    return (1.0 - smooth) * base / 8.0 + smooth * base


def fetch(pairs, sems):
    copies = [
        pltpu.make_async_copy(source, target, sems.at[i])
        for i, (source, target) in enumerate(pairs)
    ]
    for copy in copies:
        copy.start()
    for copy in copies:
        copy.wait()


def norm_body(first_hbm, second_hbm, gain_hbm, out_ref, first_ref, second_ref, gain_ref, sems):
    fetch(((first_hbm, first_ref), (second_hbm, second_ref), (gain_hbm, gain_ref)), sems)
    gain = gain_ref[...].astype(F32)
    factors = []
    for ref in (first_ref, second_ref):
        values = ref[...].astype(F32)
        factors.append(lax.rsqrt(jnp.mean(values * values, axis=-1, keepdims=True) + 1e-05))
    factor = jnp.concatenate(factors, axis=0)
    for i in range(gain.shape[0]):
        at = slice(i * HEAD, (i + 1) * HEAD)
        values = jnp.concatenate((first_ref[:, at].astype(F32), second_ref[:, at].astype(F32)))
        out_ref[:, at] = (values * factor * gain[i : i + 1]).astype(BF16)


def prep_body(
    sizes, rank, own, key_cols, adapters,
    index_ref, length_hbm, adapter_hbm, slot_hbm,
    held_ref, local_ref, cos_ref, sin_ref, kcos_ref, ksin_ref, place_ref, unplace_ref, send_ref,
    order_ref, take_ref, length_ref, adapter_ref, slot_ref, sems,
):
    fetch(((length_hbm, length_ref), (adapter_hbm, adapter_ref), (slot_hbm, slot_ref)), sems)
    far, near, cores = sizes
    n = far * near * cores
    rows = own * STEPS
    all_rows = n * rows
    heads = HEADS // n
    sent = send_ref.shape[0] // n
    index = index_ref[0]
    core_at = index % cores
    near_at = index // cores % near
    far_at = index // (cores * near)

    def device_of(block, sign):
        c, m, f = block // (far * near), block // far % near, block % far
        f = (far_at + sign * f + far) % far
        m = (near_at + sign * m + near) % near
        c = (core_at + sign * c + cores) % cores
        return (f * near + m) * cores + c

    def iota(shape, axis):
        return lax.broadcasted_iota(jnp.int32, shape, axis)

    def split(row):
        return row // rows, row % rows // own, row % own

    block, step, mine = split(iota((all_rows, 1), 0))
    device = device_of(block, -1)
    request = device * own + mine
    length = jnp.zeros_like(request)
    adapter = jnp.zeros_like(request)
    for j in range(length_ref.shape[0]):
        length = jnp.where(request == j, length_ref[j], length)
        adapter = jnp.where(request == j, adapter_ref[j], adapter)
    slot = jnp.zeros_like(request)
    for j in range(slot_ref.shape[0]):
        slot = jnp.where(adapter == j, slot_ref[j], slot)
    held_ref[...] = slot
    local_ref[...] = slot - index * adapters
    position = (length + step).astype(F32)
    lane = iota((1, HEAD), 1)
    odd = jnp.where(lane % 2 == 0, -1.0, 1.0)
    angle = position * scaled_frequency(lane // 2)
    cos_ref[...] = jnp.cos(angle)
    sin_ref[...] = jnp.sin(angle) * odd
    angle = position * scaled_frequency((index * key_cols + lane) % HEAD // 2)
    kcos_ref[...] = jnp.where(lane < key_cols, jnp.cos(angle), 1.0)
    ksin_ref[...] = jnp.where(lane < key_cols, jnp.sin(angle) * odd, 0.0)

    def hot(ref, row, column):
        ref[...] = jnp.where(row == column, 1.0, 0.0).astype(BF16)

    absolute = (device * STEPS + step) * own + mine
    hot(unplace_ref, absolute, iota((1, all_rows), 1))
    block, step, mine = split(iota((1, all_rows), 1))
    absolute = (device_of(block, -1) * STEPS + step) * own + mine
    hot(place_ref, iota((all_rows, 1), 0), absolute)

    column = iota((1, send_ref.shape[1]), 1)
    h = column // all_rows
    block, step, mine = split(column % all_rows)
    wanted = device_of(block, -1) * sent + jnp.where(
        h < heads, (mine * heads + h) * STEPS + step, rows * heads + mine * STEPS + step
    )
    hot(send_ref, iota((n * sent, 1), 0), wanted)

    row = iota((order_ref.shape[0], 1), 0)
    mine, head, step = row // (HEADS * STEPS), row // STEPS % HEADS, row % STEPS
    wanted = (head // heads) * sent + (mine * heads + head % heads) * STEPS + step
    hot(order_ref, wanted, iota((1, n * sent), 1))

    row = iota((take_ref.shape[0], 1), 0)
    h = row // all_rows
    block, step, mine = split(row % all_rows)
    wanted = device_of(block, 1) * rows * heads + (mine * heads + h) * STEPS + step
    hot(take_ref, wanted, iota((1, take_ref.shape[1]), 1))


def low_body(rank, groups, *refs):
    parts, (qd_ref, vd_ref, local_ref, place_ref, x_ref, out_ref) = refs[:groups], refs[groups:]
    rows = parts[0].shape[1]
    sets = max(1, 16 // rows)
    for p, part in enumerate(parts):
        for i in range(0, part.shape[0], sets):
            at = (p * part.shape[0] + i) * rows
            for lane in range(0, x_ref.shape[1], 1024):
                lanes = slice(lane, lane + 1024)
                block = [part[i + j, :, lanes].astype(F32) for j in range(sets)]
                x_ref[at : at + sets * rows, lanes] = jnp.concatenate(block, axis=0).astype(BF16)
    adapters = qd_ref.shape[0] // rank
    maps = jnp.concatenate((qd_ref[...], vd_ref[...]), axis=0)
    low = dot_nt(x_ref[...], maps)
    lane = lax.broadcasted_iota(jnp.int32, low.shape, 1)
    low = jnp.where(lane // rank % adapters == local_ref[...], low, 0.0)
    total = 0.0
    for a in range(adapters):
        q = low[:, a * rank : (a + 1) * rank]
        v = low[:, (adapters + a) * rank : (adapters + a + 1) * rank]
        total = total + jnp.concatenate((q, v), axis=1)
    rows = dot(place_ref[...], total.astype(BF16))
    pack = HEAD // (2 * rank)
    step = rows.shape[0] // pack
    packed = jnp.concatenate([rows[i * step : (i + 1) * step] for i in range(pack)], axis=1)
    out_ref[...] = packed.astype(BF16)


def join_body(*refs):
    total = refs[0][...].astype(F32)
    for ref in refs[1:-1]:
        total = total + ref[...].astype(F32)
    refs[-1][...] = total.astype(BF16)


def base_body(depth, x_ref, q_ref, k_ref, v_ref, oq_ref, okv_ref):
    oq_ref[...] = jnp.zeros_like(oq_ref)
    okv_ref[...] = jnp.zeros_like(okv_ref)
    columns = k_ref.shape[0]
    narrow = jnp.zeros((HEAD - 2 * columns, depth), BF16)

    @pl.loop(0, x_ref.shape[1] // depth)
    def _(i):
        at = pl.ds(pl.multiple_of(i * depth, depth), depth)
        x = x_ref[:, at]
        oq_ref[...] += dot(x, q_ref[at, :])
        both = (k_ref[:, at], v_ref[:, at])
        if 2 * columns < HEAD:
            both += (narrow,)
        okv_ref[...] += dot_nt(x, jnp.concatenate(both, axis=0))


def turned(values, cosine, sine):
    lane = lax.broadcasted_iota(jnp.int32, values.shape, 1)
    width = values.shape[1]
    ahead = pltpu.roll(values, width - 1, 1)
    behind = pltpu.roll(values, 1, 1)
    return values * cosine + jnp.where(lane % 2 == 0, ahead, behind) * sine


def ready_body(
    rank, lows, oq_ref, okv_ref, *refs
):
    low_refs = refs[:lows]
    (
        unplace_ref, slot_ref, uq_ref, uv_ref, cos_ref, sin_ref, kcos_ref, ksin_ref, send_ref, out_ref,
    ) = refs[lows:]
    packed = low_refs[0][...].astype(F32)
    for ref in low_refs[1:]:
        packed = packed + ref[...].astype(F32)
    pack = HEAD // (2 * rank)
    low = jnp.concatenate(
        [packed[:, i * 2 * rank : (i + 1) * 2 * rank] for i in range(pack)], axis=0
    )
    low = dot(unplace_ref[...], low.astype(BF16)).astype(BF16)
    wide = uq_ref.shape[0]
    lane = lax.broadcasted_iota(jnp.int32, (low.shape[0], wide), 1)
    here = lane // rank == slot_ref[...]
    row = lax.broadcasted_iota(jnp.int32, (2 * rank, wide), 0)
    column = lax.broadcasted_iota(jnp.int32, (2 * rank, wide), 1)
    spread_q = jnp.where(column % rank == row, 1.0, 0.0).astype(BF16)
    spread_v = jnp.where(column % rank + rank == row, 1.0, 0.0).astype(BF16)
    wide_q = jnp.where(here, dot(low, spread_q), 0.0).astype(BF16)
    wide_v = jnp.where(here, dot(low, spread_v), 0.0).astype(BF16)
    query = oq_ref[...] + dot(wide_q, uq_ref[...])
    fresh = turned(okv_ref[...], kcos_ref[...], ksin_ref[...])
    columns = uv_ref.shape[1]
    value = dot(wide_v, uv_ref[...])
    pieces = [jnp.zeros((value.shape[0], columns), F32), value]
    if 2 * columns < HEAD:
        pieces.append(jnp.zeros((value.shape[0], HEAD - 2 * columns), F32))
    fresh = fresh + jnp.concatenate(pieces, axis=1)
    cosine, sine = cos_ref[...], sin_ref[...]
    parts = []
    for h in range(query.shape[1] // HEAD):
        parts.append(turned(query[:, h * HEAD : (h + 1) * HEAD], cosine, sine))
    parts.append(fresh)
    stacked = jnp.concatenate(parts, axis=0).astype(BF16)
    out_ref[...] = dot(send_ref[...], stacked).astype(BF16).reshape(out_ref.shape)


def attend_body(own, columns, index_ref, len_ref, x_ref, order_ref, k_ref, v_ref, ctx_ref, nk_ref, nv_ref, s_ref):
    n, span = x_ref.shape[0], k_ref.shape[1]
    group = HEADS // KV_HEADS
    local = HEADS // n
    rows = own * STEPS
    mine = group * STEPS
    x = x_ref[...]
    queries = dot(order_ref[...], x.reshape(n * x.shape[1], HEAD)).astype(BF16)
    wide = x.astype(F32)
    first = rows * local
    fresh = [wide[i, first : first + rows] for i in range(n)]
    each = n // KV_HEADS
    keys, values = [], []
    for g in range(KV_HEADS):
        pieces = fresh[g * each : (g + 1) * each]
        keys.append(jnp.concatenate([p[:, :columns] for p in pieces], axis=1))
        values.append(jnp.concatenate([p[:, columns : 2 * columns] for p in pieces], axis=1))
    new_keys = jnp.concatenate(keys, axis=1)
    new_values = jnp.concatenate(values, axis=1)
    for b in range(own):
        at = slice(b * STEPS, (b + 1) * STEPS)
        nk_ref[b] = new_keys[at].astype(BF16)
        nv_ref[b] = new_values[at].astype(BF16)
    pad = jnp.zeros((16 - rows, HEAD), F32)
    keys = [jnp.concatenate((k, pad), axis=0).astype(BF16) for k in keys]
    values = [jnp.concatenate((v, pad), axis=0).astype(BF16) for v in values]
    scale = HEAD ** (-0.5)
    contexts = []
    for b in range(own):
        q = queries[b * KV_HEADS * mine : (b + 1) * KV_HEADS * mine]
        cached, newer = [], []
        for g in range(KV_HEADS):
            qg = q[g * mine : (g + 1) * mine]
            cached.append(dot_nt(qg, k_ref[b, :, g * HEAD : (g + 1) * HEAD]))
            newer.append(dot_nt(qg, keys[g]))
        cached = jnp.concatenate(cached, axis=0) * scale
        newer = jnp.concatenate(newer, axis=0) * scale
        place = lax.broadcasted_iota(jnp.int32, cached.shape, 1)
        cached = jnp.where(place < len_ref[index_ref[0] * own + b], cached, -1e30)
        step = lax.broadcasted_iota(jnp.int32, newer.shape, 0) % STEPS
        at = lax.broadcasted_iota(jnp.int32, newer.shape, 1) - b * STEPS
        newer = jnp.where((at >= 0) & (at <= step), newer, -1e30)
        top = jnp.maximum(
            jnp.max(cached, axis=1, keepdims=True), jnp.max(newer, axis=1, keepdims=True)
        )
        cached = jnp.exp(cached - top)
        newer = jnp.exp(newer - top)
        total = jnp.sum(cached, axis=1, keepdims=True) + jnp.sum(newer, axis=1, keepdims=True)
        cached = (cached / total).astype(BF16)
        newer = (newer / total).astype(BF16)
        for g in range(KV_HEADS):
            at_rows = slice(g * mine, (g + 1) * mine)
            part = dot(cached[at_rows], v_ref[b, :, g * HEAD : (g + 1) * HEAD])
            s_ref[(b * KV_HEADS + g) * mine : (b * KV_HEADS + g + 1) * mine] = part + dot(
                newer[at_rows], values[g]
            )
    step = local * STEPS
    half = KV_HEADS * mine
    for i in range(n):
        block = [s_ref[b * half + i * step : b * half + (i + 1) * step] for b in range(own)]
        ctx_ref[i] = jnp.concatenate(block, axis=0).astype(BF16)


def out_body(tile, ctx_ref, take_ref, w_ref, mine_ref, other_ref, a_ref):
    rows = a_ref.shape[0]
    n = ctx_ref.shape[0]
    x = ctx_ref[...].reshape(n * ctx_ref.shape[1], HEAD)
    taken = dot(take_ref[...], x).astype(BF16)
    for h in range(a_ref.shape[1] // HEAD):
        a_ref[:, h * HEAD : (h + 1) * HEAD] = taken[h * rows : (h + 1) * rows]
    half = mine_ref.shape[0]

    @pl.loop(0, w_ref.shape[1] // tile)
    def _(i):
        at = pl.ds(pl.multiple_of(i * tile, tile), tile)
        product = dot(a_ref[...], w_ref[:, at])
        mine_ref[:, at] = product[:half]
        other_ref[:, at] = product[half:]


def near_body(mine_ref, came_ref, *refs):
    rows = refs[0].shape[0]
    total = mine_ref[...] + came_ref[...]
    refs[0][...] = total[:rows]
    for m, ref in enumerate(refs[1:], 1):
        ref[...] = total[m * rows : (m + 1) * rows].astype(BF16)


def far_body(came, *refs):
    total = refs[0][...]
    for ref in refs[1 : 1 + came]:
        total = total + ref[...].astype(F32)
    refs = refs[1 + came :]
    rows = refs[0].shape[0]
    refs[0][...] = total[:rows]
    for f, ref in enumerate(refs[1:], 1):
        ref[...] = total[f * rows : (f + 1) * rows].astype(BF16)


def last_body(came, first_ref, second_ref, keep_ref, *refs):
    one_ref, two_ref = refs[came:]
    total = keep_ref[...]
    for ref in refs[:came]:
        total = total + ref[...].astype(F32)
    own = one_ref.shape[0]
    one_ref[...] = (first_ref[...].astype(F32) + total[:own]).astype(BF16)
    two_ref[...] = (second_ref[...].astype(F32) + total[own:]).astype(BF16)


def shards(
    sizes,
    residual_first,
    residual_second,
    attention_norm_gain,
    query_matrix,
    key_matrix,
    value_matrix,
    output_matrix,
    query_down_weights,
    value_down_weights,
    query_up_weights,
    value_up_weights,
    rotated_key_cache,
    stored_value_cache,
    lengths,
    request_adapter,
    adapter_slot,
):
    far, near, cores = sizes
    n = far * near * cores
    index = lax.axis_index("serve")
    own, width = residual_first.shape
    adapters, _, rank = query_down_weights.shape
    query_cols = query_matrix.shape[1]
    key_cols = key_matrix.shape[1]
    local = query_cols // HEAD
    rows = own * STEPS
    all_rows = n * rows
    stored = query_up_weights.shape[0]

    def partner(f, m, c):
        pairs = []
        for z in range(far):
            for y in range(near):
                for k in range(cores):
                    to = (((z + f) % far) * near + (y + m) % near) * cores + (k + c) % cores
                    pairs.append(((z * near + y) * cores + k, to))
        return pairs

    def shift(value, f, m, c):
        return lax.ppermute(value, "serve", partner(f, m, c))

    gain = attention_norm_gain.reshape(width // HEAD, HEAD)
    normed = whole_call(
        norm_body,
        jax.ShapeDtypeStruct((rows, width), BF16),
        (residual_first, residual_second, gain),
        hbm=3,
        scratch=[
            pltpu.VMEM((own, width), BF16),
            pltpu.VMEM((own, width), BF16),
            pltpu.VMEM(gain.shape, BF16),
            pltpu.SemaphoreType.DMA((3,)),
        ],
        cost=1.0,
    )
    normed = normed[None]
    groups = [jnp.concatenate([normed] + [shift(normed, f, 0, 0) for f in range(1, far)])]
    groups += [shift(groups[0], 0, m, 0) for m in range(1, near)]

    groups[0], at = lax.optimization_barrier((groups[0], index[None]))
    sent = -(-(rows * local + rows) // 8) * 8
    narrow = jax.ShapeDtypeStruct((all_rows, 1), jnp.int32)
    table = jax.ShapeDtypeStruct((all_rows, HEAD), F32)
    square = jax.ShapeDtypeStruct((all_rows, all_rows), BF16)
    slot, near_slot, cosine, sine, key_cosine, key_sine, place, unplace, send, order, take = whole_call(
        functools.partial(prep_body, sizes, rank, own, key_cols, adapters),
        (
            narrow,
            narrow,
            table,
            table,
            table,
            table,
            square,
            square,
            jax.ShapeDtypeStruct((n * sent, all_rows * (local + 1)), BF16),
            jax.ShapeDtypeStruct((own * HEADS * STEPS, n * sent), BF16),
            jax.ShapeDtypeStruct((all_rows * local, n * rows * local), BF16),
        ),
        (at, lengths, request_adapter, adapter_slot),
        smem=1,
        hbm=3,
        scratch=[
            pltpu.SMEM(lengths.shape, jnp.int32),
            pltpu.SMEM(request_adapter.shape, jnp.int32),
            pltpu.SMEM(adapter_slot.shape, jnp.int32),
            pltpu.SemaphoreType.DMA((3,)),
        ],
        cost=4.0,
    )
    slot, groups[1] = lax.optimization_barrier((slot, groups[1]))

    groups += [shift(group, 0, 0, c) for c in range(1, cores) for group in groups[:near]]

    query_down = jnp.swapaxes(query_down_weights, 1, 2).reshape(adapters * rank, width)
    value_down = jnp.swapaxes(value_down_weights, 1, 2).reshape(adapters * rank, width)
    packed_rows = all_rows * 2 * rank // HEAD
    x, low = whole_call(
        functools.partial(low_body, rank, len(groups)),
        (
            jax.ShapeDtypeStruct((all_rows, width), BF16),
            jax.ShapeDtypeStruct((packed_rows, HEAD), BF16),
        ),
        (*groups, query_down, value_down, near_slot, place),
        cost=0.3,
    )
    lows = [shift(low, 0, m, c) for m in range(near) for c in range(cores) if m + c]
    low = whole_call(
        join_body, jax.ShapeDtypeStruct(low.shape, BF16), (low, *lows), cost=0.1
    )
    lows = [low] + [shift(low, f, 0, 0) for f in range(1, far)]

    base_q, base_kv = whole_call(
        functools.partial(base_body, 2048),
        (
            jax.ShapeDtypeStruct((all_rows, query_cols), F32),
            jax.ShapeDtypeStruct((all_rows, HEAD), F32),
        ),
        (x, query_matrix, key_matrix.T, value_matrix.T),
        cost=0.6,
    )

    ready = whole_call(
        functools.partial(ready_body, rank, len(lows)),
        jax.ShapeDtypeStruct((n, sent, HEAD), BF16),
        (
            base_q,
            base_kv,
            *lows,
            unplace,
            slot,
            query_up_weights.reshape(stored * rank, query_cols),
            value_up_weights.reshape(stored * rank, key_cols),
            cosine,
            sine,
            key_cosine,
            key_sine,
            send,
        ),
        cost=0.9,
    )
    arrived = lax.all_to_all(ready, "serve", split_axis=0, concat_axis=0, tiled=True)

    context, new_keys, new_values = whole_call(
        functools.partial(attend_body, own, key_cols),
        (
            jax.ShapeDtypeStruct((n, rows * local, HEAD), BF16),
            jax.ShapeDtypeStruct((own, STEPS, KV_HEADS * HEAD), BF16),
            jax.ShapeDtypeStruct((own, STEPS, KV_HEADS * HEAD), BF16),
        ),
        (index[None], lengths, arrived, order, rotated_key_cache, stored_value_cache),
        smem=2,
        scratch=[pltpu.VMEM((own * HEADS * STEPS, HEAD), F32)],
        cost=1.0,
    )
    context = lax.all_to_all(context, "serve", split_axis=0, concat_axis=0, tiled=True)

    kinds = jax.ShapeDtypeStruct((all_rows // cores, width), F32)
    mine, other = whole_call(
        functools.partial(out_body, 1024),
        (kinds, kinds),
        (context, take, output_matrix),
        scratch=[pltpu.VMEM((all_rows, query_cols), BF16)],
        cost=0.5,
    )

    def kind(count, dtype):
        return jax.ShapeDtypeStruct((count * rows, width), dtype)

    keep, *others = whole_call(
        near_body,
        (kind(far, F32),) + (kind(far, BF16),) * (near - 1),
        (mine, shift(other, 0, 0, 1)),
        cost=0.1,
    )
    others = [shift(other, 0, m, 0) for m, other in enumerate(others, 1)]
    keep, *others = whole_call(
        functools.partial(far_body, len(others)),
        (kind(1, F32),) + (kind(1, BF16),) * (far - 1),
        (keep, *others),
        cost=0.1,
    )
    others = [shift(other, f, 0, 0) for f, other in enumerate(others, 1)]
    result = jax.ShapeDtypeStruct((own, width), BF16)
    out_one, out_two = whole_call(
        functools.partial(last_body, len(others)),
        (result, result),
        (residual_first, residual_second, keep, *others),
        cost=0.1,
    )
    return (out_one, out_two, new_keys, new_values)


def solution(mesh):
    n = mesh.shape["serve"]
    sizes = (n // 4, 2, 2)
    return jax.shard_map(
        functools.partial(shards, sizes),
        mesh=mesh,
        in_specs=(
            P(("replica", "serve"), None),
            P(("replica", "serve"), None),
            P(),
            P(None, "serve"),
            P(None, "serve"),
            P(None, "serve"),
            P("serve", None),
            P("serve", None, None),
            P("serve", None, None),
            P(None, None, "serve"),
            P(None, None, "serve"),
            P(("replica", "serve"), None, None),
            P(("replica", "serve"), None, None),
            P("replica"),
            P("replica"),
            P(),
        ),
        out_specs=(
            P(("replica", "serve"), None),
            P(("replica", "serve"), None),
            P(("replica", "serve"), None, None),
            P(("replica", "serve"), None, None),
        ),
        check_vma=False,
    )
```

```python
import functools
import math

import jax
import jax.numpy as jnp
from jax import lax
from jax.experimental import pallas as pl
from jax.experimental.pallas import tpu as pltpu
from jax.sharding import PartitionSpec as P

HEADS = 64
KV_HEADS = 8
HEAD = 128
STEPS = 2
LIMIT = 8 * 1024 * 1024
PEAK = 1.15e9
NT = (((1,), (1,)), ((), ()))
F32 = jnp.float32
BF16 = jnp.bfloat16


def dot(a, b):
    return jnp.dot(a, b, preferred_element_type=F32)


def dot_nt(a, b):
    return lax.dot_general(a, b, NT, preferred_element_type=F32)


def whole_call(body, out_shape, args, cost, smem=0, hbm=0, scratch=()):
    specs = [pl.BlockSpec(memory_space=pltpu.SMEM)] * smem
    specs += [pl.BlockSpec(memory_space=pltpu.HBM)] * hbm
    specs += [pl.BlockSpec(memory_space=pltpu.VMEM)] * (len(args) - smem - hbm)
    many = isinstance(out_shape, (tuple, list))
    vmem = pl.BlockSpec(memory_space=pltpu.VMEM)
    return pl.pallas_call(
        body,
        out_shape=out_shape,
        in_specs=specs,
        out_specs=tuple(vmem for _ in out_shape) if many else vmem,
        scratch_shapes=list(scratch),
        compiler_params=pltpu.CompilerParams(vmem_limit_bytes=LIMIT),
        cost_estimate=pl.CostEstimate(
            flops=int(cost * PEAK), bytes_accessed=0, transcendentals=0
        ),
    )(*args)


def scaled_frequency(pair_index):
    base = jnp.exp(pair_index.astype(F32) * (-2.0 * math.log(500000.0) / HEAD))
    wavelength = 2.0 * math.pi / base
    smooth = jnp.clip((8192.0 / wavelength - 1.0) / 3.0, 0.0, 1.0)
    return (1.0 - smooth) * base / 8.0 + smooth * base


def fetch(pairs, sems):
    copies = [
        pltpu.make_async_copy(source, target, sems.at[i])
        for i, (source, target) in enumerate(pairs)
    ]
    for copy in copies:
        copy.start()
    for copy in copies:
        copy.wait()


def norm_body(
    first_hbm, second_hbm, gain_hbm, long_ref, short_ref, first_ref, second_ref, gain_ref, sems
):
    fetch(((first_hbm, first_ref), (second_hbm, second_ref), (gain_hbm, gain_ref)), sems)
    gain = gain_ref[...].astype(F32)
    factors = []
    for ref in (first_ref, second_ref):
        values = ref[...].astype(F32)
        factors.append(lax.rsqrt(jnp.mean(values * values, axis=-1, keepdims=True) + 1e-05))
    factor = jnp.concatenate(factors, axis=0)
    for i in range(gain.shape[0]):
        at = slice(i * HEAD, (i + 1) * HEAD)
        values = jnp.concatenate((first_ref[:, at].astype(F32), second_ref[:, at].astype(F32)))
        values = (values * factor * gain[i : i + 1]).astype(BF16)
        cut = long_ref.shape[1]
        if i * HEAD < cut:
            long_ref[:, at] = values
        else:
            short_ref[:, i * HEAD - cut : (i + 1) * HEAD - cut] = values


def prep_body(
    sizes, rank, own, key_cols, adapters,
    index_ref, length_hbm, adapter_hbm, slot_hbm,
    held_ref, local_ref, cos_ref, sin_ref, kcos_ref, ksin_ref, place_ref, unplace_ref, send_ref,
    order_ref, take_ref, length_ref, adapter_ref, slot_ref, sems,
):
    fetch(((length_hbm, length_ref), (adapter_hbm, adapter_ref), (slot_hbm, slot_ref)), sems)
    far, near, cores = sizes
    n = far * near * cores
    rows = own * STEPS
    all_rows = n * rows
    heads = HEADS // n
    sent = send_ref.shape[0] // n
    index = index_ref[0]
    core_at = index % cores
    near_at = index // cores % near
    far_at = index // (cores * near)

    def device_of(block, sign):
        c, m, f = block // (far * near), block // far % near, block % far
        f = (far_at + sign * f + far) % far
        m = (near_at + sign * m + near) % near
        c = (core_at + sign * c + cores) % cores
        return (f * near + m) * cores + c

    def iota(shape, axis):
        return lax.broadcasted_iota(jnp.int32, shape, axis)

    def split(row):
        return row // rows, row % rows // own, row % own

    block, step, mine = split(iota((all_rows, 1), 0))
    device = device_of(block, -1)
    request = device * own + mine
    length = jnp.zeros_like(request)
    adapter = jnp.zeros_like(request)
    for j in range(length_ref.shape[0]):
        length = jnp.where(request == j, length_ref[j], length)
        adapter = jnp.where(request == j, adapter_ref[j], adapter)
    slot = jnp.zeros_like(request)
    for j in range(slot_ref.shape[0]):
        slot = jnp.where(adapter == j, slot_ref[j], slot)
    held_ref[...] = slot
    local_ref[...] = slot - index * adapters
    position = (length + step).astype(F32)
    lane = iota((1, HEAD), 1)
    odd = jnp.where(lane % 2 == 0, -1.0, 1.0)
    angle = position * scaled_frequency(lane // 2)
    cos_ref[...] = jnp.cos(angle)
    sin_ref[...] = jnp.sin(angle) * odd
    angle = position * scaled_frequency((index * key_cols + lane) % HEAD // 2)
    kcos_ref[...] = jnp.where(lane < key_cols, jnp.cos(angle), 1.0)
    ksin_ref[...] = jnp.where(lane < key_cols, jnp.sin(angle) * odd, 0.0)

    def hot(ref, row, column):
        ref[...] = jnp.where(row == column, 1.0, 0.0).astype(BF16)

    absolute = (device * STEPS + step) * own + mine
    hot(unplace_ref, absolute, iota((1, all_rows), 1))
    block, step, mine = split(iota((1, all_rows), 1))
    absolute = (device_of(block, -1) * STEPS + step) * own + mine
    hot(place_ref, iota((all_rows, 1), 0), absolute)

    column = iota((1, send_ref.shape[1]), 1)
    h = column // all_rows
    block, step, mine = split(column % all_rows)
    wanted = device_of(block, -1) * sent + jnp.where(
        h < heads, (mine * heads + h) * STEPS + step, rows * heads + mine * STEPS + step
    )
    hot(send_ref, iota((n * sent, 1), 0), wanted)

    row = iota((order_ref.shape[0], 1), 0)
    mine, head, step = row // (HEADS * STEPS), row // STEPS % HEADS, row % STEPS
    wanted = (head // heads) * sent + (mine * heads + head % heads) * STEPS + step
    hot(order_ref, wanted, iota((1, n * sent), 1))

    row = iota((take_ref.shape[0], 1), 0)
    h = row // all_rows
    block, step, mine = split(row % all_rows)
    c, m, f = block // (far * near), block // far % near, block % far
    c, m, f = (cores - c) % cores, (near - m) % near, (far - f) % far
    wanted = ((f * near + m) * cores + c) * rows * heads + (mine * heads + h) * STEPS + step
    hot(take_ref, wanted, iota((1, take_ref.shape[1]), 1))


def low_body(rank, sizes, *refs):
    far, near, cores = sizes
    longs, shorts = refs[: cores * near], refs[cores * near : cores * near + 2 * cores]
    qd_ref, vd_ref, local_ref, place_ref, x_ref, out_ref = refs[cores * near + 2 * cores :]
    rows, cut = longs[0].shape[1:]
    sets = max(1, 16 // rows)

    def fill(at, start, parts):
        for lane in range(0, parts[0][0].shape[-1], 1024):
            lanes = slice(lane, lane + 1024)
            block = [ref[(*where, slice(None), lanes)].astype(F32) for ref, *where in parts]
            block = jnp.concatenate(block, axis=0).astype(BF16)
            x_ref[at : at + sets * rows, start + lane : start + lane + 1024] = block

    for c in range(cores):
        for m in range(near):
            for f in range(0, far, sets):
                at = ((c * near + m) * far + f) * rows
                group = range(f, f + sets)
                fill(at, 0, [(longs[c * near + m], g) for g in group])
                here, there = shorts[2 * c : 2 * c + 2]
                fill(at, cut, [(there, g - 1, m) if g else (here, m) for g in group])
    adapters = qd_ref.shape[0] // rank
    maps = jnp.concatenate((qd_ref[...], vd_ref[...]), axis=0)
    low = dot_nt(x_ref[...], maps)
    lane = lax.broadcasted_iota(jnp.int32, low.shape, 1)
    low = jnp.where(lane // rank % adapters == local_ref[...], low, 0.0)
    total = 0.0
    for a in range(adapters):
        q = low[:, a * rank : (a + 1) * rank]
        v = low[:, (adapters + a) * rank : (adapters + a + 1) * rank]
        total = total + jnp.concatenate((q, v), axis=1)
    rows = dot(place_ref[...], total.astype(BF16))
    pack = HEAD // (2 * rank)
    step = rows.shape[0] // pack
    packed = jnp.concatenate([rows[i * step : (i + 1) * step] for i in range(pack)], axis=1)
    out_ref[...] = packed.astype(BF16)


def join_body(*refs):
    total = refs[0][...].astype(F32)
    for ref in refs[1:-1]:
        total = total + ref[...].astype(F32)
    refs[-1][...] = total.astype(BF16)


def base_body(depth, x_ref, q_ref, k_ref, v_ref, oq_ref, okv_ref):
    oq_ref[...] = jnp.zeros_like(oq_ref)
    okv_ref[...] = jnp.zeros_like(okv_ref)
    columns = k_ref.shape[0]
    narrow = jnp.zeros((HEAD - 2 * columns, depth), BF16)

    @pl.loop(0, x_ref.shape[1] // depth)
    def _(i):
        at = pl.ds(pl.multiple_of(i * depth, depth), depth)
        x = x_ref[:, at]
        oq_ref[...] += dot(x, q_ref[at, :])
        both = (k_ref[:, at], v_ref[:, at])
        if 2 * columns < HEAD:
            both += (narrow,)
        okv_ref[...] += dot_nt(x, jnp.concatenate(both, axis=0))


def turned(values, cosine, sine):
    lane = lax.broadcasted_iota(jnp.int32, values.shape, 1)
    width = values.shape[1]
    ahead = pltpu.roll(values, width - 1, 1)
    behind = pltpu.roll(values, 1, 1)
    return values * cosine + jnp.where(lane % 2 == 0, ahead, behind) * sine


def ready_body(
    rank, lows, oq_ref, okv_ref, *refs
):
    low_refs = refs[:lows]
    (
        unplace_ref, slot_ref, uq_ref, uv_ref, cos_ref, sin_ref, kcos_ref, ksin_ref, send_ref, out_ref,
    ) = refs[lows:]
    packed = low_refs[0][...].astype(F32)
    for ref in low_refs[1:]:
        packed = packed + ref[...].astype(F32)
    pack = HEAD // (2 * rank)
    low = jnp.concatenate(
        [packed[:, i * 2 * rank : (i + 1) * 2 * rank] for i in range(pack)], axis=0
    )
    low = dot(unplace_ref[...], low.astype(BF16)).astype(BF16)
    wide = uq_ref.shape[0]
    lane = lax.broadcasted_iota(jnp.int32, (low.shape[0], wide), 1)
    here = lane // rank == slot_ref[...]
    row = lax.broadcasted_iota(jnp.int32, (2 * rank, wide), 0)
    column = lax.broadcasted_iota(jnp.int32, (2 * rank, wide), 1)
    spread_q = jnp.where(column % rank == row, 1.0, 0.0).astype(BF16)
    spread_v = jnp.where(column % rank + rank == row, 1.0, 0.0).astype(BF16)
    wide_q = jnp.where(here, dot(low, spread_q), 0.0).astype(BF16)
    wide_v = jnp.where(here, dot(low, spread_v), 0.0).astype(BF16)
    query = oq_ref[...] + dot(wide_q, uq_ref[...])
    fresh = turned(okv_ref[...], kcos_ref[...], ksin_ref[...])
    columns = uv_ref.shape[1]
    value = dot(wide_v, uv_ref[...])
    pieces = [jnp.zeros((value.shape[0], columns), F32), value]
    if 2 * columns < HEAD:
        pieces.append(jnp.zeros((value.shape[0], HEAD - 2 * columns), F32))
    fresh = fresh + jnp.concatenate(pieces, axis=1)
    cosine, sine = cos_ref[...], sin_ref[...]
    parts = []
    for h in range(query.shape[1] // HEAD):
        parts.append(turned(query[:, h * HEAD : (h + 1) * HEAD], cosine, sine))
    parts.append(fresh)
    stacked = jnp.concatenate(parts, axis=0).astype(BF16)
    out_ref[...] = dot(send_ref[...], stacked).astype(BF16).reshape(out_ref.shape)


def attend_body(
    sizes, own, columns, index_ref, len_ref, x_ref, order_ref, k_ref, v_ref, nk_ref, nv_ref, *refs
):
    far, near, cores = sizes
    ctx_refs, s_ref = refs[:-1], refs[-1]
    n, span = x_ref.shape[0], k_ref.shape[1]
    group = HEADS // KV_HEADS
    local = HEADS // n
    rows = own * STEPS
    mine = group * STEPS
    x = x_ref[...]
    queries = dot(order_ref[...], x.reshape(n * x.shape[1], HEAD)).astype(BF16)
    wide = x.astype(F32)
    first = rows * local
    fresh = [wide[i, first : first + rows] for i in range(n)]
    each = n // KV_HEADS
    keys, values = [], []
    for g in range(KV_HEADS):
        pieces = fresh[g * each : (g + 1) * each]
        keys.append(jnp.concatenate([p[:, :columns] for p in pieces], axis=1))
        values.append(jnp.concatenate([p[:, columns : 2 * columns] for p in pieces], axis=1))
    new_keys = jnp.concatenate(keys, axis=1)
    new_values = jnp.concatenate(values, axis=1)
    for b in range(own):
        at = slice(b * STEPS, (b + 1) * STEPS)
        nk_ref[b] = new_keys[at].astype(BF16)
        nv_ref[b] = new_values[at].astype(BF16)
    pad = jnp.zeros((16 - rows, HEAD), F32)
    keys = [jnp.concatenate((k, pad), axis=0).astype(BF16) for k in keys]
    values = [jnp.concatenate((v, pad), axis=0).astype(BF16) for v in values]
    scale = HEAD ** (-0.5)
    contexts = []
    for b in range(own):
        q = queries[b * KV_HEADS * mine : (b + 1) * KV_HEADS * mine]
        cached, newer = [], []
        for g in range(KV_HEADS):
            qg = q[g * mine : (g + 1) * mine]
            cached.append(dot_nt(qg, k_ref[b, :, g * HEAD : (g + 1) * HEAD]))
            newer.append(dot_nt(qg, keys[g]))
        cached = jnp.concatenate(cached, axis=0) * scale
        newer = jnp.concatenate(newer, axis=0) * scale
        place = lax.broadcasted_iota(jnp.int32, cached.shape, 1)
        cached = jnp.where(place < len_ref[index_ref[0] * own + b], cached, -1e30)
        step = lax.broadcasted_iota(jnp.int32, newer.shape, 0) % STEPS
        at = lax.broadcasted_iota(jnp.int32, newer.shape, 1) - b * STEPS
        newer = jnp.where((at >= 0) & (at <= step), newer, -1e30)
        top = jnp.maximum(
            jnp.max(cached, axis=1, keepdims=True), jnp.max(newer, axis=1, keepdims=True)
        )
        cached = jnp.exp(cached - top)
        newer = jnp.exp(newer - top)
        total = jnp.sum(cached, axis=1, keepdims=True) + jnp.sum(newer, axis=1, keepdims=True)
        cached = (cached / total).astype(BF16)
        newer = (newer / total).astype(BF16)
        for g in range(KV_HEADS):
            at_rows = slice(g * mine, (g + 1) * mine)
            part = dot(cached[at_rows], v_ref[b, :, g * HEAD : (g + 1) * HEAD])
            s_ref[(b * KV_HEADS + g) * mine : (b * KV_HEADS + g + 1) * mine] = part + dot(
                newer[at_rows], values[g]
            )
    step = local * STEPS
    half = KV_HEADS * mine
    index = index_ref[0]
    core_at = index % cores
    near_at = index // cores % near
    far_at = index // (cores * near)
    for p, ref in enumerate(ctx_refs):
        m, c = p // cores, p % cores
        for f in range(far):
            i = ((far_at + f) % far * near + (near_at + m) % near) * cores + (core_at + c) % cores
            at = pl.multiple_of(i * step, step)
            block = [s_ref[pl.ds(b * half + at, step)] for b in range(own)]
            ref[f] = jnp.concatenate(block, axis=0).astype(BF16)


def take_body(came, *refs):
    ctx_refs, (take_ref, w_ref, a_ref, mine_ref, other_ref) = refs[:came], refs[came:]
    rows = a_ref.shape[0]
    x = jnp.concatenate([ref[...].reshape(-1, HEAD) for ref in ctx_refs], axis=0)
    taken = dot(take_ref[...], x).astype(BF16)
    for h in range(a_ref.shape[1] // HEAD):
        a_ref[:, h * HEAD : (h + 1) * HEAD] = taken[h * rows : (h + 1) * rows]
    out_body(0, a_ref, w_ref, mine_ref, other_ref)


def out_body(start, a_ref, w_ref, mine_ref, other_ref):
    half = mine_ref.shape[0]
    tile = 1024

    @pl.loop(0, mine_ref.shape[1] // tile)
    def _(i):
        at = pl.ds(pl.multiple_of(i * tile, tile), tile)
        product = dot(a_ref[...], w_ref[:, pl.ds(pl.multiple_of(start + i * tile, tile), tile)])
        mine_ref[:, at] = product[:half]
        other_ref[:, at] = product[half:]


def far_first_body(near, mine_ref, came_ref, *refs):
    total = mine_ref[...] + came_ref[...]
    rows = refs[0].shape[0] // near
    for f, ref in enumerate(refs):
        blocks = [(m * len(refs) + f) * rows for m in range(near)]
        value = jnp.concatenate([total[at : at + rows] for at in blocks], axis=0)
        ref[...] = value.astype(ref.dtype)


def pack_body(came, *refs):
    for f, ref in enumerate(refs[came:]):
        for p in range(came):
            ref[p] = refs[p][f]


def near_body(mine_ref, came_ref, *refs):
    rows = refs[0].shape[0]
    total = mine_ref[...] + came_ref[...]
    refs[0][...] = total[:rows]
    for m, ref in enumerate(refs[1:], 1):
        ref[...] = total[m * rows : (m + 1) * rows].astype(BF16)


def far_body(came, *refs):
    total = refs[0][...]
    for ref in refs[1 : 1 + came]:
        total = total + ref[...].astype(F32)
    refs = refs[1 + came :]
    rows = refs[0].shape[0]
    refs[0][...] = total[:rows]
    for f, ref in enumerate(refs[1:], 1):
        ref[...] = total[f * rows : (f + 1) * rows].astype(BF16)


def last_body(longs, first_ref, second_ref, *refs):
    one_ref, two_ref = refs[-2:]
    totals = []
    for part in (refs[:longs], refs[longs:-2]):
        total = part[0][...]
        for ref in part[1:]:
            total = total + ref[...].astype(F32)
        totals.append(total)
    total = jnp.concatenate(totals, axis=1)
    own = one_ref.shape[0]
    one_ref[...] = (first_ref[...].astype(F32) + total[:own]).astype(BF16)
    two_ref[...] = (second_ref[...].astype(F32) + total[own:]).astype(BF16)


def shards(
    sizes,
    residual_first,
    residual_second,
    attention_norm_gain,
    query_matrix,
    key_matrix,
    value_matrix,
    output_matrix,
    query_down_weights,
    value_down_weights,
    query_up_weights,
    value_up_weights,
    rotated_key_cache,
    stored_value_cache,
    lengths,
    request_adapter,
    adapter_slot,
):
    far, near, cores = sizes
    n = far * near * cores
    index = lax.axis_index("serve")
    own, width = residual_first.shape
    adapters, _, rank = query_down_weights.shape
    query_cols = query_matrix.shape[1]
    key_cols = key_matrix.shape[1]
    local = query_cols // HEAD
    rows = own * STEPS
    all_rows = n * rows
    stored = query_up_weights.shape[0]

    def partner(f, m, c):
        pairs = []
        for z in range(far):
            for y in range(near):
                for k in range(cores):
                    to = (((z + f) % far) * near + (y + m) % near) * cores + (k + c) % cores
                    pairs.append(((z * near + y) * cores + k, to))
        return pairs

    def shift(value, f, m, c):
        return lax.ppermute(value, "serve", partner(f, m, c))

    def swap(value, bit):
        return lax.ppermute(value, "serve", [(i, i ^ bit) for i in range(n)])

    gain = attention_norm_gain.reshape(width // HEAD, HEAD)
    cut = width * 5 // 8
    normed, short = whole_call(
        norm_body,
        (
            jax.ShapeDtypeStruct((rows, cut), BF16),
            jax.ShapeDtypeStruct((rows, width - cut), BF16),
        ),
        (residual_first, residual_second, gain),
        hbm=3,
        scratch=[
            pltpu.VMEM((own, width), BF16),
            pltpu.VMEM((own, width), BF16),
            pltpu.VMEM(gain.shape, BF16),
            pltpu.SemaphoreType.DMA((3,)),
        ],
        cost=1.0,
    )
    normed, short = normed[None], short[None]
    shorts = [jnp.concatenate([short] + [shift(short, 0, m, 0) for m in range(1, near)])]
    longs = [jnp.concatenate([normed] + [shift(normed, f, 0, 0) for f in range(1, far)])]
    longs += [shift(longs[0], 0, m, 0) for m in range(1, near)]
    shorts.append(jnp.stack([shift(shorts[0], f, 0, 0) for f in range(1, far)]))

    longs[0], at = lax.optimization_barrier((longs[0], index[None]))
    sent = -(-(rows * local + rows) // 8) * 8
    narrow = jax.ShapeDtypeStruct((all_rows, 1), jnp.int32)
    table = jax.ShapeDtypeStruct((all_rows, HEAD), F32)
    square = jax.ShapeDtypeStruct((all_rows, all_rows), BF16)
    slot, near_slot, cosine, sine, key_cosine, key_sine, place, unplace, send, order, take = whole_call(
        functools.partial(prep_body, sizes, rank, own, key_cols, adapters),
        (
            narrow,
            narrow,
            table,
            table,
            table,
            table,
            square,
            square,
            jax.ShapeDtypeStruct((n * sent, all_rows * (local + 1)), BF16),
            jax.ShapeDtypeStruct((own * HEADS * STEPS, n * sent), BF16),
            jax.ShapeDtypeStruct((all_rows * local, n * rows * local), BF16),
        ),
        (at, lengths, request_adapter, adapter_slot),
        smem=1,
        hbm=3,
        scratch=[
            pltpu.SMEM(lengths.shape, jnp.int32),
            pltpu.SMEM(request_adapter.shape, jnp.int32),
            pltpu.SMEM(adapter_slot.shape, jnp.int32),
            pltpu.SemaphoreType.DMA((3,)),
        ],
        cost=4.0,
    )
    slot, longs[1] = lax.optimization_barrier((slot, longs[1]))

    longs += [shift(part, 0, 0, c) for c in range(1, cores) for part in longs[:near]]
    shorts += [shift(part, 0, 0, c) for c in range(1, cores) for part in shorts[:2]]

    query_down = jnp.swapaxes(query_down_weights, 1, 2).reshape(adapters * rank, width)
    value_down = jnp.swapaxes(value_down_weights, 1, 2).reshape(adapters * rank, width)
    packed_rows = all_rows * 2 * rank // HEAD
    x, low = whole_call(
        functools.partial(low_body, rank, sizes),
        (
            jax.ShapeDtypeStruct((all_rows, width), BF16),
            jax.ShapeDtypeStruct((packed_rows, HEAD), BF16),
        ),
        (*longs, *shorts, query_down, value_down, near_slot, place),
        cost=0.3,
    )
    bit = 1
    while 2 * bit < n:
        low = whole_call(
            join_body, jax.ShapeDtypeStruct(low.shape, BF16), (low, swap(low, bit)), cost=0.1
        )
        bit *= 2
    lows = [low, swap(low, bit)]

    base_q, base_kv = whole_call(
        functools.partial(base_body, 2048),
        (
            jax.ShapeDtypeStruct((all_rows, query_cols), F32),
            jax.ShapeDtypeStruct((all_rows, HEAD), F32),
        ),
        (x, query_matrix, key_matrix.T, value_matrix.T),
        cost=0.6,
    )

    ready = whole_call(
        functools.partial(ready_body, rank, len(lows)),
        jax.ShapeDtypeStruct((n, sent, HEAD), BF16),
        (
            base_q,
            base_kv,
            *lows,
            unplace,
            slot,
            query_up_weights.reshape(stored * rank, query_cols),
            value_up_weights.reshape(stored * rank, key_cols),
            cosine,
            sine,
            key_cosine,
            key_sine,
            send,
        ),
        cost=0.9,
    )
    arrived = lax.all_to_all(ready, "serve", split_axis=0, concat_axis=0, tiled=True)

    fresh = jax.ShapeDtypeStruct((own, STEPS, KV_HEADS * HEAD), BF16)
    plane = near * cores
    new_keys, new_values, *context = whole_call(
        functools.partial(attend_body, sizes, own, key_cols),
        (fresh, fresh) + (jax.ShapeDtypeStruct((far, rows * local, HEAD), BF16),) * plane,
        (index[None], lengths, arrived, order, rotated_key_cache, stored_value_cache),
        smem=2,
        scratch=[pltpu.VMEM((own * HEADS * STEPS, HEAD), F32)],
        cost=1.0,
    )
    context = context[:1] + [shift(context[p], 0, p // cores, p % cores) for p in range(1, plane)]
    context = whole_call(
        functools.partial(pack_body, plane),
        (jax.ShapeDtypeStruct((plane, rows * local, HEAD), BF16),) * far,
        tuple(context),
        cost=0.1,
    )
    context = [context[0]] + [shift(context[f], f, 0, 0) for f in range(1, far)]

    half = all_rows // cores

    def kinds(count, columns):
        return (jax.ShapeDtypeStruct((count, columns), F32),) * 2

    taken, mine_long, other_long = whole_call(
        functools.partial(take_body, far),
        (jax.ShapeDtypeStruct((all_rows, query_cols), BF16),) + kinds(half, cut),
        (*context, take, output_matrix),
        cost=0.4,
    )
    mine_short, other_short = whole_call(
        functools.partial(out_body, cut),
        kinds(half, width - cut),
        (taken, output_matrix),
        cost=0.3,
    )

    def kind(count, columns, dtype):
        return jax.ShapeDtypeStruct((count * rows, columns), dtype)

    keep, *others = whole_call(
        near_body,
        (kind(far, cut, F32),) + (kind(far, cut, BF16),) * (near - 1),
        (mine_long, shift(other_long, 0, 0, 1)),
        cost=0.1,
    )
    others = [shift(other, 0, m, 0) for m, other in enumerate(others, 1)]
    short, *sides = whole_call(
        functools.partial(far_first_body, near),
        (kind(near, width - cut, F32),) + (kind(near, width - cut, BF16),) * (far - 1),
        (mine_short, shift(other_short, 0, 0, 1)),
        cost=0.1,
    )
    sides = [shift(side, f, 0, 0) for f, side in enumerate(sides, 1)]
    keep, *others = whole_call(
        functools.partial(far_body, len(others)),
        (kind(1, cut, F32),) + (kind(1, cut, BF16),) * (far - 1),
        (keep, *others),
        cost=0.1,
    )
    others = [shift(other, f, 0, 0) for f, other in enumerate(others, 1)]
    short, *sides = whole_call(
        functools.partial(far_body, len(sides)),
        (kind(1, width - cut, F32),) + (kind(1, width - cut, BF16),) * (near - 1),
        (short, *sides),
        cost=0.1,
    )
    sides = [shift(side, 0, m, 0) for m, side in enumerate(sides, 1)]
    result = jax.ShapeDtypeStruct((own, width), BF16)
    out_one, out_two = whole_call(
        functools.partial(last_body, 1 + len(others)),
        (result, result),
        (residual_first, residual_second, keep, *others, short, *sides),
        cost=0.1,
    )
    return (out_one, out_two, new_keys, new_values)


def solution(mesh):
    n = mesh.shape["serve"]
    sizes = (n // 4, 2, 2)
    return jax.shard_map(
        functools.partial(shards, sizes),
        mesh=mesh,
        in_specs=(
            P(("replica", "serve"), None),
            P(("replica", "serve"), None),
            P(),
            P(None, "serve"),
            P(None, "serve"),
            P(None, "serve"),
            P("serve", None),
            P("serve", None, None),
            P("serve", None, None),
            P(None, None, "serve"),
            P(None, None, "serve"),
            P(("replica", "serve"), None, None),
            P(("replica", "serve"), None, None),
            P("replica"),
            P("replica"),
            P(),
        ),
        out_specs=(
            P(("replica", "serve"), None),
            P(("replica", "serve"), None),
            P(("replica", "serve"), None, None),
            P(("replica", "serve"), None, None),
        ),
        check_vma=False,
    )
```

```python
import functools
import math

import jax
import jax.numpy as jnp
from jax import lax
from jax.experimental import pallas as pl
from jax.experimental.pallas import tpu as pltpu
from jax.sharding import PartitionSpec as P

HEADS = 64
KV_HEADS = 8
HEAD = 128
STEPS = 2
LIMIT = 8 * 1024 * 1024
PEAK = 1.15e9
NT = (((1,), (1,)), ((), ()))
F32 = jnp.float32
BF16 = jnp.bfloat16


def dot(a, b):
    return jnp.dot(a, b, preferred_element_type=F32)


def dot_nt(a, b):
    return lax.dot_general(a, b, NT, preferred_element_type=F32)


def whole_call(body, out_shape, args, cost, smem=0, hbm=0, scratch=()):
    specs = [pl.BlockSpec(memory_space=pltpu.SMEM)] * smem
    specs += [pl.BlockSpec(memory_space=pltpu.HBM)] * hbm
    specs += [pl.BlockSpec(memory_space=pltpu.VMEM)] * (len(args) - smem - hbm)
    many = isinstance(out_shape, (tuple, list))
    vmem = pl.BlockSpec(memory_space=pltpu.VMEM)
    return pl.pallas_call(
        body,
        out_shape=out_shape,
        in_specs=specs,
        out_specs=tuple(vmem for _ in out_shape) if many else vmem,
        scratch_shapes=list(scratch),
        compiler_params=pltpu.CompilerParams(vmem_limit_bytes=LIMIT),
        cost_estimate=pl.CostEstimate(
            flops=int(cost * PEAK), bytes_accessed=0, transcendentals=0
        ),
    )(*args)


def scaled_frequency(pair_index):
    base = jnp.exp(pair_index.astype(F32) * (-2.0 * math.log(500000.0) / HEAD))
    wavelength = 2.0 * math.pi / base
    smooth = jnp.clip((8192.0 / wavelength - 1.0) / 3.0, 0.0, 1.0)
    return (1.0 - smooth) * base / 8.0 + smooth * base


def fetch(pairs, sems):
    copies = [
        pltpu.make_async_copy(source, target, sems.at[i])
        for i, (source, target) in enumerate(pairs)
    ]
    for copy in copies:
        copy.start()
    for copy in copies:
        copy.wait()


def norm_body(first_hbm, second_hbm, gain_hbm, out_ref, first_ref, second_ref, gain_ref, sems):
    fetch(((first_hbm, first_ref), (second_hbm, second_ref), (gain_hbm, gain_ref)), sems)
    gain = gain_ref[...].astype(F32)
    factors = []
    for ref in (first_ref, second_ref):
        values = ref[...].astype(F32)
        factors.append(lax.rsqrt(jnp.mean(values * values, axis=-1, keepdims=True) + 1e-05))
    factor = jnp.concatenate(factors, axis=0)
    for i in range(gain.shape[0]):
        at = slice(i * HEAD, (i + 1) * HEAD)
        values = jnp.concatenate((first_ref[:, at].astype(F32), second_ref[:, at].astype(F32)))
        out_ref[:, at] = (values * factor * gain[i : i + 1]).astype(BF16)


def prep_body(
    sizes, rank, own, key_cols, adapters,
    index_ref, length_hbm, adapter_hbm, slot_hbm,
    held_ref, local_ref, cos_ref, sin_ref, kcos_ref, ksin_ref, place_ref, unplace_ref, send_ref,
    order_ref, take_ref, length_ref, adapter_ref, slot_ref, sems,
):
    fetch(((length_hbm, length_ref), (adapter_hbm, adapter_ref), (slot_hbm, slot_ref)), sems)
    far, near, cores = sizes
    n = far * near * cores
    rows = own * STEPS
    all_rows = n * rows
    heads = HEADS // n
    sent = send_ref.shape[0] // n
    index = index_ref[0]
    core_at = index % cores
    near_at = index // cores % near
    far_at = index // (cores * near)

    def device_of(block, sign):
        c, m, f = block // (far * near), block // far % near, block % far
        f = f if sign < 0 else (far_at + f) % far
        m = (near_at + sign * m + near) % near
        c = (core_at + sign * c + cores) % cores
        return (f * near + m) * cores + c

    def iota(shape, axis):
        return lax.broadcasted_iota(jnp.int32, shape, axis)

    def split(row):
        return row // rows, row % rows // own, row % own

    block, step, mine = split(iota((all_rows, 1), 0))
    device = device_of(block, -1)
    request = device * own + mine
    length = jnp.zeros_like(request)
    adapter = jnp.zeros_like(request)
    for j in range(length_ref.shape[0]):
        length = jnp.where(request == j, length_ref[j], length)
        adapter = jnp.where(request == j, adapter_ref[j], adapter)
    slot = jnp.zeros_like(request)
    for j in range(slot_ref.shape[0]):
        slot = jnp.where(adapter == j, slot_ref[j], slot)
    held_ref[...] = slot
    local_ref[...] = slot - index * adapters
    position = (length + step).astype(F32)
    lane = iota((1, HEAD), 1)
    odd = jnp.where(lane % 2 == 0, -1.0, 1.0)
    angle = position * scaled_frequency(lane // 2)
    cos_ref[...] = jnp.cos(angle)
    sin_ref[...] = jnp.sin(angle) * odd
    angle = position * scaled_frequency((index * key_cols + lane) % HEAD // 2)
    kcos_ref[...] = jnp.where(lane < key_cols, jnp.cos(angle), 1.0)
    ksin_ref[...] = jnp.where(lane < key_cols, jnp.sin(angle) * odd, 0.0)

    def hot(ref, row, column):
        ref[...] = jnp.where(row == column, 1.0, 0.0).astype(BF16)

    absolute = (device * STEPS + step) * own + mine
    hot(unplace_ref, absolute, iota((1, all_rows), 1))
    block, step, mine = split(iota((1, all_rows), 1))
    absolute = (device_of(block, -1) * STEPS + step) * own + mine
    hot(place_ref, iota((all_rows, 1), 0), absolute)

    column = iota((1, send_ref.shape[1]), 1)
    h = column // all_rows
    block, step, mine = split(column % all_rows)
    wanted = device_of(block, -1) * sent + jnp.where(
        h < heads, (mine * heads + h) * STEPS + step, rows * heads + mine * STEPS + step
    )
    hot(send_ref, iota((n * sent, 1), 0), wanted)

    row = iota((order_ref.shape[0], 1), 0)
    mine, head, step = row // (HEADS * STEPS), row // STEPS % HEADS, row % STEPS
    wanted = (head // heads) * sent + (mine * heads + head % heads) * STEPS + step
    hot(order_ref, wanted, iota((1, n * sent), 1))

    row = iota((take_ref.shape[0], 1), 0)
    h = row // all_rows
    block, step, mine = split(row % all_rows)
    wanted = device_of(block, 1) * rows * heads + (mine * heads + h) * STEPS + step
    hot(take_ref, wanted, iota((1, take_ref.shape[1]), 1))


def low_body(rank, groups, *refs):
    parts, (qd_ref, vd_ref, local_ref, place_ref, x_ref, out_ref) = refs[:groups], refs[groups:]
    rows = parts[0].shape[1]
    sets = max(1, 16 // rows)
    for p, part in enumerate(parts):
        for i in range(0, part.shape[0], sets):
            at = (p * part.shape[0] + i) * rows
            for lane in range(0, x_ref.shape[1], 1024):
                lanes = slice(lane, lane + 1024)
                block = [part[i + j, :, lanes].astype(F32) for j in range(sets)]
                x_ref[at : at + sets * rows, lanes] = jnp.concatenate(block, axis=0).astype(BF16)
    adapters = qd_ref.shape[0] // rank
    maps = jnp.concatenate((qd_ref[...], vd_ref[...]), axis=0)
    low = dot_nt(x_ref[...], maps)
    lane = lax.broadcasted_iota(jnp.int32, low.shape, 1)
    low = jnp.where(lane // rank % adapters == local_ref[...], low, 0.0)
    total = 0.0
    for a in range(adapters):
        q = low[:, a * rank : (a + 1) * rank]
        v = low[:, (adapters + a) * rank : (adapters + a + 1) * rank]
        total = total + jnp.concatenate((q, v), axis=1)
    rows = dot(place_ref[...], total.astype(BF16))
    pack = HEAD // (2 * rank)
    step = rows.shape[0] // pack
    packed = jnp.concatenate([rows[i * step : (i + 1) * step] for i in range(pack)], axis=1)
    out_ref[...] = packed.astype(BF16)


def join_body(came_ref, out_ref):
    out_ref[...] = jnp.sum(came_ref[...].astype(F32), axis=0).astype(BF16)


def base_body(depth, x_ref, q_ref, k_ref, v_ref, oq_ref, okv_ref):
    oq_ref[...] = jnp.zeros_like(oq_ref)
    okv_ref[...] = jnp.zeros_like(okv_ref)
    columns = k_ref.shape[0]
    narrow = jnp.zeros((HEAD - 2 * columns, depth), BF16)

    @pl.loop(0, x_ref.shape[1] // depth)
    def _(i):
        at = pl.ds(pl.multiple_of(i * depth, depth), depth)
        x = x_ref[:, at]
        oq_ref[...] += dot(x, q_ref[at, :])
        both = (k_ref[:, at], v_ref[:, at])
        if 2 * columns < HEAD:
            both += (narrow,)
        okv_ref[...] += dot_nt(x, jnp.concatenate(both, axis=0))


def turned(values, cosine, sine):
    lane = lax.broadcasted_iota(jnp.int32, values.shape, 1)
    width = values.shape[1]
    ahead = pltpu.roll(values, width - 1, 1)
    behind = pltpu.roll(values, 1, 1)
    return values * cosine + jnp.where(lane % 2 == 0, ahead, behind) * sine


def ready_body(
    rank, oq_ref, okv_ref, low_ref, unplace_ref, slot_ref, uq_ref, uv_ref, cos_ref, sin_ref,
    kcos_ref, ksin_ref, send_ref, out_ref,
):
    packed = jnp.sum(low_ref[...].astype(F32), axis=0)
    pack = HEAD // (2 * rank)
    low = jnp.concatenate(
        [packed[:, i * 2 * rank : (i + 1) * 2 * rank] for i in range(pack)], axis=0
    )
    low = dot(unplace_ref[...], low.astype(BF16)).astype(BF16)
    wide = uq_ref.shape[0]
    lane = lax.broadcasted_iota(jnp.int32, (low.shape[0], wide), 1)
    here = lane // rank == slot_ref[...]
    row = lax.broadcasted_iota(jnp.int32, (2 * rank, wide), 0)
    column = lax.broadcasted_iota(jnp.int32, (2 * rank, wide), 1)
    spread_q = jnp.where(column % rank == row, 1.0, 0.0).astype(BF16)
    spread_v = jnp.where(column % rank + rank == row, 1.0, 0.0).astype(BF16)
    wide_q = jnp.where(here, dot(low, spread_q), 0.0).astype(BF16)
    wide_v = jnp.where(here, dot(low, spread_v), 0.0).astype(BF16)
    query = oq_ref[...] + dot(wide_q, uq_ref[...])
    fresh = turned(okv_ref[...], kcos_ref[...], ksin_ref[...])
    columns = uv_ref.shape[1]
    value = dot(wide_v, uv_ref[...])
    pieces = [jnp.zeros((value.shape[0], columns), F32), value]
    if 2 * columns < HEAD:
        pieces.append(jnp.zeros((value.shape[0], HEAD - 2 * columns), F32))
    fresh = fresh + jnp.concatenate(pieces, axis=1)
    cosine, sine = cos_ref[...], sin_ref[...]
    parts = []
    for h in range(query.shape[1] // HEAD):
        parts.append(turned(query[:, h * HEAD : (h + 1) * HEAD], cosine, sine))
    parts.append(fresh)
    stacked = jnp.concatenate(parts, axis=0).astype(BF16)
    out_ref[...] = dot(send_ref[...], stacked).astype(BF16).reshape(out_ref.shape)


def attend_body(
    own, columns, index_ref, len_ref, x_ref, order_ref, k_ref, v_ref, nk_ref, nv_ref, ctx_ref, s_ref
):
    n, span = x_ref.shape[0], k_ref.shape[1]
    group = HEADS // KV_HEADS
    local = HEADS // n
    rows = own * STEPS
    mine = group * STEPS
    x = x_ref[...]
    queries = dot(order_ref[...], x.reshape(n * x.shape[1], HEAD)).astype(BF16)
    wide = x.astype(F32)
    first = rows * local
    fresh = [wide[i, first : first + rows] for i in range(n)]
    each = n // KV_HEADS
    keys, values = [], []
    for g in range(KV_HEADS):
        pieces = fresh[g * each : (g + 1) * each]
        keys.append(jnp.concatenate([p[:, :columns] for p in pieces], axis=1))
        values.append(jnp.concatenate([p[:, columns : 2 * columns] for p in pieces], axis=1))
    new_keys = jnp.concatenate(keys, axis=1)
    new_values = jnp.concatenate(values, axis=1)
    for b in range(own):
        at = slice(b * STEPS, (b + 1) * STEPS)
        nk_ref[b] = new_keys[at].astype(BF16)
        nv_ref[b] = new_values[at].astype(BF16)
    pad = jnp.zeros((16 - rows, HEAD), F32)
    keys = [jnp.concatenate((k, pad), axis=0).astype(BF16) for k in keys]
    values = [jnp.concatenate((v, pad), axis=0).astype(BF16) for v in values]
    scale = HEAD ** (-0.5)
    contexts = []
    for b in range(own):
        q = queries[b * KV_HEADS * mine : (b + 1) * KV_HEADS * mine]
        cached, newer = [], []
        for g in range(KV_HEADS):
            qg = q[g * mine : (g + 1) * mine]
            cached.append(dot_nt(qg, k_ref[b, :, g * HEAD : (g + 1) * HEAD]))
            newer.append(dot_nt(qg, keys[g]))
        cached = jnp.concatenate(cached, axis=0) * scale
        newer = jnp.concatenate(newer, axis=0) * scale
        place = lax.broadcasted_iota(jnp.int32, cached.shape, 1)
        cached = jnp.where(place < len_ref[index_ref[0] * own + b], cached, -1e30)
        step = lax.broadcasted_iota(jnp.int32, newer.shape, 0) % STEPS
        at = lax.broadcasted_iota(jnp.int32, newer.shape, 1) - b * STEPS
        newer = jnp.where((at >= 0) & (at <= step), newer, -1e30)
        top = jnp.maximum(
            jnp.max(cached, axis=1, keepdims=True), jnp.max(newer, axis=1, keepdims=True)
        )
        cached = jnp.exp(cached - top)
        newer = jnp.exp(newer - top)
        total = jnp.sum(cached, axis=1, keepdims=True) + jnp.sum(newer, axis=1, keepdims=True)
        cached = (cached / total).astype(BF16)
        newer = (newer / total).astype(BF16)
        for g in range(KV_HEADS):
            at_rows = slice(g * mine, (g + 1) * mine)
            part = dot(cached[at_rows], v_ref[b, :, g * HEAD : (g + 1) * HEAD])
            s_ref[(b * KV_HEADS + g) * mine : (b * KV_HEADS + g + 1) * mine] = part + dot(
                newer[at_rows], values[g]
            )
    step = local * STEPS
    half = KV_HEADS * mine
    for i in range(n):
        block = [s_ref[b * half + i * step : b * half + (i + 1) * step] for b in range(own)]
        ctx_ref[i] = jnp.concatenate(block, axis=0).astype(BF16)


def take_body(ctx_ref, take_ref, w_ref, a_ref, mine_ref, other_ref):
    rows = a_ref.shape[0]
    x = ctx_ref[...].reshape(-1, HEAD)
    taken = dot(take_ref[...], x).astype(BF16)
    for h in range(a_ref.shape[1] // HEAD):
        a_ref[:, h * HEAD : (h + 1) * HEAD] = taken[h * rows : (h + 1) * rows]
    out_body(0, a_ref, w_ref, mine_ref, other_ref)


def out_body(start, a_ref, w_ref, mine_ref, other_ref):
    half = mine_ref.shape[0]
    tile = 1024

    @pl.loop(0, mine_ref.shape[1] // tile)
    def _(i):
        at = pl.ds(pl.multiple_of(i * tile, tile), tile)
        product = dot(a_ref[...], w_ref[:, pl.ds(pl.multiple_of(start + i * tile, tile), tile)])
        mine_ref[:, at] = product[:half]
        other_ref[:, at] = product[half:]


def far_first_body(near, mine_ref, came_ref, *refs):
    total = mine_ref[...] + came_ref[...]
    rows = refs[0].shape[0] // near
    for f, ref in enumerate(refs):
        blocks = [(m * len(refs) + f) * rows for m in range(near)]
        value = jnp.concatenate([total[at : at + rows] for at in blocks], axis=0)
        ref[...] = value.astype(ref.dtype)


def near_body(mine_ref, came_ref, *refs):
    rows = refs[0].shape[0]
    total = mine_ref[...] + came_ref[...]
    refs[0][...] = total[:rows]
    for m, ref in enumerate(refs[1:], 1):
        ref[...] = total[m * rows : (m + 1) * rows].astype(BF16)


def far_body(came, *refs):
    total = refs[0][...]
    for ref in refs[1 : 1 + came]:
        total = total + ref[...].astype(F32)
    refs = refs[1 + came :]
    rows = refs[0].shape[0]
    refs[0][...] = total[:rows]
    for f, ref in enumerate(refs[1:], 1):
        ref[...] = total[f * rows : (f + 1) * rows].astype(BF16)


def last_body(longs, first_ref, second_ref, *refs):
    one_ref, two_ref = refs[-2:]
    totals = []
    for part in (refs[:longs], refs[longs:-2]):
        total = part[0][...]
        for ref in part[1:]:
            total = total + ref[...].astype(F32)
        totals.append(total)
    total = jnp.concatenate(totals, axis=1)
    own = one_ref.shape[0]
    one_ref[...] = (first_ref[...].astype(F32) + total[:own]).astype(BF16)
    two_ref[...] = (second_ref[...].astype(F32) + total[own:]).astype(BF16)


def shards(
    sizes,
    residual_first,
    residual_second,
    attention_norm_gain,
    query_matrix,
    key_matrix,
    value_matrix,
    output_matrix,
    query_down_weights,
    value_down_weights,
    query_up_weights,
    value_up_weights,
    rotated_key_cache,
    stored_value_cache,
    lengths,
    request_adapter,
    adapter_slot,
):
    far, near, cores = sizes
    n = far * near * cores
    index = lax.axis_index("serve")
    own, width = residual_first.shape
    adapters, _, rank = query_down_weights.shape
    query_cols = query_matrix.shape[1]
    key_cols = key_matrix.shape[1]
    local = query_cols // HEAD
    rows = own * STEPS
    all_rows = n * rows
    stored = query_up_weights.shape[0]

    def partner(f, m, c):
        pairs = []
        for z in range(far):
            for y in range(near):
                for k in range(cores):
                    to = (((z + f) % far) * near + (y + m) % near) * cores + (k + c) % cores
                    pairs.append(((z * near + y) * cores + k, to))
        return pairs

    def shift(value, f, m, c):
        return lax.ppermute(value, "serve", partner(f, m, c))

    plane = near * cores

    def along_far(value):
        groups = [[f * plane + p for f in range(far)] for p in range(plane)]
        return lax.all_gather(value, "serve", axis_index_groups=groups)

    def along_plane(value):
        groups = [[f * plane + p for p in range(plane)] for f in range(far)]
        return lax.all_gather(value, "serve", axis_index_groups=groups)

    gain = attention_norm_gain.reshape(width // HEAD, HEAD)
    normed = whole_call(
        norm_body,
        jax.ShapeDtypeStruct((rows, width), BF16),
        (residual_first, residual_second, gain),
        hbm=3,
        scratch=[
            pltpu.VMEM((own, width), BF16),
            pltpu.VMEM((own, width), BF16),
            pltpu.VMEM(gain.shape, BF16),
            pltpu.SemaphoreType.DMA((3,)),
        ],
        cost=1.0,
    )
    groups = [along_far(normed)]
    groups += [shift(groups[0], 0, m, 0) for m in range(1, near)]

    groups[0], at = lax.optimization_barrier((groups[0], index[None]))
    sent = -(-(rows * local + rows) // 8) * 8
    narrow = jax.ShapeDtypeStruct((all_rows, 1), jnp.int32)
    table = jax.ShapeDtypeStruct((all_rows, HEAD), F32)
    square = jax.ShapeDtypeStruct((all_rows, all_rows), BF16)
    slot, near_slot, cosine, sine, key_cosine, key_sine, place, unplace, send, order, take = whole_call(
        functools.partial(prep_body, sizes, rank, own, key_cols, adapters),
        (
            narrow,
            narrow,
            table,
            table,
            table,
            table,
            square,
            square,
            jax.ShapeDtypeStruct((n * sent, all_rows * (local + 1)), BF16),
            jax.ShapeDtypeStruct((own * HEADS * STEPS, n * sent), BF16),
            jax.ShapeDtypeStruct((all_rows * local, n * rows * local), BF16),
        ),
        (at, lengths, request_adapter, adapter_slot),
        smem=1,
        hbm=3,
        scratch=[
            pltpu.SMEM(lengths.shape, jnp.int32),
            pltpu.SMEM(request_adapter.shape, jnp.int32),
            pltpu.SMEM(adapter_slot.shape, jnp.int32),
            pltpu.SemaphoreType.DMA((3,)),
        ],
        cost=4.0,
    )
    slot, groups[1] = lax.optimization_barrier((slot, groups[1]))

    groups += [shift(part, 0, 0, c) for c in range(1, cores) for part in groups[:near]]

    query_down = jnp.swapaxes(query_down_weights, 1, 2).reshape(adapters * rank, width)
    value_down = jnp.swapaxes(value_down_weights, 1, 2).reshape(adapters * rank, width)
    packed_rows = all_rows * 2 * rank // HEAD
    x, low = whole_call(
        functools.partial(low_body, rank, len(groups)),
        (
            jax.ShapeDtypeStruct((all_rows, width), BF16),
            jax.ShapeDtypeStruct((packed_rows, HEAD), BF16),
        ),
        (*groups, query_down, value_down, near_slot, place),
        cost=0.3,
    )
    lows = along_plane(low)
    low = whole_call(join_body, jax.ShapeDtypeStruct(low.shape, BF16), (lows,), cost=0.1)
    lows = along_far(low)

    base_q, base_kv = whole_call(
        functools.partial(base_body, 2048),
        (
            jax.ShapeDtypeStruct((all_rows, query_cols), F32),
            jax.ShapeDtypeStruct((all_rows, HEAD), F32),
        ),
        (x, query_matrix, key_matrix.T, value_matrix.T),
        cost=0.6,
    )

    ready = whole_call(
        functools.partial(ready_body, rank),
        jax.ShapeDtypeStruct((n, sent, HEAD), BF16),
        (
            base_q,
            base_kv,
            lows,
            unplace,
            slot,
            query_up_weights.reshape(stored * rank, query_cols),
            value_up_weights.reshape(stored * rank, key_cols),
            cosine,
            sine,
            key_cosine,
            key_sine,
            send,
        ),
        cost=0.9,
    )
    arrived = lax.all_to_all(ready, "serve", split_axis=0, concat_axis=0, tiled=True)

    fresh = jax.ShapeDtypeStruct((own, STEPS, KV_HEADS * HEAD), BF16)
    new_keys, new_values, context = whole_call(
        functools.partial(attend_body, own, key_cols),
        (fresh, fresh, jax.ShapeDtypeStruct((n, rows * local, HEAD), BF16)),
        (index[None], lengths, arrived, order, rotated_key_cache, stored_value_cache),
        smem=2,
        scratch=[pltpu.VMEM((own * HEADS * STEPS, HEAD), F32)],
        cost=1.0,
    )
    context = lax.all_to_all(context, "serve", split_axis=0, concat_axis=0, tiled=True)

    half = all_rows // cores
    cut = width * 5 // 8

    def kinds(count, columns):
        return (jax.ShapeDtypeStruct((count, columns), F32),) * 2

    taken, mine_long, other_long = whole_call(
        take_body,
        (jax.ShapeDtypeStruct((all_rows, query_cols), BF16),) + kinds(half, cut),
        (context, take, output_matrix),
        cost=0.4,
    )
    mine_short, other_short = whole_call(
        functools.partial(out_body, cut),
        kinds(half, width - cut),
        (taken, output_matrix),
        cost=0.3,
    )

    def kind(count, columns, dtype):
        return jax.ShapeDtypeStruct((count * rows, columns), dtype)

    keep, *others = whole_call(
        near_body,
        (kind(far, cut, F32),) + (kind(far, cut, BF16),) * (near - 1),
        (mine_long, shift(other_long, 0, 0, 1)),
        cost=0.1,
    )
    others = [shift(other, 0, m, 0) for m, other in enumerate(others, 1)]
    short, *sides = whole_call(
        functools.partial(far_first_body, near),
        (kind(near, width - cut, F32),) + (kind(near, width - cut, BF16),) * (far - 1),
        (mine_short, shift(other_short, 0, 0, 1)),
        cost=0.1,
    )
    sides = [shift(side, f, 0, 0) for f, side in enumerate(sides, 1)]
    keep, *others = whole_call(
        functools.partial(far_body, len(others)),
        (kind(1, cut, F32),) + (kind(1, cut, BF16),) * (far - 1),
        (keep, *others),
        cost=0.1,
    )
    others = [shift(other, f, 0, 0) for f, other in enumerate(others, 1)]
    short, *sides = whole_call(
        functools.partial(far_body, len(sides)),
        (kind(1, width - cut, F32),) + (kind(1, width - cut, BF16),) * (near - 1),
        (short, *sides),
        cost=0.1,
    )
    sides = [shift(side, 0, m, 0) for m, side in enumerate(sides, 1)]
    result = jax.ShapeDtypeStruct((own, width), BF16)
    out_one, out_two = whole_call(
        functools.partial(last_body, 1 + len(others)),
        (result, result),
        (residual_first, residual_second, keep, *others, short, *sides),
        cost=0.1,
    )
    return (out_one, out_two, new_keys, new_values)


def solution(mesh):
    n = mesh.shape["serve"]
    sizes = (n // 4, 2, 2)
    return jax.shard_map(
        functools.partial(shards, sizes),
        mesh=mesh,
        in_specs=(
            P(("replica", "serve"), None),
            P(("replica", "serve"), None),
            P(),
            P(None, "serve"),
            P(None, "serve"),
            P(None, "serve"),
            P("serve", None),
            P("serve", None, None),
            P("serve", None, None),
            P(None, None, "serve"),
            P(None, None, "serve"),
            P(("replica", "serve"), None, None),
            P(("replica", "serve"), None, None),
            P("replica"),
            P("replica"),
            P(),
        ),
        out_specs=(
            P(("replica", "serve"), None),
            P(("replica", "serve"), None),
            P(("replica", "serve"), None, None),
            P(("replica", "serve"), None, None),
        ),
        check_vma=False,
    )
```

```python
import functools
import math

import jax
import jax.numpy as jnp
from jax import lax
from jax.experimental import pallas as pl
from jax.experimental.pallas import tpu as pltpu
from jax.sharding import PartitionSpec as P

HEADS = 64
KV_HEADS = 8
HEAD = 128
STEPS = 2
LIMIT = 8 * 1024 * 1024
PEAK = 1.15e9
NT = (((1,), (1,)), ((), ()))
F32 = jnp.float32
BF16 = jnp.bfloat16


def dot(a, b):
    return jnp.dot(a, b, preferred_element_type=F32)


def dot_nt(a, b):
    return lax.dot_general(a, b, NT, preferred_element_type=F32)


def whole_call(body, out_shape, args, cost, smem=0, hbm=0, scratch=()):
    specs = [pl.BlockSpec(memory_space=pltpu.SMEM)] * smem
    specs += [pl.BlockSpec(memory_space=pltpu.HBM)] * hbm
    specs += [pl.BlockSpec(memory_space=pltpu.VMEM)] * (len(args) - smem - hbm)
    many = isinstance(out_shape, (tuple, list))
    vmem = pl.BlockSpec(memory_space=pltpu.VMEM)
    return pl.pallas_call(
        body,
        out_shape=out_shape,
        in_specs=specs,
        out_specs=tuple(vmem for _ in out_shape) if many else vmem,
        scratch_shapes=list(scratch),
        compiler_params=pltpu.CompilerParams(vmem_limit_bytes=LIMIT),
        cost_estimate=pl.CostEstimate(
            flops=int(cost * PEAK), bytes_accessed=0, transcendentals=0
        ),
    )(*args)


def scaled_frequency(pair_index):
    base = jnp.exp(pair_index.astype(F32) * (-2.0 * math.log(500000.0) / HEAD))
    wavelength = 2.0 * math.pi / base
    smooth = jnp.clip((8192.0 / wavelength - 1.0) / 3.0, 0.0, 1.0)
    return (1.0 - smooth) * base / 8.0 + smooth * base


def fetch(pairs, sems):
    copies = [
        pltpu.make_async_copy(source, target, sems.at[i])
        for i, (source, target) in enumerate(pairs)
    ]
    for copy in copies:
        copy.start()
    for copy in copies:
        copy.wait()


def norm_body(first_hbm, second_hbm, gain_hbm, out_ref, first_ref, second_ref, gain_ref, sems):
    fetch(((first_hbm, first_ref), (second_hbm, second_ref), (gain_hbm, gain_ref)), sems)
    gain = gain_ref[...].astype(F32)
    factors = []
    for ref in (first_ref, second_ref):
        values = ref[...].astype(F32)
        factors.append(lax.rsqrt(jnp.mean(values * values, axis=-1, keepdims=True) + 1e-05))
    factor = jnp.concatenate(factors, axis=0)
    for i in range(gain.shape[0]):
        at = slice(i * HEAD, (i + 1) * HEAD)
        values = jnp.concatenate((first_ref[:, at].astype(F32), second_ref[:, at].astype(F32)))
        out_ref[:, at] = (values * factor * gain[i : i + 1]).astype(BF16)


def frequency_body(out_ref):
    out_ref[...] = scaled_frequency(lax.broadcasted_iota(jnp.int32, out_ref.shape, 1) // 2)


def prep_body(
    sizes, rank, own, key_cols, adapters,
    index_ref, length_hbm, adapter_hbm, slot_hbm, frequency_ref,
    held_ref, local_ref, cos_ref, sin_ref, kcos_ref, ksin_ref, place_ref, unplace_ref, send_ref,
    order_ref, take_ref, length_ref, adapter_ref, slot_ref, sems,
):
    fetch(((length_hbm, length_ref), (adapter_hbm, adapter_ref), (slot_hbm, slot_ref)), sems)
    far, near, cores = sizes
    n = far * near * cores
    rows = own * STEPS
    all_rows = n * rows
    heads = HEADS // n
    sent = send_ref.shape[0] // n
    index = index_ref[0]
    core_at = index % cores
    near_at = index // cores % near
    far_at = index // (cores * near)

    def device_of(block, sign):
        c, m, f = block // (far * near), block // far % near, block % far
        f = (far_at + sign * f + far) % far
        m = (near_at + sign * m + near) % near
        c = (core_at + sign * c + cores) % cores
        return (f * near + m) * cores + c

    def iota(shape, axis):
        return lax.broadcasted_iota(jnp.int32, shape, axis)

    def split(row):
        return row // rows, row % rows // own, row % own

    block, step, mine = split(iota((all_rows, 1), 0))
    device = device_of(block, -1)
    request = device * own + mine
    length = jnp.zeros_like(request)
    adapter = jnp.zeros_like(request)
    for j in range(length_ref.shape[0]):
        length = jnp.where(request == j, length_ref[j], length)
        adapter = jnp.where(request == j, adapter_ref[j], adapter)
    slot = jnp.zeros_like(request)
    for j in range(slot_ref.shape[0]):
        slot = jnp.where(adapter == j, slot_ref[j], slot)
    held_ref[...] = slot
    local_ref[...] = slot - index * adapters
    position = (length + step).astype(F32)
    lane = iota((1, HEAD), 1)
    odd = jnp.where(lane % 2 == 0, -1.0, 1.0)
    angle = position * frequency_ref[...]
    cos_ref[...] = jnp.cos(angle)
    sin_ref[...] = jnp.sin(angle) * odd
    angle = position * scaled_frequency((index * key_cols + lane) % HEAD // 2)
    kcos_ref[...] = jnp.where(lane < key_cols, jnp.cos(angle), 1.0)
    ksin_ref[...] = jnp.where(lane < key_cols, jnp.sin(angle) * odd, 0.0)

    def hot(ref, row, column):
        ref[...] = jnp.where(row == column, 1.0, 0.0).astype(BF16)

    absolute = (device * STEPS + step) * own + mine
    hot(unplace_ref, absolute, iota((1, all_rows), 1))
    block, step, mine = split(iota((1, all_rows), 1))
    absolute = (device_of(block, -1) * STEPS + step) * own + mine
    hot(place_ref, iota((all_rows, 1), 0), absolute)

    column = iota((1, send_ref.shape[1]), 1)
    h = column // all_rows
    block, step, mine = split(column % all_rows)
    wanted = device_of(block, -1) * sent + jnp.where(
        h < heads, (mine * heads + h) * STEPS + step, rows * heads + mine * STEPS + step
    )
    hot(send_ref, iota((n * sent, 1), 0), wanted)

    row = iota((order_ref.shape[0], 1), 0)
    mine, head, step = row // (HEADS * STEPS), row // STEPS % HEADS, row % STEPS
    wanted = (head // heads) * sent + (mine * heads + head % heads) * STEPS + step
    hot(order_ref, wanted, iota((1, n * sent), 1))

    row = iota((take_ref.shape[0], 1), 0)
    h = row // all_rows
    block, step, mine = split(row % all_rows)
    device, c = device_of(block, 1), (cores - block // (far * near)) % cores
    wanted = (device // cores * cores + c) * rows * heads + (mine * heads + h) * STEPS + step
    hot(take_ref, wanted, iota((1, take_ref.shape[1]), 1))


def low_body(rank, groups, *refs):
    parts, (qd_ref, vd_ref, local_ref, place_ref, x_ref, out_ref) = refs[:groups], refs[groups:]
    rows = parts[0].shape[1]
    sets = max(1, 16 // rows)
    for p, part in enumerate(parts):
        for i in range(0, part.shape[0], sets):
            at = (p * part.shape[0] + i) * rows
            for lane in range(0, x_ref.shape[1], 1024):
                lanes = slice(lane, lane + 1024)
                block = [part[i + j, :, lanes].astype(F32) for j in range(sets)]
                x_ref[at : at + sets * rows, lanes] = jnp.concatenate(block, axis=0).astype(BF16)
    adapters = qd_ref.shape[0] // rank
    maps = jnp.concatenate((qd_ref[...], vd_ref[...]), axis=0)
    low = dot_nt(x_ref[...], maps)
    lane = lax.broadcasted_iota(jnp.int32, low.shape, 1)
    low = jnp.where(lane // rank % adapters == local_ref[...], low, 0.0)
    total = 0.0
    for a in range(adapters):
        q = low[:, a * rank : (a + 1) * rank]
        v = low[:, (adapters + a) * rank : (adapters + a + 1) * rank]
        total = total + jnp.concatenate((q, v), axis=1)
    rows = dot(place_ref[...], total.astype(BF16))
    pack = HEAD // (2 * rank)
    step = rows.shape[0] // pack
    packed = jnp.concatenate([rows[i * step : (i + 1) * step] for i in range(pack)], axis=1)
    out_ref[...] = packed.astype(BF16)


def join_body(*refs):
    total = refs[0][...].astype(F32)
    for ref in refs[1:-1]:
        total = total + ref[...].astype(F32)
    refs[-1][...] = total.astype(BF16)


def half_body(depth, start, x_ref, q_ref, out_ref):
    out_ref[...] = jnp.zeros_like(out_ref)
    columns = slice(start, start + out_ref.shape[1])

    @pl.loop(0, x_ref.shape[1] // depth)
    def _(i):
        at = pl.ds(pl.multiple_of(i * depth, depth), depth)
        out_ref[...] += dot(x_ref[:, at], q_ref[at, columns])


def narrow_body(depth, x_ref, k_ref, v_ref, out_ref):
    out_ref[...] = jnp.zeros_like(out_ref)
    columns = k_ref.shape[0]
    narrow = jnp.zeros((HEAD - 2 * columns, depth), BF16)

    @pl.loop(0, x_ref.shape[1] // depth)
    def _(i):
        at = pl.ds(pl.multiple_of(i * depth, depth), depth)
        both = (k_ref[:, at], v_ref[:, at])
        if 2 * columns < HEAD:
            both += (narrow,)
        out_ref[...] += dot_nt(x_ref[:, at], jnp.concatenate(both, axis=0))


def turned(values, cosine, sine):
    lane = lax.broadcasted_iota(jnp.int32, values.shape, 1)
    width = values.shape[1]
    ahead = pltpu.roll(values, width - 1, 1)
    behind = pltpu.roll(values, 1, 1)
    return values * cosine + jnp.where(lane % 2 == 0, ahead, behind) * sine


def ready_body(
    rank, lows, bases, *refs
):
    low_refs, base_refs = refs[:lows], refs[lows : lows + bases]
    (
        okv_ref, unplace_ref, slot_ref, uq_ref, uv_ref, cos_ref, sin_ref, kcos_ref, ksin_ref,
        send_ref, out_ref,
    ) = refs[lows + bases :]
    packed = low_refs[0][...].astype(F32)
    for ref in low_refs[1:]:
        packed = packed + ref[...].astype(F32)
    pack = HEAD // (2 * rank)
    low = jnp.concatenate(
        [packed[:, i * 2 * rank : (i + 1) * 2 * rank] for i in range(pack)], axis=0
    )
    low = dot(unplace_ref[...], low.astype(BF16)).astype(BF16)
    wide = uq_ref.shape[0]
    lane = lax.broadcasted_iota(jnp.int32, (low.shape[0], wide), 1)
    here = lane // rank == slot_ref[...]
    row = lax.broadcasted_iota(jnp.int32, (2 * rank, wide), 0)
    column = lax.broadcasted_iota(jnp.int32, (2 * rank, wide), 1)
    spread_q = jnp.where(column % rank == row, 1.0, 0.0).astype(BF16)
    spread_v = jnp.where(column % rank + rank == row, 1.0, 0.0).astype(BF16)
    wide_q = jnp.where(here, dot(low, spread_q), 0.0).astype(BF16)
    wide_v = jnp.where(here, dot(low, spread_v), 0.0).astype(BF16)
    query = jnp.concatenate([ref[...] for ref in base_refs], axis=1) + dot(wide_q, uq_ref[...])
    fresh = turned(okv_ref[...], kcos_ref[...], ksin_ref[...])
    columns = uv_ref.shape[1]
    value = dot(wide_v, uv_ref[...])
    pieces = [jnp.zeros((value.shape[0], columns), F32), value]
    if 2 * columns < HEAD:
        pieces.append(jnp.zeros((value.shape[0], HEAD - 2 * columns), F32))
    fresh = fresh + jnp.concatenate(pieces, axis=1)
    cosine, sine = cos_ref[...], sin_ref[...]
    parts = []
    for h in range(query.shape[1] // HEAD):
        parts.append(turned(query[:, h * HEAD : (h + 1) * HEAD], cosine, sine))
    parts.append(fresh)
    stacked = jnp.concatenate(parts, axis=0).astype(BF16)
    out_ref[...] = dot(send_ref[...], stacked).astype(BF16).reshape(out_ref.shape)


def attend_body(
    own, columns, index_ref, len_ref, x_ref, order_ref, k_ref, v_ref, nk_ref, nv_ref, *refs
):
    ctx_refs, s_ref = refs[:-1], refs[-1]
    n, span = x_ref.shape[0], k_ref.shape[1]
    group = HEADS // KV_HEADS
    local = HEADS // n
    rows = own * STEPS
    mine = group * STEPS
    x = x_ref[...]
    queries = dot(order_ref[...], x.reshape(n * x.shape[1], HEAD)).astype(BF16)
    wide = x.astype(F32)
    first = rows * local
    fresh = [wide[i, first : first + rows] for i in range(n)]
    each = n // KV_HEADS
    keys, values = [], []
    for g in range(KV_HEADS):
        pieces = fresh[g * each : (g + 1) * each]
        keys.append(jnp.concatenate([p[:, :columns] for p in pieces], axis=1))
        values.append(jnp.concatenate([p[:, columns : 2 * columns] for p in pieces], axis=1))
    new_keys = jnp.concatenate(keys, axis=1)
    new_values = jnp.concatenate(values, axis=1)
    for b in range(own):
        at = slice(b * STEPS, (b + 1) * STEPS)
        nk_ref[b] = new_keys[at].astype(BF16)
        nv_ref[b] = new_values[at].astype(BF16)
    pad = jnp.zeros((16 - rows, HEAD), F32)
    keys = [jnp.concatenate((k, pad), axis=0).astype(BF16) for k in keys]
    values = [jnp.concatenate((v, pad), axis=0).astype(BF16) for v in values]
    scale = HEAD ** (-0.5)
    contexts = []
    for b in range(own):
        q = queries[b * KV_HEADS * mine : (b + 1) * KV_HEADS * mine]
        cached, newer = [], []
        for g in range(KV_HEADS):
            qg = q[g * mine : (g + 1) * mine]
            cached.append(dot_nt(qg, k_ref[b, :, g * HEAD : (g + 1) * HEAD]))
            newer.append(dot_nt(qg, keys[g]))
        cached = jnp.concatenate(cached, axis=0) * scale
        newer = jnp.concatenate(newer, axis=0) * scale
        place = lax.broadcasted_iota(jnp.int32, cached.shape, 1)
        cached = jnp.where(place < len_ref[index_ref[0] * own + b], cached, -1e30)
        step = lax.broadcasted_iota(jnp.int32, newer.shape, 0) % STEPS
        at = lax.broadcasted_iota(jnp.int32, newer.shape, 1) - b * STEPS
        newer = jnp.where((at >= 0) & (at <= step), newer, -1e30)
        top = jnp.maximum(
            jnp.max(cached, axis=1, keepdims=True), jnp.max(newer, axis=1, keepdims=True)
        )
        cached = jnp.exp(cached - top)
        newer = jnp.exp(newer - top)
        total = jnp.sum(cached, axis=1, keepdims=True) + jnp.sum(newer, axis=1, keepdims=True)
        cached = (cached / total).astype(BF16)
        newer = (newer / total).astype(BF16)
        for g in range(KV_HEADS):
            at_rows = slice(g * mine, (g + 1) * mine)
            part = dot(cached[at_rows], v_ref[b, :, g * HEAD : (g + 1) * HEAD])
            s_ref[(b * KV_HEADS + g) * mine : (b * KV_HEADS + g + 1) * mine] = part + dot(
                newer[at_rows], values[g]
            )
    step = local * STEPS
    half = KV_HEADS * mine
    cores = len(ctx_refs)
    for c, ref in enumerate(ctx_refs):
        core = (index_ref[0] + c) % cores
        for i in range(n // cores):
            at = pl.multiple_of((i * cores + core) * step, step)
            block = [s_ref[pl.ds(b * half + at, step)] for b in range(own)]
            ref[i] = jnp.concatenate(block, axis=0).astype(BF16)


def pack_body(*refs):
    rows = refs[0].shape[1]
    for c, ref in enumerate(refs[:-1]):
        refs[-1][:, c * rows : (c + 1) * rows] = ref[...]


def take_body(ctx_ref, take_ref, w_ref, a_ref, mine_ref, other_ref):
    rows = a_ref.shape[0]
    x = ctx_ref[...].reshape(-1, HEAD)
    taken = dot(take_ref[...], x).astype(BF16)
    for h in range(a_ref.shape[1] // HEAD):
        a_ref[:, h * HEAD : (h + 1) * HEAD] = taken[h * rows : (h + 1) * rows]
    out_body(0, a_ref, w_ref, mine_ref, other_ref)


def out_body(start, a_ref, w_ref, mine_ref, other_ref):
    half = mine_ref.shape[0]
    tile = 1024

    @pl.loop(0, mine_ref.shape[1] // tile)
    def _(i):
        at = pl.ds(pl.multiple_of(i * tile, tile), tile)
        product = dot(a_ref[...], w_ref[:, pl.ds(pl.multiple_of(start + i * tile, tile), tile)])
        mine_ref[:, at] = product[:half]
        other_ref[:, at] = product[half:]


def far_first_body(near, mine_ref, came_ref, *refs):
    total = mine_ref[...] + came_ref[...]
    rows = refs[0].shape[0] // near
    for f, ref in enumerate(refs):
        blocks = [(m * len(refs) + f) * rows for m in range(near)]
        value = jnp.concatenate([total[at : at + rows] for at in blocks], axis=0)
        ref[...] = value.astype(ref.dtype)


def near_body(mine_ref, came_ref, *refs):
    rows = refs[0].shape[0]
    total = mine_ref[...] + came_ref[...]
    refs[0][...] = total[:rows]
    for m, ref in enumerate(refs[1:], 1):
        ref[...] = total[m * rows : (m + 1) * rows].astype(BF16)


def far_body(came, *refs):
    total = refs[0][...]
    for ref in refs[1 : 1 + came]:
        total = total + ref[...].astype(F32)
    refs = refs[1 + came :]
    rows = refs[0].shape[0]
    refs[0][...] = total[:rows]
    for f, ref in enumerate(refs[1:], 1):
        ref[...] = total[f * rows : (f + 1) * rows].astype(BF16)


def last_body(longs, first_ref, second_ref, *refs):
    one_ref, two_ref = refs[-2:]
    totals = []
    for part in (refs[:longs], refs[longs:-2]):
        total = part[0][...]
        for ref in part[1:]:
            total = total + ref[...].astype(F32)
        totals.append(total)
    total = jnp.concatenate(totals, axis=1)
    own = one_ref.shape[0]
    one_ref[...] = (first_ref[...].astype(F32) + total[:own]).astype(BF16)
    two_ref[...] = (second_ref[...].astype(F32) + total[own:]).astype(BF16)


def shards(
    sizes,
    residual_first,
    residual_second,
    attention_norm_gain,
    query_matrix,
    key_matrix,
    value_matrix,
    output_matrix,
    query_down_weights,
    value_down_weights,
    query_up_weights,
    value_up_weights,
    rotated_key_cache,
    stored_value_cache,
    lengths,
    request_adapter,
    adapter_slot,
):
    far, near, cores = sizes
    n = far * near * cores
    index = lax.axis_index("serve")
    own, width = residual_first.shape
    adapters, _, rank = query_down_weights.shape
    query_cols = query_matrix.shape[1]
    key_cols = key_matrix.shape[1]
    local = query_cols // HEAD
    rows = own * STEPS
    all_rows = n * rows
    stored = query_up_weights.shape[0]

    def partner(f, m, c):
        pairs = []
        for z in range(far):
            for y in range(near):
                for k in range(cores):
                    to = (((z + f) % far) * near + (y + m) % near) * cores + (k + c) % cores
                    pairs.append(((z * near + y) * cores + k, to))
        return pairs

    def shift(value, f, m, c):
        return lax.ppermute(value, "serve", partner(f, m, c))

    frequency = whole_call(frequency_body, jax.ShapeDtypeStruct((1, HEAD), F32), (), cost=1.0)
    gain = attention_norm_gain.reshape(width // HEAD, HEAD)
    gain, frequency = lax.optimization_barrier((gain, frequency))
    normed = whole_call(
        norm_body,
        jax.ShapeDtypeStruct((rows, width), BF16),
        (residual_first, residual_second, gain),
        hbm=3,
        scratch=[
            pltpu.VMEM((own, width), BF16),
            pltpu.VMEM((own, width), BF16),
            pltpu.VMEM(gain.shape, BF16),
            pltpu.SemaphoreType.DMA((3,)),
        ],
        cost=1.0,
    )
    normed = normed[None]
    groups = [jnp.concatenate([normed] + [shift(normed, f, 0, 0) for f in range(1, far)])]
    groups += [shift(groups[0], 0, m, 0) for m in range(1, near)]

    groups[0], at = lax.optimization_barrier((groups[0], index[None]))
    sent = -(-(rows * local + rows) // 8) * 8
    narrow = jax.ShapeDtypeStruct((all_rows, 1), jnp.int32)
    table = jax.ShapeDtypeStruct((all_rows, HEAD), F32)
    square = jax.ShapeDtypeStruct((all_rows, all_rows), BF16)
    slot, near_slot, cosine, sine, key_cosine, key_sine, place, unplace, send, order, take = whole_call(
        functools.partial(prep_body, sizes, rank, own, key_cols, adapters),
        (
            narrow,
            narrow,
            table,
            table,
            table,
            table,
            square,
            square,
            jax.ShapeDtypeStruct((n * sent, all_rows * (local + 1)), BF16),
            jax.ShapeDtypeStruct((own * HEADS * STEPS, n * sent), BF16),
            jax.ShapeDtypeStruct((all_rows * local, n * rows * local), BF16),
        ),
        (at, lengths, request_adapter, adapter_slot, frequency),
        smem=1,
        hbm=3,
        scratch=[
            pltpu.SMEM(lengths.shape, jnp.int32),
            pltpu.SMEM(request_adapter.shape, jnp.int32),
            pltpu.SMEM(adapter_slot.shape, jnp.int32),
            pltpu.SemaphoreType.DMA((3,)),
        ],
        cost=4.0,
    )
    slot, groups[1] = lax.optimization_barrier((slot, groups[1]))

    groups += [shift(part, 0, 0, c) for c in range(1, cores) for part in groups[:near]]

    query_down = jnp.swapaxes(query_down_weights, 1, 2).reshape(adapters * rank, width)
    value_down = jnp.swapaxes(value_down_weights, 1, 2).reshape(adapters * rank, width)
    packed_rows = all_rows * 2 * rank // HEAD
    x, low = whole_call(
        functools.partial(low_body, rank, len(groups)),
        (
            jax.ShapeDtypeStruct((all_rows, width), BF16),
            jax.ShapeDtypeStruct((packed_rows, HEAD), BF16),
        ),
        (*groups, query_down, value_down, near_slot, place),
        cost=0.3,
    )
    half_cols = query_cols // 2 if query_cols % 256 == 0 else query_cols
    lows = [shift(low, 0, m, c) for m in range(near) for c in range(cores) if m + c]
    base_first = whole_call(
        functools.partial(half_body, 2048, 0),
        jax.ShapeDtypeStruct((all_rows, half_cols), F32),
        (x, query_matrix),
        cost=0.3,
    )
    low = whole_call(join_body, jax.ShapeDtypeStruct(low.shape, BF16), (low, *lows), cost=0.1)
    low, base_first = lax.optimization_barrier((low, base_first))
    lows = [low] + [shift(low, f, 0, 0) for f in range(1, far)]
    bases = [base_first]
    if half_cols < query_cols:
        bases.append(
            whole_call(
                functools.partial(half_body, 2048, half_cols),
                jax.ShapeDtypeStruct((all_rows, query_cols - half_cols), F32),
                (x, query_matrix),
                cost=0.3,
            )
        )
    base_kv = whole_call(
        functools.partial(narrow_body, 2048),
        jax.ShapeDtypeStruct((all_rows, HEAD), F32),
        (x, key_matrix.T, value_matrix.T),
        cost=0.1,
    )

    ready = whole_call(
        functools.partial(ready_body, rank, len(lows), len(bases)),
        jax.ShapeDtypeStruct((n, sent, HEAD), BF16),
        (
            *lows,
            *bases,
            base_kv,
            unplace,
            slot,
            query_up_weights.reshape(stored * rank, query_cols),
            value_up_weights.reshape(stored * rank, key_cols),
            cosine,
            sine,
            key_cosine,
            key_sine,
            send,
        ),
        cost=0.9,
    )
    arrived = lax.all_to_all(ready, "serve", split_axis=0, concat_axis=0, tiled=True)

    fresh = jax.ShapeDtypeStruct((own, STEPS, KV_HEADS * HEAD), BF16)
    new_keys, new_values, *context = whole_call(
        functools.partial(attend_body, own, key_cols),
        (fresh, fresh)
        + (jax.ShapeDtypeStruct((n // cores, rows * local, HEAD), BF16),) * cores,
        (index[None], lengths, arrived, order, rotated_key_cache, stored_value_cache),
        smem=2,
        scratch=[pltpu.VMEM((own * HEADS * STEPS, HEAD), F32)],
        cost=1.0,
    )
    context = context[:1] + [shift(context[c], 0, 0, c) for c in range(1, cores)]
    context = whole_call(
        pack_body,
        jax.ShapeDtypeStruct((n // cores, cores * rows * local, HEAD), BF16),
        tuple(context),
        cost=0.1,
    )
    same_core = [[i * cores + c for i in range(n // cores)] for c in range(cores)]
    context = lax.all_to_all(
        context, "serve", split_axis=0, concat_axis=0, axis_index_groups=same_core, tiled=True
    )

    half = all_rows // cores
    cut = width * 5 // 8

    def kinds(count, columns):
        return (jax.ShapeDtypeStruct((count, columns), F32),) * 2

    taken, mine_long, other_long = whole_call(
        take_body,
        (jax.ShapeDtypeStruct((all_rows, query_cols), BF16),) + kinds(half, cut),
        (context, take, output_matrix),
        cost=0.4,
    )
    mine_short, other_short = whole_call(
        functools.partial(out_body, cut),
        kinds(half, width - cut),
        (taken, output_matrix),
        cost=0.3,
    )

    def kind(count, columns, dtype):
        return jax.ShapeDtypeStruct((count * rows, columns), dtype)

    keep, *others = whole_call(
        near_body,
        (kind(far, cut, F32),) + (kind(far, cut, BF16),) * (near - 1),
        (mine_long, shift(other_long, 0, 0, 1)),
        cost=0.1,
    )
    others = [shift(other, 0, m, 0) for m, other in enumerate(others, 1)]
    short, *sides = whole_call(
        functools.partial(far_first_body, near),
        (kind(near, width - cut, F32),) + (kind(near, width - cut, BF16),) * (far - 1),
        (mine_short, shift(other_short, 0, 0, 1)),
        cost=0.1,
    )
    sides = [shift(side, f, 0, 0) for f, side in enumerate(sides, 1)]
    short, *sides = whole_call(
        functools.partial(far_body, len(sides)),
        (kind(1, width - cut, F32),) + (kind(1, width - cut, BF16),) * (near - 1),
        (short, *sides),
        cost=0.1,
    )
    keep, short = lax.optimization_barrier((keep, short))
    keep, *others = whole_call(
        functools.partial(far_body, len(others)),
        (kind(1, cut, F32),) + (kind(1, cut, BF16),) * (far - 1),
        (keep, *others),
        cost=0.1,
    )
    others = [shift(other, f, 0, 0) for f, other in enumerate(others, 1)]
    sides = [shift(side, 0, m, 0) for m, side in enumerate(sides, 1)]
    result = jax.ShapeDtypeStruct((own, width), BF16)
    out_one, out_two = whole_call(
        functools.partial(last_body, 1 + len(others)),
        (result, result),
        (residual_first, residual_second, keep, *others, short, *sides),
        cost=0.1,
    )
    return (out_one, out_two, new_keys, new_values)


def solution(mesh):
    n = mesh.shape["serve"]
    sizes = (n // 4, 2, 2)
    return jax.shard_map(
        functools.partial(shards, sizes),
        mesh=mesh,
        in_specs=(
            P(("replica", "serve"), None),
            P(("replica", "serve"), None),
            P(),
            P(None, "serve"),
            P(None, "serve"),
            P(None, "serve"),
            P("serve", None),
            P("serve", None, None),
            P("serve", None, None),
            P(None, None, "serve"),
            P(None, None, "serve"),
            P(("replica", "serve"), None, None),
            P(("replica", "serve"), None, None),
            P("replica"),
            P("replica"),
            P(),
        ),
        out_specs=(
            P(("replica", "serve"), None),
            P(("replica", "serve"), None),
            P(("replica", "serve"), None, None),
            P(("replica", "serve"), None, None),
        ),
        check_vma=False,
    )
```

```python
import functools
import math

import jax
import jax.numpy as jnp
from jax import lax
from jax.experimental import pallas as pl
from jax.experimental.pallas import tpu as pltpu
from jax.sharding import PartitionSpec as P

HEADS = 64
KV_HEADS = 8
HEAD = 128
STEPS = 2
LIMIT = 8 * 1024 * 1024
PEAK = 1.15e9
NT = (((1,), (1,)), ((), ()))
F32 = jnp.float32
BF16 = jnp.bfloat16


def dot(a, b):
    return jnp.dot(a, b, preferred_element_type=F32)


def dot_nt(a, b):
    return lax.dot_general(a, b, NT, preferred_element_type=F32)


def whole_call(body, out_shape, args, cost, smem=0, hbm=0, scratch=()):
    specs = [pl.BlockSpec(memory_space=pltpu.SMEM)] * smem
    specs += [pl.BlockSpec(memory_space=pltpu.HBM)] * hbm
    specs += [pl.BlockSpec(memory_space=pltpu.VMEM)] * (len(args) - smem - hbm)
    many = isinstance(out_shape, (tuple, list))
    vmem = pl.BlockSpec(memory_space=pltpu.VMEM)
    return pl.pallas_call(
        body,
        out_shape=out_shape,
        in_specs=specs,
        out_specs=tuple(vmem for _ in out_shape) if many else vmem,
        scratch_shapes=list(scratch),
        compiler_params=pltpu.CompilerParams(vmem_limit_bytes=LIMIT),
        cost_estimate=pl.CostEstimate(
            flops=int(cost * PEAK), bytes_accessed=0, transcendentals=0
        ),
    )(*args)


def scaled_frequency(pair_index):
    base = jnp.exp(pair_index.astype(F32) * (-2.0 * math.log(500000.0) / HEAD))
    wavelength = 2.0 * math.pi / base
    smooth = jnp.clip((8192.0 / wavelength - 1.0) / 3.0, 0.0, 1.0)
    return (1.0 - smooth) * base / 8.0 + smooth * base


def fetch(pairs, sems):
    copies = [
        pltpu.make_async_copy(source, target, sems.at[i])
        for i, (source, target) in enumerate(pairs)
    ]
    for copy in copies:
        copy.start()
    for copy in copies:
        copy.wait()


def norm_body(first_hbm, second_hbm, gain_hbm, out_ref, first_ref, second_ref, gain_ref, sems):
    fetch(((first_hbm, first_ref), (second_hbm, second_ref), (gain_hbm, gain_ref)), sems)
    gain = gain_ref[...].astype(F32)
    factors = []
    for ref in (first_ref, second_ref):
        values = ref[...].astype(F32)
        factors.append(lax.rsqrt(jnp.mean(values * values, axis=-1, keepdims=True) + 1e-05))
    factor = jnp.concatenate(factors, axis=0)
    for i in range(gain.shape[0]):
        at = slice(i * HEAD, (i + 1) * HEAD)
        values = jnp.concatenate((first_ref[:, at].astype(F32), second_ref[:, at].astype(F32)))
        out_ref[:, at] = (values * factor * gain[i : i + 1]).astype(BF16)


def frequency_body(out_ref):
    out_ref[...] = scaled_frequency(lax.broadcasted_iota(jnp.int32, out_ref.shape, 1) // 2)


def prep_body(
    sizes, rank, own, key_cols, adapters,
    index_ref, length_hbm, adapter_hbm, slot_hbm, frequency_ref,
    held_ref, local_ref, cos_ref, sin_ref, kcos_ref, ksin_ref, place_ref, unplace_ref, send_ref,
    order_ref, take_ref, length_ref, adapter_ref, slot_ref, sems,
):
    fetch(((length_hbm, length_ref), (adapter_hbm, adapter_ref), (slot_hbm, slot_ref)), sems)
    far, near, cores = sizes
    n = far * near * cores
    rows = own * STEPS
    all_rows = n * rows
    heads = HEADS // n
    sent = send_ref.shape[0] // n
    index = index_ref[0]
    core_at = index % cores
    near_at = index // cores % near
    far_at = index // (cores * near)

    def device_of(block, sign):
        c, m, f = block // (far * near), block // far % near, block % far
        f = (far_at + sign * f + far) % far
        m = (near_at + sign * m + near) % near
        c = (core_at + sign * c + cores) % cores
        return (f * near + m) * cores + c

    def iota(shape, axis):
        return lax.broadcasted_iota(jnp.int32, shape, axis)

    def split(row):
        return row // rows, row % rows // own, row % own

    block, step, mine = split(iota((all_rows, 1), 0))
    device = device_of(block, -1)
    request = device * own + mine
    length = jnp.zeros_like(request)
    adapter = jnp.zeros_like(request)
    for j in range(length_ref.shape[0]):
        length = jnp.where(request == j, length_ref[j], length)
        adapter = jnp.where(request == j, adapter_ref[j], adapter)
    slot = jnp.zeros_like(request)
    for j in range(slot_ref.shape[0]):
        slot = jnp.where(adapter == j, slot_ref[j], slot)
    held_ref[...] = slot
    local_ref[...] = slot - index * adapters
    position = (length + step).astype(F32)
    lane = iota((1, HEAD), 1)
    odd = jnp.where(lane % 2 == 0, -1.0, 1.0)
    angle = position * frequency_ref[...]
    cos_ref[...] = jnp.cos(angle)
    sin_ref[...] = jnp.sin(angle) * odd
    angle = position * scaled_frequency((index * key_cols + lane) % HEAD // 2)
    kcos_ref[...] = jnp.where(lane < key_cols, jnp.cos(angle), 1.0)
    ksin_ref[...] = jnp.where(lane < key_cols, jnp.sin(angle) * odd, 0.0)

    def hot(ref, row, column):
        ref[...] = jnp.where(row == column, 1.0, 0.0).astype(BF16)

    absolute = (device * STEPS + step) * own + mine
    hot(unplace_ref, absolute, iota((1, all_rows), 1))
    block, step, mine = split(iota((1, all_rows), 1))
    absolute = (device_of(block, -1) * STEPS + step) * own + mine
    hot(place_ref, iota((all_rows, 1), 0), absolute)

    column = iota((1, send_ref.shape[1]), 1)
    h = column // all_rows
    block, step, mine = split(column % all_rows)
    wanted = device_of(block, -1) * sent + jnp.where(
        h < heads, (mine * heads + h) * STEPS + step, rows * heads + mine * STEPS + step
    )
    hot(send_ref, iota((n * sent, 1), 0), wanted)

    row = iota((order_ref.shape[0], 1), 0)
    mine, head, step = row // (HEADS * STEPS), row // STEPS % HEADS, row % STEPS
    wanted = (head // heads) * sent + (mine * heads + head % heads) * STEPS + step
    hot(order_ref, wanted, iota((1, n * sent), 1))

    row = iota((take_ref.shape[0], 1), 0)
    h = row // all_rows
    block, step, mine = split(row % all_rows)
    wanted = device_of(block, 1) * rows * heads + (mine * heads + h) * STEPS + step
    hot(take_ref, wanted, iota((1, take_ref.shape[1]), 1))


def low_body(rank, groups, *refs):
    parts, (qd_ref, vd_ref, local_ref, place_ref, x_ref, out_ref) = refs[:groups], refs[groups:]
    rows = parts[0].shape[1]
    sets = max(1, 16 // rows)
    blocks = [(part, i) for part in parts for i in range(part.shape[0])]
    for first in range(0, len(blocks), sets):
        group = blocks[first : first + sets]
        for lane in range(0, x_ref.shape[1], 1024):
            lanes = slice(lane, lane + 1024)
            block = [part[i, :, lanes].astype(F32) for part, i in group]
            block = jnp.concatenate(block, axis=0).astype(BF16)
            x_ref[first * rows : (first + sets) * rows, lanes] = block
    adapters = qd_ref.shape[0] // rank
    maps = jnp.concatenate((qd_ref[...], vd_ref[...]), axis=0)
    low = dot_nt(x_ref[...], maps)
    lane = lax.broadcasted_iota(jnp.int32, low.shape, 1)
    low = jnp.where(lane // rank % adapters == local_ref[...], low, 0.0)
    total = 0.0
    for a in range(adapters):
        q = low[:, a * rank : (a + 1) * rank]
        v = low[:, (adapters + a) * rank : (adapters + a + 1) * rank]
        total = total + jnp.concatenate((q, v), axis=1)
    rows = dot(place_ref[...], total.astype(BF16))
    pack = HEAD // (2 * rank)
    step = rows.shape[0] // pack
    packed = jnp.concatenate([rows[i * step : (i + 1) * step] for i in range(pack)], axis=1)
    out_ref[...] = packed.astype(BF16)


def join_body(*refs):
    total = refs[0][...].astype(F32)
    for ref in refs[1:-1]:
        total = total + ref[...].astype(F32)
    refs[-1][...] = total.astype(BF16)


def base_body(depth, start, stop, x_ref, q_ref, k_ref, v_ref, oq_ref, okv_ref):
    oq_ref[...] = jnp.zeros_like(oq_ref)
    okv_ref[...] = jnp.zeros_like(okv_ref)
    columns = k_ref.shape[0]
    narrow = jnp.zeros((HEAD - 2 * columns, depth), BF16)

    @pl.loop(start // depth, stop // depth)
    def _(i):
        at = pl.ds(pl.multiple_of(i * depth, depth), depth)
        x = x_ref[:, at]
        oq_ref[...] += dot(x, q_ref[at, :])
        both = (k_ref[:, at], v_ref[:, at])
        if 2 * columns < HEAD:
            both += (narrow,)
        okv_ref[...] += dot_nt(x, jnp.concatenate(both, axis=0))


def turned(values, cosine, sine):
    lane = lax.broadcasted_iota(jnp.int32, values.shape, 1)
    width = values.shape[1]
    ahead = pltpu.roll(values, width - 1, 1)
    behind = pltpu.roll(values, 1, 1)
    return values * cosine + jnp.where(lane % 2 == 0, ahead, behind) * sine


def ready_body(
    rank, lows, *refs
):
    low_refs = refs[:lows]
    (
        oq_ref, okv_ref, oq2_ref, okv2_ref, unplace_ref, slot_ref, uq_ref, uv_ref, cos_ref, sin_ref, kcos_ref, ksin_ref,
        send_ref, out_ref,
    ) = refs[lows:]
    packed = low_refs[0][...].astype(F32)
    for ref in low_refs[1:]:
        packed = packed + ref[...].astype(F32)
    pack = HEAD // (2 * rank)
    low = jnp.concatenate(
        [packed[:, i * 2 * rank : (i + 1) * 2 * rank] for i in range(pack)], axis=0
    )
    low = dot(unplace_ref[...], low.astype(BF16)).astype(BF16)
    wide = uq_ref.shape[0]
    lane = lax.broadcasted_iota(jnp.int32, (low.shape[0], wide), 1)
    here = lane // rank == slot_ref[...]
    row = lax.broadcasted_iota(jnp.int32, (2 * rank, wide), 0)
    column = lax.broadcasted_iota(jnp.int32, (2 * rank, wide), 1)
    spread_q = jnp.where(column % rank == row, 1.0, 0.0).astype(BF16)
    spread_v = jnp.where(column % rank + rank == row, 1.0, 0.0).astype(BF16)
    wide_q = jnp.where(here, dot(low, spread_q), 0.0).astype(BF16)
    wide_v = jnp.where(here, dot(low, spread_v), 0.0).astype(BF16)
    query = oq_ref[...] + oq2_ref[...] + dot(wide_q, uq_ref[...])
    fresh = turned(okv_ref[...] + okv2_ref[...], kcos_ref[...], ksin_ref[...])
    columns = uv_ref.shape[1]
    value = dot(wide_v, uv_ref[...])
    pieces = [jnp.zeros((value.shape[0], columns), F32), value]
    if 2 * columns < HEAD:
        pieces.append(jnp.zeros((value.shape[0], HEAD - 2 * columns), F32))
    fresh = fresh + jnp.concatenate(pieces, axis=1)
    cosine, sine = cos_ref[...], sin_ref[...]
    parts = []
    for h in range(query.shape[1] // HEAD):
        parts.append(turned(query[:, h * HEAD : (h + 1) * HEAD], cosine, sine))
    parts.append(fresh)
    stacked = jnp.concatenate(parts, axis=0).astype(BF16)
    out_ref[...] = dot(send_ref[...], stacked).astype(BF16).reshape(out_ref.shape)


def attend_body(
    own, columns, index_ref, len_ref, x_ref, order_ref, k_ref, v_ref, nk_ref, nv_ref, ctx_ref, s_ref
):
    n, span = x_ref.shape[0], k_ref.shape[1]
    group = HEADS // KV_HEADS
    local = HEADS // n
    rows = own * STEPS
    mine = group * STEPS
    x = x_ref[...]
    queries = dot(order_ref[...], x.reshape(n * x.shape[1], HEAD)).astype(BF16)
    wide = x.astype(F32)
    first = rows * local
    fresh = [wide[i, first : first + rows] for i in range(n)]
    each = n // KV_HEADS
    keys, values = [], []
    for g in range(KV_HEADS):
        pieces = fresh[g * each : (g + 1) * each]
        keys.append(jnp.concatenate([p[:, :columns] for p in pieces], axis=1))
        values.append(jnp.concatenate([p[:, columns : 2 * columns] for p in pieces], axis=1))
    new_keys = jnp.concatenate(keys, axis=1)
    new_values = jnp.concatenate(values, axis=1)
    for b in range(own):
        at = slice(b * STEPS, (b + 1) * STEPS)
        nk_ref[b] = new_keys[at].astype(BF16)
        nv_ref[b] = new_values[at].astype(BF16)
    pad = jnp.zeros((16 - rows, HEAD), F32)
    keys = [jnp.concatenate((k, pad), axis=0).astype(BF16) for k in keys]
    values = [jnp.concatenate((v, pad), axis=0).astype(BF16) for v in values]
    scale = HEAD ** (-0.5)
    contexts = []
    for b in range(own):
        q = queries[b * KV_HEADS * mine : (b + 1) * KV_HEADS * mine]
        cached, newer = [], []
        for g in range(KV_HEADS):
            qg = q[g * mine : (g + 1) * mine]
            cached.append(dot_nt(qg, k_ref[b, :, g * HEAD : (g + 1) * HEAD]))
            newer.append(dot_nt(qg, keys[g]))
        cached = jnp.concatenate(cached, axis=0) * scale
        newer = jnp.concatenate(newer, axis=0) * scale
        place = lax.broadcasted_iota(jnp.int32, cached.shape, 1)
        cached = jnp.where(place < len_ref[index_ref[0] * own + b], cached, -1e30)
        step = lax.broadcasted_iota(jnp.int32, newer.shape, 0) % STEPS
        at = lax.broadcasted_iota(jnp.int32, newer.shape, 1) - b * STEPS
        newer = jnp.where((at >= 0) & (at <= step), newer, -1e30)
        top = jnp.maximum(
            jnp.max(cached, axis=1, keepdims=True), jnp.max(newer, axis=1, keepdims=True)
        )
        cached = jnp.exp(cached - top)
        newer = jnp.exp(newer - top)
        total = jnp.sum(cached, axis=1, keepdims=True) + jnp.sum(newer, axis=1, keepdims=True)
        cached = (cached / total).astype(BF16)
        newer = (newer / total).astype(BF16)
        for g in range(KV_HEADS):
            at_rows = slice(g * mine, (g + 1) * mine)
            part = dot(cached[at_rows], v_ref[b, :, g * HEAD : (g + 1) * HEAD])
            s_ref[(b * KV_HEADS + g) * mine : (b * KV_HEADS + g + 1) * mine] = part + dot(
                newer[at_rows], values[g]
            )
    step = local * STEPS
    half = KV_HEADS * mine
    for i in range(n):
        block = [s_ref[b * half + i * step : b * half + (i + 1) * step] for b in range(own)]
        ctx_ref[i] = jnp.concatenate(block, axis=0).astype(BF16)


def take_body(ctx_ref, take_ref, w_ref, a_ref, mine_ref, other_ref):
    rows = a_ref.shape[0]
    x = ctx_ref[...].reshape(-1, HEAD)
    taken = dot(take_ref[...], x).astype(BF16)
    for h in range(a_ref.shape[1] // HEAD):
        a_ref[:, h * HEAD : (h + 1) * HEAD] = taken[h * rows : (h + 1) * rows]
    out_body(0, a_ref, w_ref, mine_ref, other_ref)


def out_body(start, a_ref, w_ref, mine_ref, other_ref):
    half = mine_ref.shape[0]
    tile = 1024

    @pl.loop(0, mine_ref.shape[1] // tile)
    def _(i):
        at = pl.ds(pl.multiple_of(i * tile, tile), tile)
        product = dot(a_ref[...], w_ref[:, pl.ds(pl.multiple_of(start + i * tile, tile), tile)])
        mine_ref[:, at] = product[:half]
        other_ref[:, at] = product[half:]


def far_first_body(near, mine_ref, came_ref, *refs):
    total = mine_ref[...] + came_ref[...]
    rows = refs[0].shape[0] // near
    for f, ref in enumerate(refs):
        blocks = [(m * len(refs) + f) * rows for m in range(near)]
        value = jnp.concatenate([total[at : at + rows] for at in blocks], axis=0)
        ref[...] = value.astype(ref.dtype)


def near_body(mine_ref, came_ref, *refs):
    rows = refs[0].shape[0]
    total = mine_ref[...] + came_ref[...]
    refs[0][...] = total[:rows]
    for m, ref in enumerate(refs[1:], 1):
        ref[...] = total[m * rows : (m + 1) * rows].astype(BF16)


def far_body(came, *refs):
    total = refs[0][...]
    for ref in refs[1 : 1 + came]:
        total = total + ref[...].astype(F32)
    refs = refs[1 + came :]
    rows = refs[0].shape[0]
    refs[0][...] = total[:rows]
    for f, ref in enumerate(refs[1:], 1):
        ref[...] = total[f * rows : (f + 1) * rows].astype(BF16)


def last_body(longs, first_ref, second_ref, *refs):
    one_ref, two_ref = refs[-2:]
    totals = []
    for part in (refs[:longs], refs[longs:-2]):
        total = part[0][...]
        for ref in part[1:]:
            total = total + ref[...].astype(F32)
        totals.append(total)
    total = jnp.concatenate(totals, axis=1)
    own = one_ref.shape[0]
    one_ref[...] = (first_ref[...].astype(F32) + total[:own]).astype(BF16)
    two_ref[...] = (second_ref[...].astype(F32) + total[own:]).astype(BF16)


def shards(
    sizes,
    residual_first,
    residual_second,
    attention_norm_gain,
    query_matrix,
    key_matrix,
    value_matrix,
    output_matrix,
    query_down_weights,
    value_down_weights,
    query_up_weights,
    value_up_weights,
    rotated_key_cache,
    stored_value_cache,
    lengths,
    request_adapter,
    adapter_slot,
):
    far, near, cores = sizes
    n = far * near * cores
    index = lax.axis_index("serve")
    own, width = residual_first.shape
    adapters, _, rank = query_down_weights.shape
    query_cols = query_matrix.shape[1]
    key_cols = key_matrix.shape[1]
    local = query_cols // HEAD
    rows = own * STEPS
    all_rows = n * rows
    stored = query_up_weights.shape[0]

    def partner(f, m, c):
        pairs = []
        for z in range(far):
            for y in range(near):
                for k in range(cores):
                    to = (((z + f) % far) * near + (y + m) % near) * cores + (k + c) % cores
                    pairs.append(((z * near + y) * cores + k, to))
        return pairs

    def shift(value, f, m, c):
        return lax.ppermute(value, "serve", partner(f, m, c))

    frequency = whole_call(frequency_body, jax.ShapeDtypeStruct((1, HEAD), F32), (), cost=3.0)
    gain = attention_norm_gain.reshape(width // HEAD, HEAD)
    gain, frequency = lax.optimization_barrier((gain, frequency))
    normed = whole_call(
        norm_body,
        jax.ShapeDtypeStruct((rows, width), BF16),
        (residual_first, residual_second, gain),
        hbm=3,
        scratch=[
            pltpu.VMEM((own, width), BF16),
            pltpu.VMEM((own, width), BF16),
            pltpu.VMEM(gain.shape, BF16),
            pltpu.SemaphoreType.DMA((3,)),
        ],
        cost=1.0,
    )
    normed = normed[None]
    fars = [shift(normed, f, 0, 0) for f in range(1, far)]
    nears = [shift(normed, 0, m, 0) for m in range(1, near)]
    rest = jnp.concatenate(fars)
    groups = [jnp.concatenate([normed, *fars, *nears[:1]])]
    groups += [shift(rest, 0, m, 0) for m in range(1, near)]

    rest, at = lax.optimization_barrier((rest, index[None]))
    sent = -(-(rows * local + rows) // 8) * 8
    narrow = jax.ShapeDtypeStruct((all_rows, 1), jnp.int32)
    table = jax.ShapeDtypeStruct((all_rows, HEAD), F32)
    square = jax.ShapeDtypeStruct((all_rows, all_rows), BF16)
    slot, near_slot, cosine, sine, key_cosine, key_sine, place, unplace, send, order, take = whole_call(
        functools.partial(prep_body, sizes, rank, own, key_cols, adapters),
        (
            narrow,
            narrow,
            table,
            table,
            table,
            table,
            square,
            square,
            jax.ShapeDtypeStruct((n * sent, all_rows * (local + 1)), BF16),
            jax.ShapeDtypeStruct((own * HEADS * STEPS, n * sent), BF16),
            jax.ShapeDtypeStruct((all_rows * local, n * rows * local), BF16),
        ),
        (at, lengths, request_adapter, adapter_slot, frequency),
        smem=1,
        hbm=3,
        scratch=[
            pltpu.SMEM(lengths.shape, jnp.int32),
            pltpu.SMEM(request_adapter.shape, jnp.int32),
            pltpu.SMEM(adapter_slot.shape, jnp.int32),
            pltpu.SemaphoreType.DMA((3,)),
        ],
        cost=4.0,
    )
    slot, groups[1] = lax.optimization_barrier((slot, groups[1]))

    groups += [shift(part, 0, 0, c) for c in range(1, cores) for part in groups[:near]]

    query_down = jnp.swapaxes(query_down_weights, 1, 2).reshape(adapters * rank, width)
    value_down = jnp.swapaxes(value_down_weights, 1, 2).reshape(adapters * rank, width)
    packed_rows = all_rows * 2 * rank // HEAD
    x, low = whole_call(
        functools.partial(low_body, rank, len(groups)),
        (
            jax.ShapeDtypeStruct((all_rows, width), BF16),
            jax.ShapeDtypeStruct((packed_rows, HEAD), BF16),
        ),
        (*groups, query_down, value_down, near_slot, place),
        cost=0.3,
    )
    def base(start, stop):
        return whole_call(
            functools.partial(base_body, 2048, start, stop),
            (
                jax.ShapeDtypeStruct((all_rows, query_cols), F32),
                jax.ShapeDtypeStruct((all_rows, HEAD), F32),
            ),
            (x, query_matrix, key_matrix.T, value_matrix.T),
            cost=0.3,
        )

    lows = [shift(low, 0, m, c) for m in range(near) for c in range(cores) if m + c]
    base_q, base_kv = base(0, width // 2)
    low = whole_call(join_body, jax.ShapeDtypeStruct(low.shape, BF16), (low, *lows), cost=0.1)
    low, base_q = lax.optimization_barrier((low, base_q))
    lows = [low] + [shift(low, f, 0, 0) for f in range(1, far)]
    bases = (base_q, base_kv, *base(width // 2, width))

    ready = whole_call(
        functools.partial(ready_body, rank, len(lows)),
        jax.ShapeDtypeStruct((n, sent, HEAD), BF16),
        (
            *lows,
            *bases,
            unplace,
            slot,
            query_up_weights.reshape(stored * rank, query_cols),
            value_up_weights.reshape(stored * rank, key_cols),
            cosine,
            sine,
            key_cosine,
            key_sine,
            send,
        ),
        cost=0.9,
    )
    arrived = lax.all_to_all(ready, "serve", split_axis=0, concat_axis=0, tiled=True)

    fresh = jax.ShapeDtypeStruct((own, STEPS, KV_HEADS * HEAD), BF16)
    new_keys, new_values, context = whole_call(
        functools.partial(attend_body, own, key_cols),
        (fresh, fresh, jax.ShapeDtypeStruct((n, rows * local, HEAD), BF16)),
        (index[None], lengths, arrived, order, rotated_key_cache, stored_value_cache),
        smem=2,
        scratch=[pltpu.VMEM((own * HEADS * STEPS, HEAD), F32)],
        cost=1.0,
    )
    context = lax.all_to_all(context, "serve", split_axis=0, concat_axis=0, tiled=True)

    half = all_rows // cores
    cut = width * 5 // 8

    def kinds(count, columns):
        return (jax.ShapeDtypeStruct((count, columns), F32),) * 2

    taken, mine_long, other_long = whole_call(
        take_body,
        (jax.ShapeDtypeStruct((all_rows, query_cols), BF16),) + kinds(half, cut),
        (context, take, output_matrix),
        cost=0.4,
    )
    mine_short, other_short = whole_call(
        functools.partial(out_body, cut),
        kinds(half, width - cut),
        (taken, output_matrix),
        cost=0.3,
    )

    def kind(count, columns, dtype):
        return jax.ShapeDtypeStruct((count * rows, columns), dtype)

    keep, *others = whole_call(
        near_body,
        (kind(far, cut, F32),) + (kind(far, cut, BF16),) * (near - 1),
        (mine_long, shift(other_long, 0, 0, 1)),
        cost=0.1,
    )
    others = [shift(other, 0, m, 0) for m, other in enumerate(others, 1)]
    short, *sides = whole_call(
        functools.partial(far_first_body, near),
        (kind(near, width - cut, F32),) + (kind(near, width - cut, BF16),) * (far - 1),
        (mine_short, shift(other_short, 0, 0, 1)),
        cost=0.1,
    )
    sides = [shift(side, f, 0, 0) for f, side in enumerate(sides, 1)]
    keep, *others = whole_call(
        functools.partial(far_body, len(others)),
        (kind(1, cut, F32),) + (kind(1, cut, BF16),) * (far - 1),
        (keep, *others),
        cost=0.1,
    )
    others = [shift(other, f, 0, 0) for f, other in enumerate(others, 1)]
    short, *sides = whole_call(
        functools.partial(far_body, len(sides)),
        (kind(1, width - cut, F32),) + (kind(1, width - cut, BF16),) * (near - 1),
        (short, *sides),
        cost=0.1,
    )
    sides = [shift(side, 0, m, 0) for m, side in enumerate(sides, 1)]
    result = jax.ShapeDtypeStruct((own, width), BF16)
    out_one, out_two = whole_call(
        functools.partial(last_body, 1 + len(others)),
        (result, result),
        (residual_first, residual_second, keep, *others, short, *sides),
        cost=0.1,
    )
    return (out_one, out_two, new_keys, new_values)


def solution(mesh):
    n = mesh.shape["serve"]
    sizes = (n // 4, 2, 2)
    return jax.shard_map(
        functools.partial(shards, sizes),
        mesh=mesh,
        in_specs=(
            P(("replica", "serve"), None),
            P(("replica", "serve"), None),
            P(),
            P(None, "serve"),
            P(None, "serve"),
            P(None, "serve"),
            P("serve", None),
            P("serve", None, None),
            P("serve", None, None),
            P(None, None, "serve"),
            P(None, None, "serve"),
            P(("replica", "serve"), None, None),
            P(("replica", "serve"), None, None),
            P("replica"),
            P("replica"),
            P(),
        ),
        out_specs=(
            P(("replica", "serve"), None),
            P(("replica", "serve"), None),
            P(("replica", "serve"), None, None),
            P(("replica", "serve"), None, None),
        ),
        check_vma=False,
    )
```

```python
import functools
import math

import jax
import jax.numpy as jnp
from jax import lax
from jax.experimental import pallas as pl
from jax.experimental.pallas import tpu as pltpu
from jax.sharding import PartitionSpec as P

HEADS = 64
KV_HEADS = 8
HEAD = 128
STEPS = 2
LIMIT = 8 * 1024 * 1024
PEAK = 1.15e9
NT = (((1,), (1,)), ((), ()))
F32 = jnp.float32
BF16 = jnp.bfloat16


def dot(a, b):
    return jnp.dot(a, b, preferred_element_type=F32)


def dot_nt(a, b):
    return lax.dot_general(a, b, NT, preferred_element_type=F32)


def whole_call(body, out_shape, args, cost, smem=0, hbm=0, scratch=()):
    specs = [pl.BlockSpec(memory_space=pltpu.SMEM)] * smem
    specs += [pl.BlockSpec(memory_space=pltpu.HBM)] * hbm
    specs += [pl.BlockSpec(memory_space=pltpu.VMEM)] * (len(args) - smem - hbm)
    many = isinstance(out_shape, (tuple, list))
    vmem = pl.BlockSpec(memory_space=pltpu.VMEM)
    return pl.pallas_call(
        body,
        out_shape=out_shape,
        in_specs=specs,
        out_specs=tuple(vmem for _ in out_shape) if many else vmem,
        scratch_shapes=list(scratch),
        compiler_params=pltpu.CompilerParams(vmem_limit_bytes=LIMIT),
        cost_estimate=pl.CostEstimate(
            flops=int(cost * PEAK), bytes_accessed=0, transcendentals=0
        ),
    )(*args)


def scaled_frequency(pair_index):
    base = jnp.exp(pair_index.astype(F32) * (-2.0 * math.log(500000.0) / HEAD))
    wavelength = 2.0 * math.pi / base
    smooth = jnp.clip((8192.0 / wavelength - 1.0) / 3.0, 0.0, 1.0)
    return (1.0 - smooth) * base / 8.0 + smooth * base


def fetch(pairs, sems):
    copies = [
        pltpu.make_async_copy(source, target, sems.at[i])
        for i, (source, target) in enumerate(pairs)
    ]
    for copy in copies:
        copy.start()
    for copy in copies:
        copy.wait()


def norm_body(first_hbm, second_hbm, gain_hbm, out_ref, first_ref, second_ref, gain_ref, sems):
    fetch(((first_hbm, first_ref), (second_hbm, second_ref), (gain_hbm, gain_ref)), sems)
    gain = gain_ref[...].astype(F32)
    factors = []
    for ref in (first_ref, second_ref):
        values = ref[...].astype(F32)
        factors.append(lax.rsqrt(jnp.mean(values * values, axis=-1, keepdims=True) + 1e-05))
    factor = jnp.concatenate(factors, axis=0)
    for i in range(gain.shape[0]):
        at = slice(i * HEAD, (i + 1) * HEAD)
        values = jnp.concatenate((first_ref[:, at].astype(F32), second_ref[:, at].astype(F32)))
        out_ref[:, at] = (values * factor * gain[i : i + 1]).astype(BF16)


def frequency_body(out_ref):
    out_ref[...] = scaled_frequency(lax.broadcasted_iota(jnp.int32, out_ref.shape, 1) // 2)


def moved(at, distance, size):
    if size & (size - 1) == 0:
        return at ^ distance
    return (at + distance) % size


def prep_body(
    sizes, rank, own, key_cols, adapters,
    index_ref, length_hbm, adapter_hbm, slot_hbm, frequency_ref,
    held_ref, local_ref, cos_ref, sin_ref, kcos_ref, ksin_ref, place_ref, unplace_ref, send_ref,
    order_ref, take_ref, length_ref, adapter_ref, slot_ref, sems,
):
    fetch(((length_hbm, length_ref), (adapter_hbm, adapter_ref), (slot_hbm, slot_ref)), sems)
    far, near, cores = sizes
    n = far * near * cores
    rows = own * STEPS
    all_rows = n * rows
    heads = HEADS // n
    sent = send_ref.shape[0] // n
    index = index_ref[0]
    core_at = index % cores
    near_at = index // cores % near
    far_at = index // (cores * near)

    def device_of(block, sign):
        c, m, f = block // (far * near), block // far % near, block % far
        f = moved(far_at, f if sign > 0 or far & (far - 1) == 0 else far - f, far)
        m = moved(near_at, m, near)
        c = moved(core_at, c, cores)
        return (f * near + m) * cores + c

    def iota(shape, axis):
        return lax.broadcasted_iota(jnp.int32, shape, axis)

    def split(row):
        return row // rows, row % rows // own, row % own

    block, step, mine = split(iota((all_rows, 1), 0))
    device = device_of(block, -1)
    request = device * own + mine
    length = jnp.zeros_like(request)
    adapter = jnp.zeros_like(request)
    for j in range(length_ref.shape[0]):
        length = jnp.where(request == j, length_ref[j], length)
        adapter = jnp.where(request == j, adapter_ref[j], adapter)
    slot = jnp.zeros_like(request)
    for j in range(slot_ref.shape[0]):
        slot = jnp.where(adapter == j, slot_ref[j], slot)
    held_ref[...] = slot
    local_ref[...] = slot - index * adapters
    position = (length + step).astype(F32)
    lane = iota((1, HEAD), 1)
    odd = jnp.where(lane % 2 == 0, -1.0, 1.0)
    angle = position * frequency_ref[...]
    cos_ref[...] = jnp.cos(angle)
    sin_ref[...] = jnp.sin(angle) * odd
    angle = position * scaled_frequency((index * key_cols + lane) % HEAD // 2)
    kcos_ref[...] = jnp.where(lane < key_cols, jnp.cos(angle), 1.0)
    ksin_ref[...] = jnp.where(lane < key_cols, jnp.sin(angle) * odd, 0.0)

    def hot(ref, row, column):
        ref[...] = jnp.where(row == column, 1.0, 0.0).astype(BF16)

    absolute = (device * STEPS + step) * own + mine
    hot(unplace_ref, absolute, iota((1, all_rows), 1))
    block, step, mine = split(iota((1, all_rows), 1))
    absolute = (device_of(block, -1) * STEPS + step) * own + mine
    hot(place_ref, iota((all_rows, 1), 0), absolute)

    column = iota((1, send_ref.shape[1]), 1)
    h = column // all_rows
    block, step, mine = split(column % all_rows)
    wanted = device_of(block, -1) * sent + jnp.where(
        h < heads, (mine * heads + h) * STEPS + step, rows * heads + mine * STEPS + step
    )
    hot(send_ref, iota((n * sent, 1), 0), wanted)

    row = iota((order_ref.shape[0], 1), 0)
    mine, head, step = row // (HEADS * STEPS), row // STEPS % HEADS, row % STEPS
    wanted = (head // heads) * sent + (mine * heads + head % heads) * STEPS + step
    hot(order_ref, wanted, iota((1, n * sent), 1))

    row = iota((take_ref.shape[0], 1), 0)
    h = row // all_rows
    block, step, mine = split(row % all_rows)
    wanted = device_of(block, 1) * rows * heads + (mine * heads + h) * STEPS + step
    hot(take_ref, wanted, iota((1, take_ref.shape[1]), 1))


def low_body(rank, groups, *refs):
    parts, (qd_ref, vd_ref, local_ref, place_ref, x_ref, out_ref) = refs[:groups], refs[groups:]
    rows = parts[0].shape[1]
    sets = max(1, 16 // rows)
    blocks = [(part, i) for part in parts for i in range(part.shape[0])]
    for first in range(0, len(blocks), sets):
        group = blocks[first : first + sets]
        for lane in range(0, x_ref.shape[1], 1024):
            lanes = slice(lane, lane + 1024)
            block = [part[i, :, lanes].astype(F32) for part, i in group]
            block = jnp.concatenate(block, axis=0).astype(BF16)
            x_ref[first * rows : (first + sets) * rows, lanes] = block
    adapters = qd_ref.shape[0] // rank
    maps = jnp.concatenate((qd_ref[...], vd_ref[...]), axis=0)
    low = dot_nt(x_ref[...], maps)
    lane = lax.broadcasted_iota(jnp.int32, low.shape, 1)
    low = jnp.where(lane // rank % adapters == local_ref[...], low, 0.0)
    total = 0.0
    for a in range(adapters):
        q = low[:, a * rank : (a + 1) * rank]
        v = low[:, (adapters + a) * rank : (adapters + a + 1) * rank]
        total = total + jnp.concatenate((q, v), axis=1)
    rows = dot(place_ref[...], total.astype(BF16))
    pack = HEAD // (2 * rank)
    step = rows.shape[0] // pack
    packed = jnp.concatenate([rows[i * step : (i + 1) * step] for i in range(pack)], axis=1)
    out_ref[...] = packed.astype(BF16)


def join_body(*refs):
    total = refs[0][...].astype(F32)
    for ref in refs[1:-1]:
        total = total + ref[...].astype(F32)
    refs[-1][...] = total.astype(BF16)


def base_body(depth, start, stop, x_ref, q_ref, k_ref, v_ref, oq_ref, okv_ref):
    oq_ref[...] = jnp.zeros_like(oq_ref)
    okv_ref[...] = jnp.zeros_like(okv_ref)
    columns = k_ref.shape[0]
    narrow = jnp.zeros((HEAD - 2 * columns, depth), BF16)

    @pl.loop(start // depth, stop // depth)
    def _(i):
        at = pl.ds(pl.multiple_of(i * depth, depth), depth)
        x = x_ref[:, at]
        oq_ref[...] += dot(x, q_ref[at, :])
        both = (k_ref[:, at], v_ref[:, at])
        if 2 * columns < HEAD:
            both += (narrow,)
        okv_ref[...] += dot_nt(x, jnp.concatenate(both, axis=0))


def turned(values, cosine, sine):
    lane = lax.broadcasted_iota(jnp.int32, values.shape, 1)
    width = values.shape[1]
    ahead = pltpu.roll(values, width - 1, 1)
    behind = pltpu.roll(values, 1, 1)
    return values * cosine + jnp.where(lane % 2 == 0, ahead, behind) * sine


def ready_body(
    rank, lows, *refs
):
    low_refs = refs[:lows]
    (
        oq_ref, okv_ref, oq2_ref, okv2_ref, unplace_ref, slot_ref, uq_ref, uv_ref, cos_ref, sin_ref, kcos_ref, ksin_ref,
        send_ref, out_ref,
    ) = refs[lows:]
    packed = low_refs[0][...].astype(F32)
    for ref in low_refs[1:]:
        packed = packed + ref[...].astype(F32)
    pack = HEAD // (2 * rank)
    low = jnp.concatenate(
        [packed[:, i * 2 * rank : (i + 1) * 2 * rank] for i in range(pack)], axis=0
    )
    low = dot(unplace_ref[...], low.astype(BF16)).astype(BF16)
    wide = uq_ref.shape[0]
    lane = lax.broadcasted_iota(jnp.int32, (low.shape[0], wide), 1)
    here = lane // rank == slot_ref[...]
    row = lax.broadcasted_iota(jnp.int32, (2 * rank, wide), 0)
    column = lax.broadcasted_iota(jnp.int32, (2 * rank, wide), 1)
    spread_q = jnp.where(column % rank == row, 1.0, 0.0).astype(BF16)
    spread_v = jnp.where(column % rank + rank == row, 1.0, 0.0).astype(BF16)
    wide_q = jnp.where(here, dot(low, spread_q), 0.0).astype(BF16)
    wide_v = jnp.where(here, dot(low, spread_v), 0.0).astype(BF16)
    query = oq_ref[...] + oq2_ref[...] + dot(wide_q, uq_ref[...])
    fresh = turned(okv_ref[...] + okv2_ref[...], kcos_ref[...], ksin_ref[...])
    columns = uv_ref.shape[1]
    value = dot(wide_v, uv_ref[...])
    pieces = [jnp.zeros((value.shape[0], columns), F32), value]
    if 2 * columns < HEAD:
        pieces.append(jnp.zeros((value.shape[0], HEAD - 2 * columns), F32))
    fresh = fresh + jnp.concatenate(pieces, axis=1)
    cosine, sine = cos_ref[...], sin_ref[...]
    parts = []
    for h in range(query.shape[1] // HEAD):
        parts.append(turned(query[:, h * HEAD : (h + 1) * HEAD], cosine, sine))
    parts.append(fresh)
    stacked = jnp.concatenate(parts, axis=0).astype(BF16)
    out_ref[...] = dot(send_ref[...], stacked).astype(BF16).reshape(out_ref.shape)


def attend_body(
    own, columns, index_ref, len_ref, x_ref, order_ref, k_ref, v_ref, nk_ref, nv_ref, ctx_ref, s_ref
):
    n, span = x_ref.shape[0], k_ref.shape[1]
    group = HEADS // KV_HEADS
    local = HEADS // n
    rows = own * STEPS
    mine = group * STEPS
    x = x_ref[...]
    queries = dot(order_ref[...], x.reshape(n * x.shape[1], HEAD)).astype(BF16)
    wide = x.astype(F32)
    first = rows * local
    fresh = [wide[i, first : first + rows] for i in range(n)]
    each = n // KV_HEADS
    keys, values = [], []
    for g in range(KV_HEADS):
        pieces = fresh[g * each : (g + 1) * each]
        keys.append(jnp.concatenate([p[:, :columns] for p in pieces], axis=1))
        values.append(jnp.concatenate([p[:, columns : 2 * columns] for p in pieces], axis=1))
    new_keys = jnp.concatenate(keys, axis=1)
    new_values = jnp.concatenate(values, axis=1)
    for b in range(own):
        at = slice(b * STEPS, (b + 1) * STEPS)
        nk_ref[b] = new_keys[at].astype(BF16)
        nv_ref[b] = new_values[at].astype(BF16)
    pad = jnp.zeros((16 - rows, HEAD), F32)
    keys = [jnp.concatenate((k, pad), axis=0).astype(BF16) for k in keys]
    values = [jnp.concatenate((v, pad), axis=0).astype(BF16) for v in values]
    scale = HEAD ** (-0.5)
    contexts = []
    for b in range(own):
        q = queries[b * KV_HEADS * mine : (b + 1) * KV_HEADS * mine]
        cached, newer = [], []
        for g in range(KV_HEADS):
            qg = q[g * mine : (g + 1) * mine]
            cached.append(dot_nt(qg, k_ref[b, :, g * HEAD : (g + 1) * HEAD]))
            newer.append(dot_nt(qg, keys[g]))
        cached = jnp.concatenate(cached, axis=0) * scale
        newer = jnp.concatenate(newer, axis=0) * scale
        place = lax.broadcasted_iota(jnp.int32, cached.shape, 1)
        cached = jnp.where(place < len_ref[index_ref[0] * own + b], cached, -1e30)
        step = lax.broadcasted_iota(jnp.int32, newer.shape, 0) % STEPS
        at = lax.broadcasted_iota(jnp.int32, newer.shape, 1) - b * STEPS
        newer = jnp.where((at >= 0) & (at <= step), newer, -1e30)
        top = jnp.maximum(
            jnp.max(cached, axis=1, keepdims=True), jnp.max(newer, axis=1, keepdims=True)
        )
        cached = jnp.exp(cached - top)
        newer = jnp.exp(newer - top)
        total = jnp.sum(cached, axis=1, keepdims=True) + jnp.sum(newer, axis=1, keepdims=True)
        cached = (cached / total).astype(BF16)
        newer = (newer / total).astype(BF16)
        for g in range(KV_HEADS):
            at_rows = slice(g * mine, (g + 1) * mine)
            part = dot(cached[at_rows], v_ref[b, :, g * HEAD : (g + 1) * HEAD])
            s_ref[(b * KV_HEADS + g) * mine : (b * KV_HEADS + g + 1) * mine] = part + dot(
                newer[at_rows], values[g]
            )
    step = local * STEPS
    half = KV_HEADS * mine
    for i in range(n):
        block = [s_ref[b * half + i * step : b * half + (i + 1) * step] for b in range(own)]
        ctx_ref[i] = jnp.concatenate(block, axis=0).astype(BF16)


def take_body(ctx_ref, take_ref, w_ref, a_ref, mine_ref, other_ref):
    rows = a_ref.shape[0]
    x = ctx_ref[...].reshape(-1, HEAD)
    taken = dot(take_ref[...], x).astype(BF16)
    for h in range(a_ref.shape[1] // HEAD):
        a_ref[:, h * HEAD : (h + 1) * HEAD] = taken[h * rows : (h + 1) * rows]
    out_body(0, a_ref, w_ref, mine_ref, other_ref)


def out_body(start, a_ref, w_ref, mine_ref, other_ref):
    half = mine_ref.shape[0]
    tile = 1024

    @pl.loop(0, mine_ref.shape[1] // tile)
    def _(i):
        at = pl.ds(pl.multiple_of(i * tile, tile), tile)
        product = dot(a_ref[...], w_ref[:, pl.ds(pl.multiple_of(start + i * tile, tile), tile)])
        mine_ref[:, at] = product[:half]
        other_ref[:, at] = product[half:]


def far_first_body(near, mine_ref, came_ref, *refs):
    total = mine_ref[...] + came_ref[...]
    rows = refs[0].shape[0] // near
    for f, ref in enumerate(refs):
        blocks = [(m * len(refs) + f) * rows for m in range(near)]
        value = jnp.concatenate([total[at : at + rows] for at in blocks], axis=0)
        ref[...] = value.astype(ref.dtype)


def near_body(mine_ref, came_ref, *refs):
    rows = refs[0].shape[0]
    total = mine_ref[...] + came_ref[...]
    refs[0][...] = total[:rows]
    for m, ref in enumerate(refs[1:], 1):
        ref[...] = total[m * rows : (m + 1) * rows].astype(BF16)


def far_body(came, *refs):
    total = refs[0][...]
    for ref in refs[1 : 1 + came]:
        total = total + ref[...].astype(F32)
    refs = refs[1 + came :]
    rows = refs[0].shape[0]
    refs[0][...] = total[:rows]
    for f, ref in enumerate(refs[1:], 1):
        ref[...] = total[f * rows : (f + 1) * rows].astype(ref.dtype)


def last_body(longs, first_ref, second_ref, *refs):
    one_ref, two_ref = refs[-2:]
    totals = []
    for part in (refs[:longs], refs[longs:-2]):
        total = part[0][...]
        for ref in part[1:]:
            total = total + ref[...].astype(F32)
        totals.append(total)
    total = jnp.concatenate(totals, axis=1)
    own = one_ref.shape[0]
    one_ref[...] = (first_ref[...].astype(F32) + total[:own]).astype(BF16)
    two_ref[...] = (second_ref[...].astype(F32) + total[own:]).astype(BF16)


def shards(
    sizes,
    residual_first,
    residual_second,
    attention_norm_gain,
    query_matrix,
    key_matrix,
    value_matrix,
    output_matrix,
    query_down_weights,
    value_down_weights,
    query_up_weights,
    value_up_weights,
    rotated_key_cache,
    stored_value_cache,
    lengths,
    request_adapter,
    adapter_slot,
):
    far, near, cores = sizes
    n = far * near * cores
    index = lax.axis_index("serve")
    own, width = residual_first.shape
    adapters, _, rank = query_down_weights.shape
    query_cols = query_matrix.shape[1]
    key_cols = key_matrix.shape[1]
    local = query_cols // HEAD
    rows = own * STEPS
    all_rows = n * rows
    stored = query_up_weights.shape[0]

    def partner(f, m, c):
        pairs = []
        for z in range(far):
            for y in range(near):
                for k in range(cores):
                    to = moved(z, f, far) * near + moved(y, m, near)
                    to = to * cores + moved(k, c, cores)
                    pairs.append(((z * near + y) * cores + k, to))
        return pairs

    def shift(value, f, m, c):
        return lax.ppermute(value, "serve", partner(f, m, c))

    frequency = whole_call(frequency_body, jax.ShapeDtypeStruct((1, HEAD), F32), (), cost=3.0)
    gain = attention_norm_gain.reshape(width // HEAD, HEAD)
    gain, frequency = lax.optimization_barrier((gain, frequency))
    normed = whole_call(
        norm_body,
        jax.ShapeDtypeStruct((rows, width), BF16),
        (residual_first, residual_second, gain),
        hbm=3,
        scratch=[
            pltpu.VMEM((own, width), BF16),
            pltpu.VMEM((own, width), BF16),
            pltpu.VMEM(gain.shape, BF16),
            pltpu.SemaphoreType.DMA((3,)),
        ],
        cost=1.0,
    )
    normed = normed[None]
    fars = [shift(normed, f, 0, 0) for f in range(1, far)]
    nears = [shift(normed, 0, m, 0) for m in range(1, near)]
    rest = jnp.concatenate(fars)
    groups = [jnp.concatenate([normed, *fars, *nears[:1]])]
    groups += [shift(rest, 0, m, 0) for m in range(1, near)]

    rest, at = lax.optimization_barrier((rest, index[None]))
    sent = -(-(rows * local + rows) // 8) * 8
    narrow = jax.ShapeDtypeStruct((all_rows, 1), jnp.int32)
    table = jax.ShapeDtypeStruct((all_rows, HEAD), F32)
    square = jax.ShapeDtypeStruct((all_rows, all_rows), BF16)
    slot, near_slot, cosine, sine, key_cosine, key_sine, place, unplace, send, order, take = whole_call(
        functools.partial(prep_body, sizes, rank, own, key_cols, adapters),
        (
            narrow,
            narrow,
            table,
            table,
            table,
            table,
            square,
            square,
            jax.ShapeDtypeStruct((n * sent, all_rows * (local + 1)), BF16),
            jax.ShapeDtypeStruct((own * HEADS * STEPS, n * sent), BF16),
            jax.ShapeDtypeStruct((all_rows * local, n * rows * local), BF16),
        ),
        (at, lengths, request_adapter, adapter_slot, frequency),
        smem=1,
        hbm=3,
        scratch=[
            pltpu.SMEM(lengths.shape, jnp.int32),
            pltpu.SMEM(request_adapter.shape, jnp.int32),
            pltpu.SMEM(adapter_slot.shape, jnp.int32),
            pltpu.SemaphoreType.DMA((3,)),
        ],
        cost=4.0,
    )
    slot, groups[1] = lax.optimization_barrier((slot, groups[1]))

    groups += [shift(part, 0, 0, c) for c in range(1, cores) for part in groups[:near]]

    query_down = jnp.swapaxes(query_down_weights, 1, 2).reshape(adapters * rank, width)
    value_down = jnp.swapaxes(value_down_weights, 1, 2).reshape(adapters * rank, width)
    packed_rows = all_rows * 2 * rank // HEAD
    x, low = whole_call(
        functools.partial(low_body, rank, len(groups)),
        (
            jax.ShapeDtypeStruct((all_rows, width), BF16),
            jax.ShapeDtypeStruct((packed_rows, HEAD), BF16),
        ),
        (*groups, query_down, value_down, near_slot, place),
        cost=0.3,
    )
    def base(start, stop):
        return whole_call(
            functools.partial(base_body, 2048, start, stop),
            (
                jax.ShapeDtypeStruct((all_rows, query_cols), F32),
                jax.ShapeDtypeStruct((all_rows, HEAD), F32),
            ),
            (x, query_matrix, key_matrix.T, value_matrix.T),
            cost=0.3,
        )

    lows = [shift(low, 0, m, c) for m in range(near) for c in range(cores) if m + c]
    base_q, base_kv = base(0, width // 2)
    low = whole_call(join_body, jax.ShapeDtypeStruct(low.shape, BF16), (low, *lows), cost=0.1)
    low, base_q = lax.optimization_barrier((low, base_q))
    lows = [low] + [shift(low, f, 0, 0) for f in range(1, far)]
    bases = (base_q, base_kv, *base(width // 2, width))

    ready = whole_call(
        functools.partial(ready_body, rank, len(lows)),
        jax.ShapeDtypeStruct((n, sent, HEAD), BF16),
        (
            *lows,
            *bases,
            unplace,
            slot,
            query_up_weights.reshape(stored * rank, query_cols),
            value_up_weights.reshape(stored * rank, key_cols),
            cosine,
            sine,
            key_cosine,
            key_sine,
            send,
        ),
        cost=0.9,
    )
    arrived = lax.all_to_all(ready, "serve", split_axis=0, concat_axis=0, tiled=True)

    fresh = jax.ShapeDtypeStruct((own, STEPS, KV_HEADS * HEAD), BF16)
    new_keys, new_values, context = whole_call(
        functools.partial(attend_body, own, key_cols),
        (fresh, fresh, jax.ShapeDtypeStruct((n, rows * local, HEAD), BF16)),
        (index[None], lengths, arrived, order, rotated_key_cache, stored_value_cache),
        smem=2,
        scratch=[pltpu.VMEM((own * HEADS * STEPS, HEAD), F32)],
        cost=1.0,
    )
    context = lax.all_to_all(context, "serve", split_axis=0, concat_axis=0, tiled=True)

    half = all_rows // cores
    cut = width * 5 // 8

    def kinds(count, columns):
        return (jax.ShapeDtypeStruct((count, columns), F32),) * 2

    taken, mine_long, other_long = whole_call(
        take_body,
        (jax.ShapeDtypeStruct((all_rows, query_cols), BF16),) + kinds(half, cut),
        (context, take, output_matrix),
        cost=0.4,
    )
    mine_short, other_short = whole_call(
        functools.partial(out_body, cut),
        kinds(half, width - cut),
        (taken, output_matrix),
        cost=0.3,
    )

    def kind(count, columns, dtype):
        return jax.ShapeDtypeStruct((count * rows, columns), dtype)

    keep, *others = whole_call(
        near_body,
        (kind(far, cut, F32),) + (kind(far, cut, BF16),) * (near - 1),
        (mine_long, shift(other_long, 0, 0, 1)),
        cost=0.1,
    )
    others = [shift(other, 0, m, 0) for m, other in enumerate(others, 1)]
    short, *sides = whole_call(
        functools.partial(far_first_body, near),
        (kind(near, width - cut, F32),) + (kind(near, width - cut, BF16),) * (far - 1),
        (mine_short, shift(other_short, 0, 0, 1)),
        cost=0.1,
    )
    sides = [shift(side, f, 0, 0) for f, side in enumerate(sides, 1)]
    keep, *others = whole_call(
        functools.partial(far_body, len(others)),
        (kind(1, cut, F32),) + (kind(1, cut, BF16),) * (far - 1),
        (keep, *others),
        cost=0.1,
    )
    others = [shift(other, f, 0, 0) for f, other in enumerate(others, 1)]
    short, *sides = whole_call(
        functools.partial(far_body, len(sides)),
        (kind(1, width - cut, F32),) * near,
        (short, *sides),
        cost=0.1,
    )
    sides = [shift(side, 0, m, 0) for m, side in enumerate(sides, 1)]
    result = jax.ShapeDtypeStruct((own, width), BF16)
    out_one, out_two = whole_call(
        functools.partial(last_body, 1 + len(others)),
        (result, result),
        (residual_first, residual_second, keep, *others, short, *sides),
        cost=0.1,
    )
    return (out_one, out_two, new_keys, new_values)


def solution(mesh):
    n = mesh.shape["serve"]
    sizes = (n // 4, 2, 2)
    return jax.shard_map(
        functools.partial(shards, sizes),
        mesh=mesh,
        in_specs=(
            P(("replica", "serve"), None),
            P(("replica", "serve"), None),
            P(),
            P(None, "serve"),
            P(None, "serve"),
            P(None, "serve"),
            P("serve", None),
            P("serve", None, None),
            P("serve", None, None),
            P(None, None, "serve"),
            P(None, None, "serve"),
            P(("replica", "serve"), None, None),
            P(("replica", "serve"), None, None),
            P("replica"),
            P("replica"),
            P(),
        ),
        out_specs=(
            P(("replica", "serve"), None),
            P(("replica", "serve"), None),
            P(("replica", "serve"), None, None),
            P(("replica", "serve"), None, None),
        ),
        check_vma=False,
    )
```

```python
import functools
import math

import jax
import jax.numpy as jnp
from jax import lax
from jax.experimental import pallas as pl
from jax.experimental.pallas import tpu as pltpu
from jax.sharding import PartitionSpec as P

HEADS = 64
KV_HEADS = 8
HEAD = 128
STEPS = 2
LIMIT = 8 * 1024 * 1024
PEAK = 1.15e9
NT = (((1,), (1,)), ((), ()))
F32 = jnp.float32
BF16 = jnp.bfloat16


def dot(a, b):
    return jnp.dot(a, b, preferred_element_type=F32)


def dot_nt(a, b):
    return lax.dot_general(a, b, NT, preferred_element_type=F32)


def whole_call(body, out_shape, args, cost, smem=0, hbm=0, scratch=()):
    specs = [pl.BlockSpec(memory_space=pltpu.SMEM)] * smem
    specs += [pl.BlockSpec(memory_space=pltpu.HBM)] * hbm
    specs += [pl.BlockSpec(memory_space=pltpu.VMEM)] * (len(args) - smem - hbm)
    many = isinstance(out_shape, (tuple, list))
    vmem = pl.BlockSpec(memory_space=pltpu.VMEM)
    return pl.pallas_call(
        body,
        out_shape=out_shape,
        in_specs=specs,
        out_specs=tuple(vmem for _ in out_shape) if many else vmem,
        scratch_shapes=list(scratch),
        compiler_params=pltpu.CompilerParams(vmem_limit_bytes=LIMIT),
        cost_estimate=pl.CostEstimate(
            flops=int(cost * PEAK), bytes_accessed=0, transcendentals=0
        ),
    )(*args)


def scaled_frequency(pair_index):
    base = jnp.exp(pair_index.astype(F32) * (-2.0 * math.log(500000.0) / HEAD))
    wavelength = 2.0 * math.pi / base
    smooth = jnp.clip((8192.0 / wavelength - 1.0) / 3.0, 0.0, 1.0)
    return (1.0 - smooth) * base / 8.0 + smooth * base


def fetch(pairs, sems):
    copies = [
        pltpu.make_async_copy(source, target, sems.at[i])
        for i, (source, target) in enumerate(pairs)
    ]
    for copy in copies:
        copy.start()
    for copy in copies:
        copy.wait()


def norm_body(first_hbm, second_hbm, gain_hbm, out_ref, first_ref, second_ref, gain_ref, sems):
    fetch(((first_hbm, first_ref), (second_hbm, second_ref), (gain_hbm, gain_ref)), sems)
    gain = gain_ref[...].astype(F32)
    factors = []
    for ref in (first_ref, second_ref):
        values = ref[...].astype(F32)
        factors.append(lax.rsqrt(jnp.mean(values * values, axis=-1, keepdims=True) + 1e-05))
    factor = jnp.concatenate(factors, axis=0)
    for i in range(gain.shape[0]):
        at = slice(i * HEAD, (i + 1) * HEAD)
        values = jnp.concatenate((first_ref[:, at].astype(F32), second_ref[:, at].astype(F32)))
        out_ref[:, at] = (values * factor * gain[i : i + 1]).astype(BF16)


def frequency_body(out_ref):
    out_ref[...] = scaled_frequency(lax.broadcasted_iota(jnp.int32, out_ref.shape, 1) // 2)


def prep_body(
    sizes, rank, own, key_cols, adapters,
    index_ref, length_hbm, adapter_hbm, slot_hbm, frequency_ref,
    held_ref, local_ref, cos_ref, sin_ref, kcos_ref, ksin_ref, place_ref, unplace_ref, send_ref,
    order_ref, take_ref, length_ref, adapter_ref, slot_ref, sems,
):
    fetch(((length_hbm, length_ref), (adapter_hbm, adapter_ref), (slot_hbm, slot_ref)), sems)
    far, near, cores = sizes
    n = far * near * cores
    rows = own * STEPS
    all_rows = n * rows
    heads = HEADS // n
    sent = send_ref.shape[0] // n
    index = index_ref[0]
    core_at = index % cores
    near_at = index // cores % near
    far_at = index // (cores * near)

    def device_of(block, sign):
        c, m, f = block // (far * near), block // far % near, block % far
        f = (far_at + sign * f + far) % far
        m = (near_at + sign * m + near) % near
        c = (core_at + sign * c + cores) % cores
        return (f * near + m) * cores + c

    def iota(shape, axis):
        return lax.broadcasted_iota(jnp.int32, shape, axis)

    def split(row):
        return row // rows, row % rows // own, row % own

    block, step, mine = split(iota((all_rows, 1), 0))
    device = device_of(block, -1)
    request = device * own + mine
    length = jnp.zeros_like(request)
    adapter = jnp.zeros_like(request)
    for j in range(length_ref.shape[0]):
        length = jnp.where(request == j, length_ref[j], length)
        adapter = jnp.where(request == j, adapter_ref[j], adapter)
    slot = jnp.zeros_like(request)
    for j in range(slot_ref.shape[0]):
        slot = jnp.where(adapter == j, slot_ref[j], slot)
    held_ref[...] = slot
    local_ref[...] = slot - index * adapters
    position = (length + step).astype(F32)
    lane = iota((1, HEAD), 1)
    odd = jnp.where(lane % 2 == 0, -1.0, 1.0)
    angle = position * frequency_ref[...]
    cos_ref[...] = jnp.cos(angle)
    sin_ref[...] = jnp.sin(angle) * odd
    angle = position * scaled_frequency((index * key_cols + lane) % HEAD // 2)
    kcos_ref[...] = jnp.where(lane < key_cols, jnp.cos(angle), 1.0)
    ksin_ref[...] = jnp.where(lane < key_cols, jnp.sin(angle) * odd, 0.0)

    def hot(ref, row, column):
        ref[...] = jnp.where(row == column, 1.0, 0.0).astype(BF16)

    absolute = (device * STEPS + step) * own + mine
    hot(unplace_ref, absolute, iota((1, all_rows), 1))
    block, step, mine = split(iota((1, all_rows), 1))
    absolute = (device_of(block, -1) * STEPS + step) * own + mine
    hot(place_ref, iota((all_rows, 1), 0), absolute)

    column = iota((1, send_ref.shape[1]), 1)
    h = column // all_rows
    block, step, mine = split(column % all_rows)
    wanted = device_of(block, -1) * sent + jnp.where(
        h < heads, (mine * heads + h) * STEPS + step, rows * heads + mine * STEPS + step
    )
    hot(send_ref, iota((n * sent, 1), 0), wanted)

    row = iota((order_ref.shape[0], 1), 0)
    mine, head, step = row // (HEADS * STEPS), row // STEPS % HEADS, row % STEPS
    wanted = (head // heads) * sent + (mine * heads + head % heads) * STEPS + step
    hot(order_ref, wanted, iota((1, n * sent), 1))

    row = iota((take_ref.shape[0], 1), 0)
    h = row // all_rows
    block, step, mine = split(row % all_rows)
    wanted = device_of(block, 1) * rows * heads + (mine * heads + h) * STEPS + step
    hot(take_ref, wanted, iota((1, take_ref.shape[1]), 1))


def low_body(rank, groups, *refs):
    parts, (qd_ref, vd_ref, local_ref, place_ref, x_ref, out_ref) = refs[:groups], refs[groups:]
    rows = parts[0].shape[1]
    sets = max(1, 16 // rows)
    blocks = [(part, i) for part in parts for i in range(part.shape[0])]
    for first in range(0, len(blocks), sets):
        group = blocks[first : first + sets]
        for lane in range(0, x_ref.shape[1], 1024):
            lanes = slice(lane, lane + 1024)
            block = [part[i, :, lanes].astype(F32) for part, i in group]
            block = jnp.concatenate(block, axis=0).astype(BF16)
            x_ref[first * rows : (first + sets) * rows, lanes] = block
    adapters = qd_ref.shape[0] // rank
    maps = jnp.concatenate((qd_ref[...], vd_ref[...]), axis=0)
    low = dot_nt(x_ref[...], maps)
    lane = lax.broadcasted_iota(jnp.int32, low.shape, 1)
    low = jnp.where(lane // rank % adapters == local_ref[...], low, 0.0)
    total = 0.0
    for a in range(adapters):
        q = low[:, a * rank : (a + 1) * rank]
        v = low[:, (adapters + a) * rank : (adapters + a + 1) * rank]
        total = total + jnp.concatenate((q, v), axis=1)
    rows = dot(place_ref[...], total.astype(BF16))
    pack = HEAD // (2 * rank)
    step = rows.shape[0] // pack
    packed = jnp.concatenate([rows[i * step : (i + 1) * step] for i in range(pack)], axis=1)
    out_ref[...] = packed.astype(BF16)


def join_body(*refs):
    total = refs[0][...].astype(F32)
    for ref in refs[1:-1]:
        total = total + ref[...].astype(F32)
    refs[-1][...] = total.astype(BF16)


def base_body(depth, start, stop, x_ref, q_ref, k_ref, v_ref, oq_ref, okv_ref):
    oq_ref[...] = jnp.zeros_like(oq_ref)
    okv_ref[...] = jnp.zeros_like(okv_ref)
    columns = k_ref.shape[0]
    narrow = jnp.zeros((HEAD - 2 * columns, depth), BF16)

    @pl.loop(start // depth, stop // depth)
    def _(i):
        at = pl.ds(pl.multiple_of(i * depth, depth), depth)
        x = x_ref[:, at]
        oq_ref[...] += dot(x, q_ref[at, :])
        both = (k_ref[:, at], v_ref[:, at])
        if 2 * columns < HEAD:
            both += (narrow,)
        okv_ref[...] += dot_nt(x, jnp.concatenate(both, axis=0))


def turned(values, cosine, sine):
    lane = lax.broadcasted_iota(jnp.int32, values.shape, 1)
    width = values.shape[1]
    ahead = pltpu.roll(values, width - 1, 1)
    behind = pltpu.roll(values, 1, 1)
    return values * cosine + jnp.where(lane % 2 == 0, ahead, behind) * sine


def ready_body(
    rank, lows, *refs
):
    low_refs = refs[:lows]
    (
        oq_ref, okv_ref, oq2_ref, okv2_ref, unplace_ref, slot_ref, uq_ref, uv_ref, cos_ref, sin_ref, kcos_ref, ksin_ref,
        send_ref, out_ref,
    ) = refs[lows:]
    packed = low_refs[0][...].astype(F32)
    for ref in low_refs[1:]:
        packed = packed + ref[...].astype(F32)
    pack = HEAD // (2 * rank)
    low = jnp.concatenate(
        [packed[:, i * 2 * rank : (i + 1) * 2 * rank] for i in range(pack)], axis=0
    )
    low = dot(unplace_ref[...], low.astype(BF16)).astype(BF16)
    wide = uq_ref.shape[0]
    lane = lax.broadcasted_iota(jnp.int32, (low.shape[0], wide), 1)
    here = lane // rank == slot_ref[...]
    row = lax.broadcasted_iota(jnp.int32, (2 * rank, wide), 0)
    column = lax.broadcasted_iota(jnp.int32, (2 * rank, wide), 1)
    spread_q = jnp.where(column % rank == row, 1.0, 0.0).astype(BF16)
    spread_v = jnp.where(column % rank + rank == row, 1.0, 0.0).astype(BF16)
    wide_q = jnp.where(here, dot(low, spread_q), 0.0).astype(BF16)
    wide_v = jnp.where(here, dot(low, spread_v), 0.0).astype(BF16)
    query = oq_ref[...] + oq2_ref[...] + dot(wide_q, uq_ref[...])
    fresh = turned(okv_ref[...] + okv2_ref[...], kcos_ref[...], ksin_ref[...])
    columns = uv_ref.shape[1]
    value = dot(wide_v, uv_ref[...])
    pieces = [jnp.zeros((value.shape[0], columns), F32), value]
    if 2 * columns < HEAD:
        pieces.append(jnp.zeros((value.shape[0], HEAD - 2 * columns), F32))
    fresh = fresh + jnp.concatenate(pieces, axis=1)
    cosine, sine = cos_ref[...], sin_ref[...]
    parts = []
    for h in range(query.shape[1] // HEAD):
        parts.append(turned(query[:, h * HEAD : (h + 1) * HEAD], cosine, sine))
    parts.append(fresh)
    stacked = jnp.concatenate(parts, axis=0).astype(BF16)
    out_ref[...] = dot(send_ref[...], stacked).astype(BF16).reshape(out_ref.shape)


def attend_body(
    own, columns, index_ref, len_ref, x_ref, order_ref, k_ref, v_ref, nk_ref, nv_ref, ctx_ref, s_ref
):
    n, span = x_ref.shape[0], k_ref.shape[1]
    group = HEADS // KV_HEADS
    local = HEADS // n
    rows = own * STEPS
    mine = group * STEPS
    x = x_ref[...]
    queries = dot(order_ref[...], x.reshape(n * x.shape[1], HEAD)).astype(BF16)
    wide = x.astype(F32)
    first = rows * local
    fresh = [wide[i, first : first + rows] for i in range(n)]
    each = n // KV_HEADS
    keys, values = [], []
    for g in range(KV_HEADS):
        pieces = fresh[g * each : (g + 1) * each]
        keys.append(jnp.concatenate([p[:, :columns] for p in pieces], axis=1))
        values.append(jnp.concatenate([p[:, columns : 2 * columns] for p in pieces], axis=1))
    new_keys = jnp.concatenate(keys, axis=1)
    new_values = jnp.concatenate(values, axis=1)
    for b in range(own):
        at = slice(b * STEPS, (b + 1) * STEPS)
        nk_ref[b] = new_keys[at].astype(BF16)
        nv_ref[b] = new_values[at].astype(BF16)
    pad = jnp.zeros((16 - rows, HEAD), F32)
    keys = [jnp.concatenate((k, pad), axis=0).astype(BF16) for k in keys]
    values = [jnp.concatenate((v, pad), axis=0).astype(BF16) for v in values]
    scale = HEAD ** (-0.5)
    contexts = []
    for b in range(own):
        q = queries[b * KV_HEADS * mine : (b + 1) * KV_HEADS * mine]
        cached, newer = [], []
        for g in range(KV_HEADS):
            qg = q[g * mine : (g + 1) * mine]
            cached.append(dot_nt(qg, k_ref[b, :, g * HEAD : (g + 1) * HEAD]))
            newer.append(dot_nt(qg, keys[g]))
        cached = jnp.concatenate(cached, axis=0) * scale
        newer = jnp.concatenate(newer, axis=0) * scale
        place = lax.broadcasted_iota(jnp.int32, cached.shape, 1)
        cached = jnp.where(place < len_ref[index_ref[0] * own + b], cached, -1e30)
        step = lax.broadcasted_iota(jnp.int32, newer.shape, 0) % STEPS
        at = lax.broadcasted_iota(jnp.int32, newer.shape, 1) - b * STEPS
        newer = jnp.where((at >= 0) & (at <= step), newer, -1e30)
        top = jnp.maximum(
            jnp.max(cached, axis=1, keepdims=True), jnp.max(newer, axis=1, keepdims=True)
        )
        cached = jnp.exp(cached - top)
        newer = jnp.exp(newer - top)
        total = jnp.sum(cached, axis=1, keepdims=True) + jnp.sum(newer, axis=1, keepdims=True)
        cached = (cached / total).astype(BF16)
        newer = (newer / total).astype(BF16)
        for g in range(KV_HEADS):
            at_rows = slice(g * mine, (g + 1) * mine)
            part = dot(cached[at_rows], v_ref[b, :, g * HEAD : (g + 1) * HEAD])
            s_ref[(b * KV_HEADS + g) * mine : (b * KV_HEADS + g + 1) * mine] = part + dot(
                newer[at_rows], values[g]
            )
    step = local * STEPS
    half = KV_HEADS * mine
    for i in range(n):
        block = [s_ref[b * half + i * step : b * half + (i + 1) * step] for b in range(own)]
        ctx_ref[i] = jnp.concatenate(block, axis=0).astype(BF16)


def take_body(ctx_ref, take_ref, w_ref, a_ref, mine_ref, other_ref):
    rows = a_ref.shape[0]
    x = ctx_ref[...].reshape(-1, HEAD)
    taken = dot(take_ref[...], x).astype(BF16)
    for h in range(a_ref.shape[1] // HEAD):
        a_ref[:, h * HEAD : (h + 1) * HEAD] = taken[h * rows : (h + 1) * rows]
    out_body(0, a_ref, w_ref, mine_ref, other_ref)


def out_body(start, a_ref, w_ref, mine_ref, other_ref):
    half = mine_ref.shape[0]
    tile = 1024

    @pl.loop(0, mine_ref.shape[1] // tile)
    def _(i):
        at = pl.ds(pl.multiple_of(i * tile, tile), tile)
        product = dot(a_ref[...], w_ref[:, pl.ds(pl.multiple_of(start + i * tile, tile), tile)])
        mine_ref[:, at] = product[:half]
        other_ref[:, at] = product[half:]


def near_body(mine_ref, came_ref, mine2_ref, came2_ref, keep_ref, *refs):
    cut = mine_ref.shape[1]
    kept, rows = keep_ref.shape[0], refs[0].shape[0]
    for lanes, mine, came in (
        (slice(0, cut), mine_ref, came_ref),
        (slice(cut, None), mine2_ref, came2_ref),
    ):
        keep_ref[:, lanes] = mine[:kept] + came[:kept]
        for f, ref in enumerate(refs):
            at = slice(kept + f * rows, kept + (f + 1) * rows)
            ref[:, lanes] = (mine[at] + came[at]).astype(BF16)


def far_body(f, keep_ref, came_ref, out_ref):
    rows = out_ref.shape[0]
    total = keep_ref[f * rows : (f + 1) * rows] + came_ref[...].astype(F32)
    out_ref[...] = total.astype(BF16)


def last_body(first_ref, second_ref, keep_ref, *refs):
    came, (one_ref, two_ref) = refs[:-2], refs[-2:]
    total = keep_ref[: came[0].shape[0]]
    for ref in came:
        total = total + ref[...].astype(F32)
    own = one_ref.shape[0]
    one_ref[...] = (first_ref[...].astype(F32) + total[:own]).astype(BF16)
    two_ref[...] = (second_ref[...].astype(F32) + total[own:]).astype(BF16)


def shards(
    sizes,
    residual_first,
    residual_second,
    attention_norm_gain,
    query_matrix,
    key_matrix,
    value_matrix,
    output_matrix,
    query_down_weights,
    value_down_weights,
    query_up_weights,
    value_up_weights,
    rotated_key_cache,
    stored_value_cache,
    lengths,
    request_adapter,
    adapter_slot,
):
    far, near, cores = sizes
    n = far * near * cores
    index = lax.axis_index("serve")
    own, width = residual_first.shape
    adapters, _, rank = query_down_weights.shape
    query_cols = query_matrix.shape[1]
    key_cols = key_matrix.shape[1]
    local = query_cols // HEAD
    rows = own * STEPS
    all_rows = n * rows
    stored = query_up_weights.shape[0]

    def partner(f, m, c):
        pairs = []
        for z in range(far):
            for y in range(near):
                for k in range(cores):
                    to = (((z + f) % far) * near + (y + m) % near) * cores + (k + c) % cores
                    pairs.append(((z * near + y) * cores + k, to))
        return pairs

    def shift(value, f, m, c):
        return lax.ppermute(value, "serve", partner(f, m, c))

    frequency = whole_call(frequency_body, jax.ShapeDtypeStruct((1, HEAD), F32), (), cost=3.0)
    gain = attention_norm_gain.reshape(width // HEAD, HEAD)
    gain, frequency = lax.optimization_barrier((gain, frequency))
    normed = whole_call(
        norm_body,
        jax.ShapeDtypeStruct((rows, width), BF16),
        (residual_first, residual_second, gain),
        hbm=3,
        scratch=[
            pltpu.VMEM((own, width), BF16),
            pltpu.VMEM((own, width), BF16),
            pltpu.VMEM(gain.shape, BF16),
            pltpu.SemaphoreType.DMA((3,)),
        ],
        cost=1.0,
    )
    normed = normed[None]
    fars = [shift(normed, f, 0, 0) for f in range(1, far)]
    nears = [shift(normed, 0, 1, 0)] + [shift(part, 0, 1, 0) for part in fars]
    groups = [jnp.concatenate([normed, *fars, nears[0]]), jnp.concatenate(nears[1:-1]), nears[-1]]

    at = index[None]
    sent = -(-(rows * local + rows) // 8) * 8
    narrow = jax.ShapeDtypeStruct((all_rows, 1), jnp.int32)
    table = jax.ShapeDtypeStruct((all_rows, HEAD), F32)
    square = jax.ShapeDtypeStruct((all_rows, all_rows), BF16)
    slot, near_slot, cosine, sine, key_cosine, key_sine, place, unplace, send, order, take = whole_call(
        functools.partial(prep_body, sizes, rank, own, key_cols, adapters),
        (
            narrow,
            narrow,
            table,
            table,
            table,
            table,
            square,
            square,
            jax.ShapeDtypeStruct((n * sent, all_rows * (local + 1)), BF16),
            jax.ShapeDtypeStruct((own * HEADS * STEPS, n * sent), BF16),
            jax.ShapeDtypeStruct((all_rows * local, n * rows * local), BF16),
        ),
        (at, lengths, request_adapter, adapter_slot, frequency),
        smem=1,
        hbm=3,
        scratch=[
            pltpu.SMEM(lengths.shape, jnp.int32),
            pltpu.SMEM(request_adapter.shape, jnp.int32),
            pltpu.SMEM(adapter_slot.shape, jnp.int32),
            pltpu.SemaphoreType.DMA((3,)),
        ],
        cost=4.0,
    )
    slot, groups[-1] = lax.optimization_barrier((slot, groups[-1]))

    groups += [shift(part, 0, 0, 1) for part in groups]

    query_down = jnp.swapaxes(query_down_weights, 1, 2).reshape(adapters * rank, width)
    value_down = jnp.swapaxes(value_down_weights, 1, 2).reshape(adapters * rank, width)
    packed_rows = all_rows * 2 * rank // HEAD
    x, low = whole_call(
        functools.partial(low_body, rank, len(groups)),
        (
            jax.ShapeDtypeStruct((all_rows, width), BF16),
            jax.ShapeDtypeStruct((packed_rows, HEAD), BF16),
        ),
        (*groups, query_down, value_down, near_slot, place),
        cost=0.3,
    )
    def base(start, stop):
        return whole_call(
            functools.partial(base_body, 2048, start, stop),
            (
                jax.ShapeDtypeStruct((all_rows, query_cols), F32),
                jax.ShapeDtypeStruct((all_rows, HEAD), F32),
            ),
            (x, query_matrix, key_matrix.T, value_matrix.T),
            cost=0.3,
        )

    lows = [shift(low, 0, m, c) for m in range(near) for c in range(cores) if m + c]
    base_q, base_kv = base(0, width // 2)
    low = whole_call(join_body, jax.ShapeDtypeStruct(low.shape, BF16), (low, *lows), cost=0.1)
    low, base_q = lax.optimization_barrier((low, base_q))
    lows = [low] + [shift(low, f, 0, 0) for f in range(1, far)]
    bases = (base_q, base_kv, *base(width // 2, width))

    ready = whole_call(
        functools.partial(ready_body, rank, len(lows)),
        jax.ShapeDtypeStruct((n, sent, HEAD), BF16),
        (
            *lows,
            *bases,
            unplace,
            slot,
            query_up_weights.reshape(stored * rank, query_cols),
            value_up_weights.reshape(stored * rank, key_cols),
            cosine,
            sine,
            key_cosine,
            key_sine,
            send,
        ),
        cost=0.9,
    )
    arrived = lax.all_to_all(ready, "serve", split_axis=0, concat_axis=0, tiled=True)

    fresh = jax.ShapeDtypeStruct((own, STEPS, KV_HEADS * HEAD), BF16)
    new_keys, new_values, context = whole_call(
        functools.partial(attend_body, own, key_cols),
        (fresh, fresh, jax.ShapeDtypeStruct((n, rows * local, HEAD), BF16)),
        (index[None], lengths, arrived, order, rotated_key_cache, stored_value_cache),
        smem=2,
        scratch=[pltpu.VMEM((own * HEADS * STEPS, HEAD), F32)],
        cost=1.0,
    )
    context = lax.all_to_all(context, "serve", split_axis=0, concat_axis=0, tiled=True)

    half = all_rows // cores
    cut = width * 5 // 8

    def kinds(count, columns):
        return (jax.ShapeDtypeStruct((count, columns), F32),) * 2

    taken, mine_long, other_long = whole_call(
        take_body,
        (jax.ShapeDtypeStruct((all_rows, query_cols), BF16),) + kinds(half, cut),
        (context, take, output_matrix),
        cost=0.4,
    )
    mine_short, other_short = whole_call(
        functools.partial(out_body, cut),
        kinds(half, width - cut),
        (taken, output_matrix),
        cost=0.3,
    )

    message = jax.ShapeDtypeStruct((rows, width), BF16)
    keep, *others = whole_call(
        near_body,
        (jax.ShapeDtypeStruct((far * rows, width), F32),) + (message,) * far,
        (
            mine_long,
            shift(other_long, 0, 0, 1),
            mine_short,
            shift(other_short, 0, 0, 1),
        ),
        cost=0.2,
    )
    came = []
    for f in range(1, far):
        folded = whole_call(
            functools.partial(far_body, f),
            message,
            (keep, shift(others[f], 0, 1, 0)),
            cost=0.1,
        )
        came.append(shift(folded, f, 0, 0))
    came.append(shift(others[0], 0, 1, 0))
    result = jax.ShapeDtypeStruct((own, width), BF16)
    out_one, out_two = whole_call(
        last_body,
        (result, result),
        (residual_first, residual_second, keep, *came),
        cost=0.1,
    )
    return (out_one, out_two, new_keys, new_values)


def solution(mesh):
    n = mesh.shape["serve"]
    sizes = (n // 4, 2, 2)
    return jax.shard_map(
        functools.partial(shards, sizes),
        mesh=mesh,
        in_specs=(
            P(("replica", "serve"), None),
            P(("replica", "serve"), None),
            P(),
            P(None, "serve"),
            P(None, "serve"),
            P(None, "serve"),
            P("serve", None),
            P("serve", None, None),
            P("serve", None, None),
            P(None, None, "serve"),
            P(None, None, "serve"),
            P(("replica", "serve"), None, None),
            P(("replica", "serve"), None, None),
            P("replica"),
            P("replica"),
            P(),
        ),
        out_specs=(
            P(("replica", "serve"), None),
            P(("replica", "serve"), None),
            P(("replica", "serve"), None, None),
            P(("replica", "serve"), None, None),
        ),
        check_vma=False,
    )
```

```python
import functools
import math

import jax
import jax.numpy as jnp
from jax import lax
from jax.experimental import pallas as pl
from jax.experimental.pallas import tpu as pltpu
from jax.sharding import PartitionSpec as P

HEADS = 64
KV_HEADS = 8
HEAD = 128
STEPS = 2
LIMIT = 8 * 1024 * 1024
PEAK = 1.15e9
NT = (((1,), (1,)), ((), ()))
F32 = jnp.float32
BF16 = jnp.bfloat16


def dot(a, b):
    return jnp.dot(a, b, preferred_element_type=F32)


def dot_nt(a, b):
    return lax.dot_general(a, b, NT, preferred_element_type=F32)


def whole_call(body, out_shape, args, cost, smem=0, hbm=0, scratch=()):
    specs = [pl.BlockSpec(memory_space=pltpu.SMEM)] * smem
    specs += [pl.BlockSpec(memory_space=pltpu.HBM)] * hbm
    specs += [pl.BlockSpec(memory_space=pltpu.VMEM)] * (len(args) - smem - hbm)
    many = isinstance(out_shape, (tuple, list))
    vmem = pl.BlockSpec(memory_space=pltpu.VMEM)
    return pl.pallas_call(
        body,
        out_shape=out_shape,
        in_specs=specs,
        out_specs=tuple(vmem for _ in out_shape) if many else vmem,
        scratch_shapes=list(scratch),
        compiler_params=pltpu.CompilerParams(vmem_limit_bytes=LIMIT),
        cost_estimate=pl.CostEstimate(
            flops=int(cost * PEAK), bytes_accessed=0, transcendentals=0
        ),
    )(*args)


def scaled_frequency(pair_index):
    base = jnp.exp(pair_index.astype(F32) * (-2.0 * math.log(500000.0) / HEAD))
    wavelength = 2.0 * math.pi / base
    smooth = jnp.clip((8192.0 / wavelength - 1.0) / 3.0, 0.0, 1.0)
    return (1.0 - smooth) * base / 8.0 + smooth * base


def fetch(pairs, sems):
    copies = [
        pltpu.make_async_copy(source, target, sems.at[i])
        for i, (source, target) in enumerate(pairs)
    ]
    for copy in copies:
        copy.start()
    for copy in copies:
        copy.wait()


def norm_body(first_hbm, second_hbm, gain_hbm, out_ref, first_ref, second_ref, gain_ref, sems):
    fetch(((first_hbm, first_ref), (second_hbm, second_ref), (gain_hbm, gain_ref)), sems)
    gain = gain_ref[...].astype(F32)
    factors = []
    for ref in (first_ref, second_ref):
        values = ref[...].astype(F32)
        factors.append(lax.rsqrt(jnp.mean(values * values, axis=-1, keepdims=True) + 1e-05))
    factor = jnp.concatenate(factors, axis=0)
    for i in range(gain.shape[0]):
        at = slice(i * HEAD, (i + 1) * HEAD)
        values = jnp.concatenate((first_ref[:, at].astype(F32), second_ref[:, at].astype(F32)))
        out_ref[:, at] = (values * factor * gain[i : i + 1]).astype(BF16)


def frequency_body(out_ref):
    out_ref[...] = scaled_frequency(lax.broadcasted_iota(jnp.int32, out_ref.shape, 1) // 2)


def prep_body(
    sizes, rank, own, key_cols, adapters,
    index_ref, length_hbm, adapter_hbm, slot_hbm, frequency_ref,
    held_ref, local_ref, cos_ref, sin_ref, kcos_ref, ksin_ref, place_ref, unplace_ref, send_ref,
    order_ref, take_ref, length_ref, adapter_ref, slot_ref, sems,
):
    fetch(((length_hbm, length_ref), (adapter_hbm, adapter_ref), (slot_hbm, slot_ref)), sems)
    far, near, cores = sizes
    n = far * near * cores
    rows = own * STEPS
    all_rows = n * rows
    heads = HEADS // n
    sent = send_ref.shape[0] // n
    index = index_ref[0]
    core_at = index % cores
    near_at = index // cores % near
    far_at = index // (cores * near)

    def device_of(block, sign):
        c, m, f = block // (far * near), block // far % near, block % far
        f = (far_at + sign * f + far) % far
        m = (near_at + sign * m + near) % near
        c = (core_at + sign * c + cores) % cores
        return (f * near + m) * cores + c

    def iota(shape, axis):
        return lax.broadcasted_iota(jnp.int32, shape, axis)

    def split(row):
        return row // rows, row % rows // own, row % own

    block, step, mine = split(iota((all_rows, 1), 0))
    device = device_of(block, -1)
    request = device * own + mine
    length = jnp.zeros_like(request)
    adapter = jnp.zeros_like(request)
    for j in range(length_ref.shape[0]):
        length = jnp.where(request == j, length_ref[j], length)
        adapter = jnp.where(request == j, adapter_ref[j], adapter)
    slot = jnp.zeros_like(request)
    for j in range(slot_ref.shape[0]):
        slot = jnp.where(adapter == j, slot_ref[j], slot)
    held_ref[...] = slot
    shared = cores * adapters
    place = slot - index // cores * shared
    turned_place = (place - core_at * adapters + shared) % shared
    local_ref[...] = jnp.where((place >= 0) & (place < shared), turned_place, -1)
    position = (length + step).astype(F32)
    lane = iota((1, HEAD), 1)
    odd = jnp.where(lane % 2 == 0, -1.0, 1.0)
    angle = position * frequency_ref[...]
    cos_ref[...] = jnp.cos(angle)
    sin_ref[...] = jnp.sin(angle) * odd
    angle = position * scaled_frequency((index * key_cols + lane) % HEAD // 2)
    kcos_ref[...] = jnp.where(lane < key_cols, jnp.cos(angle), 1.0)
    ksin_ref[...] = jnp.where(lane < key_cols, jnp.sin(angle) * odd, 0.0)

    def hot(ref, row, column):
        ref[...] = jnp.where(row == column, 1.0, 0.0).astype(BF16)

    absolute = (device * STEPS + step) * own + mine
    hot(unplace_ref, absolute, iota((1, all_rows), 1))
    block, step, mine = split(iota((1, all_rows), 1))
    absolute = (device_of(block, -1) * STEPS + step) * own + mine
    hot(place_ref, iota((all_rows, 1), 0), absolute)

    column = iota((1, send_ref.shape[1]), 1)
    h = column // all_rows
    block, step, mine = split(column % all_rows)
    wanted = device_of(block, -1) * sent + jnp.where(
        h < heads, (mine * heads + h) * STEPS + step, rows * heads + mine * STEPS + step
    )
    hot(send_ref, iota((n * sent, 1), 0), wanted)

    row = iota((order_ref.shape[0], 1), 0)
    mine, head, step = row // (HEADS * STEPS), row // STEPS % HEADS, row % STEPS
    wanted = (head // heads) * sent + (mine * heads + head % heads) * STEPS + step
    hot(order_ref, wanted, iota((1, n * sent), 1))

    row = iota((take_ref.shape[0], 1), 0)
    h = row // all_rows
    block, step, mine = split(row % all_rows)
    wanted = device_of(block, 1) * rows * heads + (mine * heads + h) * STEPS + step
    hot(take_ref, wanted, iota((1, take_ref.shape[1]), 1))


def low_body(rank, groups, *refs):
    parts, refs = refs[:groups], refs[groups:]
    *map_refs, local_ref, place_ref, x_ref, out_ref = refs
    rows = parts[0].shape[1]
    sets = max(1, 16 // rows)
    blocks = [(part, i) for part in parts for i in range(part.shape[0])]
    for first in range(0, len(blocks), sets):
        group = blocks[first : first + sets]
        for lane in range(0, x_ref.shape[1], 1024):
            lanes = slice(lane, lane + 1024)
            block = [part[i, :, lanes].astype(F32) for part, i in group]
            block = jnp.concatenate(block, axis=0).astype(BF16)
            x_ref[first * rows : (first + sets) * rows, lanes] = block
    maps = jnp.concatenate([ref[...] for ref in map_refs], axis=0)
    adapters = maps.shape[0] // (2 * rank)
    low = dot_nt(x_ref[...], maps)
    lane = lax.broadcasted_iota(jnp.int32, low.shape, 1)
    low = jnp.where(lane // rank % adapters == local_ref[...], low, 0.0)
    total = 0.0
    for a in range(adapters):
        q = low[:, a * rank : (a + 1) * rank]
        v = low[:, (adapters + a) * rank : (adapters + a + 1) * rank]
        total = total + jnp.concatenate((q, v), axis=1)
    rows = dot(place_ref[...], total.astype(BF16))
    pack = HEAD // (2 * rank)
    step = rows.shape[0] // pack
    packed = jnp.concatenate([rows[i * step : (i + 1) * step] for i in range(pack)], axis=1)
    out_ref[...] = packed.astype(BF16)


def join_body(*refs):
    total = refs[0][...].astype(F32)
    for ref in refs[1:-1]:
        total = total + ref[...].astype(F32)
    refs[-1][...] = total.astype(BF16)


def base_body(depth, start, stop, x_ref, q_ref, k_ref, v_ref, oq_ref, okv_ref):
    oq_ref[...] = jnp.zeros_like(oq_ref)
    okv_ref[...] = jnp.zeros_like(okv_ref)
    columns = k_ref.shape[0]
    narrow = jnp.zeros((HEAD - 2 * columns, depth), BF16)

    @pl.loop(start // depth, stop // depth)
    def _(i):
        at = pl.ds(pl.multiple_of(i * depth, depth), depth)
        x = x_ref[:, at]
        oq_ref[...] += dot(x, q_ref[at, :])
        both = (k_ref[:, at], v_ref[:, at])
        if 2 * columns < HEAD:
            both += (narrow,)
        okv_ref[...] += dot_nt(x, jnp.concatenate(both, axis=0))


def turned(values, cosine, sine):
    lane = lax.broadcasted_iota(jnp.int32, values.shape, 1)
    width = values.shape[1]
    ahead = pltpu.roll(values, width - 1, 1)
    behind = pltpu.roll(values, 1, 1)
    return values * cosine + jnp.where(lane % 2 == 0, ahead, behind) * sine


def ready_body(
    rank, lows, *refs
):
    low_refs = refs[:lows]
    (
        oq_ref, okv_ref, oq2_ref, okv2_ref, unplace_ref, slot_ref, uq_ref, uv_ref, cos_ref, sin_ref, kcos_ref, ksin_ref,
        send_ref, out_ref,
    ) = refs[lows:]
    packed = low_refs[0][...].astype(F32)
    for ref in low_refs[1:]:
        packed = packed + ref[...].astype(F32)
    pack = HEAD // (2 * rank)
    low = jnp.concatenate(
        [packed[:, i * 2 * rank : (i + 1) * 2 * rank] for i in range(pack)], axis=0
    )
    low = dot(unplace_ref[...], low.astype(BF16)).astype(BF16)
    wide = uq_ref.shape[0]
    lane = lax.broadcasted_iota(jnp.int32, (low.shape[0], wide), 1)
    here = lane // rank == slot_ref[...]
    row = lax.broadcasted_iota(jnp.int32, (2 * rank, wide), 0)
    column = lax.broadcasted_iota(jnp.int32, (2 * rank, wide), 1)
    spread_q = jnp.where(column % rank == row, 1.0, 0.0).astype(BF16)
    spread_v = jnp.where(column % rank + rank == row, 1.0, 0.0).astype(BF16)
    wide_q = jnp.where(here, dot(low, spread_q), 0.0).astype(BF16)
    wide_v = jnp.where(here, dot(low, spread_v), 0.0).astype(BF16)
    query = oq_ref[...] + oq2_ref[...] + dot(wide_q, uq_ref[...])
    fresh = turned(okv_ref[...] + okv2_ref[...], kcos_ref[...], ksin_ref[...])
    columns = uv_ref.shape[1]
    value = dot(wide_v, uv_ref[...])
    pieces = [jnp.zeros((value.shape[0], columns), F32), value]
    if 2 * columns < HEAD:
        pieces.append(jnp.zeros((value.shape[0], HEAD - 2 * columns), F32))
    fresh = fresh + jnp.concatenate(pieces, axis=1)
    cosine, sine = cos_ref[...], sin_ref[...]
    parts = []
    for h in range(query.shape[1] // HEAD):
        parts.append(turned(query[:, h * HEAD : (h + 1) * HEAD], cosine, sine))
    parts.append(fresh)
    stacked = jnp.concatenate(parts, axis=0).astype(BF16)
    out_ref[...] = dot(send_ref[...], stacked).astype(BF16).reshape(out_ref.shape)


def attend_body(
    own, columns, index_ref, len_ref, x_ref, order_ref, k_ref, v_ref, nk_ref, nv_ref, ctx_ref, s_ref
):
    n, span = x_ref.shape[0], k_ref.shape[1]
    group = HEADS // KV_HEADS
    local = HEADS // n
    rows = own * STEPS
    mine = group * STEPS
    x = x_ref[...]
    queries = dot(order_ref[...], x.reshape(n * x.shape[1], HEAD)).astype(BF16)
    wide = x.astype(F32)
    first = rows * local
    fresh = [wide[i, first : first + rows] for i in range(n)]
    each = n // KV_HEADS
    keys, values = [], []
    for g in range(KV_HEADS):
        pieces = fresh[g * each : (g + 1) * each]
        keys.append(jnp.concatenate([p[:, :columns] for p in pieces], axis=1))
        values.append(jnp.concatenate([p[:, columns : 2 * columns] for p in pieces], axis=1))
    new_keys = jnp.concatenate(keys, axis=1)
    new_values = jnp.concatenate(values, axis=1)
    for b in range(own):
        at = slice(b * STEPS, (b + 1) * STEPS)
        nk_ref[b] = new_keys[at].astype(BF16)
        nv_ref[b] = new_values[at].astype(BF16)
    pad = jnp.zeros((16 - rows, HEAD), F32)
    keys = [jnp.concatenate((k, pad), axis=0).astype(BF16) for k in keys]
    values = [jnp.concatenate((v, pad), axis=0).astype(BF16) for v in values]
    scale = HEAD ** (-0.5)
    contexts = []
    for b in range(own):
        q = queries[b * KV_HEADS * mine : (b + 1) * KV_HEADS * mine]
        cached, newer = [], []
        for g in range(0, KV_HEADS, 2):
            one, two = q[g * mine : (g + 1) * mine], q[(g + 1) * mine : (g + 2) * mine]
            none = jnp.zeros_like(one)
            pair = jnp.concatenate(
                (jnp.concatenate((one, none), axis=1), jnp.concatenate((none, two), axis=1)),
                axis=0,
            )
            cached.append(dot_nt(pair, k_ref[b, :, g * HEAD : (g + 2) * HEAD]))
            newer.append(dot_nt(pair, jnp.concatenate(keys[g : g + 2], axis=1)))
        cached = jnp.concatenate(cached, axis=0) * scale
        newer = jnp.concatenate(newer, axis=0) * scale
        place = lax.broadcasted_iota(jnp.int32, cached.shape, 1)
        cached = jnp.where(place < len_ref[index_ref[0] * own + b], cached, -1e30)
        step = lax.broadcasted_iota(jnp.int32, newer.shape, 0) % STEPS
        at = lax.broadcasted_iota(jnp.int32, newer.shape, 1) - b * STEPS
        newer = jnp.where((at >= 0) & (at <= step), newer, -1e30)
        top = jnp.maximum(
            jnp.max(cached, axis=1, keepdims=True), jnp.max(newer, axis=1, keepdims=True)
        )
        cached = jnp.exp(cached - top)
        newer = jnp.exp(newer - top)
        total = jnp.sum(cached, axis=1, keepdims=True) + jnp.sum(newer, axis=1, keepdims=True)
        cached = (cached / total).astype(BF16)
        newer = (newer / total).astype(BF16)
        for g in range(0, KV_HEADS, 2):
            at_rows = slice(g * mine, (g + 2) * mine)
            part = dot(cached[at_rows], v_ref[b, :, g * HEAD : (g + 2) * HEAD])
            part = part + dot(newer[at_rows], jnp.concatenate(values[g : g + 2], axis=1))
            at = (b * KV_HEADS + g) * mine
            s_ref[at : at + mine] = part[:mine, :HEAD]
            s_ref[at + mine : at + 2 * mine] = part[mine:, HEAD:]
    step = local * STEPS
    half = KV_HEADS * mine
    for i in range(n):
        block = [s_ref[b * half + i * step : b * half + (i + 1) * step] for b in range(own)]
        ctx_ref[i] = jnp.concatenate(block, axis=0).astype(BF16)


def take_body(ctx_ref, take_ref, w_ref, a_ref, mine_ref, other_ref):
    rows = a_ref.shape[0]
    x = ctx_ref[...].reshape(-1, HEAD)
    taken = dot(take_ref[...], x).astype(BF16)
    for h in range(a_ref.shape[1] // HEAD):
        a_ref[:, h * HEAD : (h + 1) * HEAD] = taken[h * rows : (h + 1) * rows]
    out_body(0, a_ref, w_ref, mine_ref, other_ref)


def out_body(start, a_ref, w_ref, mine_ref, other_ref):
    half = mine_ref.shape[0]
    tile = 1024

    @pl.loop(0, mine_ref.shape[1] // tile)
    def _(i):
        at = pl.ds(pl.multiple_of(i * tile, tile), tile)
        product = dot(a_ref[...], w_ref[:, pl.ds(pl.multiple_of(start + i * tile, tile), tile)])
        mine_ref[:, at] = product[:half]
        other_ref[:, at] = product[half:]


def far_first_body(near, mine_ref, came_ref, *refs):
    total = mine_ref[...] + came_ref[...]
    rows = refs[0].shape[0] // near
    for f, ref in enumerate(refs):
        blocks = [(m * len(refs) + f) * rows for m in range(near)]
        value = jnp.concatenate([total[at : at + rows] for at in blocks], axis=0)
        ref[...] = value.astype(ref.dtype)


def near_body(mine_ref, came_ref, *refs):
    rows = refs[0].shape[0]
    total = mine_ref[...] + came_ref[...]
    refs[0][...] = total[:rows]
    for m, ref in enumerate(refs[1:], 1):
        ref[...] = total[m * rows : (m + 1) * rows].astype(BF16)


def far_body(came, *refs):
    total = refs[0][...]
    for ref in refs[1 : 1 + came]:
        total = total + ref[...].astype(F32)
    refs = refs[1 + came :]
    rows = refs[0].shape[0]
    refs[0][...] = total[:rows]
    for f, ref in enumerate(refs[1:], 1):
        ref[...] = total[f * rows : (f + 1) * rows].astype(BF16)


def last_body(longs, first_ref, second_ref, *refs):
    one_ref, two_ref = refs[-2:]
    totals = []
    for part in (refs[:longs], refs[longs:-2]):
        total = part[0][...]
        for ref in part[1:]:
            total = total + ref[...].astype(F32)
        totals.append(total)
    total = jnp.concatenate(totals, axis=1)
    own = one_ref.shape[0]
    one_ref[...] = (first_ref[...].astype(F32) + total[:own]).astype(BF16)
    two_ref[...] = (second_ref[...].astype(F32) + total[own:]).astype(BF16)


def shards(
    sizes,
    residual_first,
    residual_second,
    attention_norm_gain,
    query_matrix,
    key_matrix,
    value_matrix,
    output_matrix,
    query_down_weights,
    value_down_weights,
    query_up_weights,
    value_up_weights,
    rotated_key_cache,
    stored_value_cache,
    lengths,
    request_adapter,
    adapter_slot,
):
    far, near, cores = sizes
    n = far * near * cores
    index = lax.axis_index("serve")
    own, width = residual_first.shape
    adapters, _, rank = query_down_weights.shape
    query_cols = query_matrix.shape[1]
    key_cols = key_matrix.shape[1]
    local = query_cols // HEAD
    rows = own * STEPS
    all_rows = n * rows
    stored = query_up_weights.shape[0]

    def partner(f, m, c):
        pairs = []
        for z in range(far):
            for y in range(near):
                for k in range(cores):
                    to = (((z + f) % far) * near + (y + m) % near) * cores + (k + c) % cores
                    pairs.append(((z * near + y) * cores + k, to))
        return pairs

    def shift(value, f, m, c):
        return lax.ppermute(value, "serve", partner(f, m, c))

    frequency = whole_call(frequency_body, jax.ShapeDtypeStruct((1, HEAD), F32), (), cost=3.0)
    gain = attention_norm_gain.reshape(width // HEAD, HEAD)
    gain, frequency = lax.optimization_barrier((gain, frequency))
    normed = whole_call(
        norm_body,
        jax.ShapeDtypeStruct((rows, width), BF16),
        (residual_first, residual_second, gain),
        hbm=3,
        scratch=[
            pltpu.VMEM((own, width), BF16),
            pltpu.VMEM((own, width), BF16),
            pltpu.VMEM(gain.shape, BF16),
            pltpu.SemaphoreType.DMA((3,)),
        ],
        cost=1.0,
    )
    normed = normed[None]
    fars = [shift(normed, f, 0, 0) for f in range(1, far)]
    nears = [shift(normed, 0, m, 0) for m in range(1, near)]
    rest = jnp.concatenate(fars)
    groups = [jnp.concatenate([normed, *fars, *nears[:1]])]
    groups += [shift(rest, 0, m, 0) for m in range(1, near)]
    query_down = jnp.swapaxes(query_down_weights, 1, 2).reshape(adapters * rank, width)
    value_down = jnp.swapaxes(value_down_weights, 1, 2).reshape(adapters * rank, width)
    query_down, value_down, rest = lax.optimization_barrier((query_down, value_down, rest))

    rest, at = lax.optimization_barrier((rest, index[None]))
    sent = -(-(rows * local + rows) // 8) * 8
    narrow = jax.ShapeDtypeStruct((all_rows, 1), jnp.int32)
    table = jax.ShapeDtypeStruct((all_rows, HEAD), F32)
    square = jax.ShapeDtypeStruct((all_rows, all_rows), BF16)
    slot, near_slot, cosine, sine, key_cosine, key_sine, place, unplace, send, order, take = whole_call(
        functools.partial(prep_body, sizes, rank, own, key_cols, adapters),
        (
            narrow,
            narrow,
            table,
            table,
            table,
            table,
            square,
            square,
            jax.ShapeDtypeStruct((n * sent, all_rows * (local + 1)), BF16),
            jax.ShapeDtypeStruct((own * HEADS * STEPS, n * sent), BF16),
            jax.ShapeDtypeStruct((all_rows * local, n * rows * local), BF16),
        ),
        (at, lengths, request_adapter, adapter_slot, frequency),
        smem=1,
        hbm=3,
        scratch=[
            pltpu.SMEM(lengths.shape, jnp.int32),
            pltpu.SMEM(request_adapter.shape, jnp.int32),
            pltpu.SMEM(adapter_slot.shape, jnp.int32),
            pltpu.SemaphoreType.DMA((3,)),
        ],
        cost=4.0,
    )
    slot, groups[1] = lax.optimization_barrier((slot, groups[1]))

    groups += [shift(part, 0, 0, c) for c in range(1, cores) for part in groups[:near]]

    packed_rows = all_rows * 2 * rank // HEAD
    x, low = whole_call(
        functools.partial(low_body, rank, len(groups)),
        (
            jax.ShapeDtypeStruct((all_rows, width), BF16),
            jax.ShapeDtypeStruct((packed_rows, HEAD), BF16),
        ),
        (
            *groups,
            *[query_down, *[shift(query_down, 0, 0, c) for c in range(1, cores)]],
            *[value_down, *[shift(value_down, 0, 0, c) for c in range(1, cores)]],
            near_slot,
            place,
        ),
        cost=0.3,
    )
    def base(start, stop):
        return whole_call(
            functools.partial(base_body, 2048, start, stop),
            (
                jax.ShapeDtypeStruct((all_rows, query_cols), F32),
                jax.ShapeDtypeStruct((all_rows, HEAD), F32),
            ),
            (x, query_matrix, key_matrix.T, value_matrix.T),
            cost=0.3,
        )

    lows = [shift(low, 0, m, 0) for m in range(1, near)]
    base_q, base_kv = base(0, width // 2)
    low = whole_call(join_body, jax.ShapeDtypeStruct(low.shape, BF16), (low, *lows), cost=0.1)
    low, base_q = lax.optimization_barrier((low, base_q))
    lows = [low] + [shift(low, f, 0, 0) for f in range(1, far)]
    bases = (base_q, base_kv, *base(width // 2, width))

    ready = whole_call(
        functools.partial(ready_body, rank, len(lows)),
        jax.ShapeDtypeStruct((n, sent, HEAD), BF16),
        (
            *lows,
            *bases,
            unplace,
            slot,
            query_up_weights.reshape(stored * rank, query_cols),
            value_up_weights.reshape(stored * rank, key_cols),
            cosine,
            sine,
            key_cosine,
            key_sine,
            send,
        ),
        cost=0.9,
    )
    arrived = lax.all_to_all(ready, "serve", split_axis=0, concat_axis=0, tiled=True)

    fresh = jax.ShapeDtypeStruct((own, STEPS, KV_HEADS * HEAD), BF16)
    new_keys, new_values, context = whole_call(
        functools.partial(attend_body, own, key_cols),
        (fresh, fresh, jax.ShapeDtypeStruct((n, rows * local, HEAD), BF16)),
        (index[None], lengths, arrived, order, rotated_key_cache, stored_value_cache),
        smem=2,
        scratch=[pltpu.VMEM((own * HEADS * STEPS, HEAD), F32)],
        cost=1.0,
    )
    context = lax.all_to_all(context, "serve", split_axis=0, concat_axis=0, tiled=True)

    half = all_rows // cores
    cut = width // 2

    def kinds(count, columns):
        return (jax.ShapeDtypeStruct((count, columns), F32),) * 2

    taken, mine_long, other_long = whole_call(
        take_body,
        (jax.ShapeDtypeStruct((all_rows, query_cols), BF16),) + kinds(half, cut),
        (context, take, output_matrix),
        cost=0.4,
    )
    mine_short, other_short = whole_call(
        functools.partial(out_body, cut),
        kinds(half, width - cut),
        (taken, output_matrix),
        cost=0.3,
    )

    def kind(count, columns, dtype):
        return jax.ShapeDtypeStruct((count * rows, columns), dtype)

    keep, *others = whole_call(
        near_body,
        (kind(far, cut, F32),) + (kind(far, cut, BF16),) * (near - 1),
        (mine_long, shift(other_long, 0, 0, 1)),
        cost=0.1,
    )
    others = [shift(other, 0, m, 0) for m, other in enumerate(others, 1)]
    short, *sides = whole_call(
        functools.partial(far_first_body, near),
        (kind(near, width - cut, F32),) + (kind(near, width - cut, BF16),) * (far - 1),
        (mine_short, shift(other_short, 0, 0, 1)),
        cost=0.1,
    )
    sides = [shift(side, f, 0, 0) for f, side in enumerate(sides, 1)]
    keep, *others = whole_call(
        functools.partial(far_body, len(others)),
        (kind(1, cut, F32),) + (kind(1, cut, BF16),) * (far - 1),
        (keep, *others),
        cost=0.1,
    )
    others = [shift(other, f, 0, 0) for f, other in enumerate(others, 1)]
    short, *sides = whole_call(
        functools.partial(far_body, len(sides)),
        (kind(1, width - cut, F32),) + (kind(1, width - cut, BF16),) * (near - 1),
        (short, *sides),
        cost=0.1,
    )
    sides = [shift(side, 0, m, 0) for m, side in enumerate(sides, 1)]
    result = jax.ShapeDtypeStruct((own, width), BF16)
    out_one, out_two = whole_call(
        functools.partial(last_body, 1 + len(others)),
        (result, result),
        (residual_first, residual_second, keep, *others, short, *sides),
        cost=0.1,
    )
    return (out_one, out_two, new_keys, new_values)


def solution(mesh):
    n = mesh.shape["serve"]
    sizes = (n // 4, 2, 2)
    return jax.shard_map(
        functools.partial(shards, sizes),
        mesh=mesh,
        in_specs=(
            P(("replica", "serve"), None),
            P(("replica", "serve"), None),
            P(),
            P(None, "serve"),
            P(None, "serve"),
            P(None, "serve"),
            P("serve", None),
            P("serve", None, None),
            P("serve", None, None),
            P(None, None, "serve"),
            P(None, None, "serve"),
            P(("replica", "serve"), None, None),
            P(("replica", "serve"), None, None),
            P("replica"),
            P("replica"),
            P(),
        ),
        out_specs=(
            P(("replica", "serve"), None),
            P(("replica", "serve"), None),
            P(("replica", "serve"), None, None),
            P(("replica", "serve"), None, None),
        ),
        check_vma=False,
    )
```

```python
import functools
import math

import jax
import jax.numpy as jnp
from jax import lax
from jax.experimental import pallas as pl
from jax.experimental.pallas import tpu as pltpu
from jax.sharding import PartitionSpec as P

HEADS = 64
KV_HEADS = 8
HEAD = 128
STEPS = 2
LIMIT = 8 * 1024 * 1024
PEAK = 1.15e9
NT = (((1,), (1,)), ((), ()))
F32 = jnp.float32
BF16 = jnp.bfloat16


def dot(a, b):
    return jnp.dot(a, b, preferred_element_type=F32)


def dot_nt(a, b):
    return lax.dot_general(a, b, NT, preferred_element_type=F32)


def whole_call(body, out_shape, args, cost, smem=0, hbm=0, scratch=()):
    specs = [pl.BlockSpec(memory_space=pltpu.SMEM)] * smem
    specs += [pl.BlockSpec(memory_space=pltpu.HBM)] * hbm
    specs += [pl.BlockSpec(memory_space=pltpu.VMEM)] * (len(args) - smem - hbm)
    many = isinstance(out_shape, (tuple, list))
    vmem = pl.BlockSpec(memory_space=pltpu.VMEM)
    return pl.pallas_call(
        body,
        out_shape=out_shape,
        in_specs=specs,
        out_specs=tuple(vmem for _ in out_shape) if many else vmem,
        scratch_shapes=list(scratch),
        compiler_params=pltpu.CompilerParams(vmem_limit_bytes=LIMIT),
        cost_estimate=pl.CostEstimate(
            flops=int(cost * PEAK), bytes_accessed=0, transcendentals=0
        ),
    )(*args)


def scaled_frequency(pair_index):
    base = jnp.exp(pair_index.astype(F32) * (-2.0 * math.log(500000.0) / HEAD))
    wavelength = 2.0 * math.pi / base
    smooth = jnp.clip((8192.0 / wavelength - 1.0) / 3.0, 0.0, 1.0)
    return (1.0 - smooth) * base / 8.0 + smooth * base


def fetch(pairs, sems):
    copies = [
        pltpu.make_async_copy(source, target, sems.at[i])
        for i, (source, target) in enumerate(pairs)
    ]
    for copy in copies:
        copy.start()
    for copy in copies:
        copy.wait()


def norm_body(first_hbm, second_hbm, gain_hbm, out_ref, first_ref, second_ref, gain_ref, sems):
    fetch(((first_hbm, first_ref), (second_hbm, second_ref), (gain_hbm, gain_ref)), sems)
    gain = gain_ref[...].astype(F32)
    factors = []
    for ref in (first_ref, second_ref):
        values = ref[...].astype(F32)
        factors.append(lax.rsqrt(jnp.mean(values * values, axis=-1, keepdims=True) + 1e-05))
    factor = jnp.concatenate(factors, axis=0)
    for i in range(gain.shape[0]):
        at = slice(i * HEAD, (i + 1) * HEAD)
        values = jnp.concatenate((first_ref[:, at].astype(F32), second_ref[:, at].astype(F32)))
        out_ref[:, at] = (values * factor * gain[i : i + 1]).astype(BF16)


def frequency_body(out_ref):
    out_ref[...] = scaled_frequency(lax.broadcasted_iota(jnp.int32, out_ref.shape, 1) // 2)


def prep_body(
    sizes, rank, own, key_cols, adapters,
    index_ref, length_hbm, adapter_hbm, slot_hbm, frequency_ref,
    held_ref, local_ref, cos_ref, sin_ref, kcos_ref, ksin_ref, place_ref, unplace_ref, send_ref,
    order_ref, take_ref, length_ref, adapter_ref, slot_ref, sems,
):
    fetch(((length_hbm, length_ref), (adapter_hbm, adapter_ref), (slot_hbm, slot_ref)), sems)
    far, near, cores = sizes
    n = far * near * cores
    rows = own * STEPS
    all_rows = n * rows
    heads = HEADS // n
    sent = send_ref.shape[0] // n
    index = index_ref[0]
    core_at = index % cores
    near_at = index // cores % near
    far_at = index // (cores * near)

    def device_of(block, sign):
        c, m, f = block // (far * near), block // far % near, block % far
        f = (far_at + sign * f + far) % far
        m = (near_at + sign * m + near) % near
        c = (core_at + sign * c + cores) % cores
        return (f * near + m) * cores + c

    def iota(shape, axis):
        return lax.broadcasted_iota(jnp.int32, shape, axis)

    def split(row):
        return row // rows, row % rows // own, row % own

    block, step, mine = split(iota((all_rows, 1), 0))
    device = device_of(block, -1)
    request = device * own + mine
    length = jnp.zeros_like(request)
    adapter = jnp.zeros_like(request)
    for j in range(length_ref.shape[0]):
        length = jnp.where(request == j, length_ref[j], length)
        adapter = jnp.where(request == j, adapter_ref[j], adapter)
    slot = jnp.zeros_like(request)
    for j in range(slot_ref.shape[0]):
        slot = jnp.where(adapter == j, slot_ref[j], slot)
    held_ref[...] = slot
    shared = cores * adapters
    place = slot - index // cores * shared
    turned_place = (place - core_at * adapters + shared) % shared
    local_ref[...] = jnp.where((place >= 0) & (place < shared), turned_place, -1)
    position = (length + step).astype(F32)
    lane = iota((1, HEAD), 1)
    odd = jnp.where(lane % 2 == 0, -1.0, 1.0)
    angle = position * frequency_ref[...]
    cos_ref[...] = jnp.cos(angle)
    sin_ref[...] = jnp.sin(angle) * odd
    angle = position * scaled_frequency((index * key_cols + lane) % HEAD // 2)
    kcos_ref[...] = jnp.where(lane < key_cols, jnp.cos(angle), 1.0)
    ksin_ref[...] = jnp.where(lane < key_cols, jnp.sin(angle) * odd, 0.0)

    def hot(ref, row, column):
        ref[...] = jnp.where(row == column, 1.0, 0.0).astype(BF16)

    absolute = (device * STEPS + step) * own + mine
    hot(unplace_ref, absolute, iota((1, all_rows), 1))
    block, step, mine = split(iota((1, all_rows), 1))
    absolute = (device_of(block, -1) * STEPS + step) * own + mine
    hot(place_ref, iota((all_rows, 1), 0), absolute)

    column = iota((1, send_ref.shape[1]), 1)
    h = column // all_rows
    block, step, mine = split(column % all_rows)
    wanted = device_of(block, -1) * sent + jnp.where(
        h < heads, (mine * heads + h) * STEPS + step, rows * heads + mine * STEPS + step
    )
    hot(send_ref, iota((n * sent, 1), 0), wanted)

    row = iota((order_ref.shape[0], 1), 0)
    mine, head, step = row // (HEADS * STEPS), row // STEPS % HEADS, row % STEPS
    wanted = (head // heads) * sent + (mine * heads + head % heads) * STEPS + step
    hot(order_ref, wanted, iota((1, n * sent), 1))

    row = iota((take_ref.shape[0], 1), 0)
    h = row // all_rows
    block, step, mine = split(row % all_rows)
    wanted = device_of(block, 1) * rows * heads + (mine * heads + h) * STEPS + step
    hot(take_ref, wanted, iota((1, take_ref.shape[1]), 1))


def low_body(rank, groups, *refs):
    parts, refs = refs[:groups], refs[groups:]
    *map_refs, local_ref, place_ref, x_ref, out_ref = refs
    rows = parts[0].shape[1]
    sets = max(1, 16 // rows)
    blocks = [(part, i) for part in parts for i in range(part.shape[0])]
    for first in range(0, len(blocks), sets):
        group = blocks[first : first + sets]
        for lane in range(0, x_ref.shape[1], 1024):
            lanes = slice(lane, lane + 1024)
            block = [part[i, :, lanes].astype(F32) for part, i in group]
            block = jnp.concatenate(block, axis=0).astype(BF16)
            x_ref[first * rows : (first + sets) * rows, lanes] = block
    maps = jnp.concatenate([ref[...] for ref in map_refs], axis=0)
    adapters = maps.shape[0] // (2 * rank)
    low = dot_nt(x_ref[...], maps)
    lane = lax.broadcasted_iota(jnp.int32, low.shape, 1)
    low = jnp.where(lane // rank % adapters == local_ref[...], low, 0.0)
    total = 0.0
    for a in range(adapters):
        q = low[:, a * rank : (a + 1) * rank]
        v = low[:, (adapters + a) * rank : (adapters + a + 1) * rank]
        total = total + jnp.concatenate((q, v), axis=1)
    rows = dot(place_ref[...], total.astype(BF16))
    pack = HEAD // (2 * rank)
    step = rows.shape[0] // pack
    packed = jnp.concatenate([rows[i * step : (i + 1) * step] for i in range(pack)], axis=1)
    out_ref[...] = packed.astype(BF16)


def join_body(*refs):
    total = refs[0][...].astype(F32)
    for ref in refs[1:-1]:
        total = total + ref[...].astype(F32)
    refs[-1][...] = total.astype(BF16)


def base_body(depth, start, stop, x_ref, q_ref, k_ref, v_ref, oq_ref, okv_ref):
    oq_ref[...] = jnp.zeros_like(oq_ref)
    okv_ref[...] = jnp.zeros_like(okv_ref)
    columns = k_ref.shape[0]
    narrow = jnp.zeros((HEAD - 2 * columns, depth), BF16)

    @pl.loop(start // depth, stop // depth)
    def _(i):
        at = pl.ds(pl.multiple_of(i * depth, depth), depth)
        x = x_ref[:, at]
        oq_ref[...] += dot(x, q_ref[at, :])
        both = (k_ref[:, at], v_ref[:, at])
        if 2 * columns < HEAD:
            both += (narrow,)
        okv_ref[...] += dot_nt(x, jnp.concatenate(both, axis=0))


def turned(values, cosine, sine):
    lane = lax.broadcasted_iota(jnp.int32, values.shape, 1)
    width = values.shape[1]
    ahead = pltpu.roll(values, width - 1, 1)
    behind = pltpu.roll(values, 1, 1)
    return values * cosine + jnp.where(lane % 2 == 0, ahead, behind) * sine


def ready_body(
    rank, lows, *refs
):
    low_refs = refs[:lows]
    (
        oq_ref, okv_ref, oq2_ref, okv2_ref, unplace_ref, slot_ref, uq_ref, uv_ref, cos_ref, sin_ref, kcos_ref, ksin_ref,
        send_ref, out_ref,
    ) = refs[lows:]
    packed = low_refs[0][...].astype(F32)
    for ref in low_refs[1:]:
        packed = packed + ref[...].astype(F32)
    pack = HEAD // (2 * rank)
    low = jnp.concatenate(
        [packed[:, i * 2 * rank : (i + 1) * 2 * rank] for i in range(pack)], axis=0
    )
    low = dot(unplace_ref[...], low.astype(BF16)).astype(BF16)
    wide = uq_ref.shape[0]
    lane = lax.broadcasted_iota(jnp.int32, (low.shape[0], wide), 1)
    here = lane // rank == slot_ref[...]
    row = lax.broadcasted_iota(jnp.int32, (2 * rank, wide), 0)
    column = lax.broadcasted_iota(jnp.int32, (2 * rank, wide), 1)
    spread_q = jnp.where(column % rank == row, 1.0, 0.0).astype(BF16)
    spread_v = jnp.where(column % rank + rank == row, 1.0, 0.0).astype(BF16)
    wide_q = jnp.where(here, dot(low, spread_q), 0.0).astype(BF16)
    wide_v = jnp.where(here, dot(low, spread_v), 0.0).astype(BF16)
    query = oq_ref[...] + oq2_ref[...] + dot(wide_q, uq_ref[...])
    fresh = turned(okv_ref[...] + okv2_ref[...], kcos_ref[...], ksin_ref[...])
    columns = uv_ref.shape[1]
    value = dot(wide_v, uv_ref[...])
    pieces = [jnp.zeros((value.shape[0], columns), F32), value]
    if 2 * columns < HEAD:
        pieces.append(jnp.zeros((value.shape[0], HEAD - 2 * columns), F32))
    fresh = fresh + jnp.concatenate(pieces, axis=1)
    cosine, sine = cos_ref[...], sin_ref[...]
    parts = []
    for h in range(query.shape[1] // HEAD):
        parts.append(turned(query[:, h * HEAD : (h + 1) * HEAD], cosine, sine))
    parts.append(fresh)
    stacked = jnp.concatenate(parts, axis=0).astype(BF16)
    out_ref[...] = dot(send_ref[...], stacked).astype(BF16).reshape(out_ref.shape)


def attend_body(
    own, columns, index_ref, len_ref, x_ref, order_ref, k_ref, v_ref, nk_ref, nv_ref, ctx_ref, s_ref
):
    n, span = x_ref.shape[0], k_ref.shape[1]
    group = HEADS // KV_HEADS
    local = HEADS // n
    rows = own * STEPS
    mine = group * STEPS
    x = x_ref[...]
    queries = dot(order_ref[...], x.reshape(n * x.shape[1], HEAD)).astype(BF16)
    wide = x.astype(F32)
    first = rows * local
    fresh = [wide[i, first : first + rows] for i in range(n)]
    each = n // KV_HEADS
    keys, values = [], []
    for g in range(KV_HEADS):
        pieces = fresh[g * each : (g + 1) * each]
        keys.append(jnp.concatenate([p[:, :columns] for p in pieces], axis=1))
        values.append(jnp.concatenate([p[:, columns : 2 * columns] for p in pieces], axis=1))
    new_keys = jnp.concatenate(keys, axis=1)
    new_values = jnp.concatenate(values, axis=1)
    for b in range(own):
        at = slice(b * STEPS, (b + 1) * STEPS)
        nk_ref[b] = new_keys[at].astype(BF16)
        nv_ref[b] = new_values[at].astype(BF16)
    pad = jnp.zeros((16 - rows, HEAD), F32)
    keys = [jnp.concatenate((k, pad), axis=0).astype(BF16) for k in keys]
    values = [jnp.concatenate((v, pad), axis=0).astype(BF16) for v in values]
    scale = HEAD ** (-0.5)
    contexts = []
    for b in range(own):
        q = queries[b * KV_HEADS * mine : (b + 1) * KV_HEADS * mine]
        cached, newer = [], []
        for g in range(KV_HEADS):
            qg = q[g * mine : (g + 1) * mine]
            cached.append(dot_nt(qg, k_ref[b, :, g * HEAD : (g + 1) * HEAD]))
            newer.append(dot_nt(qg, keys[g]))
        cached = jnp.concatenate(cached, axis=0) * scale
        newer = jnp.concatenate(newer, axis=0) * scale
        place = lax.broadcasted_iota(jnp.int32, cached.shape, 1)
        cached = jnp.where(place < len_ref[index_ref[0] * own + b], cached, -1e30)
        step = lax.broadcasted_iota(jnp.int32, newer.shape, 0) % STEPS
        at = lax.broadcasted_iota(jnp.int32, newer.shape, 1) - b * STEPS
        newer = jnp.where((at >= 0) & (at <= step), newer, -1e30)
        top = jnp.maximum(
            jnp.max(cached, axis=1, keepdims=True), jnp.max(newer, axis=1, keepdims=True)
        )
        cached = jnp.exp(cached - top)
        newer = jnp.exp(newer - top)
        total = jnp.sum(cached, axis=1, keepdims=True) + jnp.sum(newer, axis=1, keepdims=True)
        share = 1.0 / total
        cached = (cached * share).astype(BF16)
        newer = (newer * share).astype(BF16)
        for g in range(KV_HEADS):
            at_rows = slice(g * mine, (g + 1) * mine)
            part = dot(cached[at_rows], v_ref[b, :, g * HEAD : (g + 1) * HEAD])
            s_ref[(b * KV_HEADS + g) * mine : (b * KV_HEADS + g + 1) * mine] = part + dot(
                newer[at_rows], values[g]
            )
    step = local * STEPS
    half = KV_HEADS * mine
    for i in range(n):
        block = [s_ref[b * half + i * step : b * half + (i + 1) * step] for b in range(own)]
        ctx_ref[i] = jnp.concatenate(block, axis=0).astype(BF16)


def take_body(ctx_ref, take_ref, w_ref, a_ref, mine_ref, other_ref):
    rows = a_ref.shape[0]
    x = ctx_ref[...].reshape(-1, HEAD)
    taken = dot(take_ref[...], x).astype(BF16)
    for h in range(a_ref.shape[1] // HEAD):
        a_ref[:, h * HEAD : (h + 1) * HEAD] = taken[h * rows : (h + 1) * rows]
    out_body(0, a_ref, w_ref, mine_ref, other_ref)


def out_body(start, a_ref, w_ref, mine_ref, other_ref):
    half = mine_ref.shape[0]
    tile = 1024

    @pl.loop(0, mine_ref.shape[1] // tile)
    def _(i):
        at = pl.ds(pl.multiple_of(i * tile, tile), tile)
        product = dot(a_ref[...], w_ref[:, pl.ds(pl.multiple_of(start + i * tile, tile), tile)])
        mine_ref[:, at] = product[:half]
        other_ref[:, at] = product[half:]


def far_first_body(near, mine_ref, came_ref, *refs):
    total = mine_ref[...] + came_ref[...]
    rows = refs[0].shape[0] // near
    for f, ref in enumerate(refs):
        blocks = [(m * len(refs) + f) * rows for m in range(near)]
        value = jnp.concatenate([total[at : at + rows] for at in blocks], axis=0)
        ref[...] = value.astype(ref.dtype)


def near_body(mine_ref, came_ref, *refs):
    rows = refs[0].shape[0]
    total = mine_ref[...] + came_ref[...]
    refs[0][...] = total[:rows]
    for m, ref in enumerate(refs[1:], 1):
        ref[...] = total[m * rows : (m + 1) * rows].astype(BF16)


def far_body(came, *refs):
    total = refs[0][...]
    for ref in refs[1 : 1 + came]:
        total = total + ref[...].astype(F32)
    refs = refs[1 + came :]
    rows = refs[0].shape[0]
    refs[0][...] = total[:rows]
    for f, ref in enumerate(refs[1:], 1):
        ref[...] = total[f * rows : (f + 1) * rows].astype(BF16)


def last_body(longs, first_ref, second_ref, *refs):
    one_ref, two_ref = refs[-2:]
    totals = []
    for part in (refs[:longs], refs[longs:-2]):
        total = part[0][...]
        for ref in part[1:]:
            total = total + ref[...].astype(F32)
        totals.append(total)
    total = jnp.concatenate(totals, axis=1)
    own = one_ref.shape[0]
    one_ref[...] = (first_ref[...].astype(F32) + total[:own]).astype(BF16)
    two_ref[...] = (second_ref[...].astype(F32) + total[own:]).astype(BF16)


def shards(
    sizes,
    residual_first,
    residual_second,
    attention_norm_gain,
    query_matrix,
    key_matrix,
    value_matrix,
    output_matrix,
    query_down_weights,
    value_down_weights,
    query_up_weights,
    value_up_weights,
    rotated_key_cache,
    stored_value_cache,
    lengths,
    request_adapter,
    adapter_slot,
):
    far, near, cores = sizes
    n = far * near * cores
    index = lax.axis_index("serve")
    own, width = residual_first.shape
    adapters, _, rank = query_down_weights.shape
    query_cols = query_matrix.shape[1]
    key_cols = key_matrix.shape[1]
    local = query_cols // HEAD
    rows = own * STEPS
    all_rows = n * rows
    stored = query_up_weights.shape[0]

    def partner(f, m, c):
        pairs = []
        for z in range(far):
            for y in range(near):
                for k in range(cores):
                    to = (((z + f) % far) * near + (y + m) % near) * cores + (k + c) % cores
                    pairs.append(((z * near + y) * cores + k, to))
        return pairs

    def shift(value, f, m, c):
        return lax.ppermute(value, "serve", partner(f, m, c))

    frequency = whole_call(frequency_body, jax.ShapeDtypeStruct((1, HEAD), F32), (), cost=3.0)
    gain = attention_norm_gain.reshape(width // HEAD, HEAD)
    gain, frequency = lax.optimization_barrier((gain, frequency))
    normed = whole_call(
        norm_body,
        jax.ShapeDtypeStruct((rows, width), BF16),
        (residual_first, residual_second, gain),
        hbm=3,
        scratch=[
            pltpu.VMEM((own, width), BF16),
            pltpu.VMEM((own, width), BF16),
            pltpu.VMEM(gain.shape, BF16),
            pltpu.SemaphoreType.DMA((3,)),
        ],
        cost=1.0,
    )
    normed = normed[None]
    fars = [shift(normed, f, 0, 0) for f in range(1, far)]
    nears = [shift(normed, 0, m, 0) for m in range(1, near)]
    rest = jnp.concatenate(fars)
    groups = [jnp.concatenate([normed, *fars, *nears[:1]])]
    groups += [shift(rest, 0, m, 0) for m in range(1, near)]
    query_down = jnp.swapaxes(query_down_weights, 1, 2).reshape(adapters * rank, width)
    value_down = jnp.swapaxes(value_down_weights, 1, 2).reshape(adapters * rank, width)
    query_down, value_down, rest = lax.optimization_barrier((query_down, value_down, rest))

    rest, at = lax.optimization_barrier((rest, index[None]))
    sent = -(-(rows * local + rows) // 8) * 8
    narrow = jax.ShapeDtypeStruct((all_rows, 1), jnp.int32)
    table = jax.ShapeDtypeStruct((all_rows, HEAD), F32)
    square = jax.ShapeDtypeStruct((all_rows, all_rows), BF16)
    slot, near_slot, cosine, sine, key_cosine, key_sine, place, unplace, send, order, take = whole_call(
        functools.partial(prep_body, sizes, rank, own, key_cols, adapters),
        (
            narrow,
            narrow,
            table,
            table,
            table,
            table,
            square,
            square,
            jax.ShapeDtypeStruct((n * sent, all_rows * (local + 1)), BF16),
            jax.ShapeDtypeStruct((own * HEADS * STEPS, n * sent), BF16),
            jax.ShapeDtypeStruct((all_rows * local, n * rows * local), BF16),
        ),
        (at, lengths, request_adapter, adapter_slot, frequency),
        smem=1,
        hbm=3,
        scratch=[
            pltpu.SMEM(lengths.shape, jnp.int32),
            pltpu.SMEM(request_adapter.shape, jnp.int32),
            pltpu.SMEM(adapter_slot.shape, jnp.int32),
            pltpu.SemaphoreType.DMA((3,)),
        ],
        cost=4.0,
    )
    slot, groups[1] = lax.optimization_barrier((slot, groups[1]))

    groups += [shift(part, 0, 0, c) for c in range(1, cores) for part in groups[:near]]

    packed_rows = all_rows * 2 * rank // HEAD
    x, low = whole_call(
        functools.partial(low_body, rank, len(groups)),
        (
            jax.ShapeDtypeStruct((all_rows, width), BF16),
            jax.ShapeDtypeStruct((packed_rows, HEAD), BF16),
        ),
        (
            *groups,
            *[query_down, *[shift(query_down, 0, 0, c) for c in range(1, cores)]],
            *[value_down, *[shift(value_down, 0, 0, c) for c in range(1, cores)]],
            near_slot,
            place,
        ),
        cost=0.3,
    )
    def base(start, stop):
        return whole_call(
            functools.partial(base_body, 2048, start, stop),
            (
                jax.ShapeDtypeStruct((all_rows, query_cols), F32),
                jax.ShapeDtypeStruct((all_rows, HEAD), F32),
            ),
            (x, query_matrix, key_matrix.T, value_matrix.T),
            cost=0.3,
        )

    lows = [shift(low, 0, m, 0) for m in range(1, near)]
    base_q, base_kv = base(0, width // 2)
    low = whole_call(join_body, jax.ShapeDtypeStruct(low.shape, BF16), (low, *lows), cost=0.1)
    low, base_q = lax.optimization_barrier((low, base_q))
    lows = [low] + [shift(low, f, 0, 0) for f in range(1, far)]
    bases = (base_q, base_kv, *base(width // 2, width))

    ready = whole_call(
        functools.partial(ready_body, rank, len(lows)),
        jax.ShapeDtypeStruct((n, sent, HEAD), BF16),
        (
            *lows,
            *bases,
            unplace,
            slot,
            query_up_weights.reshape(stored * rank, query_cols),
            value_up_weights.reshape(stored * rank, key_cols),
            cosine,
            sine,
            key_cosine,
            key_sine,
            send,
        ),
        cost=0.9,
    )
    arrived = lax.all_to_all(ready, "serve", split_axis=0, concat_axis=0, tiled=True)

    fresh = jax.ShapeDtypeStruct((own, STEPS, KV_HEADS * HEAD), BF16)
    new_keys, new_values, context = whole_call(
        functools.partial(attend_body, own, key_cols),
        (fresh, fresh, jax.ShapeDtypeStruct((n, rows * local, HEAD), BF16)),
        (index[None], lengths, arrived, order, rotated_key_cache, stored_value_cache),
        smem=2,
        scratch=[pltpu.VMEM((own * HEADS * STEPS, HEAD), F32)],
        cost=1.0,
    )
    context = lax.all_to_all(context, "serve", split_axis=0, concat_axis=0, tiled=True)

    half = all_rows // cores
    cut = width * 5 // 8

    def kinds(count, columns):
        return (jax.ShapeDtypeStruct((count, columns), F32),) * 2

    taken, mine_long, other_long = whole_call(
        take_body,
        (jax.ShapeDtypeStruct((all_rows, query_cols), BF16),) + kinds(half, cut),
        (context, take, output_matrix),
        cost=0.4,
    )
    mine_short, other_short = whole_call(
        functools.partial(out_body, cut),
        kinds(half, width - cut),
        (taken, output_matrix),
        cost=0.3,
    )

    def kind(count, columns, dtype):
        return jax.ShapeDtypeStruct((count * rows, columns), dtype)

    keep, *others = whole_call(
        near_body,
        (kind(far, cut, F32),) + (kind(far, cut, BF16),) * (near - 1),
        (mine_long, shift(other_long, 0, 0, 1)),
        cost=0.1,
    )
    others = [shift(other, 0, m, 0) for m, other in enumerate(others, 1)]
    short, *sides = whole_call(
        functools.partial(far_first_body, near),
        (kind(near, width - cut, F32),) + (kind(near, width - cut, BF16),) * (far - 1),
        (mine_short, shift(other_short, 0, 0, 1)),
        cost=0.1,
    )
    sides = [shift(side, f, 0, 0) for f, side in enumerate(sides, 1)]
    keep, *others = whole_call(
        functools.partial(far_body, len(others)),
        (kind(1, cut, F32),) + (kind(1, cut, BF16),) * (far - 1),
        (keep, *others),
        cost=0.1,
    )
    others = [shift(other, f, 0, 0) for f, other in enumerate(others, 1)]
    short, *sides = whole_call(
        functools.partial(far_body, len(sides)),
        (kind(1, width - cut, F32),) + (kind(1, width - cut, BF16),) * (near - 1),
        (short, *sides),
        cost=0.1,
    )
    sides = [shift(side, 0, m, 0) for m, side in enumerate(sides, 1)]
    result = jax.ShapeDtypeStruct((own, width), BF16)
    out_one, out_two = whole_call(
        functools.partial(last_body, 1 + len(others)),
        (result, result),
        (residual_first, residual_second, keep, *others, short, *sides),
        cost=0.1,
    )
    return (out_one, out_two, new_keys, new_values)


def solution(mesh):
    n = mesh.shape["serve"]
    sizes = (n // 4, 2, 2)
    return jax.shard_map(
        functools.partial(shards, sizes),
        mesh=mesh,
        in_specs=(
            P(("replica", "serve"), None),
            P(("replica", "serve"), None),
            P(),
            P(None, "serve"),
            P(None, "serve"),
            P(None, "serve"),
            P("serve", None),
            P("serve", None, None),
            P("serve", None, None),
            P(None, None, "serve"),
            P(None, None, "serve"),
            P(("replica", "serve"), None, None),
            P(("replica", "serve"), None, None),
            P("replica"),
            P("replica"),
            P(),
        ),
        out_specs=(
            P(("replica", "serve"), None),
            P(("replica", "serve"), None),
            P(("replica", "serve"), None, None),
            P(("replica", "serve"), None, None),
        ),
        check_vma=False,
    )
```

```python
import functools
import math

import jax
import jax.numpy as jnp
from jax import lax
from jax.experimental import pallas as pl
from jax.experimental.pallas import tpu as pltpu
from jax.sharding import PartitionSpec as P

HEADS = 64
KV_HEADS = 8
HEAD = 128
STEPS = 2
LIMIT = 8 * 1024 * 1024
PEAK = 1.15e9
NT = (((1,), (1,)), ((), ()))
F32 = jnp.float32
BF16 = jnp.bfloat16


def dot(a, b):
    return jnp.dot(a, b, preferred_element_type=F32)


def dot_nt(a, b):
    return lax.dot_general(a, b, NT, preferred_element_type=F32)


def whole_call(body, out_shape, args, cost, smem=0, hbm=0, scratch=()):
    specs = [pl.BlockSpec(memory_space=pltpu.SMEM)] * smem
    specs += [pl.BlockSpec(memory_space=pltpu.HBM)] * hbm
    specs += [pl.BlockSpec(memory_space=pltpu.VMEM)] * (len(args) - smem - hbm)
    many = isinstance(out_shape, (tuple, list))
    vmem = pl.BlockSpec(memory_space=pltpu.VMEM)
    return pl.pallas_call(
        body,
        out_shape=out_shape,
        in_specs=specs,
        out_specs=tuple(vmem for _ in out_shape) if many else vmem,
        scratch_shapes=list(scratch),
        compiler_params=pltpu.CompilerParams(vmem_limit_bytes=LIMIT),
        cost_estimate=pl.CostEstimate(
            flops=int(cost * PEAK), bytes_accessed=0, transcendentals=0
        ),
    )(*args)


def scaled_frequency(pair_index):
    base = jnp.exp(pair_index.astype(F32) * (-2.0 * math.log(500000.0) / HEAD))
    wavelength = 2.0 * math.pi / base
    smooth = jnp.clip((8192.0 / wavelength - 1.0) / 3.0, 0.0, 1.0)
    return (1.0 - smooth) * base / 8.0 + smooth * base


def fetch(pairs, sems):
    copies = [
        pltpu.make_async_copy(source, target, sems.at[i])
        for i, (source, target) in enumerate(pairs)
    ]
    for copy in copies:
        copy.start()
    for copy in copies:
        copy.wait()


def norm_body(first_hbm, second_hbm, gain_hbm, out_ref, first_ref, second_ref, gain_ref, sems):
    fetch(((first_hbm, first_ref), (second_hbm, second_ref), (gain_hbm, gain_ref)), sems)
    gain = gain_ref[...].astype(F32)
    factors = []
    for ref in (first_ref, second_ref):
        values = ref[...].astype(F32)
        factors.append(lax.rsqrt(jnp.mean(values * values, axis=-1, keepdims=True) + 1e-05))
    factor = jnp.concatenate(factors, axis=0)
    for i in range(gain.shape[0]):
        at = slice(i * HEAD, (i + 1) * HEAD)
        values = jnp.concatenate((first_ref[:, at].astype(F32), second_ref[:, at].astype(F32)))
        out_ref[:, at] = (values * factor * gain[i : i + 1]).astype(BF16)


def frequency_body(out_ref):
    out_ref[...] = scaled_frequency(lax.broadcasted_iota(jnp.int32, out_ref.shape, 1) // 2)


def prep_body(
    sizes, rank, own, key_cols, adapters,
    index_ref, length_hbm, adapter_hbm, slot_hbm, frequency_ref,
    held_ref, local_ref, cos_ref, sin_ref, kcos_ref, ksin_ref, place_ref, unplace_ref, send_ref,
    order_ref, take_ref, length_ref, adapter_ref, slot_ref, sems,
):
    fetch(((length_hbm, length_ref), (adapter_hbm, adapter_ref), (slot_hbm, slot_ref)), sems)
    far, near, cores = sizes
    n = far * near * cores
    rows = own * STEPS
    all_rows = n * rows
    heads = HEADS // n
    sent = send_ref.shape[0] // n
    index = index_ref[0]
    core_at = index % cores
    near_at = index // cores % near
    far_at = index // (cores * near)

    def device_of(block, sign):
        c, m, f = block // (far * near), block // far % near, block % far
        f = (far_at + sign * f + far) % far
        m = (near_at + sign * m + near) % near
        c = (core_at + sign * c + cores) % cores
        return (f * near + m) * cores + c

    def iota(shape, axis):
        return lax.broadcasted_iota(jnp.int32, shape, axis)

    def split(row):
        return row // rows, row % rows // own, row % own

    block, step, mine = split(iota((all_rows, 1), 0))
    device = device_of(block, -1)
    request = device * own + mine
    length = jnp.zeros_like(request)
    adapter = jnp.zeros_like(request)
    for j in range(length_ref.shape[0]):
        length = jnp.where(request == j, length_ref[j], length)
        adapter = jnp.where(request == j, adapter_ref[j], adapter)
    slot = jnp.zeros_like(request)
    for j in range(slot_ref.shape[0]):
        slot = jnp.where(adapter == j, slot_ref[j], slot)
    held_ref[...] = slot
    shared = cores * adapters
    place = slot - index // cores * shared
    turned_place = (place - core_at * adapters + shared) % shared
    local_ref[...] = jnp.where((place >= 0) & (place < shared), turned_place, -1)
    position = (length + step).astype(F32)
    lane = iota((1, HEAD), 1)
    odd = jnp.where(lane % 2 == 0, -1.0, 1.0)
    angle = position * frequency_ref[...]
    cos_ref[...] = jnp.cos(angle)
    sin_ref[...] = jnp.sin(angle) * odd
    angle = position * scaled_frequency((index * key_cols + lane) % HEAD // 2)
    kcos_ref[...] = jnp.where(lane < key_cols, jnp.cos(angle), 1.0)
    ksin_ref[...] = jnp.where(lane < key_cols, jnp.sin(angle) * odd, 0.0)

    def hot(ref, row, column):
        ref[...] = jnp.where(row == column, 1.0, 0.0).astype(BF16)

    absolute = (device * STEPS + step) * own + mine
    hot(unplace_ref, absolute, iota((1, all_rows), 1))
    block, step, mine = split(iota((1, all_rows), 1))
    absolute = (device_of(block, -1) * STEPS + step) * own + mine
    hot(place_ref, iota((all_rows, 1), 0), absolute)

    column = iota((1, send_ref.shape[1]), 1)
    h = column // all_rows
    block, step, mine = split(column % all_rows)
    wanted = device_of(block, -1) * sent + jnp.where(
        h < heads, (mine * heads + h) * STEPS + step, rows * heads + mine * STEPS + step
    )
    hot(send_ref, iota((n * sent, 1), 0), wanted)

    row = iota((order_ref.shape[0], 1), 0)
    mine, head, step = row // (HEADS * STEPS), row // STEPS % HEADS, row % STEPS
    wanted = (head // heads) * sent + (mine * heads + head % heads) * STEPS + step
    hot(order_ref, wanted, iota((1, n * sent), 1))

    row = iota((take_ref.shape[0], 1), 0)
    h = row // all_rows
    block, step, mine = split(row % all_rows)
    wanted = device_of(block, 1) * rows * heads + (mine * heads + h) * STEPS + step
    hot(take_ref, wanted, iota((1, take_ref.shape[1]), 1))


def low_body(rank, groups, *refs):
    parts, refs = refs[:groups], refs[groups:]
    *map_refs, local_ref, place_ref, x_ref, out_ref = refs
    rows = parts[0].shape[1]
    sets = max(1, 16 // rows)
    blocks = [(part, i) for part in parts for i in range(part.shape[0])]
    for first in range(0, len(blocks), sets):
        group = blocks[first : first + sets]
        for lane in range(0, x_ref.shape[1], 1024):
            lanes = slice(lane, lane + 1024)
            block = [part[i, :, lanes].astype(F32) for part, i in group]
            block = jnp.concatenate(block, axis=0).astype(BF16)
            x_ref[first * rows : (first + sets) * rows, lanes] = block
    maps = jnp.concatenate([ref[...] for ref in map_refs], axis=0)
    adapters = maps.shape[0] // (2 * rank)
    low = dot_nt(x_ref[...], maps)
    lane = lax.broadcasted_iota(jnp.int32, low.shape, 1)
    low = jnp.where(lane // rank % adapters == local_ref[...], low, 0.0)
    total = 0.0
    for a in range(adapters):
        q = low[:, a * rank : (a + 1) * rank]
        v = low[:, (adapters + a) * rank : (adapters + a + 1) * rank]
        total = total + jnp.concatenate((q, v), axis=1)
    rows = dot(place_ref[...], total.astype(BF16))
    pack = HEAD // (2 * rank)
    step = rows.shape[0] // pack
    packed = jnp.concatenate([rows[i * step : (i + 1) * step] for i in range(pack)], axis=1)
    out_ref[...] = packed.astype(BF16)


def join_body(cores, index_ref, own_ref, *refs):
    total = jnp.where(index_ref[0] % cores == 0, own_ref[...].astype(F32), 0.0)
    for ref in refs[:-1]:
        total = total + ref[...].astype(F32)
    refs[-1][...] = total.astype(BF16)


def base_body(depth, x_ref, q_ref, k_ref, v_ref, oq_ref, okv_ref):
    oq_ref[...] = jnp.zeros_like(oq_ref)
    okv_ref[...] = jnp.zeros_like(okv_ref)
    columns = k_ref.shape[0]
    narrow = jnp.zeros((HEAD - 2 * columns, depth), BF16)

    @pl.loop(0, x_ref.shape[1] // depth)
    def _(i):
        at = pl.ds(pl.multiple_of(i * depth, depth), depth)
        x = x_ref[:, at]
        oq_ref[...] += dot(x, q_ref[at, :])
        both = (k_ref[:, at], v_ref[:, at])
        if 2 * columns < HEAD:
            both += (narrow,)
        okv_ref[...] += dot_nt(x, jnp.concatenate(both, axis=0))


def turned(values, cosine, sine):
    lane = lax.broadcasted_iota(jnp.int32, values.shape, 1)
    width = values.shape[1]
    ahead = pltpu.roll(values, width - 1, 1)
    behind = pltpu.roll(values, 1, 1)
    return values * cosine + jnp.where(lane % 2 == 0, ahead, behind) * sine


def ready_body(
    rank, lows, *refs
):
    low_refs = refs[:lows]
    (
        oq_ref, okv_ref, unplace_ref, slot_ref, uq_ref, uv_ref, cos_ref, sin_ref, kcos_ref, ksin_ref,
        send_ref, out_ref,
    ) = refs[lows:]
    packed = low_refs[0][...].astype(F32)
    for ref in low_refs[1:]:
        packed = packed + ref[...].astype(F32)
    pack = HEAD // (2 * rank)
    low = jnp.concatenate(
        [packed[:, i * 2 * rank : (i + 1) * 2 * rank] for i in range(pack)], axis=0
    )
    low = dot(unplace_ref[...], low.astype(BF16)).astype(BF16)
    wide = uq_ref.shape[0]
    lane = lax.broadcasted_iota(jnp.int32, (low.shape[0], wide), 1)
    here = lane // rank == slot_ref[...]
    row = lax.broadcasted_iota(jnp.int32, (2 * rank, wide), 0)
    column = lax.broadcasted_iota(jnp.int32, (2 * rank, wide), 1)
    spread_q = jnp.where(column % rank == row, 1.0, 0.0).astype(BF16)
    spread_v = jnp.where(column % rank + rank == row, 1.0, 0.0).astype(BF16)
    wide_q = jnp.where(here, dot(low, spread_q), 0.0).astype(BF16)
    wide_v = jnp.where(here, dot(low, spread_v), 0.0).astype(BF16)
    query = oq_ref[...] + dot(wide_q, uq_ref[...])
    fresh = turned(okv_ref[...], kcos_ref[...], ksin_ref[...])
    columns = uv_ref.shape[1]
    value = dot(wide_v, uv_ref[...])
    pieces = [jnp.zeros((value.shape[0], columns), F32), value]
    if 2 * columns < HEAD:
        pieces.append(jnp.zeros((value.shape[0], HEAD - 2 * columns), F32))
    fresh = fresh + jnp.concatenate(pieces, axis=1)
    cosine, sine = cos_ref[...], sin_ref[...]
    parts = []
    for h in range(query.shape[1] // HEAD):
        parts.append(turned(query[:, h * HEAD : (h + 1) * HEAD], cosine, sine))
    parts.append(fresh)
    stacked = jnp.concatenate(parts, axis=0).astype(BF16)
    out_ref[...] = dot(send_ref[...], stacked).astype(BF16).reshape(out_ref.shape)


def attend_body(
    own, columns, index_ref, len_ref, x_ref, order_ref, k_ref, v_ref, nk_ref, nv_ref, ctx_ref, s_ref
):
    n, span = x_ref.shape[0], k_ref.shape[1]
    group = HEADS // KV_HEADS
    local = HEADS // n
    rows = own * STEPS
    mine = group * STEPS
    x = x_ref[...]
    queries = dot(order_ref[...], x.reshape(n * x.shape[1], HEAD)).astype(BF16)
    wide = x.astype(F32)
    first = rows * local
    fresh = [wide[i, first : first + rows] for i in range(n)]
    each = n // KV_HEADS
    keys, values = [], []
    for g in range(KV_HEADS):
        pieces = fresh[g * each : (g + 1) * each]
        keys.append(jnp.concatenate([p[:, :columns] for p in pieces], axis=1))
        values.append(jnp.concatenate([p[:, columns : 2 * columns] for p in pieces], axis=1))
    new_keys = jnp.concatenate(keys, axis=1)
    new_values = jnp.concatenate(values, axis=1)
    for b in range(own):
        at = slice(b * STEPS, (b + 1) * STEPS)
        nk_ref[b] = new_keys[at].astype(BF16)
        nv_ref[b] = new_values[at].astype(BF16)
    pad = jnp.zeros((16 - rows, HEAD), F32)
    keys = [jnp.concatenate((k, pad), axis=0).astype(BF16) for k in keys]
    values = [jnp.concatenate((v, pad), axis=0).astype(BF16) for v in values]
    scale = HEAD ** (-0.5)
    contexts = []
    for b in range(own):
        q = queries[b * KV_HEADS * mine : (b + 1) * KV_HEADS * mine]
        cached, newer = [], []
        for g in range(KV_HEADS):
            qg = q[g * mine : (g + 1) * mine]
            cached.append(dot_nt(qg, k_ref[b, :, g * HEAD : (g + 1) * HEAD]))
            newer.append(dot_nt(qg, keys[g]))
        cached = jnp.concatenate(cached, axis=0) * scale
        newer = jnp.concatenate(newer, axis=0) * scale
        place = lax.broadcasted_iota(jnp.int32, cached.shape, 1)
        cached = jnp.where(place < len_ref[index_ref[0] * own + b], cached, -1e30)
        step = lax.broadcasted_iota(jnp.int32, newer.shape, 0) % STEPS
        at = lax.broadcasted_iota(jnp.int32, newer.shape, 1) - b * STEPS
        newer = jnp.where((at >= 0) & (at <= step), newer, -1e30)
        top = jnp.maximum(
            jnp.max(cached, axis=1, keepdims=True), jnp.max(newer, axis=1, keepdims=True)
        )
        cached = jnp.exp(cached - top)
        newer = jnp.exp(newer - top)
        total = jnp.sum(cached, axis=1, keepdims=True) + jnp.sum(newer, axis=1, keepdims=True)
        share = 1.0 / total
        cached = (cached * share).astype(BF16)
        newer = (newer * share).astype(BF16)
        for g in range(KV_HEADS):
            at_rows = slice(g * mine, (g + 1) * mine)
            part = dot(cached[at_rows], v_ref[b, :, g * HEAD : (g + 1) * HEAD])
            s_ref[(b * KV_HEADS + g) * mine : (b * KV_HEADS + g + 1) * mine] = part + dot(
                newer[at_rows], values[g]
            )
    step = local * STEPS
    half = KV_HEADS * mine
    for i in range(n):
        block = [s_ref[b * half + i * step : b * half + (i + 1) * step] for b in range(own)]
        ctx_ref[i] = jnp.concatenate(block, axis=0).astype(BF16)


def take_body(ctx_ref, take_ref, w_ref, a_ref, mine_ref, other_ref):
    rows = a_ref.shape[0]
    x = ctx_ref[...].reshape(-1, HEAD)
    taken = dot(take_ref[...], x).astype(BF16)
    for h in range(a_ref.shape[1] // HEAD):
        a_ref[:, h * HEAD : (h + 1) * HEAD] = taken[h * rows : (h + 1) * rows]
    out_body(0, a_ref, w_ref, mine_ref, other_ref)


def out_body(start, a_ref, w_ref, mine_ref, other_ref):
    half = mine_ref.shape[0]
    tile = 1024

    @pl.loop(0, mine_ref.shape[1] // tile)
    def _(i):
        at = pl.ds(pl.multiple_of(i * tile, tile), tile)
        product = dot(a_ref[...], w_ref[:, pl.ds(pl.multiple_of(start + i * tile, tile), tile)])
        mine_ref[:, at] = product[:half]
        other_ref[:, at] = product[half:]


def far_first_body(near, mine_ref, came_ref, *refs):
    total = mine_ref[...] + came_ref[...]
    rows = refs[0].shape[0] // near
    for f, ref in enumerate(refs):
        blocks = [(m * len(refs) + f) * rows for m in range(near)]
        value = jnp.concatenate([total[at : at + rows] for at in blocks], axis=0)
        ref[...] = value.astype(ref.dtype)


def near_body(mine_ref, came_ref, *refs):
    rows = refs[0].shape[0]
    total = mine_ref[...] + came_ref[...]
    refs[0][...] = total[:rows]
    for m, ref in enumerate(refs[1:], 1):
        ref[...] = total[m * rows : (m + 1) * rows].astype(BF16)


def far_body(came, *refs):
    total = refs[0][...]
    for ref in refs[1 : 1 + came]:
        total = total + ref[...].astype(F32)
    refs = refs[1 + came :]
    rows = refs[0].shape[0]
    refs[0][...] = total[:rows]
    for f, ref in enumerate(refs[1:], 1):
        ref[...] = total[f * rows : (f + 1) * rows].astype(BF16)


def last_body(longs, first_ref, second_ref, *refs):
    one_ref, two_ref = refs[-2:]
    totals = []
    for part in (refs[:longs], refs[longs:-2]):
        total = part[0][...]
        for ref in part[1:]:
            total = total + ref[...].astype(F32)
        totals.append(total)
    total = jnp.concatenate(totals, axis=1)
    own = one_ref.shape[0]
    one_ref[...] = (first_ref[...].astype(F32) + total[:own]).astype(BF16)
    two_ref[...] = (second_ref[...].astype(F32) + total[own:]).astype(BF16)


def shards(
    sizes,
    residual_first,
    residual_second,
    attention_norm_gain,
    query_matrix,
    key_matrix,
    value_matrix,
    output_matrix,
    query_down_weights,
    value_down_weights,
    query_up_weights,
    value_up_weights,
    rotated_key_cache,
    stored_value_cache,
    lengths,
    request_adapter,
    adapter_slot,
):
    far, near, cores = sizes
    n = far * near * cores
    index = lax.axis_index("serve")
    own, width = residual_first.shape
    adapters, _, rank = query_down_weights.shape
    query_cols = query_matrix.shape[1]
    key_cols = key_matrix.shape[1]
    local = query_cols // HEAD
    rows = own * STEPS
    all_rows = n * rows
    stored = query_up_weights.shape[0]

    def partner(f, m, c):
        pairs = []
        for z in range(far):
            for y in range(near):
                for k in range(cores):
                    to = (((z + f) % far) * near + (y + m) % near) * cores + (k + c) % cores
                    pairs.append(((z * near + y) * cores + k, to))
        return pairs

    def shift(value, f, m, c):
        return lax.ppermute(value, "serve", partner(f, m, c))

    frequency = whole_call(frequency_body, jax.ShapeDtypeStruct((1, HEAD), F32), (), cost=3.0)
    gain = attention_norm_gain.reshape(width // HEAD, HEAD)
    gain, frequency = lax.optimization_barrier((gain, frequency))
    normed = whole_call(
        norm_body,
        jax.ShapeDtypeStruct((rows, width), BF16),
        (residual_first, residual_second, gain),
        hbm=3,
        scratch=[
            pltpu.VMEM((own, width), BF16),
            pltpu.VMEM((own, width), BF16),
            pltpu.VMEM(gain.shape, BF16),
            pltpu.SemaphoreType.DMA((3,)),
        ],
        cost=1.0,
    )
    normed = normed[None]
    fars = [shift(normed, f, 0, 0) for f in range(1, far)]
    nears = [shift(normed, 0, m, 0) for m in range(1, near)]
    rest = jnp.concatenate(fars)
    groups = [jnp.concatenate([normed, *fars, *nears[:1]])]
    groups += [shift(rest, 0, m, 0) for m in range(1, near)]
    query_down = jnp.swapaxes(query_down_weights, 1, 2).reshape(adapters * rank, width)
    value_down = jnp.swapaxes(value_down_weights, 1, 2).reshape(adapters * rank, width)
    query_down, value_down, rest = lax.optimization_barrier((query_down, value_down, rest))

    rest, at = lax.optimization_barrier((rest, index[None]))
    sent = -(-(rows * local + rows) // 8) * 8
    narrow = jax.ShapeDtypeStruct((all_rows, 1), jnp.int32)
    table = jax.ShapeDtypeStruct((all_rows, HEAD), F32)
    square = jax.ShapeDtypeStruct((all_rows, all_rows), BF16)
    slot, near_slot, cosine, sine, key_cosine, key_sine, place, unplace, send, order, take = whole_call(
        functools.partial(prep_body, sizes, rank, own, key_cols, adapters),
        (
            narrow,
            narrow,
            table,
            table,
            table,
            table,
            square,
            square,
            jax.ShapeDtypeStruct((n * sent, all_rows * (local + 1)), BF16),
            jax.ShapeDtypeStruct((own * HEADS * STEPS, n * sent), BF16),
            jax.ShapeDtypeStruct((all_rows * local, n * rows * local), BF16),
        ),
        (at, lengths, request_adapter, adapter_slot, frequency),
        smem=1,
        hbm=3,
        scratch=[
            pltpu.SMEM(lengths.shape, jnp.int32),
            pltpu.SMEM(request_adapter.shape, jnp.int32),
            pltpu.SMEM(adapter_slot.shape, jnp.int32),
            pltpu.SemaphoreType.DMA((3,)),
        ],
        cost=4.0,
    )
    slot, groups[1] = lax.optimization_barrier((slot, groups[1]))

    groups += [shift(part, 0, 0, c) for c in range(1, cores) for part in groups[:near]]

    packed_rows = all_rows * 2 * rank // HEAD
    x, low = whole_call(
        functools.partial(low_body, rank, len(groups)),
        (
            jax.ShapeDtypeStruct((all_rows, width), BF16),
            jax.ShapeDtypeStruct((packed_rows, HEAD), BF16),
        ),
        (
            *groups,
            *[query_down, *[shift(query_down, 0, 0, c) for c in range(1, cores)]],
            *[value_down, *[shift(value_down, 0, 0, c) for c in range(1, cores)]],
            near_slot,
            place,
        ),
        cost=0.3,
    )
    def spread(value, f):
        pairs = []
        for z in range(far):
            for y in range(near):
                for k in range(cores):
                    if f or k % near:
                        to = ((z + f) % far * near + (y + k) % near) * cores + k
                        pairs.append(((z * near + y) * cores + k, to))
        return lax.ppermute(value, "serve", pairs)

    lows = [spread(low, f) for f in range(far)]
    base_q, base_kv = whole_call(
        functools.partial(base_body, 2048),
        (
            jax.ShapeDtypeStruct((all_rows, query_cols), F32),
            jax.ShapeDtypeStruct((all_rows, HEAD), F32),
        ),
        (x, query_matrix, key_matrix.T, value_matrix.T),
        cost=0.6,
    )
    lows[0], base_q = lax.optimization_barrier((lows[0], base_q))
    low = whole_call(
        functools.partial(join_body, cores),
        jax.ShapeDtypeStruct(low.shape, BF16),
        (index[None], low, *lows),
        smem=1,
        cost=0.1,
    )
    lows = [low] + [shift(low, 0, 0, c) for c in range(1, cores)]

    ready = whole_call(
        functools.partial(ready_body, rank, len(lows)),
        jax.ShapeDtypeStruct((n, sent, HEAD), BF16),
        (
            *lows,
            base_q,
            base_kv,
            unplace,
            slot,
            query_up_weights.reshape(stored * rank, query_cols),
            value_up_weights.reshape(stored * rank, key_cols),
            cosine,
            sine,
            key_cosine,
            key_sine,
            send,
        ),
        cost=0.9,
    )
    arrived = lax.all_to_all(ready, "serve", split_axis=0, concat_axis=0, tiled=True)

    fresh = jax.ShapeDtypeStruct((own, STEPS, KV_HEADS * HEAD), BF16)
    new_keys, new_values, context = whole_call(
        functools.partial(attend_body, own, key_cols),
        (fresh, fresh, jax.ShapeDtypeStruct((n, rows * local, HEAD), BF16)),
        (index[None], lengths, arrived, order, rotated_key_cache, stored_value_cache),
        smem=2,
        scratch=[pltpu.VMEM((own * HEADS * STEPS, HEAD), F32)],
        cost=1.0,
    )
    context = lax.all_to_all(context, "serve", split_axis=0, concat_axis=0, tiled=True)

    half = all_rows // cores
    cut = width * 5 // 8

    def kinds(count, columns):
        return (jax.ShapeDtypeStruct((count, columns), F32),) * 2

    taken, mine_long, other_long = whole_call(
        take_body,
        (jax.ShapeDtypeStruct((all_rows, query_cols), BF16),) + kinds(half, cut),
        (context, take, output_matrix),
        cost=0.4,
    )
    mine_short, other_short = whole_call(
        functools.partial(out_body, cut),
        kinds(half, width - cut),
        (taken, output_matrix),
        cost=0.3,
    )

    def kind(count, columns, dtype):
        return jax.ShapeDtypeStruct((count * rows, columns), dtype)

    keep, *others = whole_call(
        near_body,
        (kind(far, cut, F32),) + (kind(far, cut, BF16),) * (near - 1),
        (mine_long, shift(other_long, 0, 0, 1)),
        cost=0.1,
    )
    others = [shift(other, 0, m, 0) for m, other in enumerate(others, 1)]
    short, *sides = whole_call(
        functools.partial(far_first_body, near),
        (kind(near, width - cut, F32),) + (kind(near, width - cut, BF16),) * (far - 1),
        (mine_short, shift(other_short, 0, 0, 1)),
        cost=0.1,
    )
    sides = [shift(side, f, 0, 0) for f, side in enumerate(sides, 1)]
    keep, *others = whole_call(
        functools.partial(far_body, len(others)),
        (kind(1, cut, F32),) + (kind(1, cut, BF16),) * (far - 1),
        (keep, *others),
        cost=0.1,
    )
    others = [shift(other, f, 0, 0) for f, other in enumerate(others, 1)]
    short, *sides = whole_call(
        functools.partial(far_body, len(sides)),
        (kind(1, width - cut, F32),) + (kind(1, width - cut, BF16),) * (near - 1),
        (short, *sides),
        cost=0.1,
    )
    sides = [shift(side, 0, m, 0) for m, side in enumerate(sides, 1)]
    result = jax.ShapeDtypeStruct((own, width), BF16)
    out_one, out_two = whole_call(
        functools.partial(last_body, 1 + len(others)),
        (result, result),
        (residual_first, residual_second, keep, *others, short, *sides),
        cost=0.1,
    )
    return (out_one, out_two, new_keys, new_values)


def solution(mesh):
    n = mesh.shape["serve"]
    sizes = (n // 4, 2, 2)
    return jax.shard_map(
        functools.partial(shards, sizes),
        mesh=mesh,
        in_specs=(
            P(("replica", "serve"), None),
            P(("replica", "serve"), None),
            P(),
            P(None, "serve"),
            P(None, "serve"),
            P(None, "serve"),
            P("serve", None),
            P("serve", None, None),
            P("serve", None, None),
            P(None, None, "serve"),
            P(None, None, "serve"),
            P(("replica", "serve"), None, None),
            P(("replica", "serve"), None, None),
            P("replica"),
            P("replica"),
            P(),
        ),
        out_specs=(
            P(("replica", "serve"), None),
            P(("replica", "serve"), None),
            P(("replica", "serve"), None, None),
            P(("replica", "serve"), None, None),
        ),
        check_vma=False,
    )
```

```python
import functools
import math

import jax
import jax.numpy as jnp
from jax import lax
from jax.experimental import pallas as pl
from jax.experimental.pallas import tpu as pltpu
from jax.sharding import PartitionSpec as P

HEADS = 64
KV_HEADS = 8
HEAD = 128
STEPS = 2
LIMIT = 8 * 1024 * 1024
PEAK = 1.15e9
NT = (((1,), (1,)), ((), ()))
F32 = jnp.float32
BF16 = jnp.bfloat16


def dot(a, b):
    return jnp.dot(a, b, preferred_element_type=F32)


def dot_nt(a, b):
    return lax.dot_general(a, b, NT, preferred_element_type=F32)


def whole_call(body, out_shape, args, cost, smem=0, hbm=0, scratch=()):
    specs = [pl.BlockSpec(memory_space=pltpu.SMEM)] * smem
    specs += [pl.BlockSpec(memory_space=pltpu.HBM)] * hbm
    specs += [pl.BlockSpec(memory_space=pltpu.VMEM)] * (len(args) - smem - hbm)
    many = isinstance(out_shape, (tuple, list))
    vmem = pl.BlockSpec(memory_space=pltpu.VMEM)
    return pl.pallas_call(
        body,
        out_shape=out_shape,
        in_specs=specs,
        out_specs=tuple(vmem for _ in out_shape) if many else vmem,
        scratch_shapes=list(scratch),
        compiler_params=pltpu.CompilerParams(vmem_limit_bytes=LIMIT),
        cost_estimate=pl.CostEstimate(
            flops=int(cost * PEAK), bytes_accessed=0, transcendentals=0
        ),
    )(*args)


def scaled_frequency(pair_index):
    base = jnp.exp(pair_index.astype(F32) * (-2.0 * math.log(500000.0) / HEAD))
    wavelength = 2.0 * math.pi / base
    smooth = jnp.clip((8192.0 / wavelength - 1.0) / 3.0, 0.0, 1.0)
    return (1.0 - smooth) * base / 8.0 + smooth * base


def fetch(pairs, sems):
    copies = [
        pltpu.make_async_copy(source, target, sems.at[i])
        for i, (source, target) in enumerate(pairs)
    ]
    for copy in copies:
        copy.start()
    for copy in copies:
        copy.wait()


def norm_body(first_hbm, second_hbm, gain_hbm, out_ref, first_ref, second_ref, gain_ref, sems):
    fetch(((first_hbm, first_ref), (second_hbm, second_ref), (gain_hbm, gain_ref)), sems)
    gain = gain_ref[...].astype(F32)
    factors = []
    for ref in (first_ref, second_ref):
        values = ref[...].astype(F32)
        factors.append(lax.rsqrt(jnp.mean(values * values, axis=-1, keepdims=True) + 1e-05))
    factor = jnp.concatenate(factors, axis=0)
    for i in range(gain.shape[0]):
        at = slice(i * HEAD, (i + 1) * HEAD)
        values = jnp.concatenate((first_ref[:, at].astype(F32), second_ref[:, at].astype(F32)))
        out_ref[:, at] = (values * factor * gain[i : i + 1]).astype(BF16)


def frequency_body(out_ref):
    out_ref[...] = scaled_frequency(lax.broadcasted_iota(jnp.int32, out_ref.shape, 1) // 2)


def prep_body(
    sizes, rank, own, key_cols, adapters,
    index_ref, length_hbm, adapter_hbm, slot_hbm, frequency_ref,
    held_ref, local_ref, cos_ref, sin_ref, kcos_ref, ksin_ref, place_ref, unplace_ref, send_ref,
    order_ref, take_ref, length_ref, adapter_ref, slot_ref, sems,
):
    fetch(((length_hbm, length_ref), (adapter_hbm, adapter_ref), (slot_hbm, slot_ref)), sems)
    far, near, cores = sizes
    n = far * near * cores
    rows = own * STEPS
    all_rows = n * rows
    heads = HEADS // n
    sent = send_ref.shape[0] // n
    index = index_ref[0]
    core_at = index % cores
    near_at = index // cores % near
    far_at = index // (cores * near)

    def device_of(block, sign):
        c, m, f = block // (far * near), block // far % near, block % far
        f = (far_at + sign * f + far) % far
        m = (near_at + sign * m + near) % near
        c = (core_at + sign * c + cores) % cores
        return (f * near + m) * cores + c

    def iota(shape, axis):
        return lax.broadcasted_iota(jnp.int32, shape, axis)

    def split(row):
        return row // rows, row % rows // own, row % own

    block, step, mine = split(iota((all_rows, 1), 0))
    device = device_of(block, -1)
    request = device * own + mine
    length = jnp.zeros_like(request)
    adapter = jnp.zeros_like(request)
    for j in range(length_ref.shape[0]):
        length = jnp.where(request == j, length_ref[j], length)
        adapter = jnp.where(request == j, adapter_ref[j], adapter)
    slot = jnp.zeros_like(request)
    for j in range(slot_ref.shape[0]):
        slot = jnp.where(adapter == j, slot_ref[j], slot)
    held_ref[...] = slot
    local_ref[...] = slot - index * adapters
    position = (length + step).astype(F32)
    lane = iota((1, HEAD), 1)
    odd = jnp.where(lane % 2 == 0, -1.0, 1.0)
    angle = position * frequency_ref[...]
    cos_ref[...] = jnp.cos(angle)
    sin_ref[...] = jnp.sin(angle) * odd
    angle = position * scaled_frequency((index * key_cols + lane) % HEAD // 2)
    kcos_ref[...] = jnp.where(lane < key_cols, jnp.cos(angle), 1.0)
    ksin_ref[...] = jnp.where(lane < key_cols, jnp.sin(angle) * odd, 0.0)

    def hot(ref, row, column):
        ref[...] = jnp.where(row == column, 1.0, 0.0).astype(BF16)

    absolute = (device * STEPS + step) * own + mine
    hot(unplace_ref, absolute, iota((1, all_rows), 1))
    block, step, mine = split(iota((1, all_rows), 1))
    absolute = (device_of(block, -1) * STEPS + step) * own + mine
    hot(place_ref, iota((all_rows, 1), 0), absolute)

    column = iota((1, send_ref.shape[1]), 1)
    h = column // all_rows
    block, step, mine = split(column % all_rows)
    wanted = device_of(block, -1) * sent + jnp.where(
        h < heads, (mine * heads + h) * STEPS + step, rows * heads + mine * STEPS + step
    )
    hot(send_ref, iota((n * sent, 1), 0), wanted)

    row = iota((order_ref.shape[0], 1), 0)
    mine, head, step = row // (HEADS * STEPS), row // STEPS % HEADS, row % STEPS
    wanted = (head // heads) * sent + (mine * heads + head % heads) * STEPS + step
    hot(order_ref, wanted, iota((1, n * sent), 1))

    row = iota((take_ref.shape[0], 1), 0)
    h = row // all_rows
    block, step, mine = split(row % all_rows)
    wanted = device_of(block, 1) * rows * heads + (mine * heads + h) * STEPS + step
    hot(take_ref, wanted, iota((1, take_ref.shape[1]), 1))


def low_body(rank, groups, *refs):
    parts, (qd_ref, vd_ref, local_ref, place_ref, x_ref, out_ref) = refs[:groups], refs[groups:]
    rows = parts[0].shape[1]
    sets = max(1, 16 // rows)
    blocks = [(part, i) for part in parts for i in range(part.shape[0])]
    for first in range(0, len(blocks), sets):
        group = blocks[first : first + sets]
        for lane in range(0, x_ref.shape[1], 1024):
            lanes = slice(lane, lane + 1024)
            block = [part[i, :, lanes].astype(F32) for part, i in group]
            block = jnp.concatenate(block, axis=0).astype(BF16)
            x_ref[first * rows : (first + sets) * rows, lanes] = block
    adapters = qd_ref.shape[0] // rank
    maps = jnp.concatenate((qd_ref[...], vd_ref[...]), axis=0)
    low = dot_nt(x_ref[...], maps)
    lane = lax.broadcasted_iota(jnp.int32, low.shape, 1)
    low = jnp.where(lane // rank % adapters == local_ref[...], low, 0.0)
    total = 0.0
    for a in range(adapters):
        q = low[:, a * rank : (a + 1) * rank]
        v = low[:, (adapters + a) * rank : (adapters + a + 1) * rank]
        total = total + jnp.concatenate((q, v), axis=1)
    rows = dot(place_ref[...], total.astype(BF16))
    pack = HEAD // (2 * rank)
    step = rows.shape[0] // pack
    packed = jnp.concatenate([rows[i * step : (i + 1) * step] for i in range(pack)], axis=1)
    out_ref[...] = packed.astype(BF16)


def join_body(*refs):
    total = refs[0][...].astype(F32)
    for ref in refs[1:-1]:
        total = total + ref[...].astype(F32)
    refs[-1][...] = total.astype(BF16)


def base_body(depth, start, stop, x_ref, q_ref, k_ref, v_ref, oq_ref, okv_ref):
    oq_ref[...] = jnp.zeros_like(oq_ref)
    okv_ref[...] = jnp.zeros_like(okv_ref)
    columns = k_ref.shape[0]
    narrow = jnp.zeros((HEAD - 2 * columns, depth), BF16)

    @pl.loop(start // depth, stop // depth)
    def _(i):
        at = pl.ds(pl.multiple_of(i * depth, depth), depth)
        x = x_ref[:, at]
        oq_ref[...] += dot(x, q_ref[at, :])
        both = (k_ref[:, at], v_ref[:, at])
        if 2 * columns < HEAD:
            both += (narrow,)
        okv_ref[...] += dot_nt(x, jnp.concatenate(both, axis=0))


def turned(values, cosine, sine):
    lane = lax.broadcasted_iota(jnp.int32, values.shape, 1)
    width = values.shape[1]
    ahead = pltpu.roll(values, width - 1, 1)
    behind = pltpu.roll(values, 1, 1)
    return values * cosine + jnp.where(lane % 2 == 0, ahead, behind) * sine


def ready_body(
    rank, lows, *refs
):
    low_refs = refs[:lows]
    (
        oq_ref, okv_ref, oq2_ref, okv2_ref, unplace_ref, slot_ref, uq_ref, uv_ref, cos_ref, sin_ref, kcos_ref, ksin_ref,
        send_ref, out_ref,
    ) = refs[lows:]
    packed = low_refs[0][...].astype(F32)
    for ref in low_refs[1:]:
        packed = packed + ref[...].astype(F32)
    pack = HEAD // (2 * rank)
    low = jnp.concatenate(
        [packed[:, i * 2 * rank : (i + 1) * 2 * rank] for i in range(pack)], axis=0
    )
    low = dot(unplace_ref[...], low.astype(BF16)).astype(BF16)
    wide = uq_ref.shape[0]
    lane = lax.broadcasted_iota(jnp.int32, (low.shape[0], wide), 1)
    here = lane // rank == slot_ref[...]
    row = lax.broadcasted_iota(jnp.int32, (2 * rank, wide), 0)
    column = lax.broadcasted_iota(jnp.int32, (2 * rank, wide), 1)
    spread_q = jnp.where(column % rank == row, 1.0, 0.0).astype(BF16)
    spread_v = jnp.where(column % rank + rank == row, 1.0, 0.0).astype(BF16)
    wide_q = jnp.where(here, dot(low, spread_q), 0.0).astype(BF16)
    wide_v = jnp.where(here, dot(low, spread_v), 0.0).astype(BF16)
    query = oq_ref[...] + oq2_ref[...] + dot(wide_q, uq_ref[...])
    fresh = turned(okv_ref[...] + okv2_ref[...], kcos_ref[...], ksin_ref[...])
    columns = uv_ref.shape[1]
    value = dot(wide_v, uv_ref[...])
    pieces = [jnp.zeros((value.shape[0], columns), F32), value]
    if 2 * columns < HEAD:
        pieces.append(jnp.zeros((value.shape[0], HEAD - 2 * columns), F32))
    fresh = fresh + jnp.concatenate(pieces, axis=1)
    cosine, sine = cos_ref[...], sin_ref[...]
    parts = []
    for h in range(query.shape[1] // HEAD):
        parts.append(turned(query[:, h * HEAD : (h + 1) * HEAD], cosine, sine))
    parts.append(fresh)
    stacked = jnp.concatenate(parts, axis=0).astype(BF16)
    out_ref[...] = dot(send_ref[...], stacked).astype(BF16).reshape(out_ref.shape)


def attend_body(
    own, columns, index_ref, len_ref, x_ref, order_ref, k_ref, v_ref, nk_ref, nv_ref, ctx_ref, s_ref
):
    n, span = x_ref.shape[0], k_ref.shape[1]
    group = HEADS // KV_HEADS
    local = HEADS // n
    rows = own * STEPS
    mine = group * STEPS
    x = x_ref[...]
    queries = dot(order_ref[...], x.reshape(n * x.shape[1], HEAD)).astype(BF16)
    wide = x.astype(F32)
    first = rows * local
    fresh = [wide[i, first : first + rows] for i in range(n)]
    each = n // KV_HEADS
    keys, values = [], []
    for g in range(KV_HEADS):
        pieces = fresh[g * each : (g + 1) * each]
        keys.append(jnp.concatenate([p[:, :columns] for p in pieces], axis=1))
        values.append(jnp.concatenate([p[:, columns : 2 * columns] for p in pieces], axis=1))
    new_keys = jnp.concatenate(keys, axis=1)
    new_values = jnp.concatenate(values, axis=1)
    for b in range(own):
        at = slice(b * STEPS, (b + 1) * STEPS)
        nk_ref[b] = new_keys[at].astype(BF16)
        nv_ref[b] = new_values[at].astype(BF16)
    pad = jnp.zeros((16 - rows, HEAD), F32)
    keys = [jnp.concatenate((k, pad), axis=0).astype(BF16) for k in keys]
    values = [jnp.concatenate((v, pad), axis=0).astype(BF16) for v in values]
    scale = HEAD ** (-0.5)
    contexts = []
    for b in range(own):
        q = queries[b * KV_HEADS * mine : (b + 1) * KV_HEADS * mine]
        cached, newer = [], []
        for g in range(0, KV_HEADS, 2):
            one, two = q[g * mine : (g + 1) * mine], q[(g + 1) * mine : (g + 2) * mine]
            none = jnp.zeros_like(one)
            pair = jnp.concatenate(
                (jnp.concatenate((one, none), axis=1), jnp.concatenate((none, two), axis=1)),
                axis=0,
            )
            cached.append(dot_nt(k_ref[b, :, g * HEAD : (g + 2) * HEAD], pair))
            newer.append(dot_nt(jnp.concatenate(keys[g : g + 2], axis=1), pair))
        cached = jnp.concatenate(cached, axis=1) * scale
        newer = jnp.concatenate(newer, axis=1) * scale
        place = lax.broadcasted_iota(jnp.int32, cached.shape, 0)
        cached = jnp.where(place < len_ref[index_ref[0] * own + b], cached, -1e30)
        step = lax.broadcasted_iota(jnp.int32, newer.shape, 1) % STEPS
        at = lax.broadcasted_iota(jnp.int32, newer.shape, 0) - b * STEPS
        newer = jnp.where((at >= 0) & (at <= step), newer, -1e30)
        top = jnp.maximum(
            jnp.max(cached, axis=0, keepdims=True), jnp.max(newer, axis=0, keepdims=True)
        )
        cached = jnp.exp(cached - top)
        newer = jnp.exp(newer - top)
        total = jnp.sum(cached, axis=0, keepdims=True) + jnp.sum(newer, axis=0, keepdims=True)
        share = 1.0 / total
        newer = jnp.concatenate(
            (newer, jnp.zeros((HEAD - newer.shape[0], newer.shape[1]), F32)), axis=0
        )
        cached = (cached * share).T.astype(BF16)
        newer = (newer * share).T.astype(BF16)[:, : 16]
        for g in range(0, KV_HEADS, 2):
            at_rows = slice(g * mine, (g + 2) * mine)
            part = dot(cached[at_rows], v_ref[b, :, g * HEAD : (g + 2) * HEAD])
            part = part + dot(newer[at_rows], jnp.concatenate(values[g : g + 2], axis=1))
            at = (b * KV_HEADS + g) * mine
            s_ref[at : at + mine] = part[:mine, :HEAD]
            s_ref[at + mine : at + 2 * mine] = part[mine:, HEAD:]
    step = local * STEPS
    half = KV_HEADS * mine
    for i in range(n):
        block = [s_ref[b * half + i * step : b * half + (i + 1) * step] for b in range(own)]
        ctx_ref[i] = jnp.concatenate(block, axis=0).astype(BF16)


def take_body(ctx_ref, take_ref, w_ref, a_ref, mine_ref, other_ref):
    rows = a_ref.shape[0]
    x = ctx_ref[...].reshape(-1, HEAD)
    taken = dot(take_ref[...], x).astype(BF16)
    for h in range(a_ref.shape[1] // HEAD):
        a_ref[:, h * HEAD : (h + 1) * HEAD] = taken[h * rows : (h + 1) * rows]
    out_body(0, a_ref, w_ref, mine_ref, other_ref)


def out_body(start, a_ref, w_ref, mine_ref, other_ref):
    half = mine_ref.shape[0]
    tile = 1024

    @pl.loop(0, mine_ref.shape[1] // tile)
    def _(i):
        at = pl.ds(pl.multiple_of(i * tile, tile), tile)
        product = dot(a_ref[...], w_ref[:, pl.ds(pl.multiple_of(start + i * tile, tile), tile)])
        mine_ref[:, at] = product[:half]
        other_ref[:, at] = product[half:]


def far_first_body(near, mine_ref, came_ref, *refs):
    total = mine_ref[...] + came_ref[...]
    rows = refs[0].shape[0] // near
    for f, ref in enumerate(refs):
        blocks = [(m * len(refs) + f) * rows for m in range(near)]
        value = jnp.concatenate([total[at : at + rows] for at in blocks], axis=0)
        ref[...] = value.astype(ref.dtype)


def near_body(mine_ref, came_ref, *refs):
    rows = refs[0].shape[0]
    total = mine_ref[...] + came_ref[...]
    refs[0][...] = total[:rows]
    for m, ref in enumerate(refs[1:], 1):
        ref[...] = total[m * rows : (m + 1) * rows].astype(BF16)


def far_body(came, *refs):
    total = refs[0][...]
    for ref in refs[1 : 1 + came]:
        total = total + ref[...].astype(F32)
    refs = refs[1 + came :]
    rows = refs[0].shape[0]
    refs[0][...] = total[:rows]
    for f, ref in enumerate(refs[1:], 1):
        ref[...] = total[f * rows : (f + 1) * rows].astype(BF16)


def last_body(longs, first_ref, second_ref, *refs):
    one_ref, two_ref = refs[-2:]
    totals = []
    for part in (refs[:longs], refs[longs:-2]):
        total = part[0][...]
        for ref in part[1:]:
            total = total + ref[...].astype(F32)
        totals.append(total)
    total = jnp.concatenate(totals, axis=1)
    own = one_ref.shape[0]
    one_ref[...] = (first_ref[...].astype(F32) + total[:own]).astype(BF16)
    two_ref[...] = (second_ref[...].astype(F32) + total[own:]).astype(BF16)


def shards(
    sizes,
    residual_first,
    residual_second,
    attention_norm_gain,
    query_matrix,
    key_matrix,
    value_matrix,
    output_matrix,
    query_down_weights,
    value_down_weights,
    query_up_weights,
    value_up_weights,
    rotated_key_cache,
    stored_value_cache,
    lengths,
    request_adapter,
    adapter_slot,
):
    far, near, cores = sizes
    n = far * near * cores
    index = lax.axis_index("serve")
    own, width = residual_first.shape
    adapters, _, rank = query_down_weights.shape
    query_cols = query_matrix.shape[1]
    key_cols = key_matrix.shape[1]
    local = query_cols // HEAD
    rows = own * STEPS
    all_rows = n * rows
    stored = query_up_weights.shape[0]

    def partner(f, m, c):
        pairs = []
        for z in range(far):
            for y in range(near):
                for k in range(cores):
                    to = (((z + f) % far) * near + (y + m) % near) * cores + (k + c) % cores
                    pairs.append(((z * near + y) * cores + k, to))
        return pairs

    def shift(value, f, m, c):
        return lax.ppermute(value, "serve", partner(f, m, c))

    frequency = whole_call(frequency_body, jax.ShapeDtypeStruct((1, HEAD), F32), (), cost=3.0)
    gain = attention_norm_gain.reshape(width // HEAD, HEAD)
    gain, frequency = lax.optimization_barrier((gain, frequency))
    normed = whole_call(
        norm_body,
        jax.ShapeDtypeStruct((rows, width), BF16),
        (residual_first, residual_second, gain),
        hbm=3,
        scratch=[
            pltpu.VMEM((own, width), BF16),
            pltpu.VMEM((own, width), BF16),
            pltpu.VMEM(gain.shape, BF16),
            pltpu.SemaphoreType.DMA((3,)),
        ],
        cost=1.0,
    )
    normed = normed[None]
    fars = [shift(normed, f, 0, 0) for f in range(1, far)]
    nears = [shift(normed, 0, m, 0) for m in range(1, near)]
    rest = jnp.concatenate(fars)
    groups = [jnp.concatenate([normed, *fars, *nears[:1]])]
    groups += [shift(rest, 0, m, 0) for m in range(1, near)]

    rest, at = lax.optimization_barrier((rest, index[None]))
    sent = -(-(rows * local + rows) // 8) * 8
    narrow = jax.ShapeDtypeStruct((all_rows, 1), jnp.int32)
    table = jax.ShapeDtypeStruct((all_rows, HEAD), F32)
    square = jax.ShapeDtypeStruct((all_rows, all_rows), BF16)
    slot, near_slot, cosine, sine, key_cosine, key_sine, place, unplace, send, order, take = whole_call(
        functools.partial(prep_body, sizes, rank, own, key_cols, adapters),
        (
            narrow,
            narrow,
            table,
            table,
            table,
            table,
            square,
            square,
            jax.ShapeDtypeStruct((n * sent, all_rows * (local + 1)), BF16),
            jax.ShapeDtypeStruct((own * HEADS * STEPS, n * sent), BF16),
            jax.ShapeDtypeStruct((all_rows * local, n * rows * local), BF16),
        ),
        (at, lengths, request_adapter, adapter_slot, frequency),
        smem=1,
        hbm=3,
        scratch=[
            pltpu.SMEM(lengths.shape, jnp.int32),
            pltpu.SMEM(request_adapter.shape, jnp.int32),
            pltpu.SMEM(adapter_slot.shape, jnp.int32),
            pltpu.SemaphoreType.DMA((3,)),
        ],
        cost=4.0,
    )
    slot, groups[1] = lax.optimization_barrier((slot, groups[1]))

    groups += [shift(part, 0, 0, c) for c in range(1, cores) for part in groups[:near]]

    query_down = jnp.swapaxes(query_down_weights, 1, 2).reshape(adapters * rank, width)
    value_down = jnp.swapaxes(value_down_weights, 1, 2).reshape(adapters * rank, width)
    packed_rows = all_rows * 2 * rank // HEAD
    x, low = whole_call(
        functools.partial(low_body, rank, len(groups)),
        (
            jax.ShapeDtypeStruct((all_rows, width), BF16),
            jax.ShapeDtypeStruct((packed_rows, HEAD), BF16),
        ),
        (*groups, query_down, value_down, near_slot, place),
        cost=0.3,
    )
    def base(start, stop):
        return whole_call(
            functools.partial(base_body, 2048, start, stop),
            (
                jax.ShapeDtypeStruct((all_rows, query_cols), F32),
                jax.ShapeDtypeStruct((all_rows, HEAD), F32),
            ),
            (x, query_matrix, key_matrix.T, value_matrix.T),
            cost=0.3,
        )

    lows = [shift(low, 0, m, c) for m in range(near) for c in range(cores) if m + c]
    base_q, base_kv = base(0, width // 2)
    low = whole_call(join_body, jax.ShapeDtypeStruct(low.shape, BF16), (low, *lows), cost=0.1)
    low, base_q = lax.optimization_barrier((low, base_q))
    lows = [low] + [shift(low, f, 0, 0) for f in range(1, far)]
    bases = (base_q, base_kv, *base(width // 2, width))

    ready = whole_call(
        functools.partial(ready_body, rank, len(lows)),
        jax.ShapeDtypeStruct((n, sent, HEAD), BF16),
        (
            *lows,
            *bases,
            unplace,
            slot,
            query_up_weights.reshape(stored * rank, query_cols),
            value_up_weights.reshape(stored * rank, key_cols),
            cosine,
            sine,
            key_cosine,
            key_sine,
            send,
        ),
        cost=0.9,
    )
    arrived = lax.all_to_all(ready, "serve", split_axis=0, concat_axis=0, tiled=True)

    fresh = jax.ShapeDtypeStruct((own, STEPS, KV_HEADS * HEAD), BF16)
    new_keys, new_values, context = whole_call(
        functools.partial(attend_body, own, key_cols),
        (fresh, fresh, jax.ShapeDtypeStruct((n, rows * local, HEAD), BF16)),
        (index[None], lengths, arrived, order, rotated_key_cache, stored_value_cache),
        smem=2,
        scratch=[pltpu.VMEM((own * HEADS * STEPS, HEAD), F32)],
        cost=1.0,
    )
    context = lax.all_to_all(context, "serve", split_axis=0, concat_axis=0, tiled=True)

    half = all_rows // cores
    cut = width * 5 // 8

    def kinds(count, columns):
        return (jax.ShapeDtypeStruct((count, columns), F32),) * 2

    taken, mine_long, other_long = whole_call(
        take_body,
        (jax.ShapeDtypeStruct((all_rows, query_cols), BF16),) + kinds(half, cut),
        (context, take, output_matrix),
        cost=0.4,
    )
    mine_short, other_short = whole_call(
        functools.partial(out_body, cut),
        kinds(half, width - cut),
        (taken, output_matrix),
        cost=0.3,
    )

    def kind(count, columns, dtype):
        return jax.ShapeDtypeStruct((count * rows, columns), dtype)

    keep, *others = whole_call(
        near_body,
        (kind(far, cut, F32),) + (kind(far, cut, BF16),) * (near - 1),
        (mine_long, shift(other_long, 0, 0, 1)),
        cost=0.1,
    )
    others = [shift(other, 0, m, 0) for m, other in enumerate(others, 1)]
    short, *sides = whole_call(
        functools.partial(far_first_body, near),
        (kind(near, width - cut, F32),) + (kind(near, width - cut, BF16),) * (far - 1),
        (mine_short, shift(other_short, 0, 0, 1)),
        cost=0.1,
    )
    sides = [shift(side, f, 0, 0) for f, side in enumerate(sides, 1)]
    keep, *others = whole_call(
        functools.partial(far_body, len(others)),
        (kind(1, cut, F32),) + (kind(1, cut, BF16),) * (far - 1),
        (keep, *others),
        cost=0.1,
    )
    others = [shift(other, f, 0, 0) for f, other in enumerate(others, 1)]
    short, *sides = whole_call(
        functools.partial(far_body, len(sides)),
        (kind(1, width - cut, F32),) + (kind(1, width - cut, BF16),) * (near - 1),
        (short, *sides),
        cost=0.1,
    )
    sides = [shift(side, 0, m, 0) for m, side in enumerate(sides, 1)]
    result = jax.ShapeDtypeStruct((own, width), BF16)
    out_one, out_two = whole_call(
        functools.partial(last_body, 1 + len(others)),
        (result, result),
        (residual_first, residual_second, keep, *others, short, *sides),
        cost=0.1,
    )
    return (out_one, out_two, new_keys, new_values)


def solution(mesh):
    n = mesh.shape["serve"]
    sizes = (n // 4, 2, 2)
    return jax.shard_map(
        functools.partial(shards, sizes),
        mesh=mesh,
        in_specs=(
            P(("replica", "serve"), None),
            P(("replica", "serve"), None),
            P(),
            P(None, "serve"),
            P(None, "serve"),
            P(None, "serve"),
            P("serve", None),
            P("serve", None, None),
            P("serve", None, None),
            P(None, None, "serve"),
            P(None, None, "serve"),
            P(("replica", "serve"), None, None),
            P(("replica", "serve"), None, None),
            P("replica"),
            P("replica"),
            P(),
        ),
        out_specs=(
            P(("replica", "serve"), None),
            P(("replica", "serve"), None),
            P(("replica", "serve"), None, None),
            P(("replica", "serve"), None, None),
        ),
        check_vma=False,
    )
```

```python
import functools
import math

import jax
import jax.numpy as jnp
from jax import lax
from jax.experimental import pallas as pl
from jax.experimental.pallas import tpu as pltpu
from jax.sharding import PartitionSpec as P

HEADS = 64
KV_HEADS = 8
HEAD = 128
STEPS = 2
LIMIT = 8 * 1024 * 1024
PEAK = 1.15e9
NT = (((1,), (1,)), ((), ()))
F32 = jnp.float32
BF16 = jnp.bfloat16


def dot(a, b):
    return jnp.dot(a, b, preferred_element_type=F32)


def dot_nt(a, b):
    return lax.dot_general(a, b, NT, preferred_element_type=F32)


def whole_call(body, out_shape, args, cost, smem=0, hbm=0, scratch=()):
    specs = [pl.BlockSpec(memory_space=pltpu.SMEM)] * smem
    specs += [pl.BlockSpec(memory_space=pltpu.HBM)] * hbm
    specs += [pl.BlockSpec(memory_space=pltpu.VMEM)] * (len(args) - smem - hbm)
    many = isinstance(out_shape, (tuple, list))
    vmem = pl.BlockSpec(memory_space=pltpu.VMEM)
    return pl.pallas_call(
        body,
        out_shape=out_shape,
        in_specs=specs,
        out_specs=tuple(vmem for _ in out_shape) if many else vmem,
        scratch_shapes=list(scratch),
        compiler_params=pltpu.CompilerParams(vmem_limit_bytes=LIMIT),
        cost_estimate=pl.CostEstimate(
            flops=int(cost * PEAK), bytes_accessed=0, transcendentals=0
        ),
    )(*args)


def scaled_frequency(pair_index):
    base = jnp.exp(pair_index.astype(F32) * (-2.0 * math.log(500000.0) / HEAD))
    wavelength = 2.0 * math.pi / base
    smooth = jnp.clip((8192.0 / wavelength - 1.0) / 3.0, 0.0, 1.0)
    return (1.0 - smooth) * base / 8.0 + smooth * base


def fetch(pairs, sems):
    copies = [
        pltpu.make_async_copy(source, target, sems.at[i])
        for i, (source, target) in enumerate(pairs)
    ]
    for copy in copies:
        copy.start()
    for copy in copies:
        copy.wait()


def norm_body(first_hbm, second_hbm, gain_hbm, out_ref, first_ref, second_ref, gain_ref, sems):
    fetch(((first_hbm, first_ref), (second_hbm, second_ref), (gain_hbm, gain_ref)), sems)
    gain = gain_ref[...].astype(F32)
    factors = []
    for ref in (first_ref, second_ref):
        values = ref[...].astype(F32)
        factors.append(lax.rsqrt(jnp.mean(values * values, axis=-1, keepdims=True) + 1e-05))
    factor = jnp.concatenate(factors, axis=0)
    for i in range(gain.shape[0]):
        at = slice(i * HEAD, (i + 1) * HEAD)
        values = jnp.concatenate((first_ref[:, at].astype(F32), second_ref[:, at].astype(F32)))
        out_ref[:, at] = (values * factor * gain[i : i + 1]).astype(BF16)


def frequency_body(out_ref):
    out_ref[...] = scaled_frequency(lax.broadcasted_iota(jnp.int32, out_ref.shape, 1) // 2)


def prep_body(
    sizes, rank, own, key_cols, adapters,
    index_ref, length_hbm, adapter_hbm, slot_hbm, frequency_ref,
    held_ref, local_ref, cos_ref, sin_ref, kcos_ref, ksin_ref, place_ref, unplace_ref, send_ref,
    order_ref, take_ref, length_ref, adapter_ref, slot_ref, sems,
):
    fetch(((length_hbm, length_ref), (adapter_hbm, adapter_ref), (slot_hbm, slot_ref)), sems)
    far, near, cores = sizes
    n = far * near * cores
    rows = own * STEPS
    all_rows = n * rows
    heads = HEADS // n
    sent = send_ref.shape[0] // n
    index = index_ref[0]
    core_at = index % cores
    near_at = index // cores % near
    far_at = index // (cores * near)

    def device_of(block, sign):
        c, m, f = block // (far * near), block // far % near, block % far
        f = (far_at + sign * f + far) % far
        m = (near_at + sign * m + near) % near
        c = (core_at + sign * c + cores) % cores
        return (f * near + m) * cores + c

    def iota(shape, axis):
        return lax.broadcasted_iota(jnp.int32, shape, axis)

    def split(row):
        return row // rows, row % rows // own, row % own

    block, step, mine = split(iota((all_rows, 1), 0))
    device = device_of(block, -1)
    request = device * own + mine
    length = jnp.zeros_like(request)
    adapter = jnp.zeros_like(request)
    for j in range(length_ref.shape[0]):
        length = jnp.where(request == j, length_ref[j], length)
        adapter = jnp.where(request == j, adapter_ref[j], adapter)
    slot = jnp.zeros_like(request)
    for j in range(slot_ref.shape[0]):
        slot = jnp.where(adapter == j, slot_ref[j], slot)
    held_ref[...] = slot
    local_ref[...] = slot - index * adapters
    position = (length + step).astype(F32)
    lane = iota((1, HEAD), 1)
    odd = jnp.where(lane % 2 == 0, -1.0, 1.0)
    angle = position * frequency_ref[...]
    cos_ref[...] = jnp.cos(angle)
    sin_ref[...] = jnp.sin(angle) * odd
    angle = position * scaled_frequency((index * key_cols + lane) % HEAD // 2)
    kcos_ref[...] = jnp.where(lane < key_cols, jnp.cos(angle), 1.0)
    ksin_ref[...] = jnp.where(lane < key_cols, jnp.sin(angle) * odd, 0.0)

    def hot(ref, row, column):
        ref[...] = jnp.where(row == column, 1.0, 0.0).astype(BF16)

    absolute = (device * STEPS + step) * own + mine
    hot(unplace_ref, absolute, iota((1, all_rows), 1))
    block, step, mine = split(iota((1, all_rows), 1))
    absolute = (device_of(block, -1) * STEPS + step) * own + mine
    hot(place_ref, iota((all_rows, 1), 0), absolute)

    column = iota((1, send_ref.shape[1]), 1)
    h = column // all_rows
    block, step, mine = split(column % all_rows)
    wanted = device_of(block, -1) * sent + jnp.where(
        h < heads, (mine * heads + h) * STEPS + step, rows * heads + mine * STEPS + step
    )
    hot(send_ref, iota((n * sent, 1), 0), wanted)

    row = iota((order_ref.shape[0], 1), 0)
    mine, head, step = row // (HEADS * STEPS), row // STEPS % HEADS, row % STEPS
    wanted = (head // heads) * sent + (mine * heads + head % heads) * STEPS + step
    hot(order_ref, wanted, iota((1, n * sent), 1))

    row = iota((take_ref.shape[0], 1), 0)
    h = row // all_rows
    block, step, mine = split(row % all_rows)
    wanted = device_of(block, 1) * rows * heads + (mine * heads + h) * STEPS + step
    hot(take_ref, wanted, iota((1, take_ref.shape[1]), 1))


def low_body(rank, groups, *refs):
    parts, (qd_ref, vd_ref, local_ref, place_ref, x_ref, out_ref) = refs[:groups], refs[groups:]
    rows = parts[0].shape[1]
    sets = max(1, 16 // rows)
    blocks = [(part, i) for part in parts for i in range(part.shape[0])]
    for first in range(0, len(blocks), sets):
        group = blocks[first : first + sets]
        for lane in range(0, x_ref.shape[1], 1024):
            lanes = slice(lane, lane + 1024)
            block = [part[i, :, lanes].astype(F32) for part, i in group]
            block = jnp.concatenate(block, axis=0).astype(BF16)
            x_ref[first * rows : (first + sets) * rows, lanes] = block
    adapters = qd_ref.shape[0] // rank
    maps = jnp.concatenate((qd_ref[...], vd_ref[...]), axis=0)
    low = dot_nt(x_ref[...], maps)
    lane = lax.broadcasted_iota(jnp.int32, low.shape, 1)
    low = jnp.where(lane // rank % adapters == local_ref[...], low, 0.0)
    total = 0.0
    for a in range(adapters):
        q = low[:, a * rank : (a + 1) * rank]
        v = low[:, (adapters + a) * rank : (adapters + a + 1) * rank]
        total = total + jnp.concatenate((q, v), axis=1)
    rows = dot(place_ref[...], total.astype(BF16))
    pack = HEAD // (2 * rank)
    step = rows.shape[0] // pack
    packed = jnp.concatenate([rows[i * step : (i + 1) * step] for i in range(pack)], axis=1)
    out_ref[...] = packed.astype(BF16)


def join_body(*refs):
    total = refs[0][...].astype(F32)
    for ref in refs[1:-1]:
        total = total + ref[...].astype(F32)
    refs[-1][...] = total.astype(BF16)


def base_body(depth, start, stop, x_ref, q_ref, k_ref, v_ref, oq_ref, okv_ref):
    oq_ref[...] = jnp.zeros_like(oq_ref)
    okv_ref[...] = jnp.zeros_like(okv_ref)
    columns = k_ref.shape[0]
    narrow = jnp.zeros((HEAD - 2 * columns, depth), BF16)

    @pl.loop(start // depth, stop // depth)
    def _(i):
        at = pl.ds(pl.multiple_of(i * depth, depth), depth)
        x = x_ref[:, at]
        oq_ref[...] += dot(x, q_ref[at, :])
        both = (k_ref[:, at], v_ref[:, at])
        if 2 * columns < HEAD:
            both += (narrow,)
        okv_ref[...] += dot_nt(x, jnp.concatenate(both, axis=0))


def turned(values, cosine, sine):
    lane = lax.broadcasted_iota(jnp.int32, values.shape, 1)
    width = values.shape[1]
    ahead = pltpu.roll(values, width - 1, 1)
    behind = pltpu.roll(values, 1, 1)
    return values * cosine + jnp.where(lane % 2 == 0, ahead, behind) * sine


def ready_body(
    rank, lows, *refs
):
    low_refs = refs[:lows]
    (
        oq_ref, okv_ref, oq2_ref, okv2_ref, unplace_ref, slot_ref, uq_ref, uv_ref, cos_ref, sin_ref, kcos_ref, ksin_ref,
        send_ref, out_ref,
    ) = refs[lows:]
    packed = low_refs[0][...].astype(F32)
    for ref in low_refs[1:]:
        packed = packed + ref[...].astype(F32)
    pack = HEAD // (2 * rank)
    low = jnp.concatenate(
        [packed[:, i * 2 * rank : (i + 1) * 2 * rank] for i in range(pack)], axis=0
    )
    low = dot(unplace_ref[...], low.astype(BF16)).astype(BF16)
    wide = uq_ref.shape[0]
    lane = lax.broadcasted_iota(jnp.int32, (low.shape[0], wide), 1)
    here = lane // rank == slot_ref[...]
    row = lax.broadcasted_iota(jnp.int32, (2 * rank, wide), 0)
    column = lax.broadcasted_iota(jnp.int32, (2 * rank, wide), 1)
    spread_q = jnp.where(column % rank == row, 1.0, 0.0).astype(BF16)
    spread_v = jnp.where(column % rank + rank == row, 1.0, 0.0).astype(BF16)
    wide_q = jnp.where(here, dot(low, spread_q), 0.0).astype(BF16)
    wide_v = jnp.where(here, dot(low, spread_v), 0.0).astype(BF16)
    query = oq_ref[...] + oq2_ref[...] + dot(wide_q, uq_ref[...])
    fresh = turned(okv_ref[...] + okv2_ref[...], kcos_ref[...], ksin_ref[...])
    columns = uv_ref.shape[1]
    value = dot(wide_v, uv_ref[...])
    pieces = [jnp.zeros((value.shape[0], columns), F32), value]
    if 2 * columns < HEAD:
        pieces.append(jnp.zeros((value.shape[0], HEAD - 2 * columns), F32))
    fresh = fresh + jnp.concatenate(pieces, axis=1)
    cosine, sine = cos_ref[...], sin_ref[...]
    parts = []
    for h in range(query.shape[1] // HEAD):
        parts.append(turned(query[:, h * HEAD : (h + 1) * HEAD], cosine, sine))
    parts.append(fresh)
    stacked = jnp.concatenate(parts, axis=0).astype(BF16)
    out_ref[...] = dot(send_ref[...], stacked).astype(BF16).reshape(out_ref.shape)


def attend_body(
    own, columns, index_ref, len_ref, x_ref, order_ref, k_ref, v_ref, nk_ref, nv_ref, ctx_ref, s_ref
):
    n, span = x_ref.shape[0], k_ref.shape[1]
    group = HEADS // KV_HEADS
    local = HEADS // n
    rows = own * STEPS
    mine = group * STEPS
    x = x_ref[...]
    queries = dot(order_ref[...], x.reshape(n * x.shape[1], HEAD)).astype(BF16)
    wide = x.astype(F32)
    first = rows * local
    fresh = [wide[i, first : first + rows] for i in range(n)]
    each = n // KV_HEADS
    keys, values = [], []
    for g in range(KV_HEADS):
        pieces = fresh[g * each : (g + 1) * each]
        keys.append(jnp.concatenate([p[:, :columns] for p in pieces], axis=1))
        values.append(jnp.concatenate([p[:, columns : 2 * columns] for p in pieces], axis=1))
    new_keys = jnp.concatenate(keys, axis=1)
    new_values = jnp.concatenate(values, axis=1)
    for b in range(own):
        at = slice(b * STEPS, (b + 1) * STEPS)
        nk_ref[b] = new_keys[at].astype(BF16)
        nv_ref[b] = new_values[at].astype(BF16)
    pad = jnp.zeros((16 - rows, HEAD), F32)
    keys = [jnp.concatenate((k, pad), axis=0).astype(BF16) for k in keys]
    values = [jnp.concatenate((v, pad), axis=0).astype(BF16) for v in values]
    scale = HEAD ** (-0.5)
    contexts = []
    for b in range(own):
        q = queries[b * KV_HEADS * mine : (b + 1) * KV_HEADS * mine]
        cached, newer = [], []
        for g in range(KV_HEADS):
            qg = q[g * mine : (g + 1) * mine]
            cached.append(dot_nt(qg, k_ref[b, :, g * HEAD : (g + 1) * HEAD]))
            newer.append(dot_nt(qg, keys[g]))
        cached = jnp.concatenate(cached, axis=0) * scale
        newer = jnp.concatenate(newer, axis=0) * scale
        place = lax.broadcasted_iota(jnp.int32, cached.shape, 1)
        cached = jnp.where(place < len_ref[index_ref[0] * own + b], cached, -1e30)
        step = lax.broadcasted_iota(jnp.int32, newer.shape, 0) % STEPS
        at = lax.broadcasted_iota(jnp.int32, newer.shape, 1) - b * STEPS
        newer = jnp.where((at >= 0) & (at <= step), newer, -1e30)
        top = jnp.maximum(
            jnp.max(cached, axis=1, keepdims=True), jnp.max(newer, axis=1, keepdims=True)
        )
        cached = jnp.exp(cached - top)
        newer = jnp.exp(newer - top)
        total = jnp.sum(cached, axis=1, keepdims=True) + jnp.sum(newer, axis=1, keepdims=True)
        cached = (cached / total).astype(BF16)
        newer = (newer / total).astype(BF16)
        for g in range(KV_HEADS):
            at_rows = slice(g * mine, (g + 1) * mine)
            part = dot(cached[at_rows], v_ref[b, :, g * HEAD : (g + 1) * HEAD])
            s_ref[(b * KV_HEADS + g) * mine : (b * KV_HEADS + g + 1) * mine] = part + dot(
                newer[at_rows], values[g]
            )
    step = local * STEPS
    half = KV_HEADS * mine
    for i in range(n):
        block = [s_ref[b * half + i * step : b * half + (i + 1) * step] for b in range(own)]
        ctx_ref[i] = jnp.concatenate(block, axis=0).astype(BF16)


def take_body(ctx_ref, take_ref, w_ref, a_ref, mine_ref, other_ref):
    rows = a_ref.shape[0]
    x = ctx_ref[...].reshape(-1, HEAD)
    taken = dot(take_ref[...], x).astype(BF16)
    for h in range(a_ref.shape[1] // HEAD):
        a_ref[:, h * HEAD : (h + 1) * HEAD] = taken[h * rows : (h + 1) * rows]
    out_body(0, a_ref, w_ref, mine_ref, other_ref)


def out_body(start, a_ref, w_ref, mine_ref, other_ref):
    half = mine_ref.shape[0]
    tile = 512

    @pl.loop(0, mine_ref.shape[1] // tile)
    def _(i):
        at = pl.ds(pl.multiple_of(i * tile, tile), tile)
        product = dot(a_ref[...], w_ref[:, pl.ds(pl.multiple_of(start + i * tile, tile), tile)])
        mine_ref[:, at] = product[:half]
        other_ref[:, at] = product[half:]


def far_first_body(near, mine_ref, came_ref, *refs):
    total = mine_ref[...] + came_ref[...]
    rows = refs[0].shape[0] // near
    for f, ref in enumerate(refs):
        blocks = [(m * len(refs) + f) * rows for m in range(near)]
        value = jnp.concatenate([total[at : at + rows] for at in blocks], axis=0)
        ref[...] = value.astype(ref.dtype)


def near_body(mine_ref, came_ref, *refs):
    rows = refs[0].shape[0]
    total = mine_ref[...] + came_ref[...]
    refs[0][...] = total[:rows]
    for m, ref in enumerate(refs[1:], 1):
        ref[...] = total[m * rows : (m + 1) * rows].astype(BF16)


def far_body(came, *refs):
    total = refs[0][...]
    for ref in refs[1 : 1 + came]:
        total = total + ref[...].astype(F32)
    refs = refs[1 + came :]
    rows = refs[0].shape[0]
    refs[0][...] = total[:rows]
    for f, ref in enumerate(refs[1:], 1):
        ref[...] = total[f * rows : (f + 1) * rows].astype(BF16)


def last_body(longs, first_ref, second_ref, *refs):
    one_ref, two_ref = refs[-2:]
    totals = []
    for part in (refs[:longs], refs[longs:-2]):
        total = part[0][...]
        for ref in part[1:]:
            total = total + ref[...].astype(F32)
        totals.append(total)
    total = jnp.concatenate(totals, axis=1)
    own = one_ref.shape[0]
    one_ref[...] = (first_ref[...].astype(F32) + total[:own]).astype(BF16)
    two_ref[...] = (second_ref[...].astype(F32) + total[own:]).astype(BF16)


def shards(
    sizes,
    residual_first,
    residual_second,
    attention_norm_gain,
    query_matrix,
    key_matrix,
    value_matrix,
    output_matrix,
    query_down_weights,
    value_down_weights,
    query_up_weights,
    value_up_weights,
    rotated_key_cache,
    stored_value_cache,
    lengths,
    request_adapter,
    adapter_slot,
):
    far, near, cores = sizes
    n = far * near * cores
    index = lax.axis_index("serve")
    own, width = residual_first.shape
    adapters, _, rank = query_down_weights.shape
    query_cols = query_matrix.shape[1]
    key_cols = key_matrix.shape[1]
    local = query_cols // HEAD
    rows = own * STEPS
    all_rows = n * rows
    stored = query_up_weights.shape[0]

    def partner(f, m, c):
        pairs = []
        for z in range(far):
            for y in range(near):
                for k in range(cores):
                    to = (((z + f) % far) * near + (y + m) % near) * cores + (k + c) % cores
                    pairs.append(((z * near + y) * cores + k, to))
        return pairs

    def shift(value, f, m, c):
        return lax.ppermute(value, "serve", partner(f, m, c))

    frequency = whole_call(frequency_body, jax.ShapeDtypeStruct((1, HEAD), F32), (), cost=3.0)
    gain = attention_norm_gain.reshape(width // HEAD, HEAD)
    gain, frequency = lax.optimization_barrier((gain, frequency))
    normed = whole_call(
        norm_body,
        jax.ShapeDtypeStruct((rows, width), BF16),
        (residual_first, residual_second, gain),
        hbm=3,
        scratch=[
            pltpu.VMEM((own, width), BF16),
            pltpu.VMEM((own, width), BF16),
            pltpu.VMEM(gain.shape, BF16),
            pltpu.SemaphoreType.DMA((3,)),
        ],
        cost=1.0,
    )
    normed = normed[None]
    fars = [shift(normed, f, 0, 0) for f in range(1, far)]
    nears = [shift(normed, 0, m, 0) for m in range(1, near)]
    rest = jnp.concatenate(fars)
    groups = [jnp.concatenate([normed, *fars, *nears[:1]])]
    groups += [shift(rest, 0, m, 0) for m in range(1, near)]

    rest, at = lax.optimization_barrier((rest, index[None]))
    sent = -(-(rows * local + rows) // 8) * 8
    narrow = jax.ShapeDtypeStruct((all_rows, 1), jnp.int32)
    table = jax.ShapeDtypeStruct((all_rows, HEAD), F32)
    square = jax.ShapeDtypeStruct((all_rows, all_rows), BF16)
    slot, near_slot, cosine, sine, key_cosine, key_sine, place, unplace, send, order, take = whole_call(
        functools.partial(prep_body, sizes, rank, own, key_cols, adapters),
        (
            narrow,
            narrow,
            table,
            table,
            table,
            table,
            square,
            square,
            jax.ShapeDtypeStruct((n * sent, all_rows * (local + 1)), BF16),
            jax.ShapeDtypeStruct((own * HEADS * STEPS, n * sent), BF16),
            jax.ShapeDtypeStruct((all_rows * local, n * rows * local), BF16),
        ),
        (at, lengths, request_adapter, adapter_slot, frequency),
        smem=1,
        hbm=3,
        scratch=[
            pltpu.SMEM(lengths.shape, jnp.int32),
            pltpu.SMEM(request_adapter.shape, jnp.int32),
            pltpu.SMEM(adapter_slot.shape, jnp.int32),
            pltpu.SemaphoreType.DMA((3,)),
        ],
        cost=4.0,
    )
    slot, groups[1] = lax.optimization_barrier((slot, groups[1]))

    groups += [shift(part, 0, 0, c) for c in range(1, cores) for part in groups[:near]]

    query_down = jnp.swapaxes(query_down_weights, 1, 2).reshape(adapters * rank, width)
    value_down = jnp.swapaxes(value_down_weights, 1, 2).reshape(adapters * rank, width)
    packed_rows = all_rows * 2 * rank // HEAD
    x, low = whole_call(
        functools.partial(low_body, rank, len(groups)),
        (
            jax.ShapeDtypeStruct((all_rows, width), BF16),
            jax.ShapeDtypeStruct((packed_rows, HEAD), BF16),
        ),
        (*groups, query_down, value_down, near_slot, place),
        cost=0.3,
    )
    def base(start, stop):
        return whole_call(
            functools.partial(base_body, 2048, start, stop),
            (
                jax.ShapeDtypeStruct((all_rows, query_cols), F32),
                jax.ShapeDtypeStruct((all_rows, HEAD), F32),
            ),
            (x, query_matrix, key_matrix.T, value_matrix.T),
            cost=0.3,
        )

    lows = [shift(low, 0, m, c) for m in range(near) for c in range(cores) if m + c]
    base_q, base_kv = base(0, width // 2)
    low = whole_call(join_body, jax.ShapeDtypeStruct(low.shape, BF16), (low, *lows), cost=0.1)
    low, base_q = lax.optimization_barrier((low, base_q))
    lows = [low] + [shift(low, f, 0, 0) for f in range(1, far)]
    bases = (base_q, base_kv, *base(width // 2, width))

    ready = whole_call(
        functools.partial(ready_body, rank, len(lows)),
        jax.ShapeDtypeStruct((n, sent, HEAD), BF16),
        (
            *lows,
            *bases,
            unplace,
            slot,
            query_up_weights.reshape(stored * rank, query_cols),
            value_up_weights.reshape(stored * rank, key_cols),
            cosine,
            sine,
            key_cosine,
            key_sine,
            send,
        ),
        cost=0.9,
    )
    arrived = lax.all_to_all(ready, "serve", split_axis=0, concat_axis=0, tiled=True)

    fresh = jax.ShapeDtypeStruct((own, STEPS, KV_HEADS * HEAD), BF16)
    new_keys, new_values, context = whole_call(
        functools.partial(attend_body, own, key_cols),
        (fresh, fresh, jax.ShapeDtypeStruct((n, rows * local, HEAD), BF16)),
        (index[None], lengths, arrived, order, rotated_key_cache, stored_value_cache),
        smem=2,
        scratch=[pltpu.VMEM((own * HEADS * STEPS, HEAD), F32)],
        cost=1.0,
    )
    context = lax.all_to_all(context, "serve", split_axis=0, concat_axis=0, tiled=True)

    half = all_rows // cores
    cut = width * 18 // 32

    def kinds(count, columns):
        return (jax.ShapeDtypeStruct((count, columns), F32),) * 2

    taken, mine_long, other_long = whole_call(
        take_body,
        (jax.ShapeDtypeStruct((all_rows, query_cols), BF16),) + kinds(half, cut),
        (context, take, output_matrix),
        cost=0.4,
    )
    mine_short, other_short = whole_call(
        functools.partial(out_body, cut),
        kinds(half, width - cut),
        (taken, output_matrix),
        cost=0.3,
    )

    def kind(count, columns, dtype):
        return jax.ShapeDtypeStruct((count * rows, columns), dtype)

    keep, *others = whole_call(
        near_body,
        (kind(far, cut, F32),) + (kind(far, cut, BF16),) * (near - 1),
        (mine_long, shift(other_long, 0, 0, 1)),
        cost=0.1,
    )
    others = [shift(other, 0, m, 0) for m, other in enumerate(others, 1)]
    short, *sides = whole_call(
        functools.partial(far_first_body, near),
        (kind(near, width - cut, F32),) + (kind(near, width - cut, BF16),) * (far - 1),
        (mine_short, shift(other_short, 0, 0, 1)),
        cost=0.1,
    )
    sides = [shift(side, f, 0, 0) for f, side in enumerate(sides, 1)]
    keep, *others = whole_call(
        functools.partial(far_body, len(others)),
        (kind(1, cut, F32),) + (kind(1, cut, BF16),) * (far - 1),
        (keep, *others),
        cost=0.1,
    )
    others = [shift(other, f, 0, 0) for f, other in enumerate(others, 1)]
    short, *sides = whole_call(
        functools.partial(far_body, len(sides)),
        (kind(1, width - cut, F32),) + (kind(1, width - cut, BF16),) * (near - 1),
        (short, *sides),
        cost=0.1,
    )
    sides = [shift(side, 0, m, 0) for m, side in enumerate(sides, 1)]
    result = jax.ShapeDtypeStruct((own, width), BF16)
    out_one, out_two = whole_call(
        functools.partial(last_body, 1 + len(others)),
        (result, result),
        (residual_first, residual_second, keep, *others, short, *sides),
        cost=0.1,
    )
    return (out_one, out_two, new_keys, new_values)


def solution(mesh):
    n = mesh.shape["serve"]
    sizes = (n // 4, 2, 2)
    return jax.shard_map(
        functools.partial(shards, sizes),
        mesh=mesh,
        in_specs=(
            P(("replica", "serve"), None),
            P(("replica", "serve"), None),
            P(),
            P(None, "serve"),
            P(None, "serve"),
            P(None, "serve"),
            P("serve", None),
            P("serve", None, None),
            P("serve", None, None),
            P(None, None, "serve"),
            P(None, None, "serve"),
            P(("replica", "serve"), None, None),
            P(("replica", "serve"), None, None),
            P("replica"),
            P("replica"),
            P(),
        ),
        out_specs=(
            P(("replica", "serve"), None),
            P(("replica", "serve"), None),
            P(("replica", "serve"), None, None),
            P(("replica", "serve"), None, None),
        ),
        check_vma=False,
    )
```

```python
import functools
import math

import jax
import jax.numpy as jnp
from jax import lax
from jax.experimental import pallas as pl
from jax.experimental.pallas import tpu as pltpu
from jax.sharding import PartitionSpec as P

HEADS = 64
KV_HEADS = 8
HEAD = 128
STEPS = 2
LIMIT = 8 * 1024 * 1024
PEAK = 1.15e9
NT = (((1,), (1,)), ((), ()))
F32 = jnp.float32
BF16 = jnp.bfloat16


def dot(a, b):
    return jnp.dot(a, b, preferred_element_type=F32)


def dot_nt(a, b):
    return lax.dot_general(a, b, NT, preferred_element_type=F32)


def whole_call(body, out_shape, args, cost, smem=0, hbm=0, scratch=()):
    specs = [pl.BlockSpec(memory_space=pltpu.SMEM)] * smem
    specs += [pl.BlockSpec(memory_space=pltpu.HBM)] * hbm
    specs += [pl.BlockSpec(memory_space=pltpu.VMEM)] * (len(args) - smem - hbm)
    many = isinstance(out_shape, (tuple, list))
    vmem = pl.BlockSpec(memory_space=pltpu.VMEM)
    return pl.pallas_call(
        body,
        out_shape=out_shape,
        in_specs=specs,
        out_specs=tuple(vmem for _ in out_shape) if many else vmem,
        scratch_shapes=list(scratch),
        compiler_params=pltpu.CompilerParams(vmem_limit_bytes=LIMIT),
        cost_estimate=pl.CostEstimate(
            flops=int(cost * PEAK), bytes_accessed=0, transcendentals=0
        ),
    )(*args)


def scaled_frequency(pair_index):
    base = jnp.exp(pair_index.astype(F32) * (-2.0 * math.log(500000.0) / HEAD))
    wavelength = 2.0 * math.pi / base
    smooth = jnp.clip((8192.0 / wavelength - 1.0) / 3.0, 0.0, 1.0)
    return (1.0 - smooth) * base / 8.0 + smooth * base


def fetch(pairs, sems):
    copies = [
        pltpu.make_async_copy(source, target, sems.at[i])
        for i, (source, target) in enumerate(pairs)
    ]
    for copy in copies:
        copy.start()
    for copy in copies:
        copy.wait()


def norm_body(first_hbm, second_hbm, gain_hbm, out_ref, first_ref, second_ref, gain_ref, sems):
    fetch(((first_hbm, first_ref), (second_hbm, second_ref), (gain_hbm, gain_ref)), sems)
    gain = gain_ref[...].astype(F32)
    factors = []
    for ref in (first_ref, second_ref):
        values = ref[...].astype(F32)
        factors.append(lax.rsqrt(jnp.mean(values * values, axis=-1, keepdims=True) + 1e-05))
    factor = jnp.concatenate(factors, axis=0)
    for i in range(gain.shape[0]):
        at = slice(i * HEAD, (i + 1) * HEAD)
        values = jnp.concatenate((first_ref[:, at].astype(F32), second_ref[:, at].astype(F32)))
        out_ref[:, at] = (values * factor * gain[i : i + 1]).astype(BF16)


def frequency_body(out_ref):
    out_ref[...] = scaled_frequency(lax.broadcasted_iota(jnp.int32, out_ref.shape, 1) // 2)


def prep_body(
    sizes, rank, own, key_cols, adapters,
    index_ref, length_hbm, adapter_hbm, slot_hbm, frequency_ref,
    held_ref, local_ref, cos_ref, sin_ref, kcos_ref, ksin_ref, place_ref, unplace_ref, send_ref,
    order_ref, take_ref, length_ref, adapter_ref, slot_ref, sems,
):
    fetch(((length_hbm, length_ref), (adapter_hbm, adapter_ref), (slot_hbm, slot_ref)), sems)
    far, near, cores = sizes
    n = far * near * cores
    rows = own * STEPS
    all_rows = n * rows
    heads = HEADS // n
    sent = send_ref.shape[0] // n
    index = index_ref[0]
    core_at = index % cores
    near_at = index // cores % near
    far_at = index // (cores * near)

    def device_of(block, sign):
        c, m, f = block // (far * near), block // far % near, block % far
        f = (far_at + sign * f + far) % far
        m = (near_at + sign * m + near) % near
        c = (core_at + sign * c + cores) % cores
        return (f * near + m) * cores + c

    def iota(shape, axis):
        return lax.broadcasted_iota(jnp.int32, shape, axis)

    def split(row):
        return row // rows, row % rows // own, row % own

    block, step, mine = split(iota((all_rows, 1), 0))
    device = device_of(block, -1)
    request = device * own + mine
    length = jnp.zeros_like(request)
    adapter = jnp.zeros_like(request)
    for j in range(length_ref.shape[0]):
        length = jnp.where(request == j, length_ref[j], length)
        adapter = jnp.where(request == j, adapter_ref[j], adapter)
    slot = jnp.zeros_like(request)
    for j in range(slot_ref.shape[0]):
        slot = jnp.where(adapter == j, slot_ref[j], slot)
    held_ref[...] = slot
    local_ref[...] = slot - index * adapters
    position = (length + step).astype(F32)
    lane = iota((1, HEAD), 1)
    odd = jnp.where(lane % 2 == 0, -1.0, 1.0)
    angle = position * frequency_ref[...]
    cos_ref[...] = jnp.cos(angle)
    sin_ref[...] = jnp.sin(angle) * odd
    angle = position * scaled_frequency((index * key_cols + lane) % HEAD // 2)
    kcos_ref[...] = jnp.where(lane < key_cols, jnp.cos(angle), 1.0)
    ksin_ref[...] = jnp.where(lane < key_cols, jnp.sin(angle) * odd, 0.0)

    def hot(ref, row, column):
        ref[...] = jnp.where(row == column, 1.0, 0.0).astype(BF16)

    absolute = (device * STEPS + step) * own + mine
    hot(unplace_ref, absolute, iota((1, all_rows), 1))
    block, step, mine = split(iota((1, all_rows), 1))
    absolute = (device_of(block, -1) * STEPS + step) * own + mine
    hot(place_ref, iota((all_rows, 1), 0), absolute)

    column = iota((1, send_ref.shape[1]), 1)
    h = column // all_rows
    block, step, mine = split(column % all_rows)
    wanted = device_of(block, -1) * sent + jnp.where(
        h < heads, (mine * heads + h) * STEPS + step, rows * heads + mine * STEPS + step
    )
    hot(send_ref, iota((n * sent, 1), 0), wanted)

    row = iota((order_ref.shape[0], 1), 0)
    mine, head, step = row // (HEADS * STEPS), row // STEPS % HEADS, row % STEPS
    wanted = (head // heads) * sent + (mine * heads + head % heads) * STEPS + step
    hot(order_ref, wanted, iota((1, n * sent), 1))

    row = iota((take_ref.shape[0], 1), 0)
    h = row // all_rows
    block, step, mine = split(row % all_rows)
    wanted = device_of(block, 1) * rows * heads + (mine * heads + h) * STEPS + step
    hot(take_ref, wanted, iota((1, take_ref.shape[1]), 1))


def low_body(rank, groups, *refs):
    parts, (qd_ref, vd_ref, local_ref, place_ref, x_ref, out_ref) = refs[:groups], refs[groups:]
    rows = parts[0].shape[1]
    sets = max(1, 16 // rows)
    blocks = [(part, i) for part in parts for i in range(part.shape[0])]
    for first in range(0, len(blocks), sets):
        group = blocks[first : first + sets]
        for lane in range(0, x_ref.shape[1], 1024):
            lanes = slice(lane, lane + 1024)
            block = [part[i, :, lanes].astype(F32) for part, i in group]
            block = jnp.concatenate(block, axis=0).astype(BF16)
            x_ref[first * rows : (first + sets) * rows, lanes] = block
    adapters = qd_ref.shape[0] // rank
    maps = jnp.concatenate((qd_ref[...], vd_ref[...]), axis=0)
    low = dot_nt(x_ref[...], maps)
    lane = lax.broadcasted_iota(jnp.int32, low.shape, 1)
    low = jnp.where(lane // rank % adapters == local_ref[...], low, 0.0)
    total = 0.0
    for a in range(adapters):
        q = low[:, a * rank : (a + 1) * rank]
        v = low[:, (adapters + a) * rank : (adapters + a + 1) * rank]
        total = total + jnp.concatenate((q, v), axis=1)
    rows = dot(place_ref[...], total.astype(BF16))
    pack = HEAD // (2 * rank)
    step = rows.shape[0] // pack
    packed = jnp.concatenate([rows[i * step : (i + 1) * step] for i in range(pack)], axis=1)
    out_ref[...] = packed.astype(BF16)


def join_body(*refs):
    total = refs[0][...].astype(F32)
    for ref in refs[1:-1]:
        total = total + ref[...].astype(F32)
    refs[-1][...] = total.astype(BF16)


def base_body(depth, start, stop, x_ref, q_ref, k_ref, v_ref, oq_ref, okv_ref):
    columns = k_ref.shape[0]
    narrow = jnp.zeros((HEAD - 2 * columns, depth), BF16)
    query, fresh = 0.0, 0.0
    for first in range(start, stop, depth):
        at = slice(first, first + depth)
        x = x_ref[:, at]
        query = query + dot(x, q_ref[at, :])
        both = (k_ref[:, at], v_ref[:, at])
        if 2 * columns < HEAD:
            both += (narrow,)
        fresh = fresh + dot_nt(x, jnp.concatenate(both, axis=0))
    oq_ref[...] = query
    okv_ref[...] = fresh


def turned(values, cosine, sine):
    lane = lax.broadcasted_iota(jnp.int32, values.shape, 1)
    width = values.shape[1]
    ahead = pltpu.roll(values, width - 1, 1)
    behind = pltpu.roll(values, 1, 1)
    return values * cosine + jnp.where(lane % 2 == 0, ahead, behind) * sine


def ready_body(
    rank, lows, *refs
):
    low_refs = refs[:lows]
    (
        oq_ref, okv_ref, oq2_ref, okv2_ref, unplace_ref, slot_ref, uq_ref, uv_ref, cos_ref, sin_ref, kcos_ref, ksin_ref,
        send_ref, out_ref,
    ) = refs[lows:]
    packed = low_refs[0][...].astype(F32)
    for ref in low_refs[1:]:
        packed = packed + ref[...].astype(F32)
    pack = HEAD // (2 * rank)
    low = jnp.concatenate(
        [packed[:, i * 2 * rank : (i + 1) * 2 * rank] for i in range(pack)], axis=0
    )
    low = dot(unplace_ref[...], low.astype(BF16)).astype(BF16)
    wide = uq_ref.shape[0]
    lane = lax.broadcasted_iota(jnp.int32, (low.shape[0], wide), 1)
    here = lane // rank == slot_ref[...]
    row = lax.broadcasted_iota(jnp.int32, (2 * rank, wide), 0)
    column = lax.broadcasted_iota(jnp.int32, (2 * rank, wide), 1)
    spread_q = jnp.where(column % rank == row, 1.0, 0.0).astype(BF16)
    spread_v = jnp.where(column % rank + rank == row, 1.0, 0.0).astype(BF16)
    wide_q = jnp.where(here, dot(low, spread_q), 0.0).astype(BF16)
    wide_v = jnp.where(here, dot(low, spread_v), 0.0).astype(BF16)
    query = oq_ref[...] + oq2_ref[...] + dot(wide_q, uq_ref[...])
    fresh = turned(okv_ref[...] + okv2_ref[...], kcos_ref[...], ksin_ref[...])
    columns = uv_ref.shape[1]
    value = dot(wide_v, uv_ref[...])
    pieces = [jnp.zeros((value.shape[0], columns), F32), value]
    if 2 * columns < HEAD:
        pieces.append(jnp.zeros((value.shape[0], HEAD - 2 * columns), F32))
    fresh = fresh + jnp.concatenate(pieces, axis=1)
    cosine, sine = cos_ref[...], sin_ref[...]
    parts = []
    for h in range(query.shape[1] // HEAD):
        parts.append(turned(query[:, h * HEAD : (h + 1) * HEAD], cosine, sine))
    parts.append(fresh)
    stacked = jnp.concatenate(parts, axis=0).astype(BF16)
    out_ref[...] = dot(send_ref[...], stacked).astype(BF16).reshape(out_ref.shape)


def attend_body(
    own, columns, index_ref, len_ref, x_ref, order_ref, k_ref, v_ref, nk_ref, nv_ref, ctx_ref, s_ref
):
    n, span = x_ref.shape[0], k_ref.shape[1]
    group = HEADS // KV_HEADS
    local = HEADS // n
    rows = own * STEPS
    mine = group * STEPS
    x = x_ref[...]
    queries = dot(order_ref[...], x.reshape(n * x.shape[1], HEAD)).astype(BF16)
    wide = x.astype(F32)
    first = rows * local
    fresh = [wide[i, first : first + rows] for i in range(n)]
    each = n // KV_HEADS
    keys, values = [], []
    for g in range(KV_HEADS):
        pieces = fresh[g * each : (g + 1) * each]
        keys.append(jnp.concatenate([p[:, :columns] for p in pieces], axis=1))
        values.append(jnp.concatenate([p[:, columns : 2 * columns] for p in pieces], axis=1))
    new_keys = jnp.concatenate(keys, axis=1)
    new_values = jnp.concatenate(values, axis=1)
    for b in range(own):
        at = slice(b * STEPS, (b + 1) * STEPS)
        nk_ref[b] = new_keys[at].astype(BF16)
        nv_ref[b] = new_values[at].astype(BF16)
    pad = jnp.zeros((16 - rows, HEAD), F32)
    keys = [jnp.concatenate((k, pad), axis=0).astype(BF16) for k in keys]
    values = [jnp.concatenate((v, pad), axis=0).astype(BF16) for v in values]
    scale = HEAD ** (-0.5)
    contexts = []
    for b in range(own):
        q = queries[b * KV_HEADS * mine : (b + 1) * KV_HEADS * mine]
        cached, newer = [], []
        for g in range(KV_HEADS):
            qg = q[g * mine : (g + 1) * mine]
            cached.append(dot_nt(qg, k_ref[b, :, g * HEAD : (g + 1) * HEAD]))
            newer.append(dot_nt(qg, keys[g]))
        cached = jnp.concatenate(cached, axis=0) * scale
        newer = jnp.concatenate(newer, axis=0) * scale
        place = lax.broadcasted_iota(jnp.int32, cached.shape, 1)
        cached = jnp.where(place < len_ref[index_ref[0] * own + b], cached, -1e30)
        step = lax.broadcasted_iota(jnp.int32, newer.shape, 0) % STEPS
        at = lax.broadcasted_iota(jnp.int32, newer.shape, 1) - b * STEPS
        newer = jnp.where((at >= 0) & (at <= step), newer, -1e30)
        top = jnp.maximum(
            jnp.max(cached, axis=1, keepdims=True), jnp.max(newer, axis=1, keepdims=True)
        )
        cached = jnp.exp(cached - top)
        newer = jnp.exp(newer - top)
        total = jnp.sum(cached, axis=1, keepdims=True) + jnp.sum(newer, axis=1, keepdims=True)
        cached = (cached / total).astype(BF16)
        newer = (newer / total).astype(BF16)
        for g in range(KV_HEADS):
            at_rows = slice(g * mine, (g + 1) * mine)
            part = dot(cached[at_rows], v_ref[b, :, g * HEAD : (g + 1) * HEAD])
            s_ref[(b * KV_HEADS + g) * mine : (b * KV_HEADS + g + 1) * mine] = part + dot(
                newer[at_rows], values[g]
            )
    step = local * STEPS
    half = KV_HEADS * mine
    for i in range(n):
        block = [s_ref[b * half + i * step : b * half + (i + 1) * step] for b in range(own)]
        ctx_ref[i] = jnp.concatenate(block, axis=0).astype(BF16)


def take_body(ctx_ref, take_ref, w_ref, a_ref, mine_ref, other_ref):
    rows = a_ref.shape[0]
    x = ctx_ref[...].reshape(-1, HEAD)
    taken = dot(take_ref[...], x).astype(BF16)
    for h in range(a_ref.shape[1] // HEAD):
        a_ref[:, h * HEAD : (h + 1) * HEAD] = taken[h * rows : (h + 1) * rows]
    out_body(0, a_ref, w_ref, mine_ref, other_ref)


def out_body(start, a_ref, w_ref, mine_ref, other_ref):
    half = mine_ref.shape[0]
    tile = 1024

    for at in range(0, mine_ref.shape[1], tile):
        product = dot(a_ref[...], w_ref[:, start + at : start + at + tile])
        mine_ref[:, at : at + tile] = product[:half]
        other_ref[:, at : at + tile] = product[half:]


def far_first_body(near, mine_ref, came_ref, *refs):
    total = mine_ref[...] + came_ref[...]
    rows = refs[0].shape[0] // near
    for f, ref in enumerate(refs):
        blocks = [(m * len(refs) + f) * rows for m in range(near)]
        value = jnp.concatenate([total[at : at + rows] for at in blocks], axis=0)
        ref[...] = value.astype(ref.dtype)


def near_body(mine_ref, came_ref, *refs):
    rows = refs[0].shape[0]
    total = mine_ref[...] + came_ref[...]
    refs[0][...] = total[:rows]
    for m, ref in enumerate(refs[1:], 1):
        ref[...] = total[m * rows : (m + 1) * rows].astype(BF16)


def far_body(came, *refs):
    total = refs[0][...]
    for ref in refs[1 : 1 + came]:
        total = total + ref[...].astype(F32)
    refs = refs[1 + came :]
    rows = refs[0].shape[0]
    refs[0][...] = total[:rows]
    for f, ref in enumerate(refs[1:], 1):
        ref[...] = total[f * rows : (f + 1) * rows].astype(BF16)


def last_body(longs, first_ref, second_ref, *refs):
    one_ref, two_ref = refs[-2:]
    totals = []
    for part in (refs[:longs], refs[longs:-2]):
        total = part[0][...]
        for ref in part[1:]:
            total = total + ref[...].astype(F32)
        totals.append(total)
    total = jnp.concatenate(totals, axis=1)
    own = one_ref.shape[0]
    one_ref[...] = (first_ref[...].astype(F32) + total[:own]).astype(BF16)
    two_ref[...] = (second_ref[...].astype(F32) + total[own:]).astype(BF16)


def shards(
    sizes,
    residual_first,
    residual_second,
    attention_norm_gain,
    query_matrix,
    key_matrix,
    value_matrix,
    output_matrix,
    query_down_weights,
    value_down_weights,
    query_up_weights,
    value_up_weights,
    rotated_key_cache,
    stored_value_cache,
    lengths,
    request_adapter,
    adapter_slot,
):
    far, near, cores = sizes
    n = far * near * cores
    index = lax.axis_index("serve")
    own, width = residual_first.shape
    adapters, _, rank = query_down_weights.shape
    query_cols = query_matrix.shape[1]
    key_cols = key_matrix.shape[1]
    local = query_cols // HEAD
    rows = own * STEPS
    all_rows = n * rows
    stored = query_up_weights.shape[0]

    def partner(f, m, c):
        pairs = []
        for z in range(far):
            for y in range(near):
                for k in range(cores):
                    to = (((z + f) % far) * near + (y + m) % near) * cores + (k + c) % cores
                    pairs.append(((z * near + y) * cores + k, to))
        return pairs

    def shift(value, f, m, c):
        return lax.ppermute(value, "serve", partner(f, m, c))

    frequency = whole_call(frequency_body, jax.ShapeDtypeStruct((1, HEAD), F32), (), cost=3.0)
    gain = attention_norm_gain.reshape(width // HEAD, HEAD)
    gain, frequency = lax.optimization_barrier((gain, frequency))
    normed = whole_call(
        norm_body,
        jax.ShapeDtypeStruct((rows, width), BF16),
        (residual_first, residual_second, gain),
        hbm=3,
        scratch=[
            pltpu.VMEM((own, width), BF16),
            pltpu.VMEM((own, width), BF16),
            pltpu.VMEM(gain.shape, BF16),
            pltpu.SemaphoreType.DMA((3,)),
        ],
        cost=1.0,
    )
    normed = normed[None]
    fars = [shift(normed, f, 0, 0) for f in range(1, far)]
    nears = [shift(normed, 0, m, 0) for m in range(1, near)]
    rest = jnp.concatenate(fars)
    groups = [jnp.concatenate([normed, *fars, *nears[:1]])]
    groups += [shift(rest, 0, m, 0) for m in range(1, near)]

    rest, at = lax.optimization_barrier((rest, index[None]))
    sent = -(-(rows * local + rows) // 8) * 8
    narrow = jax.ShapeDtypeStruct((all_rows, 1), jnp.int32)
    table = jax.ShapeDtypeStruct((all_rows, HEAD), F32)
    square = jax.ShapeDtypeStruct((all_rows, all_rows), BF16)
    slot, near_slot, cosine, sine, key_cosine, key_sine, place, unplace, send, order, take = whole_call(
        functools.partial(prep_body, sizes, rank, own, key_cols, adapters),
        (
            narrow,
            narrow,
            table,
            table,
            table,
            table,
            square,
            square,
            jax.ShapeDtypeStruct((n * sent, all_rows * (local + 1)), BF16),
            jax.ShapeDtypeStruct((own * HEADS * STEPS, n * sent), BF16),
            jax.ShapeDtypeStruct((all_rows * local, n * rows * local), BF16),
        ),
        (at, lengths, request_adapter, adapter_slot, frequency),
        smem=1,
        hbm=3,
        scratch=[
            pltpu.SMEM(lengths.shape, jnp.int32),
            pltpu.SMEM(request_adapter.shape, jnp.int32),
            pltpu.SMEM(adapter_slot.shape, jnp.int32),
            pltpu.SemaphoreType.DMA((3,)),
        ],
        cost=4.0,
    )
    slot, groups[1] = lax.optimization_barrier((slot, groups[1]))

    groups += [shift(part, 0, 0, c) for c in range(1, cores) for part in groups[:near]]

    query_down = jnp.swapaxes(query_down_weights, 1, 2).reshape(adapters * rank, width)
    value_down = jnp.swapaxes(value_down_weights, 1, 2).reshape(adapters * rank, width)
    packed_rows = all_rows * 2 * rank // HEAD
    x, low = whole_call(
        functools.partial(low_body, rank, len(groups)),
        (
            jax.ShapeDtypeStruct((all_rows, width), BF16),
            jax.ShapeDtypeStruct((packed_rows, HEAD), BF16),
        ),
        (*groups, query_down, value_down, near_slot, place),
        cost=0.3,
    )
    def base(start, stop):
        return whole_call(
            functools.partial(base_body, 2048, start, stop),
            (
                jax.ShapeDtypeStruct((all_rows, query_cols), F32),
                jax.ShapeDtypeStruct((all_rows, HEAD), F32),
            ),
            (x, query_matrix, key_matrix.T, value_matrix.T),
            cost=0.3,
        )

    lows = [shift(low, 0, m, c) for m in range(near) for c in range(cores) if m + c]
    base_q, base_kv = base(0, width // 2)
    low = whole_call(join_body, jax.ShapeDtypeStruct(low.shape, BF16), (low, *lows), cost=0.1)
    low, base_q = lax.optimization_barrier((low, base_q))
    lows = [low] + [shift(low, f, 0, 0) for f in range(1, far)]
    bases = (base_q, base_kv, *base(width // 2, width))

    ready = whole_call(
        functools.partial(ready_body, rank, len(lows)),
        jax.ShapeDtypeStruct((n, sent, HEAD), BF16),
        (
            *lows,
            *bases,
            unplace,
            slot,
            query_up_weights.reshape(stored * rank, query_cols),
            value_up_weights.reshape(stored * rank, key_cols),
            cosine,
            sine,
            key_cosine,
            key_sine,
            send,
        ),
        cost=0.9,
    )
    arrived = lax.all_to_all(ready, "serve", split_axis=0, concat_axis=0, tiled=True)

    fresh = jax.ShapeDtypeStruct((own, STEPS, KV_HEADS * HEAD), BF16)
    new_keys, new_values, context = whole_call(
        functools.partial(attend_body, own, key_cols),
        (fresh, fresh, jax.ShapeDtypeStruct((n, rows * local, HEAD), BF16)),
        (index[None], lengths, arrived, order, rotated_key_cache, stored_value_cache),
        smem=2,
        scratch=[pltpu.VMEM((own * HEADS * STEPS, HEAD), F32)],
        cost=1.0,
    )
    context = lax.all_to_all(context, "serve", split_axis=0, concat_axis=0, tiled=True)

    half = all_rows // cores
    cut = width * 5 // 8

    def kinds(count, columns):
        return (jax.ShapeDtypeStruct((count, columns), F32),) * 2

    taken, mine_long, other_long = whole_call(
        take_body,
        (jax.ShapeDtypeStruct((all_rows, query_cols), BF16),) + kinds(half, cut),
        (context, take, output_matrix),
        cost=0.4,
    )
    mine_short, other_short = whole_call(
        functools.partial(out_body, cut),
        kinds(half, width - cut),
        (taken, output_matrix),
        cost=0.3,
    )

    def kind(count, columns, dtype):
        return jax.ShapeDtypeStruct((count * rows, columns), dtype)

    keep, *others = whole_call(
        near_body,
        (kind(far, cut, F32),) + (kind(far, cut, BF16),) * (near - 1),
        (mine_long, shift(other_long, 0, 0, 1)),
        cost=0.1,
    )
    others = [shift(other, 0, m, 0) for m, other in enumerate(others, 1)]
    short, *sides = whole_call(
        functools.partial(far_first_body, near),
        (kind(near, width - cut, F32),) + (kind(near, width - cut, BF16),) * (far - 1),
        (mine_short, shift(other_short, 0, 0, 1)),
        cost=0.1,
    )
    sides = [shift(side, f, 0, 0) for f, side in enumerate(sides, 1)]
    keep, *others = whole_call(
        functools.partial(far_body, len(others)),
        (kind(1, cut, F32),) + (kind(1, cut, BF16),) * (far - 1),
        (keep, *others),
        cost=0.1,
    )
    others = [shift(other, f, 0, 0) for f, other in enumerate(others, 1)]
    short, *sides = whole_call(
        functools.partial(far_body, len(sides)),
        (kind(1, width - cut, F32),) + (kind(1, width - cut, BF16),) * (near - 1),
        (short, *sides),
        cost=0.1,
    )
    sides = [shift(side, 0, m, 0) for m, side in enumerate(sides, 1)]
    result = jax.ShapeDtypeStruct((own, width), BF16)
    out_one, out_two = whole_call(
        functools.partial(last_body, 1 + len(others)),
        (result, result),
        (residual_first, residual_second, keep, *others, short, *sides),
        cost=0.1,
    )
    return (out_one, out_two, new_keys, new_values)


def solution(mesh):
    n = mesh.shape["serve"]
    sizes = (n // 4, 2, 2)
    return jax.shard_map(
        functools.partial(shards, sizes),
        mesh=mesh,
        in_specs=(
            P(("replica", "serve"), None),
            P(("replica", "serve"), None),
            P(),
            P(None, "serve"),
            P(None, "serve"),
            P(None, "serve"),
            P("serve", None),
            P("serve", None, None),
            P("serve", None, None),
            P(None, None, "serve"),
            P(None, None, "serve"),
            P(("replica", "serve"), None, None),
            P(("replica", "serve"), None, None),
            P("replica"),
            P("replica"),
            P(),
        ),
        out_specs=(
            P(("replica", "serve"), None),
            P(("replica", "serve"), None),
            P(("replica", "serve"), None, None),
            P(("replica", "serve"), None, None),
        ),
        check_vma=False,
    )
```

```python
import functools
import math

import jax
import jax.numpy as jnp
from jax import lax
from jax.experimental import pallas as pl
from jax.experimental.pallas import tpu as pltpu
from jax.sharding import PartitionSpec as P

HEADS = 64
KV_HEADS = 8
HEAD = 128
STEPS = 2
LIMIT = 8 * 1024 * 1024
PEAK = 1.15e9
NT = (((1,), (1,)), ((), ()))
F32 = jnp.float32
BF16 = jnp.bfloat16


def dot(a, b):
    return jnp.dot(a, b, preferred_element_type=F32)


def dot_nt(a, b):
    return lax.dot_general(a, b, NT, preferred_element_type=F32)


def whole_call(body, out_shape, args, cost, smem=0, hbm=0, scratch=()):
    specs = [pl.BlockSpec(memory_space=pltpu.SMEM)] * smem
    specs += [pl.BlockSpec(memory_space=pltpu.HBM)] * hbm
    specs += [pl.BlockSpec(memory_space=pltpu.VMEM)] * (len(args) - smem - hbm)
    many = isinstance(out_shape, (tuple, list))
    vmem = pl.BlockSpec(memory_space=pltpu.VMEM)
    return pl.pallas_call(
        body,
        out_shape=out_shape,
        in_specs=specs,
        out_specs=tuple(vmem for _ in out_shape) if many else vmem,
        scratch_shapes=list(scratch),
        compiler_params=pltpu.CompilerParams(vmem_limit_bytes=LIMIT),
        cost_estimate=pl.CostEstimate(
            flops=int(cost * PEAK), bytes_accessed=0, transcendentals=0
        ),
    )(*args)


def scaled_frequency(pair_index):
    base = jnp.exp(pair_index.astype(F32) * (-2.0 * math.log(500000.0) / HEAD))
    wavelength = 2.0 * math.pi / base
    smooth = jnp.clip((8192.0 / wavelength - 1.0) / 3.0, 0.0, 1.0)
    return (1.0 - smooth) * base / 8.0 + smooth * base


def fetch(pairs, sems):
    copies = [
        pltpu.make_async_copy(source, target, sems.at[i])
        for i, (source, target) in enumerate(pairs)
    ]
    for copy in copies:
        copy.start()
    for copy in copies:
        copy.wait()


def norm_body(first_hbm, second_hbm, gain_hbm, out_ref, first_ref, second_ref, gain_ref, sems):
    fetch(((first_hbm, first_ref), (second_hbm, second_ref), (gain_hbm, gain_ref)), sems)
    gain = gain_ref[...].astype(F32)
    factors = []
    for ref in (first_ref, second_ref):
        values = ref[...].astype(F32)
        factors.append(lax.rsqrt(jnp.mean(values * values, axis=-1, keepdims=True) + 1e-05))
    factor = jnp.concatenate(factors, axis=0)
    for i in range(gain.shape[0]):
        at = slice(i * HEAD, (i + 1) * HEAD)
        values = jnp.concatenate((first_ref[:, at].astype(F32), second_ref[:, at].astype(F32)))
        out_ref[:, at] = (values * factor * gain[i : i + 1]).astype(BF16)


def frequency_body(out_ref):
    out_ref[...] = scaled_frequency(lax.broadcasted_iota(jnp.int32, out_ref.shape, 1) // 2)


def prep_body(
    sizes, rank, own, key_cols, adapters,
    index_ref, length_hbm, adapter_hbm, slot_hbm, frequency_ref,
    held_ref, local_ref, cos_ref, sin_ref, kcos_ref, ksin_ref, place_ref, unplace_ref, send_ref,
    order_ref, take_ref, length_ref, adapter_ref, slot_ref, sems,
):
    fetch(((length_hbm, length_ref), (adapter_hbm, adapter_ref), (slot_hbm, slot_ref)), sems)
    far, near, cores = sizes
    n = far * near * cores
    rows = own * STEPS
    all_rows = n * rows
    heads = HEADS // n
    sent = send_ref.shape[0] // n
    index = index_ref[0]
    core_at = index % cores
    near_at = index // cores % near
    far_at = index // (cores * near)

    def device_of(block, sign):
        c, m, f = block // (far * near), block // far % near, block % far
        f = (far_at + sign * f + far) % far
        m = (near_at + sign * m + near) % near
        c = (core_at + sign * c + cores) % cores
        return (f * near + m) * cores + c

    def iota(shape, axis):
        return lax.broadcasted_iota(jnp.int32, shape, axis)

    def split(row):
        return row // rows, row % rows // own, row % own

    block, step, mine = split(iota((all_rows, 1), 0))
    device = device_of(block, -1)
    request = device * own + mine
    length = jnp.zeros_like(request)
    adapter = jnp.zeros_like(request)
    for j in range(length_ref.shape[0]):
        length = jnp.where(request == j, length_ref[j], length)
        adapter = jnp.where(request == j, adapter_ref[j], adapter)
    slot = jnp.zeros_like(request)
    for j in range(slot_ref.shape[0]):
        slot = jnp.where(adapter == j, slot_ref[j], slot)
    held_ref[...] = slot
    local_ref[...] = slot - index * adapters
    position = (length + step).astype(F32)
    lane = iota((1, HEAD), 1)
    odd = jnp.where(lane % 2 == 0, -1.0, 1.0)
    angle = position * frequency_ref[...]
    cos_ref[...] = jnp.cos(angle)
    sin_ref[...] = jnp.sin(angle) * odd
    angle = position * scaled_frequency((index * key_cols + lane) % HEAD // 2)
    kcos_ref[...] = jnp.where(lane < key_cols, jnp.cos(angle), 1.0)
    ksin_ref[...] = jnp.where(lane < key_cols, jnp.sin(angle) * odd, 0.0)

    def hot(ref, row, column):
        ref[...] = jnp.where(row == column, 1.0, 0.0).astype(BF16)

    absolute = (device * STEPS + step) * own + mine
    hot(unplace_ref, absolute, iota((1, all_rows), 1))
    block, step, mine = split(iota((1, all_rows), 1))
    absolute = (device_of(block, -1) * STEPS + step) * own + mine
    hot(place_ref, iota((all_rows, 1), 0), absolute)

    column = iota((1, send_ref.shape[1]), 1)
    h = column // all_rows
    block, step, mine = split(column % all_rows)
    wanted = device_of(block, -1) * sent + jnp.where(
        h < heads, (mine * heads + h) * STEPS + step, rows * heads + mine * STEPS + step
    )
    hot(send_ref, iota((n * sent, 1), 0), wanted)

    row = iota((order_ref.shape[0], 1), 0)
    mine, head, step = row // (HEADS * STEPS), row // STEPS % HEADS, row % STEPS
    wanted = (head // heads) * sent + (mine * heads + head % heads) * STEPS + step
    hot(order_ref, wanted, iota((1, n * sent), 1))

    row = iota((take_ref.shape[0], 1), 0)
    h = row // all_rows
    block, step, mine = split(row % all_rows)
    wanted = device_of(block, 1) * rows * heads + (mine * heads + h) * STEPS + step
    hot(take_ref, wanted, iota((1, take_ref.shape[1]), 1))


def low_body(rank, groups, *refs):
    parts, (qd_ref, vd_ref, local_ref, place_ref, x_ref, out_ref) = refs[:groups], refs[groups:]
    rows = parts[0].shape[1]
    sets = max(1, 16 // rows)
    blocks = [(part, i) for part in parts for i in range(part.shape[0])]
    for first in range(0, len(blocks), sets):
        group = blocks[first : first + sets]
        for lane in range(0, x_ref.shape[1], 1024):
            lanes = slice(lane, lane + 1024)
            block = [part[i, :, lanes].astype(F32) for part, i in group]
            block = jnp.concatenate(block, axis=0).astype(BF16)
            x_ref[first * rows : (first + sets) * rows, lanes] = block
    adapters = qd_ref.shape[0] // rank
    maps = jnp.concatenate((qd_ref[...], vd_ref[...]), axis=0)
    low = dot_nt(x_ref[...], maps)
    lane = lax.broadcasted_iota(jnp.int32, low.shape, 1)
    low = jnp.where(lane // rank % adapters == local_ref[...], low, 0.0)
    total = 0.0
    for a in range(adapters):
        q = low[:, a * rank : (a + 1) * rank]
        v = low[:, (adapters + a) * rank : (adapters + a + 1) * rank]
        total = total + jnp.concatenate((q, v), axis=1)
    rows = dot(place_ref[...], total.astype(BF16))
    pack = HEAD // (2 * rank)
    step = rows.shape[0] // pack
    packed = jnp.concatenate([rows[i * step : (i + 1) * step] for i in range(pack)], axis=1)
    out_ref[...] = packed.astype(BF16)


def join_body(*refs):
    total = refs[0][...].astype(F32)
    for ref in refs[1:-1]:
        total = total + ref[...].astype(F32)
    refs[-1][...] = total.astype(BF16)


def base_body(depth, start, stop, x_ref, q_ref, k_ref, v_ref, oq_ref, okv_ref):
    columns = k_ref.shape[0]
    narrow = jnp.zeros((HEAD - 2 * columns, depth), BF16)
    query, fresh = 0.0, 0.0
    for first in range(start, stop, depth):
        at = slice(first, first + depth)
        x = x_ref[:, at]
        query = query + dot(x, q_ref[at, :])
        both = (k_ref[:, at], v_ref[:, at])
        if 2 * columns < HEAD:
            both += (narrow,)
        fresh = fresh + dot_nt(x, jnp.concatenate(both, axis=0))
    oq_ref[...] = query
    okv_ref[...] = fresh


def turned(values, cosine, sine):
    lane = lax.broadcasted_iota(jnp.int32, values.shape, 1)
    width = values.shape[1]
    ahead = pltpu.roll(values, width - 1, 1)
    behind = pltpu.roll(values, 1, 1)
    return values * cosine + jnp.where(lane % 2 == 0, ahead, behind) * sine


def ready_body(
    rank, lows, *refs
):
    low_refs = refs[:lows]
    (
        oq_ref, okv_ref, oq2_ref, okv2_ref, unplace_ref, slot_ref, uq_ref, uv_ref, cos_ref, sin_ref, kcos_ref, ksin_ref,
        send_ref, out_ref,
    ) = refs[lows:]
    packed = low_refs[0][...].astype(F32)
    for ref in low_refs[1:]:
        packed = packed + ref[...].astype(F32)
    pack = HEAD // (2 * rank)
    low = jnp.concatenate(
        [packed[:, i * 2 * rank : (i + 1) * 2 * rank] for i in range(pack)], axis=0
    )
    low = dot(unplace_ref[...], low.astype(BF16)).astype(BF16)
    wide = uq_ref.shape[0]
    lane = lax.broadcasted_iota(jnp.int32, (low.shape[0], wide), 1)
    here = lane // rank == slot_ref[...]
    row = lax.broadcasted_iota(jnp.int32, (2 * rank, wide), 0)
    column = lax.broadcasted_iota(jnp.int32, (2 * rank, wide), 1)
    spread_q = jnp.where(column % rank == row, 1.0, 0.0).astype(BF16)
    spread_v = jnp.where(column % rank + rank == row, 1.0, 0.0).astype(BF16)
    wide_q = jnp.where(here, dot(low, spread_q), 0.0).astype(BF16)
    wide_v = jnp.where(here, dot(low, spread_v), 0.0).astype(BF16)
    query = oq_ref[...] + oq2_ref[...] + dot(wide_q, uq_ref[...])
    fresh = turned(okv_ref[...] + okv2_ref[...], kcos_ref[...], ksin_ref[...])
    columns = uv_ref.shape[1]
    value = dot(wide_v, uv_ref[...])
    pieces = [jnp.zeros((value.shape[0], columns), F32), value]
    if 2 * columns < HEAD:
        pieces.append(jnp.zeros((value.shape[0], HEAD - 2 * columns), F32))
    fresh = fresh + jnp.concatenate(pieces, axis=1)
    cosine, sine = cos_ref[...], sin_ref[...]
    parts = []
    for h in range(query.shape[1] // HEAD):
        parts.append(turned(query[:, h * HEAD : (h + 1) * HEAD], cosine, sine))
    parts.append(fresh)
    stacked = jnp.concatenate(parts, axis=0).astype(BF16)
    out_ref[...] = dot(send_ref[...], stacked).astype(BF16).reshape(out_ref.shape)


def attend_body(
    own, columns, index_ref, len_ref, x_ref, order_ref, k_ref, v_ref, nk_ref, nv_ref, ctx_ref, s_ref
):
    n, span = x_ref.shape[0], k_ref.shape[1]
    group = HEADS // KV_HEADS
    local = HEADS // n
    rows = own * STEPS
    mine = group * STEPS
    x = x_ref[...]
    queries = dot(order_ref[...], x.reshape(n * x.shape[1], HEAD)).astype(BF16)
    wide = x.astype(F32)
    first = rows * local
    fresh = [wide[i, first : first + rows] for i in range(n)]
    each = n // KV_HEADS
    keys, values = [], []
    for g in range(KV_HEADS):
        pieces = fresh[g * each : (g + 1) * each]
        keys.append(jnp.concatenate([p[:, :columns] for p in pieces], axis=1))
        values.append(jnp.concatenate([p[:, columns : 2 * columns] for p in pieces], axis=1))
    new_keys = jnp.concatenate(keys, axis=1)
    new_values = jnp.concatenate(values, axis=1)
    for b in range(own):
        at = slice(b * STEPS, (b + 1) * STEPS)
        nk_ref[b] = new_keys[at].astype(BF16)
        nv_ref[b] = new_values[at].astype(BF16)
    pad = jnp.zeros((16 - rows, HEAD), F32)
    keys = [jnp.concatenate((k, pad), axis=0).astype(BF16) for k in keys]
    values = [jnp.concatenate((v, pad), axis=0).astype(BF16) for v in values]
    scale = HEAD ** (-0.5)
    contexts = []
    for b in range(own):
        q = queries[b * KV_HEADS * mine : (b + 1) * KV_HEADS * mine]
        cached, newer = [], []
        for g in range(KV_HEADS):
            qg = q[g * mine : (g + 1) * mine]
            cached.append(dot_nt(qg, k_ref[b, :, g * HEAD : (g + 1) * HEAD]))
            newer.append(dot_nt(qg, keys[g]))
        cached = jnp.concatenate(cached, axis=0) * scale
        newer = jnp.concatenate(newer, axis=0) * scale
        place = lax.broadcasted_iota(jnp.int32, cached.shape, 1)
        cached = jnp.where(place < len_ref[index_ref[0] * own + b], cached, -1e30)
        step = lax.broadcasted_iota(jnp.int32, newer.shape, 0) % STEPS
        at = lax.broadcasted_iota(jnp.int32, newer.shape, 1) - b * STEPS
        newer = jnp.where((at >= 0) & (at <= step), newer, -1e30)
        top = jnp.maximum(
            jnp.max(cached, axis=1, keepdims=True), jnp.max(newer, axis=1, keepdims=True)
        )
        cached = jnp.exp(cached - top)
        newer = jnp.exp(newer - top)
        total = jnp.sum(cached, axis=1, keepdims=True) + jnp.sum(newer, axis=1, keepdims=True)
        cached = (cached / total).astype(BF16)
        newer = (newer / total).astype(BF16)
        for g in range(KV_HEADS):
            at_rows = slice(g * mine, (g + 1) * mine)
            part = dot(cached[at_rows], v_ref[b, :, g * HEAD : (g + 1) * HEAD])
            s_ref[(b * KV_HEADS + g) * mine : (b * KV_HEADS + g + 1) * mine] = part + dot(
                newer[at_rows], values[g]
            )
    step = local * STEPS
    half = KV_HEADS * mine
    for i in range(n):
        block = [s_ref[b * half + i * step : b * half + (i + 1) * step] for b in range(own)]
        ctx_ref[i] = jnp.concatenate(block, axis=0).astype(BF16)


def take_body(ctx_ref, take_ref, w_ref, a_ref, mine_ref, other_ref):
    rows = a_ref.shape[0]
    x = ctx_ref[...].reshape(-1, HEAD)
    taken = dot(take_ref[...], x).astype(BF16)
    for h in range(a_ref.shape[1] // HEAD):
        a_ref[:, h * HEAD : (h + 1) * HEAD] = taken[h * rows : (h + 1) * rows]
    out_body(0, a_ref, w_ref, mine_ref, other_ref)


def out_body(start, a_ref, w_ref, mine_ref, other_ref):
    half = mine_ref.shape[0]
    tile = 1024

    for at in range(0, mine_ref.shape[1], tile):
        product = dot(a_ref[...], w_ref[:, start + at : start + at + tile])
        mine_ref[:, at : at + tile] = product[:half]
        other_ref[:, at : at + tile] = product[half:]


def far_first_body(near, mine_ref, came_ref, *refs):
    total = mine_ref[...] + came_ref[...]
    rows = refs[0].shape[0] // near
    for f, ref in enumerate(refs):
        blocks = [(m * len(refs) + f) * rows for m in range(near)]
        value = jnp.concatenate([total[at : at + rows] for at in blocks], axis=0)
        ref[...] = value.astype(ref.dtype)


def near_body(mine_ref, came_ref, *refs):
    rows = refs[0].shape[0]
    total = mine_ref[...] + came_ref[...]
    refs[0][...] = total[:rows]
    for m, ref in enumerate(refs[1:], 1):
        ref[...] = total[m * rows : (m + 1) * rows].astype(BF16)


def far_body(came, *refs):
    total = refs[0][...]
    for ref in refs[1 : 1 + came]:
        total = total + ref[...].astype(F32)
    refs = refs[1 + came :]
    rows = refs[0].shape[0]
    refs[0][...] = total[:rows]
    for f, ref in enumerate(refs[1:], 1):
        ref[...] = total[f * rows : (f + 1) * rows].astype(BF16)


def last_body(longs, first_ref, second_ref, *refs):
    one_ref, two_ref = refs[-2:]
    totals = []
    for part in (refs[:longs], refs[longs:-2]):
        total = part[0][...]
        for ref in part[1:]:
            total = total + ref[...].astype(F32)
        totals.append(total)
    total = jnp.concatenate(totals, axis=1)
    own = one_ref.shape[0]
    one_ref[...] = (first_ref[...].astype(F32) + total[:own]).astype(BF16)
    two_ref[...] = (second_ref[...].astype(F32) + total[own:]).astype(BF16)


def shards(
    sizes,
    residual_first,
    residual_second,
    attention_norm_gain,
    query_matrix,
    key_matrix,
    value_matrix,
    output_matrix,
    query_down_weights,
    value_down_weights,
    query_up_weights,
    value_up_weights,
    rotated_key_cache,
    stored_value_cache,
    lengths,
    request_adapter,
    adapter_slot,
):
    far, near, cores = sizes
    n = far * near * cores
    index = lax.axis_index("serve")
    own, width = residual_first.shape
    adapters, _, rank = query_down_weights.shape
    query_cols = query_matrix.shape[1]
    key_cols = key_matrix.shape[1]
    local = query_cols // HEAD
    rows = own * STEPS
    all_rows = n * rows
    stored = query_up_weights.shape[0]

    def partner(f, m, c):
        pairs = []
        for z in range(far):
            for y in range(near):
                for k in range(cores):
                    to = (((z + f) % far) * near + (y + m) % near) * cores + (k + c) % cores
                    pairs.append(((z * near + y) * cores + k, to))
        return pairs

    def shift(value, f, m, c):
        return lax.ppermute(value, "serve", partner(f, m, c))

    frequency = whole_call(frequency_body, jax.ShapeDtypeStruct((1, HEAD), F32), (), cost=3.0)
    gain = attention_norm_gain.reshape(width // HEAD, HEAD)
    gain, frequency = lax.optimization_barrier((gain, frequency))
    normed = whole_call(
        norm_body,
        jax.ShapeDtypeStruct((rows, width), BF16),
        (residual_first, residual_second, gain),
        hbm=3,
        scratch=[
            pltpu.VMEM((own, width), BF16),
            pltpu.VMEM((own, width), BF16),
            pltpu.VMEM(gain.shape, BF16),
            pltpu.SemaphoreType.DMA((3,)),
        ],
        cost=1.0,
    )
    normed = normed[None]
    fars = [shift(normed, f, 0, 0) for f in range(1, far)]
    sent = -(-(rows * local + rows) // 8) * 8
    narrow = jax.ShapeDtypeStruct((all_rows, 1), jnp.int32)
    table = jax.ShapeDtypeStruct((all_rows, HEAD), F32)
    square = jax.ShapeDtypeStruct((all_rows, all_rows), BF16)
    slot, near_slot, cosine, sine, key_cosine, key_sine, place, unplace, send, order, take = whole_call(
        functools.partial(prep_body, sizes, rank, own, key_cols, adapters),
        (
            narrow,
            narrow,
            table,
            table,
            table,
            table,
            square,
            square,
            jax.ShapeDtypeStruct((n * sent, all_rows * (local + 1)), BF16),
            jax.ShapeDtypeStruct((own * HEADS * STEPS, n * sent), BF16),
            jax.ShapeDtypeStruct((all_rows * local, n * rows * local), BF16),
        ),
        (index[None], lengths, request_adapter, adapter_slot, frequency),
        smem=1,
        hbm=3,
        scratch=[
            pltpu.SMEM(lengths.shape, jnp.int32),
            pltpu.SMEM(request_adapter.shape, jnp.int32),
            pltpu.SMEM(adapter_slot.shape, jnp.int32),
            pltpu.SemaphoreType.DMA((3,)),
        ],
        cost=4.0,
    )
    slot, ready_rows = lax.optimization_barrier((slot, normed))
    nears = [shift(ready_rows, 0, m, 0) for m in range(1, near)]
    rest = jnp.concatenate(fars)
    groups = [jnp.concatenate([normed, *fars, *nears[:1]])]
    groups += [shift(rest, 0, m, 0) for m in range(1, near)]

    groups += [shift(part, 0, 0, c) for c in range(1, cores) for part in groups[:near]]

    query_down = jnp.swapaxes(query_down_weights, 1, 2).reshape(adapters * rank, width)
    value_down = jnp.swapaxes(value_down_weights, 1, 2).reshape(adapters * rank, width)
    packed_rows = all_rows * 2 * rank // HEAD
    x, low = whole_call(
        functools.partial(low_body, rank, len(groups)),
        (
            jax.ShapeDtypeStruct((all_rows, width), BF16),
            jax.ShapeDtypeStruct((packed_rows, HEAD), BF16),
        ),
        (*groups, query_down, value_down, near_slot, place),
        cost=0.3,
    )
    def base(start, stop):
        return whole_call(
            functools.partial(base_body, 2048, start, stop),
            (
                jax.ShapeDtypeStruct((all_rows, query_cols), F32),
                jax.ShapeDtypeStruct((all_rows, HEAD), F32),
            ),
            (x, query_matrix, key_matrix.T, value_matrix.T),
            cost=0.3,
        )

    lows = [shift(low, 0, m, c) for m in range(near) for c in range(cores) if m + c]
    base_q, base_kv = base(0, width // 2)
    low = whole_call(join_body, jax.ShapeDtypeStruct(low.shape, BF16), (low, *lows), cost=0.1)
    low, base_q = lax.optimization_barrier((low, base_q))
    lows = [low] + [shift(low, f, 0, 0) for f in range(1, far)]
    bases = (base_q, base_kv, *base(width // 2, width))

    ready = whole_call(
        functools.partial(ready_body, rank, len(lows)),
        jax.ShapeDtypeStruct((n, sent, HEAD), BF16),
        (
            *lows,
            *bases,
            unplace,
            slot,
            query_up_weights.reshape(stored * rank, query_cols),
            value_up_weights.reshape(stored * rank, key_cols),
            cosine,
            sine,
            key_cosine,
            key_sine,
            send,
        ),
        cost=0.9,
    )
    arrived = lax.all_to_all(ready, "serve", split_axis=0, concat_axis=0, tiled=True)

    fresh = jax.ShapeDtypeStruct((own, STEPS, KV_HEADS * HEAD), BF16)
    new_keys, new_values, context = whole_call(
        functools.partial(attend_body, own, key_cols),
        (fresh, fresh, jax.ShapeDtypeStruct((n, rows * local, HEAD), BF16)),
        (index[None], lengths, arrived, order, rotated_key_cache, stored_value_cache),
        smem=2,
        scratch=[pltpu.VMEM((own * HEADS * STEPS, HEAD), F32)],
        cost=1.0,
    )
    context = lax.all_to_all(context, "serve", split_axis=0, concat_axis=0, tiled=True)

    half = all_rows // cores
    cut = width * 5 // 8

    def kinds(count, columns):
        return (jax.ShapeDtypeStruct((count, columns), F32),) * 2

    taken, mine_long, other_long = whole_call(
        take_body,
        (jax.ShapeDtypeStruct((all_rows, query_cols), BF16),) + kinds(half, cut),
        (context, take, output_matrix),
        cost=0.4,
    )
    mine_short, other_short = whole_call(
        functools.partial(out_body, cut),
        kinds(half, width - cut),
        (taken, output_matrix),
        cost=0.3,
    )

    def kind(count, columns, dtype):
        return jax.ShapeDtypeStruct((count * rows, columns), dtype)

    keep, *others = whole_call(
        near_body,
        (kind(far, cut, F32),) + (kind(far, cut, BF16),) * (near - 1),
        (mine_long, shift(other_long, 0, 0, 1)),
        cost=0.1,
    )
    others = [shift(other, 0, m, 0) for m, other in enumerate(others, 1)]
    short, *sides = whole_call(
        functools.partial(far_first_body, near),
        (kind(near, width - cut, F32),) + (kind(near, width - cut, BF16),) * (far - 1),
        (mine_short, shift(other_short, 0, 0, 1)),
        cost=0.1,
    )
    sides = [shift(side, f, 0, 0) for f, side in enumerate(sides, 1)]
    keep, *others = whole_call(
        functools.partial(far_body, len(others)),
        (kind(1, cut, F32),) + (kind(1, cut, BF16),) * (far - 1),
        (keep, *others),
        cost=0.1,
    )
    others = [shift(other, f, 0, 0) for f, other in enumerate(others, 1)]
    short, *sides = whole_call(
        functools.partial(far_body, len(sides)),
        (kind(1, width - cut, F32),) + (kind(1, width - cut, BF16),) * (near - 1),
        (short, *sides),
        cost=0.1,
    )
    sides = [shift(side, 0, m, 0) for m, side in enumerate(sides, 1)]
    result = jax.ShapeDtypeStruct((own, width), BF16)
    out_one, out_two = whole_call(
        functools.partial(last_body, 1 + len(others)),
        (result, result),
        (residual_first, residual_second, keep, *others, short, *sides),
        cost=0.1,
    )
    return (out_one, out_two, new_keys, new_values)


def solution(mesh):
    n = mesh.shape["serve"]
    sizes = (n // 4, 2, 2)
    return jax.shard_map(
        functools.partial(shards, sizes),
        mesh=mesh,
        in_specs=(
            P(("replica", "serve"), None),
            P(("replica", "serve"), None),
            P(),
            P(None, "serve"),
            P(None, "serve"),
            P(None, "serve"),
            P("serve", None),
            P("serve", None, None),
            P("serve", None, None),
            P(None, None, "serve"),
            P(None, None, "serve"),
            P(("replica", "serve"), None, None),
            P(("replica", "serve"), None, None),
            P("replica"),
            P("replica"),
            P(),
        ),
        out_specs=(
            P(("replica", "serve"), None),
            P(("replica", "serve"), None),
            P(("replica", "serve"), None, None),
            P(("replica", "serve"), None, None),
        ),
        check_vma=False,
    )
```

```python
import functools
import math

import jax
import jax.numpy as jnp
from jax import lax
from jax.experimental import pallas as pl
from jax.experimental.pallas import tpu as pltpu
from jax.sharding import PartitionSpec as P

HEADS = 64
KV_HEADS = 8
HEAD = 128
STEPS = 2
LIMIT = 8 * 1024 * 1024
PEAK = 1.15e9
NT = (((1,), (1,)), ((), ()))
F32 = jnp.float32
BF16 = jnp.bfloat16


def dot(a, b):
    return jnp.dot(a, b, preferred_element_type=F32)


def dot_nt(a, b):
    return lax.dot_general(a, b, NT, preferred_element_type=F32)


def whole_call(body, out_shape, args, cost, smem=0, hbm=0, scratch=()):
    specs = [pl.BlockSpec(memory_space=pltpu.SMEM)] * smem
    specs += [pl.BlockSpec(memory_space=pltpu.HBM)] * hbm
    specs += [pl.BlockSpec(memory_space=pltpu.VMEM)] * (len(args) - smem - hbm)
    many = isinstance(out_shape, (tuple, list))
    vmem = pl.BlockSpec(memory_space=pltpu.VMEM)
    return pl.pallas_call(
        body,
        out_shape=out_shape,
        in_specs=specs,
        out_specs=tuple(vmem for _ in out_shape) if many else vmem,
        scratch_shapes=list(scratch),
        compiler_params=pltpu.CompilerParams(vmem_limit_bytes=LIMIT),
        cost_estimate=pl.CostEstimate(
            flops=int(cost * PEAK), bytes_accessed=0, transcendentals=0
        ),
    )(*args)


def scaled_frequency(pair_index):
    base = jnp.exp(pair_index.astype(F32) * (-2.0 * math.log(500000.0) / HEAD))
    wavelength = 2.0 * math.pi / base
    smooth = jnp.clip((8192.0 / wavelength - 1.0) / 3.0, 0.0, 1.0)
    return (1.0 - smooth) * base / 8.0 + smooth * base


def fetch(pairs, sems):
    copies = [
        pltpu.make_async_copy(source, target, sems.at[i])
        for i, (source, target) in enumerate(pairs)
    ]
    for copy in copies:
        copy.start()
    for copy in copies:
        copy.wait()


def norm_body(first_hbm, second_hbm, gain_hbm, out_ref, first_ref, second_ref, gain_ref, sems):
    fetch(((first_hbm, first_ref), (second_hbm, second_ref), (gain_hbm, gain_ref)), sems)
    gain = gain_ref[...].astype(F32)
    factors = []
    for ref in (first_ref, second_ref):
        values = ref[...].astype(F32)
        factors.append(lax.rsqrt(jnp.mean(values * values, axis=-1, keepdims=True) + 1e-05))
    factor = jnp.concatenate(factors, axis=0)
    for i in range(gain.shape[0]):
        at = slice(i * HEAD, (i + 1) * HEAD)
        values = jnp.concatenate((first_ref[:, at].astype(F32), second_ref[:, at].astype(F32)))
        out_ref[:, at] = (values * factor * gain[i : i + 1]).astype(BF16)


def frequency_body(out_ref):
    out_ref[...] = scaled_frequency(lax.broadcasted_iota(jnp.int32, out_ref.shape, 1) // 2)


def prep_body(
    sizes, rank, own, key_cols, adapters,
    index_ref, length_hbm, adapter_hbm, slot_hbm, frequency_ref,
    held_ref, local_ref, cos_ref, sin_ref, kcos_ref, ksin_ref, place_ref, unplace_ref, send_ref,
    order_ref, take_ref, length_ref, adapter_ref, slot_ref, sems,
):
    fetch(((length_hbm, length_ref), (adapter_hbm, adapter_ref), (slot_hbm, slot_ref)), sems)
    far, near, cores = sizes
    n = far * near * cores
    rows = own * STEPS
    all_rows = n * rows
    heads = HEADS // n
    sent = send_ref.shape[0] // n
    index = index_ref[0]
    core_at = index % cores
    near_at = index // cores % near
    far_at = index // (cores * near)

    def device_of(block, sign):
        c, m, f = block // (far * near), block // far % near, block % far
        f = (far_at + sign * f + far) % far
        m = (near_at + sign * m + near) % near
        c = (core_at + sign * c + cores) % cores
        return (f * near + m) * cores + c

    def iota(shape, axis):
        return lax.broadcasted_iota(jnp.int32, shape, axis)

    def split(row):
        return row // rows, row % rows // own, row % own

    block, step, mine = split(iota((all_rows, 1), 0))
    device = device_of(block, -1)
    request = device * own + mine
    length = jnp.zeros_like(request)
    adapter = jnp.zeros_like(request)
    for j in range(length_ref.shape[0]):
        length = jnp.where(request == j, length_ref[j], length)
        adapter = jnp.where(request == j, adapter_ref[j], adapter)
    slot = jnp.zeros_like(request)
    for j in range(slot_ref.shape[0]):
        slot = jnp.where(adapter == j, slot_ref[j], slot)
    held_ref[...] = slot
    local_ref[...] = slot - index * adapters
    position = (length + step).astype(F32)
    lane = iota((1, HEAD), 1)
    odd = jnp.where(lane % 2 == 0, -1.0, 1.0)
    angle = position * frequency_ref[...]
    cos_ref[...] = jnp.cos(angle)
    sin_ref[...] = jnp.sin(angle) * odd
    angle = position * scaled_frequency((index * key_cols + lane) % HEAD // 2)
    kcos_ref[...] = jnp.where(lane < key_cols, jnp.cos(angle), 1.0)
    ksin_ref[...] = jnp.where(lane < key_cols, jnp.sin(angle) * odd, 0.0)

    def hot(ref, row, column):
        ref[...] = jnp.where(row == column, 1.0, 0.0).astype(BF16)

    absolute = (device * STEPS + step) * own + mine
    hot(unplace_ref, absolute, iota((1, all_rows), 1))
    block, step, mine = split(iota((1, all_rows), 1))
    absolute = (device_of(block, -1) * STEPS + step) * own + mine
    hot(place_ref, iota((all_rows, 1), 0), absolute)

    column = iota((1, send_ref.shape[1]), 1)
    h = column // all_rows
    block, step, mine = split(column % all_rows)
    wanted = device_of(block, -1) * sent + jnp.where(
        h < heads, (mine * heads + h) * STEPS + step, rows * heads + mine * STEPS + step
    )
    hot(send_ref, iota((n * sent, 1), 0), wanted)

    row = iota((order_ref.shape[0], 1), 0)
    mine, head, step = row // (HEADS * STEPS), row // STEPS % HEADS, row % STEPS
    wanted = (head // heads) * sent + (mine * heads + head % heads) * STEPS + step
    hot(order_ref, wanted, iota((1, n * sent), 1))

    row = iota((take_ref.shape[0], 1), 0)
    h = row // all_rows
    block, step, mine = split(row % all_rows)
    wanted = device_of(block, 1) * rows * heads + (mine * heads + h) * STEPS + step
    hot(take_ref, wanted, iota((1, take_ref.shape[1]), 1))


def low_body(rank, groups, *refs):
    parts, (qd_ref, vd_ref, local_ref, place_ref, x_ref, out_ref) = refs[:groups], refs[groups:]
    rows = parts[0].shape[1]
    sets = max(1, 16 // rows)
    blocks = [(part, i) for part in parts for i in range(part.shape[0])]
    for first in range(0, len(blocks), sets):
        group = blocks[first : first + sets]
        for lane in range(0, x_ref.shape[1], 1024):
            lanes = slice(lane, lane + 1024)
            block = [part[i, :, lanes].astype(F32) for part, i in group]
            block = jnp.concatenate(block, axis=0).astype(BF16)
            x_ref[first * rows : (first + sets) * rows, lanes] = block
    adapters = qd_ref.shape[0] // rank
    maps = jnp.concatenate((qd_ref[...], vd_ref[...]), axis=0)
    low = dot_nt(x_ref[...], maps)
    lane = lax.broadcasted_iota(jnp.int32, low.shape, 1)
    low = jnp.where(lane // rank % adapters == local_ref[...], low, 0.0)
    total = 0.0
    for a in range(adapters):
        q = low[:, a * rank : (a + 1) * rank]
        v = low[:, (adapters + a) * rank : (adapters + a + 1) * rank]
        total = total + jnp.concatenate((q, v), axis=1)
    rows = dot(place_ref[...], total.astype(BF16))
    pack = HEAD // (2 * rank)
    step = rows.shape[0] // pack
    packed = jnp.concatenate([rows[i * step : (i + 1) * step] for i in range(pack)], axis=1)
    out_ref[...] = packed.astype(BF16)


def join_body(*refs):
    total = refs[0][...].astype(F32)
    for ref in refs[1:-1]:
        total = total + ref[...].astype(F32)
    refs[-1][...] = total.astype(BF16)


def base_body(depth, start, stop, x_ref, q_ref, k_ref, v_ref, oq_ref, okv_ref):
    columns = k_ref.shape[0]
    narrow = jnp.zeros((HEAD - 2 * columns, depth), BF16)
    query, fresh = 0.0, 0.0
    for first in range(start, stop, depth):
        at = slice(first, first + depth)
        x = x_ref[:, at]
        query = query + dot(x, q_ref[at, :])
        both = (k_ref[:, at], v_ref[:, at])
        if 2 * columns < HEAD:
            both += (narrow,)
        fresh = fresh + dot_nt(x, jnp.concatenate(both, axis=0))
    oq_ref[...] = query
    okv_ref[...] = fresh


def turned(values, cosine, sine):
    lane = lax.broadcasted_iota(jnp.int32, values.shape, 1)
    width = values.shape[1]
    ahead = pltpu.roll(values, width - 1, 1)
    behind = pltpu.roll(values, 1, 1)
    return values * cosine + jnp.where(lane % 2 == 0, ahead, behind) * sine


def ready_body(
    rank, lows, *refs
):
    low_refs = refs[:lows]
    (
        oq_ref, okv_ref, oq2_ref, okv2_ref, unplace_ref, slot_ref, uq_ref, uv_ref, cos_ref, sin_ref, kcos_ref, ksin_ref,
        send_ref, out_ref,
    ) = refs[lows:]
    packed = low_refs[0][...].astype(F32)
    for ref in low_refs[1:]:
        packed = packed + ref[...].astype(F32)
    pack = HEAD // (2 * rank)
    low = jnp.concatenate(
        [packed[:, i * 2 * rank : (i + 1) * 2 * rank] for i in range(pack)], axis=0
    )
    low = dot(unplace_ref[...], low.astype(BF16)).astype(BF16)
    wide = uq_ref.shape[0]
    lane = lax.broadcasted_iota(jnp.int32, (low.shape[0], wide), 1)
    here = lane // rank == slot_ref[...]
    row = lax.broadcasted_iota(jnp.int32, (2 * rank, wide), 0)
    column = lax.broadcasted_iota(jnp.int32, (2 * rank, wide), 1)
    spread_q = jnp.where(column % rank == row, 1.0, 0.0).astype(BF16)
    spread_v = jnp.where(column % rank + rank == row, 1.0, 0.0).astype(BF16)
    wide_q = jnp.where(here, dot(low, spread_q), 0.0).astype(BF16)
    wide_v = jnp.where(here, dot(low, spread_v), 0.0).astype(BF16)
    query = oq_ref[...] + oq2_ref[...] + dot(wide_q, uq_ref[...])
    fresh = turned(okv_ref[...] + okv2_ref[...], kcos_ref[...], ksin_ref[...])
    columns = uv_ref.shape[1]
    value = dot(wide_v, uv_ref[...])
    pieces = [jnp.zeros((value.shape[0], columns), F32), value]
    if 2 * columns < HEAD:
        pieces.append(jnp.zeros((value.shape[0], HEAD - 2 * columns), F32))
    fresh = fresh + jnp.concatenate(pieces, axis=1)
    cosine, sine = cos_ref[...], sin_ref[...]
    parts = []
    for h in range(query.shape[1] // HEAD):
        parts.append(turned(query[:, h * HEAD : (h + 1) * HEAD], cosine, sine))
    parts.append(fresh)
    stacked = jnp.concatenate(parts, axis=0).astype(BF16)
    out_ref[...] = dot(send_ref[...], stacked).astype(BF16).reshape(out_ref.shape)


def attend_body(
    own, columns, index_ref, len_ref, x_ref, order_ref, k_ref, v_ref, nk_ref, nv_ref, ctx_ref, s_ref
):
    n, span = x_ref.shape[0], k_ref.shape[1]
    group = HEADS // KV_HEADS
    local = HEADS // n
    rows = own * STEPS
    mine = group * STEPS
    x = x_ref[...]
    queries = dot(order_ref[...], x.reshape(n * x.shape[1], HEAD)).astype(BF16)
    wide = x.astype(F32)
    first = rows * local
    fresh = [wide[i, first : first + rows] for i in range(n)]
    each = n // KV_HEADS
    keys, values = [], []
    for g in range(KV_HEADS):
        pieces = fresh[g * each : (g + 1) * each]
        keys.append(jnp.concatenate([p[:, :columns] for p in pieces], axis=1))
        values.append(jnp.concatenate([p[:, columns : 2 * columns] for p in pieces], axis=1))
    new_keys = jnp.concatenate(keys, axis=1)
    new_values = jnp.concatenate(values, axis=1)
    for b in range(own):
        at = slice(b * STEPS, (b + 1) * STEPS)
        nk_ref[b] = new_keys[at].astype(BF16)
        nv_ref[b] = new_values[at].astype(BF16)
    pad = jnp.zeros((16 - rows, HEAD), F32)
    keys = [jnp.concatenate((k, pad), axis=0).astype(BF16) for k in keys]
    values = [jnp.concatenate((v, pad), axis=0).astype(BF16) for v in values]
    scale = HEAD ** (-0.5)
    contexts = []
    for b in range(own):
        q = queries[b * KV_HEADS * mine : (b + 1) * KV_HEADS * mine]
        cached, newer = [], []
        for g in range(KV_HEADS):
            qg = q[g * mine : (g + 1) * mine]
            cached.append(dot_nt(qg, k_ref[b, :, g * HEAD : (g + 1) * HEAD]))
            newer.append(dot_nt(qg, keys[g]))
        cached = jnp.concatenate(cached, axis=0) * scale
        newer = jnp.concatenate(newer, axis=0) * scale
        place = lax.broadcasted_iota(jnp.int32, cached.shape, 1)
        cached = jnp.where(place < len_ref[index_ref[0] * own + b], cached, -1e30)
        step = lax.broadcasted_iota(jnp.int32, newer.shape, 0) % STEPS
        at = lax.broadcasted_iota(jnp.int32, newer.shape, 1) - b * STEPS
        newer = jnp.where((at >= 0) & (at <= step), newer, -1e30)
        top = jnp.maximum(
            jnp.max(cached, axis=1, keepdims=True), jnp.max(newer, axis=1, keepdims=True)
        )
        cached = jnp.exp(cached - top)
        newer = jnp.exp(newer - top)
        total = jnp.sum(cached, axis=1, keepdims=True) + jnp.sum(newer, axis=1, keepdims=True)
        cached = (cached / total).astype(BF16)
        newer = (newer / total).astype(BF16)
        for g in range(KV_HEADS):
            at_rows = slice(g * mine, (g + 1) * mine)
            part = dot(cached[at_rows], v_ref[b, :, g * HEAD : (g + 1) * HEAD])
            s_ref[(b * KV_HEADS + g) * mine : (b * KV_HEADS + g + 1) * mine] = part + dot(
                newer[at_rows], values[g]
            )
    step = local * STEPS
    half = KV_HEADS * mine
    for i in range(n):
        block = [s_ref[b * half + i * step : b * half + (i + 1) * step] for b in range(own)]
        ctx_ref[i] = jnp.concatenate(block, axis=0).astype(BF16)


def take_body(ctx_ref, take_ref, w_ref, a_ref, mine_ref, other_ref):
    rows = a_ref.shape[0]
    x = ctx_ref[...].reshape(-1, HEAD)
    taken = dot(take_ref[...], x).astype(BF16)
    for h in range(a_ref.shape[1] // HEAD):
        a_ref[:, h * HEAD : (h + 1) * HEAD] = taken[h * rows : (h + 1) * rows]
    out_body(0, a_ref, w_ref, mine_ref, other_ref)


def out_body(start, a_ref, w_ref, mine_ref, other_ref):
    half = mine_ref.shape[0]
    tile = 512

    for at in range(0, mine_ref.shape[1], tile):
        product = dot(a_ref[...], w_ref[:, start + at : start + at + tile])
        mine_ref[:, at : at + tile] = product[:half]
        other_ref[:, at : at + tile] = product[half:]


def far_first_body(near, mine_ref, came_ref, *refs):
    total = mine_ref[...] + came_ref[...]
    rows = refs[0].shape[0] // near
    for f, ref in enumerate(refs):
        blocks = [(m * len(refs) + f) * rows for m in range(near)]
        value = jnp.concatenate([total[at : at + rows] for at in blocks], axis=0)
        ref[...] = value.astype(ref.dtype)


def near_body(mine_ref, came_ref, *refs):
    rows = refs[0].shape[0]
    total = mine_ref[...] + came_ref[...]
    refs[0][...] = total[:rows]
    for m, ref in enumerate(refs[1:], 1):
        ref[...] = total[m * rows : (m + 1) * rows].astype(BF16)


def far_body(came, *refs):
    total = refs[0][...]
    for ref in refs[1 : 1 + came]:
        total = total + ref[...].astype(F32)
    refs = refs[1 + came :]
    rows = refs[0].shape[0]
    refs[0][...] = total[:rows]
    for f, ref in enumerate(refs[1:], 1):
        ref[...] = total[f * rows : (f + 1) * rows].astype(BF16)


def last_body(longs, first_ref, second_ref, *refs):
    one_ref, two_ref = refs[-2:]
    totals = []
    for part in (refs[:longs], refs[longs:-2]):
        total = part[0][...]
        for ref in part[1:]:
            total = total + ref[...].astype(F32)
        totals.append(total)
    total = jnp.concatenate(totals, axis=1)
    own = one_ref.shape[0]
    one_ref[...] = (first_ref[...].astype(F32) + total[:own]).astype(BF16)
    two_ref[...] = (second_ref[...].astype(F32) + total[own:]).astype(BF16)


def shards(
    sizes,
    residual_first,
    residual_second,
    attention_norm_gain,
    query_matrix,
    key_matrix,
    value_matrix,
    output_matrix,
    query_down_weights,
    value_down_weights,
    query_up_weights,
    value_up_weights,
    rotated_key_cache,
    stored_value_cache,
    lengths,
    request_adapter,
    adapter_slot,
):
    far, near, cores = sizes
    n = far * near * cores
    index = lax.axis_index("serve")
    own, width = residual_first.shape
    adapters, _, rank = query_down_weights.shape
    query_cols = query_matrix.shape[1]
    key_cols = key_matrix.shape[1]
    local = query_cols // HEAD
    rows = own * STEPS
    all_rows = n * rows
    stored = query_up_weights.shape[0]

    def partner(f, m, c):
        pairs = []
        for z in range(far):
            for y in range(near):
                for k in range(cores):
                    to = (((z + f) % far) * near + (y + m) % near) * cores + (k + c) % cores
                    pairs.append(((z * near + y) * cores + k, to))
        return pairs

    def shift(value, f, m, c):
        return lax.ppermute(value, "serve", partner(f, m, c))

    frequency = whole_call(frequency_body, jax.ShapeDtypeStruct((1, HEAD), F32), (), cost=3.0)
    gain = attention_norm_gain.reshape(width // HEAD, HEAD)
    gain, frequency = lax.optimization_barrier((gain, frequency))
    normed = whole_call(
        norm_body,
        jax.ShapeDtypeStruct((rows, width), BF16),
        (residual_first, residual_second, gain),
        hbm=3,
        scratch=[
            pltpu.VMEM((own, width), BF16),
            pltpu.VMEM((own, width), BF16),
            pltpu.VMEM(gain.shape, BF16),
            pltpu.SemaphoreType.DMA((3,)),
        ],
        cost=1.0,
    )
    normed = normed[None]
    fars = [shift(normed, f, 0, 0) for f in range(1, far)]
    sent = -(-(rows * local + rows) // 8) * 8
    narrow = jax.ShapeDtypeStruct((all_rows, 1), jnp.int32)
    table = jax.ShapeDtypeStruct((all_rows, HEAD), F32)
    square = jax.ShapeDtypeStruct((all_rows, all_rows), BF16)
    slot, near_slot, cosine, sine, key_cosine, key_sine, place, unplace, send, order, take = whole_call(
        functools.partial(prep_body, sizes, rank, own, key_cols, adapters),
        (
            narrow,
            narrow,
            table,
            table,
            table,
            table,
            square,
            square,
            jax.ShapeDtypeStruct((n * sent, all_rows * (local + 1)), BF16),
            jax.ShapeDtypeStruct((own * HEADS * STEPS, n * sent), BF16),
            jax.ShapeDtypeStruct((all_rows * local, n * rows * local), BF16),
        ),
        (index[None], lengths, request_adapter, adapter_slot, frequency),
        smem=1,
        hbm=3,
        scratch=[
            pltpu.SMEM(lengths.shape, jnp.int32),
            pltpu.SMEM(request_adapter.shape, jnp.int32),
            pltpu.SMEM(adapter_slot.shape, jnp.int32),
            pltpu.SemaphoreType.DMA((3,)),
        ],
        cost=4.0,
    )
    slot, ready_rows = lax.optimization_barrier((slot, normed))
    nears = [shift(ready_rows, 0, m, 0) for m in range(1, near)]
    rest = jnp.concatenate(fars)
    groups = [jnp.concatenate([normed, *fars, *nears[:1]])]
    groups += [shift(rest, 0, m, 0) for m in range(1, near)]

    groups += [shift(part, 0, 0, c) for c in range(1, cores) for part in groups[:near]]

    query_down = jnp.swapaxes(query_down_weights, 1, 2).reshape(adapters * rank, width)
    value_down = jnp.swapaxes(value_down_weights, 1, 2).reshape(adapters * rank, width)
    packed_rows = all_rows * 2 * rank // HEAD
    x, low = whole_call(
        functools.partial(low_body, rank, len(groups)),
        (
            jax.ShapeDtypeStruct((all_rows, width), BF16),
            jax.ShapeDtypeStruct((packed_rows, HEAD), BF16),
        ),
        (*groups, query_down, value_down, near_slot, place),
        cost=0.3,
    )
    def base(start, stop):
        return whole_call(
            functools.partial(base_body, 2048, start, stop),
            (
                jax.ShapeDtypeStruct((all_rows, query_cols), F32),
                jax.ShapeDtypeStruct((all_rows, HEAD), F32),
            ),
            (x, query_matrix, key_matrix.T, value_matrix.T),
            cost=0.3,
        )

    lows = [shift(low, 0, m, c) for m in range(near) for c in range(cores) if m + c]
    base_q, base_kv = base(0, width // 2)
    low = whole_call(join_body, jax.ShapeDtypeStruct(low.shape, BF16), (low, *lows), cost=0.1)
    low, base_q = lax.optimization_barrier((low, base_q))
    lows = [low] + [shift(low, f, 0, 0) for f in range(1, far)]
    bases = (base_q, base_kv, *base(width // 2, width))

    ready = whole_call(
        functools.partial(ready_body, rank, len(lows)),
        jax.ShapeDtypeStruct((n, sent, HEAD), BF16),
        (
            *lows,
            *bases,
            unplace,
            slot,
            query_up_weights.reshape(stored * rank, query_cols),
            value_up_weights.reshape(stored * rank, key_cols),
            cosine,
            sine,
            key_cosine,
            key_sine,
            send,
        ),
        cost=0.9,
    )
    arrived = lax.all_to_all(ready, "serve", split_axis=0, concat_axis=0, tiled=True)

    fresh = jax.ShapeDtypeStruct((own, STEPS, KV_HEADS * HEAD), BF16)
    new_keys, new_values, context = whole_call(
        functools.partial(attend_body, own, key_cols),
        (fresh, fresh, jax.ShapeDtypeStruct((n, rows * local, HEAD), BF16)),
        (index[None], lengths, arrived, order, rotated_key_cache, stored_value_cache),
        smem=2,
        scratch=[pltpu.VMEM((own * HEADS * STEPS, HEAD), F32)],
        cost=1.0,
    )
    context = lax.all_to_all(context, "serve", split_axis=0, concat_axis=0, tiled=True)

    half = all_rows // cores
    cut = width * 9 // 16

    def kinds(count, columns):
        return (jax.ShapeDtypeStruct((count, columns), F32),) * 2

    taken, mine_long, other_long = whole_call(
        take_body,
        (jax.ShapeDtypeStruct((all_rows, query_cols), BF16),) + kinds(half, cut),
        (context, take, output_matrix),
        cost=0.4,
    )
    mine_short, other_short = whole_call(
        functools.partial(out_body, cut),
        kinds(half, width - cut),
        (taken, output_matrix),
        cost=0.3,
    )

    def kind(count, columns, dtype):
        return jax.ShapeDtypeStruct((count * rows, columns), dtype)

    keep, *others = whole_call(
        near_body,
        (kind(far, cut, F32),) + (kind(far, cut, BF16),) * (near - 1),
        (mine_long, shift(other_long, 0, 0, 1)),
        cost=0.1,
    )
    others = [shift(other, 0, m, 0) for m, other in enumerate(others, 1)]
    short, *sides = whole_call(
        functools.partial(far_first_body, near),
        (kind(near, width - cut, F32),) + (kind(near, width - cut, BF16),) * (far - 1),
        (mine_short, shift(other_short, 0, 0, 1)),
        cost=0.1,
    )
    sides = [shift(side, f, 0, 0) for f, side in enumerate(sides, 1)]
    keep, *others = whole_call(
        functools.partial(far_body, len(others)),
        (kind(1, cut, F32),) + (kind(1, cut, BF16),) * (far - 1),
        (keep, *others),
        cost=0.1,
    )
    others = [shift(other, f, 0, 0) for f, other in enumerate(others, 1)]
    short, *sides = whole_call(
        functools.partial(far_body, len(sides)),
        (kind(1, width - cut, F32),) + (kind(1, width - cut, BF16),) * (near - 1),
        (short, *sides),
        cost=0.1,
    )
    sides = [shift(side, 0, m, 0) for m, side in enumerate(sides, 1)]
    result = jax.ShapeDtypeStruct((own, width), BF16)
    out_one, out_two = whole_call(
        functools.partial(last_body, 1 + len(others)),
        (result, result),
        (residual_first, residual_second, keep, *others, short, *sides),
        cost=0.1,
    )
    return (out_one, out_two, new_keys, new_values)


def solution(mesh):
    n = mesh.shape["serve"]
    sizes = (n // 4, 2, 2)
    return jax.shard_map(
        functools.partial(shards, sizes),
        mesh=mesh,
        in_specs=(
            P(("replica", "serve"), None),
            P(("replica", "serve"), None),
            P(),
            P(None, "serve"),
            P(None, "serve"),
            P(None, "serve"),
            P("serve", None),
            P("serve", None, None),
            P("serve", None, None),
            P(None, None, "serve"),
            P(None, None, "serve"),
            P(("replica", "serve"), None, None),
            P(("replica", "serve"), None, None),
            P("replica"),
            P("replica"),
            P(),
        ),
        out_specs=(
            P(("replica", "serve"), None),
            P(("replica", "serve"), None),
            P(("replica", "serve"), None, None),
            P(("replica", "serve"), None, None),
        ),
        check_vma=False,
    )
```
